32 devices in a mesh: rep: 2 (over x), shard: 16 (over z, y, core).
Axes of the slice: x: 2, y: 2, z: 4, core: 2. Of those that a mesh axis runs over, the one named last changes fastest.
Arguments:
- hidden_in: bfloat16 [4096, 2048], P(('rep', 'shard')), may hold values from -6 to 6
- segments: int32 [32, 128], P(('rep', 'shard')), may hold values from 0 to 7, never falling along the last dimension, each value on 1 to 64 neighbouring positions
- w_query: bfloat16 [2048, 2048], P('shard'), may hold values from -0.125 to 0.125
- w_key: bfloat16 [2048, 2048], P('shard'), may hold values from -0.125 to 0.125
- w_value: bfloat16 [2048, 2048], P('shard'), may hold values from -0.125 to 0.125
- w_output: bfloat16 [2048, 2048], P('shard'), may hold values from -0.125 to 0.125
- query_gain: bfloat16 [2048], P('shard'), may hold values from 0.099609375 to 1.8984375
- key_gain: bfloat16 [2048], P('shard'), may hold values from 0.099609375 to 1.8984375
- attn_gain: bfloat16 [2048], P('shard'), may hold values from 0.099609375 to 1.8984375
- w_gate: bfloat16 [2048, 8192], P('shard'), may hold values from -0.125 to 0.125
- w_up: bfloat16 [2048, 8192], P('shard'), may hold values from -0.125 to 0.125
- w_down: bfloat16 [8192, 2048], P('shard'), may hold values from -0.0625 to 0.0625
- ffn_gain: bfloat16 [2048], P('shard'), may hold values from 0.099609375 to 1.8984375
- out_cotangent: bfloat16 [4096, 2048], P(('rep', 'shard')), may hold values from -6 to 6
Outputs:
- hidden_out: bfloat16 [4096, 2048], P(('rep', 'shard'))
- hidden_grad: bfloat16 [4096, 2048], P(('rep', 'shard'))
- grad_query: float32 [2048, 2048], P('shard')
- grad_key: float32 [2048, 2048], P('shard')
- grad_value: float32 [2048, 2048], P('shard')
- grad_output: float32 [2048, 2048], P('shard')
- grad_query_gain: float32 [2048], P('shard')
- grad_key_gain: float32 [2048], P('shard')
- grad_attn_gain: float32 [2048], P('shard')
- grad_gate: float32 [2048, 8192], P('shard')
- grad_up: float32 [2048, 8192], P('shard')
- grad_down: float32 [8192, 2048], P('shard')
- grad_ffn_gain: float32 [2048], P('shard')
The draws below stay inside these ranges and needn't reach their ends.
Inputs may be any that keep to these rules, and one draw needn't show every extreme that they name: `segments`: in each sequence the document numbers never fall; each document has 1 to 64 tokens, and one document of each sequence has exactly that many.
All inputs are finite; a program needn't handle non-finite values.
Results may differ from the reference program's by a relative error of at most 0.018.
Values may be sent and summed in bfloat16 or wider, within the bound.
A program may use at most 512 MiB of HBM per device.

```python
import math
import jax
import jax.numpy as jnp
import numpy as np
from jax import lax

D = 2048
HEADS = 16
HEAD_DIM = 128
FF = 8192
TOK_DEV = 128
DOCS = 8
SEQS = 32
TOKENS = 4096


def block_levels(key, dims, pieces, low, high):
    gain = 1.0
    for dim, shards_of in pieces:
        draws = jax.random.uniform(jax.random.fold_in(jax.random.fold_in(key, 6), dim), (shards_of,), jnp.float32, low / len(pieces), high / len(pieces))
        gain = gain * jnp.repeat(jnp.exp(draws), dims[dim] // shards_of).reshape((-1,) + (1,) * (len(dims) - 1 - dim))
    return gain


def profile(number_of, total, limit, skew):
    weights = [(1 << 20) // math.isqrt(rank ** skew) + 1 for rank in range(2, number_of + 1)]
    surplus, counts = total - limit - (number_of - 1), [1] * (number_of - 1)
    while surplus > 0:
        movable = [i for i in range(number_of - 1) if counts[i] < limit]
        pool, budget = sum([weights[i] for i in movable]), surplus
        for i in movable:
            extra = min(limit - counts[i], max(1, budget * weights[i] // pool), surplus)
            counts[i] = counts[i] + extra
            surplus = surplus - extra
    return np.array([limit] + counts)


def ragged_sizes(rng, number_of, total, bound, skew):
    if number_of == 2:
        one = jax.random.randint(rng, (), max(1, total - bound), min(bound, total - 1) + 1)
        return jnp.stack([one, total - one])
    sizes = jnp.asarray(profile(number_of, total, bound, skew), jnp.int32)
    couples = (number_of - 1) // 2
    donor, receiver = sizes[1:1 + 2 * couples:2], sizes[2:2 + 2 * couples:2]
    slack = jnp.minimum(donor - 1, bound - receiver)
    passed = jax.random.randint(jax.random.fold_in(rng, 1), (couples,), 0, 1 << 20) % (slack + 1)
    sizes = sizes.at[1:1 + 2 * couples:2].set(donor - passed).at[2:2 + 2 * couples:2].set(receiver + passed)
    return sizes[jax.random.permutation(jax.random.fold_in(rng, 2), number_of)]


def bell_draw(stream_key, shape, deviation, reach, shards=(), kind=jnp.bfloat16):
    entries = deviation * jax.random.normal(stream_key, shape, jnp.float32)
    if shards:
        entries = entries * block_levels(stream_key, shape, shards, -0.22, 0.18)
    return jnp.clip(entries, -reach, reach).astype(kind)


def setup_inputs(seed: int = 0) -> dict:
    arg_keys = jax.random.split(jax.random.key(seed), 15)
    hidden_in = bell_draw(arg_keys[0], (TOKENS, D), 1.0, 6.0, ((0, 32),))
    segments = jax.vmap(lambda own: jnp.searchsorted(jnp.cumsum(ragged_sizes(own, DOCS, TOK_DEV, TOK_DEV // 2, 2)), jnp.arange(TOK_DEV), side="right"))(jax.random.split(arg_keys[1], SEQS)).reshape((SEQS, TOK_DEV)).astype(jnp.int32)
    w_query = bell_draw(arg_keys[2], (D, D), D ** -0.5, 0.125, ((0, 16),))
    w_key = bell_draw(arg_keys[3], (D, D), D ** -0.5, 0.125, ((0, 16),))
    w_value = bell_draw(arg_keys[4], (D, D), D ** -0.5, 0.125, ((0, 16),))
    w_output = bell_draw(arg_keys[5], (D, D), D ** -0.5, 0.125, ((0, 16),))
    query_gain = jnp.clip(1.0 + 0.18 * jax.random.normal(arg_keys[6], (D,), jnp.float32), 0.099609375, 1.8984375).astype(jnp.bfloat16)
    key_gain = jnp.clip(1.0 + 0.18 * jax.random.normal(arg_keys[7], (D,), jnp.float32), 0.099609375, 1.8984375).astype(jnp.bfloat16)
    attn_gain = jnp.clip(1.0 + 0.18 * jax.random.normal(arg_keys[8], (D,), jnp.float32), 0.099609375, 1.8984375).astype(jnp.bfloat16)
    w_gate = bell_draw(arg_keys[9], (D, FF), D ** -0.5, 0.125, ((0, 16),))
    w_up = bell_draw(arg_keys[10], (D, FF), D ** -0.5, 0.125, ((0, 16),))
    w_down = bell_draw(arg_keys[11], (FF, D), FF ** -0.5, 0.0625, ((0, 16),))
    ffn_gain = jnp.clip(1.0 + 0.18 * jax.random.normal(arg_keys[12], (D,), jnp.float32), 0.099609375, 1.8984375).astype(jnp.bfloat16)
    out_cotangent = bell_draw(arg_keys[13], (TOKENS, D), 1.0, 6.0, ((0, 32),))
    return {"hidden_in": hidden_in, "segments": segments, "w_query": w_query, "w_key": w_key, "w_value": w_value, "w_output": w_output, "query_gain": query_gain, "key_gain": key_gain, "attn_gain": attn_gain, "w_gate": w_gate, "w_up": w_up, "w_down": w_down, "ffn_gain": ffn_gain, "out_cotangent": out_cotangent}


epsilon = 1e-06
theta_base = 500000.0
neg_fill = -1e+30

@jax.custom_vjp
def low(v):
    return lax.optimization_barrier(v.astype(jnp.bfloat16)).astype(jnp.float32)

@jax.custom_vjp
def low_back(v):
    return v

def low_keep(v):
    return (low(v), None)

def low_pass(kept, grad):
    return (grad,)

def back_keep(v):
    return (v, None)

def back_low(kept, grad):
    return (low(grad),)
low.defvjp(low_keep, low_pass)
low_back.defvjp(back_keep, back_low)

def rms_scale(values):
    return lax.rsqrt(lax.optimization_barrier(jnp.mean(values * values, axis=-1, keepdims=True)) + epsilon)

def rotate(values, cosines, sines):
    half_dim = values.shape[-1] // 2
    first_half = values[..., :half_dim]
    second = values[..., half_dim:]
    return jnp.concatenate([first_half * cosines - second * sines, second * cosines + first_half * sines], axis=-1)

def forward(hidden, params, doc_ids):
    w_query, w_key, w_value, w_output, query_gain, key_gain, attn_gain, w_gate, w_up, w_down, ffn_gain = params
    group_seqs = doc_ids.shape[0]
    seq_len = doc_ids.shape[1]
    token_rows = hidden.shape[0]
    highest = lax.Precision.HIGHEST
    earlier = lax.optimization_barrier(jnp.sum((doc_ids[:, None, :] < doc_ids[:, :, None]).astype(jnp.int32), axis=2))
    positions = jnp.arange(seq_len, dtype=jnp.int32)[None, :] - earlier
    half_dim = HEAD_DIM // 2
    inverse = jnp.exp(jnp.arange(half_dim, dtype=jnp.float32) * (-2.0 * math.log(theta_base) / HEAD_DIM))
    angles = positions.astype(jnp.float32)[:, :, None] * inverse[None, None, :]
    cosines = jnp.cos(angles)[:, :, None, :]
    sines = jnp.sin(angles)[:, :, None, :]

    def norm_rope(raw_proj, gain_vec):
        normed = raw_proj * rms_scale(raw_proj) * gain_vec
        return rotate(normed.reshape(group_seqs, seq_len, HEADS, HEAD_DIM), cosines, sines)
    query_raw = low_back(jnp.dot(hidden, w_query, precision=highest))
    key_raw = low_back(jnp.dot(hidden, w_key, precision=highest))
    value_low = low(low_back(jnp.dot(hidden, w_value, precision=highest))).reshape(group_seqs, seq_len, HEADS, HEAD_DIM)
    query_low = low(norm_rope(query_raw, query_gain))
    key_low = low(norm_rope(key_raw, key_gain))
    scores = low_back(jnp.einsum('gqhd,gkhd->ghqk', query_low, key_low, precision=highest) * HEAD_DIM ** (-0.5))
    token_idx = jnp.arange(seq_len)
    allowed = (doc_ids[:, :, None] == doc_ids[:, None, :]) & (token_idx[:, None] >= token_idx[None, :])[None]
    scores = jnp.where(allowed[:, None], scores, neg_fill)
    log_norm = jax.nn.logsumexp(scores, axis=-1, keepdims=True)
    attn_prob = low(jnp.exp(scores - log_norm))
    mixed = jnp.einsum('ghqk,gkhd->gqhd', attn_prob, value_low, precision=highest).reshape(token_rows, D)
    mixed_low = low(low_back(mixed))
    attn_out = low_back(jnp.dot(mixed_low, w_output, precision=highest))
    resid = hidden + attn_out * rms_scale(attn_out) * attn_gain
    resid_low = low(resid)
    gate_proj = low_back(jnp.dot(resid_low, w_gate, precision=highest))
    up_proj = low_back(jnp.dot(resid_low, w_up, precision=highest))
    hidden_ffn = low(jax.nn.silu(gate_proj) * up_proj)
    ffn_out = low_back(jnp.dot(hidden_ffn, w_down, precision=highest))
    return resid + ffn_out * rms_scale(ffn_out) * ffn_gain

def reference(hidden_in, segments, w_query, w_key, w_value, w_output, query_gain, key_gain, attn_gain, w_gate, w_up, w_down, ffn_gain, out_cotangent):
    weights = tuple((entry.astype(jnp.float32) for entry in (w_query, w_key, w_value, w_output, query_gain, key_gain, attn_gain, w_gate, w_up, w_down, ffn_gain)))
    group_seqs = math.gcd(SEQS, max(1, 4096 // TOK_DEV))
    block_count = SEQS // group_seqs
    hidden_blocks = hidden_in.reshape(block_count, group_seqs * TOK_DEV, D)
    seg_blocks = segments.reshape(block_count, group_seqs, TOK_DEV)
    cot_blocks = out_cotangent.reshape(block_count, group_seqs * TOK_DEV, D)

    def scan_step(totals, block_item):
        hidden_block, seg_block, cot_block = block_item

        def run_layer(hidden, *params):
            return forward(hidden, params, seg_block)
        block_out, pullback = jax.vjp(run_layer, hidden_block.astype(jnp.float32), *weights)
        gradients = pullback(cot_block.astype(jnp.float32))
        totals = tuple((prior + fresh for prior, fresh in zip(totals, gradients[1:])))
        return (totals, (block_out.astype(jnp.bfloat16), gradients[0].astype(jnp.bfloat16)))
    start_totals = tuple((jnp.zeros(entry.shape, jnp.float32) for entry in weights))
    totals, (out_blocks, grad_blocks) = lax.scan(scan_step, start_totals, (hidden_blocks, seg_blocks, cot_blocks))
    return (out_blocks.reshape(TOKENS, D), grad_blocks.reshape(TOKENS, D), totals[0], totals[1], totals[2], totals[3], totals[4], totals[5], totals[6], totals[7], totals[8], totals[9], totals[10])
```

```python
import math

import jax
import jax.numpy as jnp
from jax import lax
from jax.sharding import PartitionSpec as P

HEADS = 16
HEAD_DIM = 128


epsilon = 1e-06
theta_base = 500000.0
neg_fill = -1e30


def rms_scale(values):
    return lax.rsqrt(jnp.mean(values * values, axis=-1, keepdims=True) + epsilon)


def rms_back(upstream, normed, row_scale):
    return row_scale * (upstream - normed * jnp.mean(upstream * normed, axis=-1, keepdims=True))


def rotate(values, cosines, sines):
    half_dim = values.shape[-1] // 2
    first_half = values[..., :half_dim]
    second = values[..., half_dim:]
    return jnp.concatenate(
        [first_half * cosines - second * sines, second * cosines + first_half * sines], axis=-1
    )


def dot_back(left_side, right_side):
    return lax.dot_general(
        left_side, right_side, (((1,), (1,)), ((), ())), preferred_element_type=jnp.float32
    )


def col_term(left_side, right_side):

    def block_term(row_start, row_count):
        return lax.dot_general(
            left_side, right_side, (((0,), (0,)), ((), ())), preferred_element_type=jnp.float32
        )

    return block_term


def on_device_general(
    hidden_in,
    segments,
    w_query,
    w_key,
    w_value,
    w_output,
    query_gain,
    key_gain,
    attn_gain,
    w_gate,
    w_up,
    w_down,
    ffn_gain,
    out_cotangent,
):
    length = hidden_in.shape[0]
    model_width = hidden_in.shape[1]
    ffn_width = w_gate.shape[1]
    factor = HEAD_DIM ** (-0.5)
    doc_row = segments[0]
    earlier = jnp.sum((doc_row[None, :] < doc_row[:, None]).astype(jnp.int32), axis=1)
    positions = jnp.arange(length, dtype=jnp.int32) - earlier
    half_dim = HEAD_DIM // 2
    inverse = jnp.exp(
        jnp.arange(half_dim, dtype=jnp.float32) * (-2.0 * math.log(theta_base) / HEAD_DIM)
    )
    angles = positions.astype(jnp.float32)[:, None] * inverse[None, :]
    cosines = jnp.cos(angles)[:, None, :]
    sines = jnp.sin(angles)[:, None, :]
    token_idx = jnp.arange(length)
    allowed = (doc_row[:, None] == doc_row[None, :]) & (token_idx[:, None] >= token_idx[None, :])

    def reduce_rows(term_fn, local_rows):
        return lax.psum_scatter(
            term_fn(jnp.int32(0), local_rows * lax.axis_size("shard")),
            "shard",
            scatter_dimension=0,
            tiled=True,
        )

    def norm_rope(raw_proj, gain_vec):
        normed = raw_proj * rms_scale(raw_proj) * gain_vec
        return rotate(normed.reshape(length, HEADS, HEAD_DIM), cosines, sines)

    def attend_scores(query_low, key_low):
        scores = (
            jnp.einsum("qhd,khd->hqk", query_low, key_low, preferred_element_type=jnp.float32)
            * factor
        )
        return jnp.where(allowed[None], scores, neg_fill)

    full_query, full_key, full_value, gain_query, gain_key = (
        lax.all_gather(w_query, "shard", axis=0, tiled=True),
        lax.all_gather(w_key, "shard", axis=0, tiled=True),
        lax.all_gather(w_value, "shard", axis=0, tiled=True),
        lax.all_gather(query_gain, "shard", axis=0, tiled=True),
        lax.all_gather(key_gain, "shard", axis=0, tiled=True),
    )
    query_raw = jnp.dot(hidden_in, full_query, preferred_element_type=jnp.float32)
    key_raw = jnp.dot(hidden_in, full_key, preferred_element_type=jnp.float32)
    query_low = norm_rope(query_raw, gain_query.astype(jnp.float32)).astype(jnp.bfloat16)
    key_low = norm_rope(key_raw, gain_key.astype(jnp.float32)).astype(jnp.bfloat16)
    value_low = (
        jnp.dot(hidden_in, full_value, preferred_element_type=jnp.float32)
        .astype(jnp.bfloat16)
        .reshape(length, HEADS, HEAD_DIM)
    )
    scores = attend_scores(query_low, key_low)
    row_peak = jnp.max(scores, axis=-1, keepdims=True)
    log_norm = row_peak + jnp.log(jnp.sum(jnp.exp(scores - row_peak), axis=-1, keepdims=True))
    attn_prob = jnp.exp(scores - log_norm)
    mixed_low = (
        jnp.einsum(
            "hqk,khd->qhd",
            attn_prob.astype(jnp.bfloat16),
            value_low,
            preferred_element_type=jnp.float32,
        )
        .reshape(length, model_width)
        .astype(jnp.bfloat16)
    )
    full_output, gain_attn = (
        lax.all_gather(w_output, "shard", axis=0, tiled=True),
        lax.all_gather(attn_gain, "shard", axis=0, tiled=True),
    )
    attn_out = jnp.dot(mixed_low, full_output, preferred_element_type=jnp.float32)
    attn_rms = rms_scale(attn_out)
    attn_normed = attn_out * attn_rms
    resid = hidden_in.astype(jnp.float32) + attn_normed * gain_attn.astype(jnp.float32)
    resid_low = resid.astype(jnp.bfloat16)
    full_gate, full_up = (
        lax.all_gather(w_gate, "shard", axis=0, tiled=True),
        lax.all_gather(w_up, "shard", axis=0, tiled=True),
    )
    gate_proj = jnp.dot(resid_low, full_gate, preferred_element_type=jnp.float32)
    up_proj = jnp.dot(resid_low, full_up, preferred_element_type=jnp.float32)
    gate_sig = jax.nn.sigmoid(gate_proj)
    hidden_ffn = (gate_proj * gate_sig * up_proj).astype(jnp.bfloat16)
    full_down, gain_ffn = (
        lax.all_gather(w_down, "shard", axis=0, tiled=True),
        lax.all_gather(ffn_gain, "shard", axis=0, tiled=True),
    )
    ffn_out = jnp.dot(hidden_ffn, full_down, preferred_element_type=jnp.float32)
    ffn_rms = rms_scale(ffn_out)
    ffn_normed = ffn_out * ffn_rms
    hidden_out = (resid + ffn_normed * gain_ffn.astype(jnp.float32)).astype(jnp.bfloat16)
    grad_out = out_cotangent.astype(jnp.float32)
    back_down, back_fgain = (
        lax.all_gather(w_down, "shard", axis=0, tiled=True),
        lax.all_gather(ffn_gain, "shard", axis=0, tiled=True),
    )
    ffn_gain_term = jnp.sum(grad_out * ffn_normed, axis=0)
    d_ffn_low = rms_back(grad_out * back_fgain.astype(jnp.float32), ffn_normed, ffn_rms).astype(
        jnp.bfloat16
    )
    down_grad = reduce_rows(col_term(hidden_ffn, d_ffn_low), w_down.shape[0])
    d_hidden_ffn = dot_back(d_ffn_low, back_down)
    d_gate_low = (d_hidden_ffn * up_proj * gate_sig * (1.0 + gate_proj * (1.0 - gate_sig))).astype(
        jnp.bfloat16
    )
    d_up_low = (d_hidden_ffn * gate_proj * gate_sig).astype(jnp.bfloat16)
    ffn_in_grad = reduce_rows(
        col_term(resid_low, jnp.concatenate([d_gate_low, d_up_low], axis=1)), w_gate.shape[0]
    )
    back_gate, back_up = (
        lax.all_gather(w_gate, "shard", axis=0, tiled=True),
        lax.all_gather(w_up, "shard", axis=0, tiled=True),
    )
    d_resid = grad_out + dot_back(d_gate_low, back_gate) + dot_back(d_up_low, back_up)
    back_output, back_again = (
        lax.all_gather(w_output, "shard", axis=0, tiled=True),
        lax.all_gather(attn_gain, "shard", axis=0, tiled=True),
    )
    attn_gain_term = jnp.sum(d_resid * attn_normed, axis=0)
    d_attn_low = rms_back(d_resid * back_again.astype(jnp.float32), attn_normed, attn_rms).astype(
        jnp.bfloat16
    )
    out_grad = reduce_rows(col_term(mixed_low, d_attn_low), w_output.shape[0])
    d_mixed_low = (
        dot_back(d_attn_low, back_output).astype(jnp.bfloat16).reshape(length, HEADS, HEAD_DIM)
    )
    scores_again = attend_scores(query_low, key_low)
    prob_again = jnp.exp(scores_again - log_norm)
    d_value = jnp.einsum(
        "hqk,qhd->khd",
        prob_again.astype(jnp.bfloat16),
        d_mixed_low,
        preferred_element_type=jnp.float32,
    )
    d_prob = jnp.einsum("qhd,khd->hqk", d_mixed_low, value_low, preferred_element_type=jnp.float32)
    d_scores_low = (
        prob_again * (d_prob - jnp.sum(d_prob * prob_again, axis=-1, keepdims=True))
    ).astype(jnp.bfloat16)
    d_query_rot = (
        jnp.einsum("hqk,khd->qhd", d_scores_low, key_low, preferred_element_type=jnp.float32)
        * factor
    )
    d_key_rot = (
        jnp.einsum("hqk,qhd->khd", d_scores_low, query_low, preferred_element_type=jnp.float32)
        * factor
    )
    back_query, back_key, back_value, back_qgain, back_kgain = (
        lax.all_gather(w_query, "shard", axis=0, tiled=True),
        lax.all_gather(w_key, "shard", axis=0, tiled=True),
        lax.all_gather(w_value, "shard", axis=0, tiled=True),
        lax.all_gather(query_gain, "shard", axis=0, tiled=True),
        lax.all_gather(key_gain, "shard", axis=0, tiled=True),
    )
    unused_query, query_pull = jax.vjp(norm_rope, query_raw, back_qgain.astype(jnp.float32))
    d_query_raw, query_gain_term = query_pull(d_query_rot)
    unused_key, key_pull = jax.vjp(norm_rope, key_raw, back_kgain.astype(jnp.float32))
    d_key_raw, key_gain_term = key_pull(d_key_rot)
    d_query_low = d_query_raw.astype(jnp.bfloat16)
    d_key_low = d_key_raw.astype(jnp.bfloat16)
    d_value_low = d_value.reshape(length, model_width).astype(jnp.bfloat16)
    qkv_grad = reduce_rows(
        col_term(hidden_in, jnp.concatenate([d_query_low, d_key_low, d_value_low], axis=1)),
        w_query.shape[0],
    )
    hidden_grad = (
        d_resid
        + dot_back(d_query_low, back_query)
        + dot_back(d_key_low, back_key)
        + dot_back(d_value_low, back_value)
    ).astype(jnp.bfloat16)
    gain_sums = (
        lax.psum_scatter(query_gain_term, "shard", scatter_dimension=0, tiled=True),
        lax.psum_scatter(key_gain_term, "shard", scatter_dimension=0, tiled=True),
        lax.psum_scatter(attn_gain_term, "shard", scatter_dimension=0, tiled=True),
        lax.psum_scatter(ffn_gain_term, "shard", scatter_dimension=0, tiled=True),
    )
    totals = (
        lax.psum(qkv_grad[:, :model_width].astype(jnp.bfloat16), "rep").astype(jnp.float32),
        lax.psum(qkv_grad[:, model_width : 2 * model_width].astype(jnp.bfloat16), "rep").astype(
            jnp.float32
        ),
        lax.psum(qkv_grad[:, 2 * model_width :].astype(jnp.bfloat16), "rep").astype(jnp.float32),
        lax.psum(out_grad.astype(jnp.bfloat16), "rep").astype(jnp.float32),
        lax.psum(gain_sums[0].astype(jnp.bfloat16), "rep").astype(jnp.float32),
        lax.psum(gain_sums[1].astype(jnp.bfloat16), "rep").astype(jnp.float32),
        lax.psum(gain_sums[2].astype(jnp.bfloat16), "rep").astype(jnp.float32),
        lax.psum(ffn_in_grad[:, :ffn_width].astype(jnp.bfloat16), "rep").astype(jnp.float32),
        lax.psum(ffn_in_grad[:, ffn_width:].astype(jnp.bfloat16), "rep").astype(jnp.float32),
        lax.psum(down_grad.astype(jnp.bfloat16), "rep").astype(jnp.float32),
        lax.psum(gain_sums[3].astype(jnp.bfloat16), "rep").astype(jnp.float32),
    )
    return (
        hidden_out,
        hidden_grad,
        totals[0],
        totals[1],
        totals[2],
        totals[3],
        totals[4],
        totals[5],
        totals[6],
        totals[7],
        totals[8],
        totals[9],
        totals[10],
    )


LINE = 4


def shard_perm(move):
    return [(index, move(index)) for index in range(16)]


def core_swap(values):
    return lax.ppermute(values, "shard", shard_perm(lambda index: index ^ 1))


def pair_swap(values):
    return lax.ppermute(values, "shard", shard_perm(lambda index: index ^ 2))


def rep_swap(values):
    return lax.ppermute(values, "rep", [(0, 1), (1, 0)])


def line_shift(values, steps):
    return lax.ppermute(values, "shard", shard_perm(lambda index: (index + 4 * steps) % 16))


def line_groups():
    return [[line * 4 + pair * 2 + core for line in range(4) for core in range(2)] for pair in range(2)]


def gather_tokens(block):
    mine = [block] + [line_shift(block, steps) for steps in range(1, LINE)]
    return jnp.stack(mine + [core_swap(piece) for piece in mine])


def scatter_tokens(parts):
    theirs = [core_swap(parts[LINE + k].astype(jnp.bfloat16)) for k in range(LINE)]
    joint = [parts[k] + theirs[k].astype(jnp.float32) for k in range(LINE)]
    total = joint[0]
    for k in range(1, LINE):
        total = total + line_shift(joint[k].astype(jnp.bfloat16), -k).astype(jnp.float32)
    return total


def group_sum(values):
    count, tokens = values.shape
    split = values.reshape(count, 2, LINE, tokens // (2 * LINE))
    both = split + core_swap(split)[:, ::-1]
    total = both
    for steps in range(1, LINE):
        total = total + jnp.roll(line_shift(both, steps), steps, axis=2)
    return total.reshape(count, tokens)


def by_pair(pair, own, other):
    return jnp.where(pair == 0, own, other), jnp.where(pair == 0, other, own)


def gather_columns(weight, pair):
    rows, width = weight.shape
    n = width // 16
    pieces = weight.reshape(rows, 4, 2, 2, n).transpose(1, 3, 0, 2, 4).reshape(8, rows, 2, n)
    own = lax.all_to_all(pieces, "shard", 0, 0, axis_index_groups=line_groups(), tiled=True)
    first, second = by_pair(pair, own, pair_swap(own))
    full = jnp.stack([first.reshape(4, 2, rows, 2 * n), second.reshape(4, 2, rows, 2 * n)], axis=1)
    return full.reshape(16 * rows, 2 * n)


def gather_rows(weight, pair):
    return jnp.concatenate(by_pair(pair, weight, pair_swap(weight)), axis=0)


def rep_total(values):
    low = values.astype(jnp.bfloat16)
    return low.astype(jnp.float32) + rep_swap(low).astype(jnp.float32)


def pair_total(first, second, pair):
    own, other = by_pair(pair, first, second)
    return own + pair_swap(other.astype(jnp.bfloat16)).astype(jnp.float32)


def reduce_columns(partial, pair):
    rows = partial.shape[0] // 16
    n = partial.shape[1] // 2
    split = partial.reshape(4, 2, 2, rows, 2 * n)
    mine = pair_total(split[:, 0], split[:, 1], pair).astype(jnp.bfloat16).reshape(8, rows, 2, n)
    got = lax.all_to_all(mine, "shard", 0, 0, axis_index_groups=line_groups(), tiled=True)
    return rep_total(got.reshape(4, 2, rows, 2, n).transpose(2, 0, 3, 1, 4).reshape(rows, 16 * n))


def reduce_rows_of(partial, pair):
    half = partial.shape[0] // 2
    return rep_total(pair_total(partial[:half], partial[half:], pair))


def on_device(
    hidden_in,
    segments,
    w_query,
    w_key,
    w_value,
    w_output,
    query_gain,
    key_gain,
    attn_gain,
    w_gate,
    w_up,
    w_down,
    ffn_gain,
    out_cotangent,
):
    length, model_width = hidden_in.shape
    blocks = 2 * LINE
    heads = HEADS // blocks
    factor = HEAD_DIM ** (-0.5)
    pair = (lax.axis_index("shard") // 2) % 2
    f32 = jnp.float32

    docs = gather_tokens(segments)[:, 0]
    tokens = gather_tokens(hidden_in).reshape(blocks * length, model_width)
    width = heads * HEAD_DIM
    full_query = gather_columns(w_query, pair)
    full_key = gather_columns(w_key, pair)
    full_value = gather_columns(w_value, pair)
    head_gains = gather_rows(jnp.stack([query_gain, key_gain])[None], pair).astype(f32)
    gain_query = head_gains[:, 0].reshape(width)
    gain_key = head_gains[:, 1].reshape(width)
    wide_gains = lax.all_gather(
        jnp.stack([attn_gain, ffn_gain]), "shard", axis=1, tiled=True
    ).astype(f32)
    gain_attn, gain_ffn = wide_gains[0], wide_gains[1]

    earlier = jnp.sum((docs[:, None, :] < docs[:, :, None]).astype(jnp.int32), axis=2)
    positions = jnp.arange(length, dtype=jnp.int32)[None] - earlier
    half_dim = HEAD_DIM // 2
    inverse = jnp.exp(
        jnp.arange(half_dim, dtype=f32) * (-2.0 * math.log(theta_base) / HEAD_DIM)
    )
    angles = positions.astype(f32)[:, :, None] * inverse[None, None, :]
    cosines = jnp.cos(angles)[:, :, None, :]
    sines = jnp.sin(angles)[:, :, None, :]
    token_idx = jnp.arange(length)
    allowed = (docs[:, :, None] == docs[:, None, :]) & (
        token_idx[:, None] >= token_idx[None, :]
    )[None]

    def split_heads(values):
        return values.reshape(blocks, length, heads, HEAD_DIM)

    query_raw = jnp.dot(tokens, full_query, preferred_element_type=f32)
    key_raw = jnp.dot(tokens, full_key, preferred_element_type=f32)
    squares = group_sum(
        jnp.stack([jnp.sum(query_raw * query_raw, axis=-1), jnp.sum(key_raw * key_raw, axis=-1)])
    )
    head_scales = lax.rsqrt(squares / model_width + epsilon)
    query_unit = query_raw * head_scales[0][:, None]
    key_unit = key_raw * head_scales[1][:, None]
    query_low = rotate(split_heads(query_unit * gain_query), cosines, sines).astype(jnp.bfloat16)
    key_low = rotate(split_heads(key_unit * gain_key), cosines, sines).astype(jnp.bfloat16)
    value_low = split_heads(
        jnp.dot(tokens, full_value, preferred_element_type=f32).astype(jnp.bfloat16)
    )
    scores = (
        jnp.einsum("sqhd,skhd->shqk", query_low, key_low, preferred_element_type=f32) * factor
    )
    scores = jnp.where(allowed[:, None], scores, neg_fill)
    row_peak = jnp.max(scores, axis=-1, keepdims=True)
    log_norm = row_peak + jnp.log(jnp.sum(jnp.exp(scores - row_peak), axis=-1, keepdims=True))
    attn_prob = jnp.exp(scores - log_norm)
    prob_low = attn_prob.astype(jnp.bfloat16)
    mixed_low = (
        jnp.einsum("shqk,skhd->sqhd", prob_low, value_low, preferred_element_type=f32)
        .reshape(blocks * length, width)
        .astype(jnp.bfloat16)
    )
    full_output = gather_rows(w_output, pair)

    def to_blocks(values):
        return values.reshape(blocks, length, model_width)

    attn_out = scatter_tokens(
        to_blocks(jnp.dot(mixed_low, full_output, preferred_element_type=f32))
    )
    attn_rms = rms_scale(attn_out)
    attn_normed = attn_out * attn_rms
    resid = hidden_in.astype(f32) + attn_normed * gain_attn
    resid_low = gather_tokens(resid.astype(jnp.bfloat16)).reshape(blocks * length, model_width)

    full_gate = gather_columns(w_gate, pair)
    full_up = gather_columns(w_up, pair)
    gate_proj = jnp.dot(resid_low, full_gate, preferred_element_type=f32)
    up_proj = jnp.dot(resid_low, full_up, preferred_element_type=f32)
    gate_sig = jax.nn.sigmoid(gate_proj)
    hidden_ffn = (gate_proj * gate_sig * up_proj).astype(jnp.bfloat16)
    full_down = gather_rows(w_down, pair)
    ffn_out = scatter_tokens(
        to_blocks(jnp.dot(hidden_ffn, full_down, preferred_element_type=f32))
    )
    ffn_rms = rms_scale(ffn_out)
    ffn_normed = ffn_out * ffn_rms
    hidden_out = (resid + ffn_normed * gain_ffn).astype(jnp.bfloat16)
    grad_out = out_cotangent.astype(f32)
    ffn_gain_term = jnp.sum(grad_out * ffn_normed, axis=0)
    d_ffn_low = gather_tokens(
        rms_back(grad_out * gain_ffn, ffn_normed, ffn_rms).astype(jnp.bfloat16)
    ).reshape(blocks * length, model_width)

    d_hidden_ffn = dot_back(d_ffn_low, full_down)
    d_gate_low = (d_hidden_ffn * up_proj * gate_sig * (1.0 + gate_proj * (1.0 - gate_sig))).astype(
        jnp.bfloat16
    )
    d_up_low = (d_hidden_ffn * gate_proj * gate_sig).astype(jnp.bfloat16)
    d_resid = grad_out + scatter_tokens(
        to_blocks(dot_back(d_gate_low, full_gate) + dot_back(d_up_low, full_up))
    )

    def outer(left_side, right_side):
        return lax.dot_general(
            left_side, right_side, (((0,), (0,)), ((), ())), preferred_element_type=f32
        )

    grad_down = reduce_rows_of(outer(hidden_ffn, d_ffn_low), pair)
    grad_gate = reduce_columns(outer(resid_low, d_gate_low), pair)
    grad_up = reduce_columns(outer(resid_low, d_up_low), pair)
    attn_gain_term = jnp.sum(d_resid * attn_normed, axis=0)
    d_attn_low = gather_tokens(
        rms_back(d_resid * gain_attn, attn_normed, attn_rms).astype(jnp.bfloat16)
    ).reshape(blocks * length, model_width)
    grad_output = reduce_rows_of(outer(mixed_low, d_attn_low), pair)
    d_mixed_low = split_heads(dot_back(d_attn_low, full_output).astype(jnp.bfloat16))
    d_value = jnp.einsum("shqk,sqhd->skhd", prob_low, d_mixed_low, preferred_element_type=f32)
    d_prob = jnp.einsum("sqhd,skhd->shqk", d_mixed_low, value_low, preferred_element_type=f32)
    d_scores_low = (
        attn_prob * (d_prob - jnp.sum(d_prob * attn_prob, axis=-1, keepdims=True))
    ).astype(jnp.bfloat16)
    d_query_rot = (
        jnp.einsum("shqk,skhd->sqhd", d_scores_low, key_low, preferred_element_type=f32) * factor
    )
    d_key_rot = (
        jnp.einsum("shqk,sqhd->skhd", d_scores_low, query_low, preferred_element_type=f32)
        * factor
    )
    d_query_normed = rotate(d_query_rot, cosines, -sines).reshape(blocks * length, width)
    d_key_normed = rotate(d_key_rot, cosines, -sines).reshape(blocks * length, width)
    query_gain_term = jnp.sum(d_query_normed * query_unit, axis=0)
    key_gain_term = jnp.sum(d_key_normed * key_unit, axis=0)
    query_up = d_query_normed * gain_query
    key_up = d_key_normed * gain_key
    means = (
        group_sum(
            jnp.stack(
                [jnp.sum(query_up * query_unit, axis=-1), jnp.sum(key_up * key_unit, axis=-1)]
            )
        )
        / model_width
    )
    d_query_low = (head_scales[0][:, None] * (query_up - query_unit * means[0][:, None])).astype(
        jnp.bfloat16
    )
    d_key_low = (head_scales[1][:, None] * (key_up - key_unit * means[1][:, None])).astype(
        jnp.bfloat16
    )
    d_value_low = d_value.reshape(blocks * length, width).astype(jnp.bfloat16)
    hidden_grad = (
        d_resid
        + scatter_tokens(
            to_blocks(
                dot_back(d_query_low, full_query)
                + dot_back(d_key_low, full_key)
                + dot_back(d_value_low, full_value)
            )
        )
    ).astype(jnp.bfloat16)
    grad_query = reduce_columns(outer(tokens, d_query_low), pair)
    grad_key = reduce_columns(outer(tokens, d_key_low), pair)
    grad_value = reduce_columns(outer(tokens, d_value_low), pair)
    head_terms = jnp.stack([query_gain_term, key_gain_term]).reshape(2, 2, HEAD_DIM)
    own_term, other_term = by_pair(pair, head_terms[:, 0], head_terms[:, 1])
    head_grads = own_term + pair_swap(other_term)
    wide_grads = lax.psum_scatter(
        jnp.stack([attn_gain_term, ffn_gain_term]), "shard", scatter_dimension=1, tiled=True
    )
    gain_grads = jnp.concatenate([head_grads, wide_grads])
    gain_grads = gain_grads + rep_swap(gain_grads)
    return (
        hidden_out,
        hidden_grad,
        grad_query,
        grad_key,
        grad_value,
        grad_output,
        gain_grads[0],
        gain_grads[1],
        gain_grads[2],
        grad_gate,
        grad_up,
        grad_down,
        gain_grads[3],
    )


def solution(mesh):
    placed = (
        P(("rep", "shard"), None),
        P(("rep", "shard"), None),
        P("shard", None),
        P("shard", None),
        P("shard", None),
        P("shard", None),
        P("shard"),
        P("shard"),
        P("shard"),
        P("shard", None),
        P("shard", None),
        P("shard", None),
        P("shard"),
        P(("rep", "shard"), None),
    )
    return jax.shard_map(
        on_device if mesh.shape["shard"] == 16 else on_device_general,
        mesh=mesh,
        in_specs=placed,
        out_specs=(
            P(("rep", "shard"), None),
            P(("rep", "shard"), None),
            P("shard", None),
            P("shard", None),
            P("shard", None),
            P("shard", None),
            P("shard"),
            P("shard"),
            P("shard"),
            P("shard", None),
            P("shard", None),
            P("shard", None),
            P("shard"),
        ),
        check_vma=False,
    )
```

```python
import math

import jax
import jax.numpy as jnp
from jax import lax
from jax.experimental import pallas as pl
from jax.experimental.pallas import tpu as pltpu
from jax.sharding import PartitionSpec as P

HEADS = 16
HEAD_DIM = 128


epsilon = 1e-06
theta_base = 500000.0
neg_fill = -1e30


def rms_scale(values):
    return lax.rsqrt(jnp.mean(values * values, axis=-1, keepdims=True) + epsilon)


def rms_back(upstream, normed, row_scale):
    return row_scale * (upstream - normed * jnp.mean(upstream * normed, axis=-1, keepdims=True))


def rotate(values, cosines, sines):
    half_dim = values.shape[-1] // 2
    first_half = values[..., :half_dim]
    second = values[..., half_dim:]
    return jnp.concatenate(
        [first_half * cosines - second * sines, second * cosines + first_half * sines], axis=-1
    )


def dot_back(left_side, right_side):
    return lax.dot_general(
        left_side, right_side, (((1,), (1,)), ((), ())), preferred_element_type=jnp.float32
    )


def col_term(left_side, right_side):

    def block_term(row_start, row_count):
        return lax.dot_general(
            left_side, right_side, (((0,), (0,)), ((), ())), preferred_element_type=jnp.float32
        )

    return block_term


def on_device_general(
    hidden_in,
    segments,
    w_query,
    w_key,
    w_value,
    w_output,
    query_gain,
    key_gain,
    attn_gain,
    w_gate,
    w_up,
    w_down,
    ffn_gain,
    out_cotangent,
):
    length = hidden_in.shape[0]
    model_width = hidden_in.shape[1]
    ffn_width = w_gate.shape[1]
    factor = HEAD_DIM ** (-0.5)
    doc_row = segments[0]
    earlier = jnp.sum((doc_row[None, :] < doc_row[:, None]).astype(jnp.int32), axis=1)
    positions = jnp.arange(length, dtype=jnp.int32) - earlier
    half_dim = HEAD_DIM // 2
    inverse = jnp.exp(
        jnp.arange(half_dim, dtype=jnp.float32) * (-2.0 * math.log(theta_base) / HEAD_DIM)
    )
    angles = positions.astype(jnp.float32)[:, None] * inverse[None, :]
    cosines = jnp.cos(angles)[:, None, :]
    sines = jnp.sin(angles)[:, None, :]
    token_idx = jnp.arange(length)
    allowed = (doc_row[:, None] == doc_row[None, :]) & (token_idx[:, None] >= token_idx[None, :])

    def reduce_rows(term_fn, local_rows):
        return lax.psum_scatter(
            term_fn(jnp.int32(0), local_rows * lax.axis_size("shard")),
            "shard",
            scatter_dimension=0,
            tiled=True,
        )

    def norm_rope(raw_proj, gain_vec):
        normed = raw_proj * rms_scale(raw_proj) * gain_vec
        return rotate(normed.reshape(length, HEADS, HEAD_DIM), cosines, sines)

    def attend_scores(query_low, key_low):
        scores = (
            jnp.einsum("qhd,khd->hqk", query_low, key_low, preferred_element_type=jnp.float32)
            * factor
        )
        return jnp.where(allowed[None], scores, neg_fill)

    full_query, full_key, full_value, gain_query, gain_key = (
        lax.all_gather(w_query, "shard", axis=0, tiled=True),
        lax.all_gather(w_key, "shard", axis=0, tiled=True),
        lax.all_gather(w_value, "shard", axis=0, tiled=True),
        lax.all_gather(query_gain, "shard", axis=0, tiled=True),
        lax.all_gather(key_gain, "shard", axis=0, tiled=True),
    )
    query_raw = jnp.dot(hidden_in, full_query, preferred_element_type=jnp.float32)
    key_raw = jnp.dot(hidden_in, full_key, preferred_element_type=jnp.float32)
    query_low = norm_rope(query_raw, gain_query.astype(jnp.float32)).astype(jnp.bfloat16)
    key_low = norm_rope(key_raw, gain_key.astype(jnp.float32)).astype(jnp.bfloat16)
    value_low = (
        jnp.dot(hidden_in, full_value, preferred_element_type=jnp.float32)
        .astype(jnp.bfloat16)
        .reshape(length, HEADS, HEAD_DIM)
    )
    scores = attend_scores(query_low, key_low)
    row_peak = jnp.max(scores, axis=-1, keepdims=True)
    log_norm = row_peak + jnp.log(jnp.sum(jnp.exp(scores - row_peak), axis=-1, keepdims=True))
    attn_prob = jnp.exp(scores - log_norm)
    mixed_low = (
        jnp.einsum(
            "hqk,khd->qhd",
            attn_prob.astype(jnp.bfloat16),
            value_low,
            preferred_element_type=jnp.float32,
        )
        .reshape(length, model_width)
        .astype(jnp.bfloat16)
    )
    full_output, gain_attn = (
        lax.all_gather(w_output, "shard", axis=0, tiled=True),
        lax.all_gather(attn_gain, "shard", axis=0, tiled=True),
    )
    attn_out = jnp.dot(mixed_low, full_output, preferred_element_type=jnp.float32)
    attn_rms = rms_scale(attn_out)
    attn_normed = attn_out * attn_rms
    resid = hidden_in.astype(jnp.float32) + attn_normed * gain_attn.astype(jnp.float32)
    resid_low = resid.astype(jnp.bfloat16)
    full_gate, full_up = (
        lax.all_gather(w_gate, "shard", axis=0, tiled=True),
        lax.all_gather(w_up, "shard", axis=0, tiled=True),
    )
    gate_proj = jnp.dot(resid_low, full_gate, preferred_element_type=jnp.float32)
    up_proj = jnp.dot(resid_low, full_up, preferred_element_type=jnp.float32)
    gate_sig = jax.nn.sigmoid(gate_proj)
    hidden_ffn = (gate_proj * gate_sig * up_proj).astype(jnp.bfloat16)
    full_down, gain_ffn = (
        lax.all_gather(w_down, "shard", axis=0, tiled=True),
        lax.all_gather(ffn_gain, "shard", axis=0, tiled=True),
    )
    ffn_out = jnp.dot(hidden_ffn, full_down, preferred_element_type=jnp.float32)
    ffn_rms = rms_scale(ffn_out)
    ffn_normed = ffn_out * ffn_rms
    hidden_out = (resid + ffn_normed * gain_ffn.astype(jnp.float32)).astype(jnp.bfloat16)
    grad_out = out_cotangent.astype(jnp.float32)
    back_down, back_fgain = (
        lax.all_gather(w_down, "shard", axis=0, tiled=True),
        lax.all_gather(ffn_gain, "shard", axis=0, tiled=True),
    )
    ffn_gain_term = jnp.sum(grad_out * ffn_normed, axis=0)
    d_ffn_low = rms_back(grad_out * back_fgain.astype(jnp.float32), ffn_normed, ffn_rms).astype(
        jnp.bfloat16
    )
    down_grad = reduce_rows(col_term(hidden_ffn, d_ffn_low), w_down.shape[0])
    d_hidden_ffn = dot_back(d_ffn_low, back_down)
    d_gate_low = (d_hidden_ffn * up_proj * gate_sig * (1.0 + gate_proj * (1.0 - gate_sig))).astype(
        jnp.bfloat16
    )
    d_up_low = (d_hidden_ffn * gate_proj * gate_sig).astype(jnp.bfloat16)
    ffn_in_grad = reduce_rows(
        col_term(resid_low, jnp.concatenate([d_gate_low, d_up_low], axis=1)), w_gate.shape[0]
    )
    back_gate, back_up = (
        lax.all_gather(w_gate, "shard", axis=0, tiled=True),
        lax.all_gather(w_up, "shard", axis=0, tiled=True),
    )
    d_resid = grad_out + dot_back(d_gate_low, back_gate) + dot_back(d_up_low, back_up)
    back_output, back_again = (
        lax.all_gather(w_output, "shard", axis=0, tiled=True),
        lax.all_gather(attn_gain, "shard", axis=0, tiled=True),
    )
    attn_gain_term = jnp.sum(d_resid * attn_normed, axis=0)
    d_attn_low = rms_back(d_resid * back_again.astype(jnp.float32), attn_normed, attn_rms).astype(
        jnp.bfloat16
    )
    out_grad = reduce_rows(col_term(mixed_low, d_attn_low), w_output.shape[0])
    d_mixed_low = (
        dot_back(d_attn_low, back_output).astype(jnp.bfloat16).reshape(length, HEADS, HEAD_DIM)
    )
    scores_again = attend_scores(query_low, key_low)
    prob_again = jnp.exp(scores_again - log_norm)
    d_value = jnp.einsum(
        "hqk,qhd->khd",
        prob_again.astype(jnp.bfloat16),
        d_mixed_low,
        preferred_element_type=jnp.float32,
    )
    d_prob = jnp.einsum("qhd,khd->hqk", d_mixed_low, value_low, preferred_element_type=jnp.float32)
    d_scores_low = (
        prob_again * (d_prob - jnp.sum(d_prob * prob_again, axis=-1, keepdims=True))
    ).astype(jnp.bfloat16)
    d_query_rot = (
        jnp.einsum("hqk,khd->qhd", d_scores_low, key_low, preferred_element_type=jnp.float32)
        * factor
    )
    d_key_rot = (
        jnp.einsum("hqk,qhd->khd", d_scores_low, query_low, preferred_element_type=jnp.float32)
        * factor
    )
    back_query, back_key, back_value, back_qgain, back_kgain = (
        lax.all_gather(w_query, "shard", axis=0, tiled=True),
        lax.all_gather(w_key, "shard", axis=0, tiled=True),
        lax.all_gather(w_value, "shard", axis=0, tiled=True),
        lax.all_gather(query_gain, "shard", axis=0, tiled=True),
        lax.all_gather(key_gain, "shard", axis=0, tiled=True),
    )
    unused_query, query_pull = jax.vjp(norm_rope, query_raw, back_qgain.astype(jnp.float32))
    d_query_raw, query_gain_term = query_pull(d_query_rot)
    unused_key, key_pull = jax.vjp(norm_rope, key_raw, back_kgain.astype(jnp.float32))
    d_key_raw, key_gain_term = key_pull(d_key_rot)
    d_query_low = d_query_raw.astype(jnp.bfloat16)
    d_key_low = d_key_raw.astype(jnp.bfloat16)
    d_value_low = d_value.reshape(length, model_width).astype(jnp.bfloat16)
    qkv_grad = reduce_rows(
        col_term(hidden_in, jnp.concatenate([d_query_low, d_key_low, d_value_low], axis=1)),
        w_query.shape[0],
    )
    hidden_grad = (
        d_resid
        + dot_back(d_query_low, back_query)
        + dot_back(d_key_low, back_key)
        + dot_back(d_value_low, back_value)
    ).astype(jnp.bfloat16)
    gain_sums = (
        lax.psum_scatter(query_gain_term, "shard", scatter_dimension=0, tiled=True),
        lax.psum_scatter(key_gain_term, "shard", scatter_dimension=0, tiled=True),
        lax.psum_scatter(attn_gain_term, "shard", scatter_dimension=0, tiled=True),
        lax.psum_scatter(ffn_gain_term, "shard", scatter_dimension=0, tiled=True),
    )
    totals = (
        lax.psum(qkv_grad[:, :model_width].astype(jnp.bfloat16), "rep").astype(jnp.float32),
        lax.psum(qkv_grad[:, model_width : 2 * model_width].astype(jnp.bfloat16), "rep").astype(
            jnp.float32
        ),
        lax.psum(qkv_grad[:, 2 * model_width :].astype(jnp.bfloat16), "rep").astype(jnp.float32),
        lax.psum(out_grad.astype(jnp.bfloat16), "rep").astype(jnp.float32),
        lax.psum(gain_sums[0].astype(jnp.bfloat16), "rep").astype(jnp.float32),
        lax.psum(gain_sums[1].astype(jnp.bfloat16), "rep").astype(jnp.float32),
        lax.psum(gain_sums[2].astype(jnp.bfloat16), "rep").astype(jnp.float32),
        lax.psum(ffn_in_grad[:, :ffn_width].astype(jnp.bfloat16), "rep").astype(jnp.float32),
        lax.psum(ffn_in_grad[:, ffn_width:].astype(jnp.bfloat16), "rep").astype(jnp.float32),
        lax.psum(down_grad.astype(jnp.bfloat16), "rep").astype(jnp.float32),
        lax.psum(gain_sums[3].astype(jnp.bfloat16), "rep").astype(jnp.float32),
    )
    return (
        hidden_out,
        hidden_grad,
        totals[0],
        totals[1],
        totals[2],
        totals[3],
        totals[4],
        totals[5],
        totals[6],
        totals[7],
        totals[8],
        totals[9],
        totals[10],
    )


LINE = 4


def shard_perm(move):
    return [(index, move(index)) for index in range(16)]


def core_swap(values):
    return lax.ppermute(values, "shard", shard_perm(lambda index: index ^ 1))


def pair_swap(values):
    return lax.ppermute(values, "shard", shard_perm(lambda index: index ^ 2))


def rep_swap(values):
    return lax.ppermute(values, "rep", [(0, 1), (1, 0)])


def line_shift(values, steps):
    return lax.ppermute(values, "shard", shard_perm(lambda index: (index + 4 * steps) % 16))


def line_groups():
    return [[line * 4 + pair * 2 + core for line in range(4) for core in range(2)] for pair in range(2)]


def group_sum(values):
    both = values + core_swap(values)
    return both + line_shift(both, 1) + line_shift(both, 2) + line_shift(both, 3)


def by_pair(pair, own, other):
    return jnp.where(pair == 0, own, other), jnp.where(pair == 0, other, own)


def gather_columns(weight, pair):
    rows, width = weight.shape
    n = width // 16
    pieces = weight.reshape(rows, 4, 2, 2, n).transpose(1, 3, 0, 2, 4).reshape(8, rows, 2, n)
    own = lax.all_to_all(pieces, "shard", 0, 0, axis_index_groups=line_groups(), tiled=True)
    first, second = by_pair(pair, own, pair_swap(own))
    full = jnp.stack([first.reshape(4, 2, rows, 2 * n), second.reshape(4, 2, rows, 2 * n)], axis=1)
    return full.reshape(16 * rows, 2 * n)


def gather_rows(weight, pair):
    return jnp.concatenate(by_pair(pair, weight, pair_swap(weight)), axis=0)


def rep_total(values):
    low = values.astype(jnp.bfloat16)
    return low.astype(jnp.float32) + rep_swap(low).astype(jnp.float32)


def pair_total(first, second, pair):
    own, other = by_pair(pair, first, second)
    return own + pair_swap(other.astype(jnp.bfloat16)).astype(jnp.float32)


def reduce_columns(partial, pair):
    rows = partial.shape[0] // 16
    n = partial.shape[1] // 2
    split = partial.reshape(4, 2, 2, rows, 2 * n)
    mine = pair_total(split[:, 0], split[:, 1], pair).astype(jnp.bfloat16).reshape(8, rows, 2, n)
    got = lax.all_to_all(mine, "shard", 0, 0, axis_index_groups=line_groups(), tiled=True)
    return rep_total(got.reshape(4, 2, rows, 2, n).transpose(2, 0, 3, 1, 4).reshape(rows, 16 * n))


def reduce_rows_of(partial, pair):
    half = partial.shape[0] // 2
    return rep_total(pair_total(partial[:half], partial[half:], pair))


MESH_ID = pl.DeviceIdType.MESH


class Line:
    def __init__(self):
        index = lax.axis_index("shard")
        self.rep = lax.axis_index("rep")
        self.place = index // 4
        self.pair = (index // 2) % 2
        self.core = index % 2
        self.block = self.place * 2 + self.core
        self.sibling = self.at(self.place, self.pair, 1 - self.core)
        self.right = self.at(jnp.minimum(self.place + 1, LINE - 1), self.pair, self.core)
        self.left = self.at(jnp.maximum(self.place - 1, 0), self.pair, self.core)
        self.across = self.at(self.place, 1 - self.pair, self.core)
        self.partner = (1 - self.rep, index)
        self.has_right = self.place < LINE - 1
        self.has_left = self.place > 0

    def at(self, place, pair, core):
        return (self.rep, place * 4 + pair * 2 + core)

    def piece(self, p, sign):
        return (self.place + sign * (p // 2) + LINE) % LINE, (self.core + p % 2) % 2

    def meet(self, wide):
        barrier = pltpu.get_barrier_semaphore()

        def greet(device):
            pl.semaphore_signal(barrier, inc=1, device_id=device, device_id_type=MESH_ID)

        if wide:
            for p in range(1, 2 * LINE):
                place, core = self.piece(p, 1)
                greet(self.at(place, self.pair, core))
            greet(self.across)
            greet(self.partner)
            pl.semaphore_wait(barrier, 2 * LINE + 1)
            return
        greet(self.sibling)
        pl.when(self.has_right)(lambda: greet(self.right))
        pl.when(self.has_left)(lambda: greet(self.left))
        pl.semaphore_wait(
            barrier, 1 + self.has_right.astype(jnp.int32) + self.has_left.astype(jnp.int32)
        )


def remote(source, target, send_sem, recv_sem, device):
    return pltpu.make_async_remote_copy(
        src_ref=source,
        dst_ref=target,
        send_sem=send_sem,
        recv_sem=recv_sem,
        device_id=device,
        device_id_type=MESH_ID,
    )


class Spread:
    SEMAPHORES = ((2 * LINE,),) * 4 + ((2 * LINE, 2),) * 2

    def __init__(self, line, sources, target, sems):
        self.line, self.sources, self.target = line, sources, target
        self.z_send, self.z_recv, self.y_send, self.y_recv, self.x_send, self.x_recv = sems
        self.half = sources[0].shape[0] // 2

    def rows(self, place, pair, core, rep):
        start = ((place * 4 + pair * 2 + core) * 2 + rep) * self.half
        return self.target.at[pl.ds(pl.multiple_of(start, self.half), self.half), :]

    def start(self, p):
        line, half = self.line, self.half
        place, core = line.piece(p, 1)
        here = self.rows(line.place, line.pair, line.core, line.rep)
        mine = pl.ds(pl.multiple_of(line.rep * half, half), half)
        at = 0
        for source in self.sources:
            n = source.shape[1] // 16
            for q in range(2):
                column = pl.multiple_of((place * 4 + q * 2 + core) * n, n)
                piece, goal = source.at[mine, pl.ds(column, n)], here.at[:, pl.ds(at, n)]
                if p == 0:
                    pltpu.make_async_copy(piece, goal, self.z_recv.at[0]).start()
                else:
                    remote(
                        piece, goal, self.z_send.at[p], self.z_recv.at[p], line.at(place, line.pair, core)
                    ).start()
                at += n

    def cross(self, p, pair):
        place, core = self.line.piece(p, -1)
        ref = self.rows(place, pair, core, self.line.rep)
        return remote(ref, ref, self.y_send.at[p], self.y_recv.at[p], self.line.across)

    def over(self, p, pair, rep, which):
        place, core = self.line.piece(p, -1)
        ref = self.rows(place, pair, core, rep)
        return remote(ref, ref, self.x_send.at[p, which], self.x_recv.at[p, which], self.line.partner)

    def came(self, p):
        line = self.line
        place, core = line.piece(p, -1)
        ref = self.rows(place, line.pair, core, line.rep)
        if p == 0:
            pltpu.make_async_copy(ref, ref, self.z_recv.at[0]).wait()
        else:
            remote(ref, ref, self.z_send.at[p], self.z_recv.at[p], line.sibling).wait_recv()
        self.cross(p, line.pair).start()
        self.over(p, line.pair, line.rep, 0).start()

    def onward(self, p):
        line = self.line
        self.cross(p, 1 - line.pair).wait_recv()
        self.over(p, 1 - line.pair, line.rep, 1).start()

    def finish(self):
        line = self.line
        for p in range(2 * LINE):
            if p > 0:
                ref = self.rows(line.place, line.pair, line.core, line.rep)
                remote(ref, ref, self.z_send.at[p], self.z_recv.at[p], line.sibling).wait_send()
            self.cross(p, line.pair).wait_send()
            for which, pair in ((0, line.pair), (1, 1 - line.pair)):
                self.over(p, pair, line.rep, which).wait_send()
                self.over(p, pair, 1 - line.rep, which).wait_recv()


class Stack:
    SEMAPHORES = ((3,),)

    def __init__(self, line, source, target, sems):
        self.line, self.sems = line, sems[0]
        self.source = source
        size = source.shape[0]
        self.mine = target.at[pl.ds(pl.multiple_of(line.pair * size, size), size), :]

    def here(self):
        return pltpu.make_async_copy(self.source, self.mine, self.sems.at[0])

    def there(self):
        return remote(self.source, self.mine, self.sems.at[1], self.sems.at[2], self.line.across)

    def start(self):
        self.there().start()
        self.here().start()

    def finish(self):
        self.here().wait()
        self.there().wait()


def line_scatter_joint(line, k, rows, parts, sib):
    return parts[2 * k + line.core, rows, :].astype(jnp.float32) + sib[k, rows, :].astype(jnp.float32)


def line_scatter_pass(line, j, step, way, parts, sib, sums, came, sib_recv, send_sem, came_sem):
    rows = pl.ds(pl.multiple_of(j * step, step), step)
    device = line.right if way == 0 else line.left
    ends = line.place == 0 if way == 0 else line.place == LINE - 1

    def copy(k):
        return remote(sums.at[k, rows], came.at[k, rows], send_sem.at[k, j], came_sem.at[k, j], device)

    for k in range(LINE - 1, 0, -1) if way == 0 else range(LINE - 1):

        @pl.when(line.place < k if way == 0 else line.place > k)
        def _():
            remote(
                parts.at[2 * k + line.core, rows], sib.at[k, rows], sib_recv.at[k, j], sib_recv.at[k, j], line.sibling
            ).wait_recv()

            @pl.when(ends)
            def _():
                sums[k, rows, :] = line_scatter_joint(line, k, rows, parts, sib).astype(jnp.bfloat16)

            @pl.when(jnp.logical_not(ends))
            def _():
                copy(k).wait_recv()
                sums[k, rows, :] = (
                    line_scatter_joint(line, k, rows, parts, sib) + came[k, rows, :].astype(jnp.float32)
                ).astype(jnp.bfloat16)

            copy(k).start()


def line_scatter_total(line, j, step, parts, sib, rights, lefts, sums, sib_recv, sends, right_recv, left_recv):
    rows = pl.ds(pl.multiple_of(j * step, step), step)
    me = line.place
    remote(
        parts.at[2 * me + line.core, rows], sib.at[me, rows], sib_recv.at[me, j], sib_recv.at[me, j], line.sibling
    ).wait_recv()

    @pl.when(line.has_left)
    def _():
        remote(sums.at[me, rows], rights.at[me, rows], sends.at[me, j], right_recv.at[me, j], line.left).wait_recv()

    @pl.when(line.has_right)
    def _():
        remote(sums.at[me, rows], lefts.at[me, rows], sends.at[me, j], left_recv.at[me, j], line.right).wait_recv()

    total = line_scatter_joint(line, me, rows, parts, sib)
    total = total + jnp.where(line.has_left, rights[me, rows, :].astype(jnp.float32), 0.0)
    return total + jnp.where(line.has_right, lefts[me, rows, :].astype(jnp.float32), 0.0)


def line_scatter_start(line, pieces, step, parts, sib, sib_send, sib_recv):
    def piece(j, carry):
        rows = pl.ds(pl.multiple_of(j * step, step), step)
        for k in range(LINE):
            remote(
                parts.at[2 * k + 1 - line.core, rows],
                sib.at[k, rows],
                sib_send.at[k, j],
                sib_recv.at[k, j],
                line.sibling,
            ).start()
        return carry

    lax.fori_loop(0, pieces, piece, 0)


def line_scatter_end(line, pieces, step, parts, sib, rights, lefts, sums, sib_send, right_send, left_send):
    def piece(j, carry):
        rows = pl.ds(pl.multiple_of(j * step, step), step)
        for k in range(LINE):
            remote(
                parts.at[2 * k + 1 - line.core, rows],
                sib.at[k, rows],
                sib_send.at[k, j],
                sib_send.at[k, j],
                line.sibling,
            ).wait_send()

            @pl.when(line.place < k)
            def _():
                remote(
                    sums.at[k, rows], rights.at[k, rows], right_send.at[k, j], right_send.at[k, j], line.right
                ).wait_send()

            @pl.when(line.place > k)
            def _():
                remote(
                    sums.at[k, rows], lefts.at[k, rows], left_send.at[k, j], left_send.at[k, j], line.left
                ).wait_send()

        return carry

    lax.fori_loop(0, pieces, piece, 0)


def gather_copy(line, k, j, step, core, gathered, way, sends, recvs):
    rows = pl.ds(pl.multiple_of(j * step, step), step)
    block = 2 * k + core
    device = (line.right, line.left, line.sibling)[way]
    ref = gathered.at[block, rows]
    return remote(ref, ref, sends.at[k, way, j], recvs.at[block, j], device)


def line_gather_own(line, j, step, gathered, sends, recvs):
    def copy(way):
        return gather_copy(line, line.place, j, step, line.core, gathered, way, sends, recvs)

    pl.when(line.has_right)(lambda: copy(0).start())
    pl.when(line.has_left)(lambda: copy(1).start())
    copy(2).start()


def line_gather_pass(line, hop, j, step, gathered, sends, recvs):
    for way in (0, 1):
        k = line.place - hop if way == 0 else line.place + hop
        there = k >= 0 if way == 0 else k < LINE
        onward = line.has_right if way == 0 else line.has_left
        k = jnp.clip(k, 0, LINE - 1)

        @pl.when(there)
        def _():
            gather_copy(line, k, j, step, line.core, gathered, way, sends, recvs).wait_recv()
            pl.when(onward)(
                lambda: gather_copy(line, k, j, step, line.core, gathered, way, sends, recvs).start()
            )
            gather_copy(line, k, j, step, line.core, gathered, 2, sends, recvs).start()


def line_gather_end(line, pieces, step, gathered, sends, recvs):
    def piece(j, carry):
        for k in range(LINE):
            gather_copy(line, k, j, step, 1 - line.core, gathered, 2, sends, recvs).wait_recv()
            gather_copy(line, k, j, step, line.core, gathered, 2, sends, recvs).wait_send()

            @pl.when((line.place >= k) & line.has_right)
            def _():
                gather_copy(line, k, j, step, line.core, gathered, 0, sends, recvs).wait_send()

            @pl.when((line.place <= k) & line.has_left)
            def _():
                gather_copy(line, k, j, step, line.core, gathered, 1, sends, recvs).wait_send()

        return carry

    lax.fori_loop(0, pieces, piece, 0)


def take_from(items, count):
    taken = items[:count]
    del items[:count]
    return taken


def line_call(collective_id, pieces, middle, inputs, outputs, scatter, gather, spreads=(), stacks=()):
    block = inputs[0].shape[-2:]
    step = block[0] // pieces
    n_in, n_out = len(inputs), len(outputs)
    weights = [w for group in spreads for w in group] + list(stacks)
    n_weights, n_extra = len(weights), len(spreads) + len(stacks)
    extras = [
        jax.ShapeDtypeStruct((16 * group[0].shape[0], sum(w.shape[1] for w in group) // 8), jnp.bfloat16)
        for group in spreads
    ] + [jax.ShapeDtypeStruct((2 * w.shape[0], w.shape[1]), jnp.bfloat16) for w in stacks]
    low = jnp.bfloat16
    scratch = []
    if scatter:
        scratch += [pltpu.VMEM((LINE,) + block, low) for _ in range(4)]
        scratch += [pltpu.SemaphoreType.DMA((LINE, pieces)) for _ in range(6)]
    if gather:
        scratch += [pltpu.SemaphoreType.DMA((LINE, 3, pieces)), pltpu.SemaphoreType.DMA((2 * LINE, pieces))]

    n_scratch = len(scratch)
    kinds = [Spread] * len(spreads) + [Stack] * len(stacks)
    scratch += [pltpu.SemaphoreType.DMA(shape) for kind in kinds for shape in kind.SEMAPHORES]

    def kernel(*refs):
        refs = list(refs)

        def take(count):
            taken = refs[:count]
            del refs[:count]
            return taken

        ins, given, outs, extra = take(n_in), take(n_weights), take(n_out), take(n_extra)
        rest = take(n_scratch)
        line = Line()
        moves = []
        for group in spreads:
            moves.append(Spread(line, take_from(given, len(group)), extra.pop(0), take(6)))
        heaps = [Stack(line, given.pop(0), extra.pop(0), take(1)) for _ in stacks]
        line.meet(bool(moves or heaps))
        if scatter:
            sib, rights, lefts, sums, sib_send, sib_recv, right_send, left_send, right_recv, left_recv = rest[:10]
            parts = ins[0]
            line_scatter_start(line, pieces, step, parts, sib, sib_send, sib_recv)
        if gather:
            sends, recvs = rest[-2:]

        def during(j, act):
            pl.when((j >= 0) & (j < pieces))(lambda: act(j))

        def finish(j):
            rows = pl.ds(pl.multiple_of(j * step, step), step)
            total = None
            if scatter:
                total = line_scatter_total(
                    line, j, step, parts, sib, rights, lefts, sums, sib_recv, right_send, right_recv, left_recv
                )
            values = middle(total, rows, j, ins, outs)
            if gather:
                outs[0][line.block, rows, :] = values.astype(low)
                line_gather_own(line, j, step, outs[0], sends, recvs)

        def slot(t, carry):
            if scatter:
                during(
                    t - line.place,
                    lambda j: line_scatter_pass(
                        line, j, step, 0, parts, sib, sums, rights, sib_recv, right_send, right_recv
                    ),
                )
                during(
                    t - (LINE - 1 - line.place),
                    lambda j: line_scatter_pass(
                        line, j, step, 1, parts, sib, sums, lefts, sib_recv, left_send, left_recv
                    ),
                )
                during(t - (LINE - 1), finish)
            if gather:
                for hop in range(1, LINE):
                    during(
                        t - hop - (LINE - 1 if scatter else 0),
                        lambda j, hop=hop: line_gather_pass(line, hop, j, step, outs[0], sends, recvs),
                    )
            return carry

        if not scatter:
            lax.fori_loop(0, pieces, lambda j, carry: (finish(j), carry)[1], 0)
        hops = (LINE - 1) * (int(scatter) + int(gather))
        if moves:
            for t in range(pieces + hops):
                for move in moves:
                    if t < 2 * LINE:
                        move.start(t)
                    if 3 <= t < 3 + 2 * LINE:
                        move.came(t - 3)
                    if 6 <= t < 6 + 2 * LINE:
                        move.onward(t - 6)
                if t == 2:
                    for heap in heaps:
                        heap.start()
                slot(t, 0)
            for move in moves:
                for t in range(pieces + hops, 6 + 2 * LINE):
                    if t < 3 + 2 * LINE:
                        move.came(t - 3)
                    move.onward(t - 6)
                move.finish()
            for heap in heaps:
                heap.finish()
        else:
            lax.fori_loop(0, pieces + hops, slot, 0)
        if scatter:
            line_scatter_end(
                line, pieces, step, parts, sib, rights, lefts, sums, sib_send, right_send, left_send
            )
        if gather:
            line_gather_end(line, pieces, step, outs[0], sends, recvs)

    vmem = pl.BlockSpec(memory_space=pltpu.VMEM)
    return pl.pallas_call(
        kernel,
        out_shape=[jax.ShapeDtypeStruct(shape, kind) for shape, kind in outputs] + extras,
        in_specs=[vmem] * n_in + [pl.BlockSpec(memory_space=pl.ANY)] * n_weights,
        out_specs=[vmem] * n_out + [pl.BlockSpec(memory_space=pl.ANY)] * n_extra,
        scratch_shapes=scratch,
        compiler_params=pltpu.CompilerParams(
            collective_id=collective_id, has_side_effects=True, vmem_limit_bytes=40 << 20
        ),
        cost_estimate=pl.CostEstimate(flops=10_000_000, bytes_accessed=200_000_000, transcendentals=0),
    )(*inputs, *weights)


def gather_blocks(payload, spreads, stacks, collective_id):
    def middle(total, rows, j, ins, outs):
        return ins[0][rows, :]

    shape = (2 * LINE,) + payload.shape
    return line_call(collective_id, 9, middle, [payload], [(shape, jnp.bfloat16)], False, True, spreads, stacks)


def attention_block(parts, hidden, gain, spreads, stacks, collective_id):
    def middle(total, rows, j, ins, outs):
        outs[1][rows, :] = total
        resid = ins[1][rows, :].astype(jnp.float32) + total * rms_scale(total) * ins[2][...]
        outs[2][rows, :] = resid
        return resid

    shape = hidden.shape
    return line_call(
        collective_id, 8, middle, [parts, hidden, gain],
        [(parts.shape, jnp.bfloat16), (shape, jnp.float32), (shape, jnp.float32)], True, True, spreads, stacks,
    )


def add_rows(ref, values, j):
    folded = jnp.sum(values.reshape(values.shape[0] // 8, 8, values.shape[1]), axis=0)

    @pl.when(j == 0)
    def _():
        ref[...] = folded

    @pl.when(j > 0)
    def _():
        ref[...] += folded


def ffn_block(parts, resid, cotangent, gain, collective_id):
    def middle(total, rows, j, ins, outs):
        scale = rms_scale(total)
        normed = total * scale
        grad = ins[2][rows, :].astype(jnp.float32)
        gains = ins[3][...]
        outs[1][rows, :] = (ins[1][rows, :] + normed * gains).astype(jnp.bfloat16)
        add_rows(outs[2], grad * normed, j)
        return rms_back(grad * gains, normed, scale)

    shape = resid.shape
    return line_call(
        collective_id, 8, middle, [parts, resid, cotangent, gain],
        [(parts.shape, jnp.bfloat16), (shape, jnp.bfloat16), ((8, shape[1]), jnp.float32)], True, True,
    )


def back_block(parts, cotangent, attn_out, gain, collective_id):
    def middle(total, rows, j, ins, outs):
        d_resid = ins[1][rows, :].astype(jnp.float32) + total
        outs[1][rows, :] = d_resid
        attn = ins[2][rows, :]
        scale = rms_scale(attn)
        normed = attn * scale
        add_rows(outs[2], d_resid * normed, j)
        return rms_back(d_resid * ins[3][...], normed, scale)

    shape = cotangent.shape
    return line_call(
        collective_id, 8, middle, [parts, cotangent, attn_out, gain],
        [(parts.shape, jnp.bfloat16), (shape, jnp.float32), ((8, shape[1]), jnp.float32)], True, True,
    )


def last_block(parts, d_resid, collective_id):
    def middle(total, rows, j, ins, outs):
        outs[0][rows, :] = (ins[1][rows, :] + total).astype(jnp.bfloat16)

    return line_call(
        collective_id, 8, middle, [parts, d_resid], [(d_resid.shape, jnp.bfloat16)], True, False
    )[0]


def on_device(
    hidden_in,
    segments,
    w_query,
    w_key,
    w_value,
    w_output,
    query_gain,
    key_gain,
    attn_gain,
    w_gate,
    w_up,
    w_down,
    ffn_gain,
    out_cotangent,
):
    length, model_width = hidden_in.shape
    blocks = 2 * LINE
    heads = HEADS // blocks
    factor = HEAD_DIM ** (-0.5)
    pair = (lax.axis_index("shard") // 2) % 2
    f32 = jnp.float32

    extra = jnp.concatenate(
        [query_gain, key_gain, attn_gain, ffn_gain, segments[0].astype(jnp.bfloat16)]
    )
    extra = jnp.pad(extra[None], ((0, 15), (0, model_width - extra.shape[0])))
    payload, full_qkv, full_output = gather_blocks(
        jnp.concatenate([hidden_in, extra]), [[w_query, w_key, w_value]], [w_output], 0
    )
    tokens = payload[:, :length].reshape(blocks * length, model_width)
    docs = payload[:, length, 4 * length : 5 * length].astype(jnp.int32)
    gains = payload[:, length, : 4 * length].reshape(LINE, 2, 4, length)
    gains = jnp.stack(by_pair(pair, gains, pair_swap(gains)), axis=1)
    gains = jnp.moveaxis(gains, 3, 0).reshape(4, 1, model_width).astype(f32)
    gain_attn, gain_ffn = gains[2], gains[3]
    width = heads * HEAD_DIM
    head_gains = gather_rows(jnp.stack([query_gain, key_gain])[None], pair).astype(f32)
    gain_query = head_gains[:, 0].reshape(width)
    gain_key = head_gains[:, 1].reshape(width)

    earlier = jnp.sum((docs[:, None, :] < docs[:, :, None]).astype(jnp.int32), axis=2)
    positions = jnp.arange(length, dtype=jnp.int32)[None] - earlier
    half_dim = HEAD_DIM // 2
    inverse = jnp.exp(
        jnp.arange(half_dim, dtype=f32) * (-2.0 * math.log(theta_base) / HEAD_DIM)
    )
    angles = positions.astype(f32)[:, :, None] * inverse[None, None, :]
    cosines = jnp.cos(angles)[:, :, None, :]
    sines = jnp.sin(angles)[:, :, None, :]
    token_idx = jnp.arange(length)
    allowed = (docs[:, :, None] == docs[:, None, :]) & (
        token_idx[:, None] >= token_idx[None, :]
    )[None]

    def split_heads(values):
        return values.reshape(blocks, length, heads, HEAD_DIM)

    all_raw = jnp.dot(tokens, full_qkv, preferred_element_type=f32)
    query_raw, key_raw = all_raw[:, :width], all_raw[:, width : 2 * width]
    squares = group_sum(
        jnp.stack([jnp.sum(query_raw * query_raw, axis=-1), jnp.sum(key_raw * key_raw, axis=-1)])
    )
    head_scales = lax.rsqrt(squares / model_width + epsilon)
    query_unit = query_raw * head_scales[0][:, None]
    key_unit = key_raw * head_scales[1][:, None]
    query_low = rotate(split_heads(query_unit * gain_query), cosines, sines).astype(jnp.bfloat16)
    key_low = rotate(split_heads(key_unit * gain_key), cosines, sines).astype(jnp.bfloat16)
    value_low = split_heads(all_raw[:, 2 * width :].astype(jnp.bfloat16))
    scores = (
        jnp.einsum("sqhd,skhd->shqk", query_low, key_low, preferred_element_type=f32) * factor
    )
    scores = jnp.where(allowed[:, None], scores, neg_fill)
    row_peak = jnp.max(scores, axis=-1, keepdims=True)
    log_norm = row_peak + jnp.log(jnp.sum(jnp.exp(scores - row_peak), axis=-1, keepdims=True))
    attn_prob = jnp.exp(scores - log_norm)
    prob_low = attn_prob.astype(jnp.bfloat16)
    mixed_low = (
        jnp.einsum("shqk,skhd->sqhd", prob_low, value_low, preferred_element_type=f32)
        .reshape(blocks * length, width)
        .astype(jnp.bfloat16)
    )

    def to_blocks(values):
        return values.astype(jnp.bfloat16).reshape(blocks, length, model_width)

    resid_low, attn_out, resid, full_gate, full_up, full_down = attention_block(
        to_blocks(jnp.dot(mixed_low, full_output, preferred_element_type=f32)),
        hidden_in,
        gain_attn,
        [[w_gate], [w_up]],
        [w_down],
        1,
    )
    resid_low = resid_low.reshape(blocks * length, model_width)

    gate_proj = jnp.dot(resid_low, full_gate, preferred_element_type=f32)
    up_proj = jnp.dot(resid_low, full_up, preferred_element_type=f32)
    gate_sig = jax.nn.sigmoid(gate_proj)
    hidden_ffn = (gate_proj * gate_sig * up_proj).astype(jnp.bfloat16)
    d_ffn_low, hidden_out, ffn_gain_term = ffn_block(
        to_blocks(jnp.dot(hidden_ffn, full_down, preferred_element_type=f32)),
        resid,
        out_cotangent,
        gain_ffn,
        2,
    )
    d_ffn_low = d_ffn_low.reshape(blocks * length, model_width)

    d_hidden_ffn = dot_back(d_ffn_low, full_down)
    d_gate_low = (d_hidden_ffn * up_proj * gate_sig * (1.0 + gate_proj * (1.0 - gate_sig))).astype(
        jnp.bfloat16
    )
    d_up_low = (d_hidden_ffn * gate_proj * gate_sig).astype(jnp.bfloat16)
    d_attn_low, d_resid, attn_gain_term = back_block(
        to_blocks(dot_back(d_gate_low, full_gate) + dot_back(d_up_low, full_up)),
        out_cotangent,
        attn_out,
        gain_attn,
        3,
    )
    d_attn_low = d_attn_low.reshape(blocks * length, model_width)

    def outer(left_side, right_side):
        return lax.dot_general(
            left_side, right_side, (((0,), (0,)), ((), ())), preferred_element_type=f32
        )

    grad_down = reduce_rows_of(outer(hidden_ffn, d_ffn_low), pair)
    grad_gate = reduce_columns(outer(resid_low, d_gate_low), pair)
    grad_up = reduce_columns(outer(resid_low, d_up_low), pair)
    grad_output = reduce_rows_of(outer(mixed_low, d_attn_low), pair)
    d_mixed_low = split_heads(dot_back(d_attn_low, full_output).astype(jnp.bfloat16))
    d_value = jnp.einsum("shqk,sqhd->skhd", prob_low, d_mixed_low, preferred_element_type=f32)
    d_prob = jnp.einsum("sqhd,skhd->shqk", d_mixed_low, value_low, preferred_element_type=f32)
    d_scores_low = (
        attn_prob * (d_prob - jnp.sum(d_prob * attn_prob, axis=-1, keepdims=True))
    ).astype(jnp.bfloat16)
    d_query_rot = (
        jnp.einsum("shqk,skhd->sqhd", d_scores_low, key_low, preferred_element_type=f32) * factor
    )
    d_key_rot = (
        jnp.einsum("shqk,sqhd->skhd", d_scores_low, query_low, preferred_element_type=f32)
        * factor
    )
    d_query_normed = rotate(d_query_rot, cosines, -sines).reshape(blocks * length, width)
    d_key_normed = rotate(d_key_rot, cosines, -sines).reshape(blocks * length, width)
    query_gain_term = jnp.sum(d_query_normed * query_unit, axis=0)
    key_gain_term = jnp.sum(d_key_normed * key_unit, axis=0)
    query_up = d_query_normed * gain_query
    key_up = d_key_normed * gain_key
    means = (
        group_sum(
            jnp.stack(
                [jnp.sum(query_up * query_unit, axis=-1), jnp.sum(key_up * key_unit, axis=-1)]
            )
        )
        / model_width
    )
    d_query_low = (head_scales[0][:, None] * (query_up - query_unit * means[0][:, None])).astype(
        jnp.bfloat16
    )
    d_key_low = (head_scales[1][:, None] * (key_up - key_unit * means[1][:, None])).astype(
        jnp.bfloat16
    )
    d_value_low = d_value.reshape(blocks * length, width).astype(jnp.bfloat16)
    hidden_grad = last_block(
        to_blocks(
            dot_back(jnp.concatenate([d_query_low, d_key_low, d_value_low], axis=1), full_qkv)
        ),
        d_resid,
        4,
    )
    grad_query = reduce_columns(outer(tokens, d_query_low), pair)
    grad_key = reduce_columns(outer(tokens, d_key_low), pair)
    grad_value = reduce_columns(outer(tokens, d_value_low), pair)
    head_terms = jnp.stack([query_gain_term, key_gain_term]).reshape(2, 2, HEAD_DIM)
    own_term, other_term = by_pair(pair, head_terms[:, 0], head_terms[:, 1])
    head_grads = own_term + pair_swap(other_term)
    wide_grads = lax.psum_scatter(
        jnp.stack([jnp.sum(attn_gain_term, axis=0), jnp.sum(ffn_gain_term, axis=0)]),
        "shard",
        scatter_dimension=1,
        tiled=True,
    )
    gain_grads = jnp.concatenate([head_grads, wide_grads])
    gain_grads = gain_grads + rep_swap(gain_grads)
    return (
        hidden_out,
        hidden_grad,
        grad_query,
        grad_key,
        grad_value,
        grad_output,
        gain_grads[0],
        gain_grads[1],
        gain_grads[2],
        grad_gate,
        grad_up,
        grad_down,
        gain_grads[3],
    )


def solution(mesh):
    placed = (
        P(("rep", "shard"), None),
        P(("rep", "shard"), None),
        P("shard", None),
        P("shard", None),
        P("shard", None),
        P("shard", None),
        P("shard"),
        P("shard"),
        P("shard"),
        P("shard", None),
        P("shard", None),
        P("shard", None),
        P("shard"),
        P(("rep", "shard"), None),
    )
    return jax.shard_map(
        on_device if mesh.shape["shard"] == 16 else on_device_general,
        mesh=mesh,
        in_specs=placed,
        out_specs=(
            P(("rep", "shard"), None),
            P(("rep", "shard"), None),
            P("shard", None),
            P("shard", None),
            P("shard", None),
            P("shard", None),
            P("shard"),
            P("shard"),
            P("shard"),
            P("shard", None),
            P("shard", None),
            P("shard", None),
            P("shard"),
        ),
        check_vma=False,
    )
```

```python
import math

import jax
import jax.numpy as jnp
from jax import lax
from jax.experimental import pallas as pl
from jax.experimental.pallas import tpu as pltpu
from jax.sharding import PartitionSpec as P

HEADS = 16
HEAD_DIM = 128


epsilon = 1e-06
theta_base = 500000.0
neg_fill = -1e30


def rms_scale(values):
    return lax.rsqrt(jnp.mean(values * values, axis=-1, keepdims=True) + epsilon)


def rms_back(upstream, normed, row_scale):
    return row_scale * (upstream - normed * jnp.mean(upstream * normed, axis=-1, keepdims=True))


def rotate(values, cosines, sines):
    half_dim = values.shape[-1] // 2
    first_half = values[..., :half_dim]
    second = values[..., half_dim:]
    return jnp.concatenate(
        [first_half * cosines - second * sines, second * cosines + first_half * sines], axis=-1
    )


def dot_back(left_side, right_side):
    return lax.dot_general(
        left_side, right_side, (((1,), (1,)), ((), ())), preferred_element_type=jnp.float32
    )


def col_term(left_side, right_side):

    def block_term(row_start, row_count):
        return lax.dot_general(
            left_side, right_side, (((0,), (0,)), ((), ())), preferred_element_type=jnp.float32
        )

    return block_term


def on_device_general(
    hidden_in,
    segments,
    w_query,
    w_key,
    w_value,
    w_output,
    query_gain,
    key_gain,
    attn_gain,
    w_gate,
    w_up,
    w_down,
    ffn_gain,
    out_cotangent,
):
    length = hidden_in.shape[0]
    model_width = hidden_in.shape[1]
    ffn_width = w_gate.shape[1]
    factor = HEAD_DIM ** (-0.5)
    doc_row = segments[0]
    earlier = jnp.sum((doc_row[None, :] < doc_row[:, None]).astype(jnp.int32), axis=1)
    positions = jnp.arange(length, dtype=jnp.int32) - earlier
    half_dim = HEAD_DIM // 2
    inverse = jnp.exp(
        jnp.arange(half_dim, dtype=jnp.float32) * (-2.0 * math.log(theta_base) / HEAD_DIM)
    )
    angles = positions.astype(jnp.float32)[:, None] * inverse[None, :]
    cosines = jnp.cos(angles)[:, None, :]
    sines = jnp.sin(angles)[:, None, :]
    token_idx = jnp.arange(length)
    allowed = (doc_row[:, None] == doc_row[None, :]) & (token_idx[:, None] >= token_idx[None, :])

    def reduce_rows(term_fn, local_rows):
        return lax.psum_scatter(
            term_fn(jnp.int32(0), local_rows * lax.axis_size("shard")),
            "shard",
            scatter_dimension=0,
            tiled=True,
        )

    def norm_rope(raw_proj, gain_vec):
        normed = raw_proj * rms_scale(raw_proj) * gain_vec
        return rotate(normed.reshape(length, HEADS, HEAD_DIM), cosines, sines)

    def attend_scores(query_low, key_low):
        scores = (
            jnp.einsum("qhd,khd->hqk", query_low, key_low, preferred_element_type=jnp.float32)
            * factor
        )
        return jnp.where(allowed[None], scores, neg_fill)

    full_query, full_key, full_value, gain_query, gain_key = (
        lax.all_gather(w_query, "shard", axis=0, tiled=True),
        lax.all_gather(w_key, "shard", axis=0, tiled=True),
        lax.all_gather(w_value, "shard", axis=0, tiled=True),
        lax.all_gather(query_gain, "shard", axis=0, tiled=True),
        lax.all_gather(key_gain, "shard", axis=0, tiled=True),
    )
    query_raw = jnp.dot(hidden_in, full_query, preferred_element_type=jnp.float32)
    key_raw = jnp.dot(hidden_in, full_key, preferred_element_type=jnp.float32)
    query_low = norm_rope(query_raw, gain_query.astype(jnp.float32)).astype(jnp.bfloat16)
    key_low = norm_rope(key_raw, gain_key.astype(jnp.float32)).astype(jnp.bfloat16)
    value_low = (
        jnp.dot(hidden_in, full_value, preferred_element_type=jnp.float32)
        .astype(jnp.bfloat16)
        .reshape(length, HEADS, HEAD_DIM)
    )
    scores = attend_scores(query_low, key_low)
    row_peak = jnp.max(scores, axis=-1, keepdims=True)
    log_norm = row_peak + jnp.log(jnp.sum(jnp.exp(scores - row_peak), axis=-1, keepdims=True))
    attn_prob = jnp.exp(scores - log_norm)
    mixed_low = (
        jnp.einsum(
            "hqk,khd->qhd",
            attn_prob.astype(jnp.bfloat16),
            value_low,
            preferred_element_type=jnp.float32,
        )
        .reshape(length, model_width)
        .astype(jnp.bfloat16)
    )
    full_output, gain_attn = (
        lax.all_gather(w_output, "shard", axis=0, tiled=True),
        lax.all_gather(attn_gain, "shard", axis=0, tiled=True),
    )
    attn_out = jnp.dot(mixed_low, full_output, preferred_element_type=jnp.float32)
    attn_rms = rms_scale(attn_out)
    attn_normed = attn_out * attn_rms
    resid = hidden_in.astype(jnp.float32) + attn_normed * gain_attn.astype(jnp.float32)
    resid_low = resid.astype(jnp.bfloat16)
    full_gate, full_up = (
        lax.all_gather(w_gate, "shard", axis=0, tiled=True),
        lax.all_gather(w_up, "shard", axis=0, tiled=True),
    )
    gate_proj = jnp.dot(resid_low, full_gate, preferred_element_type=jnp.float32)
    up_proj = jnp.dot(resid_low, full_up, preferred_element_type=jnp.float32)
    gate_sig = jax.nn.sigmoid(gate_proj)
    hidden_ffn = (gate_proj * gate_sig * up_proj).astype(jnp.bfloat16)
    full_down, gain_ffn = (
        lax.all_gather(w_down, "shard", axis=0, tiled=True),
        lax.all_gather(ffn_gain, "shard", axis=0, tiled=True),
    )
    ffn_out = jnp.dot(hidden_ffn, full_down, preferred_element_type=jnp.float32)
    ffn_rms = rms_scale(ffn_out)
    ffn_normed = ffn_out * ffn_rms
    hidden_out = (resid + ffn_normed * gain_ffn.astype(jnp.float32)).astype(jnp.bfloat16)
    grad_out = out_cotangent.astype(jnp.float32)
    back_down, back_fgain = (
        lax.all_gather(w_down, "shard", axis=0, tiled=True),
        lax.all_gather(ffn_gain, "shard", axis=0, tiled=True),
    )
    ffn_gain_term = jnp.sum(grad_out * ffn_normed, axis=0)
    d_ffn_low = rms_back(grad_out * back_fgain.astype(jnp.float32), ffn_normed, ffn_rms).astype(
        jnp.bfloat16
    )
    down_grad = reduce_rows(col_term(hidden_ffn, d_ffn_low), w_down.shape[0])
    d_hidden_ffn = dot_back(d_ffn_low, back_down)
    d_gate_low = (d_hidden_ffn * up_proj * gate_sig * (1.0 + gate_proj * (1.0 - gate_sig))).astype(
        jnp.bfloat16
    )
    d_up_low = (d_hidden_ffn * gate_proj * gate_sig).astype(jnp.bfloat16)
    ffn_in_grad = reduce_rows(
        col_term(resid_low, jnp.concatenate([d_gate_low, d_up_low], axis=1)), w_gate.shape[0]
    )
    back_gate, back_up = (
        lax.all_gather(w_gate, "shard", axis=0, tiled=True),
        lax.all_gather(w_up, "shard", axis=0, tiled=True),
    )
    d_resid = grad_out + dot_back(d_gate_low, back_gate) + dot_back(d_up_low, back_up)
    back_output, back_again = (
        lax.all_gather(w_output, "shard", axis=0, tiled=True),
        lax.all_gather(attn_gain, "shard", axis=0, tiled=True),
    )
    attn_gain_term = jnp.sum(d_resid * attn_normed, axis=0)
    d_attn_low = rms_back(d_resid * back_again.astype(jnp.float32), attn_normed, attn_rms).astype(
        jnp.bfloat16
    )
    out_grad = reduce_rows(col_term(mixed_low, d_attn_low), w_output.shape[0])
    d_mixed_low = (
        dot_back(d_attn_low, back_output).astype(jnp.bfloat16).reshape(length, HEADS, HEAD_DIM)
    )
    scores_again = attend_scores(query_low, key_low)
    prob_again = jnp.exp(scores_again - log_norm)
    d_value = jnp.einsum(
        "hqk,qhd->khd",
        prob_again.astype(jnp.bfloat16),
        d_mixed_low,
        preferred_element_type=jnp.float32,
    )
    d_prob = jnp.einsum("qhd,khd->hqk", d_mixed_low, value_low, preferred_element_type=jnp.float32)
    d_scores_low = (
        prob_again * (d_prob - jnp.sum(d_prob * prob_again, axis=-1, keepdims=True))
    ).astype(jnp.bfloat16)
    d_query_rot = (
        jnp.einsum("hqk,khd->qhd", d_scores_low, key_low, preferred_element_type=jnp.float32)
        * factor
    )
    d_key_rot = (
        jnp.einsum("hqk,qhd->khd", d_scores_low, query_low, preferred_element_type=jnp.float32)
        * factor
    )
    back_query, back_key, back_value, back_qgain, back_kgain = (
        lax.all_gather(w_query, "shard", axis=0, tiled=True),
        lax.all_gather(w_key, "shard", axis=0, tiled=True),
        lax.all_gather(w_value, "shard", axis=0, tiled=True),
        lax.all_gather(query_gain, "shard", axis=0, tiled=True),
        lax.all_gather(key_gain, "shard", axis=0, tiled=True),
    )
    unused_query, query_pull = jax.vjp(norm_rope, query_raw, back_qgain.astype(jnp.float32))
    d_query_raw, query_gain_term = query_pull(d_query_rot)
    unused_key, key_pull = jax.vjp(norm_rope, key_raw, back_kgain.astype(jnp.float32))
    d_key_raw, key_gain_term = key_pull(d_key_rot)
    d_query_low = d_query_raw.astype(jnp.bfloat16)
    d_key_low = d_key_raw.astype(jnp.bfloat16)
    d_value_low = d_value.reshape(length, model_width).astype(jnp.bfloat16)
    qkv_grad = reduce_rows(
        col_term(hidden_in, jnp.concatenate([d_query_low, d_key_low, d_value_low], axis=1)),
        w_query.shape[0],
    )
    hidden_grad = (
        d_resid
        + dot_back(d_query_low, back_query)
        + dot_back(d_key_low, back_key)
        + dot_back(d_value_low, back_value)
    ).astype(jnp.bfloat16)
    gain_sums = (
        lax.psum_scatter(query_gain_term, "shard", scatter_dimension=0, tiled=True),
        lax.psum_scatter(key_gain_term, "shard", scatter_dimension=0, tiled=True),
        lax.psum_scatter(attn_gain_term, "shard", scatter_dimension=0, tiled=True),
        lax.psum_scatter(ffn_gain_term, "shard", scatter_dimension=0, tiled=True),
    )
    totals = (
        lax.psum(qkv_grad[:, :model_width].astype(jnp.bfloat16), "rep").astype(jnp.float32),
        lax.psum(qkv_grad[:, model_width : 2 * model_width].astype(jnp.bfloat16), "rep").astype(
            jnp.float32
        ),
        lax.psum(qkv_grad[:, 2 * model_width :].astype(jnp.bfloat16), "rep").astype(jnp.float32),
        lax.psum(out_grad.astype(jnp.bfloat16), "rep").astype(jnp.float32),
        lax.psum(gain_sums[0].astype(jnp.bfloat16), "rep").astype(jnp.float32),
        lax.psum(gain_sums[1].astype(jnp.bfloat16), "rep").astype(jnp.float32),
        lax.psum(gain_sums[2].astype(jnp.bfloat16), "rep").astype(jnp.float32),
        lax.psum(ffn_in_grad[:, :ffn_width].astype(jnp.bfloat16), "rep").astype(jnp.float32),
        lax.psum(ffn_in_grad[:, ffn_width:].astype(jnp.bfloat16), "rep").astype(jnp.float32),
        lax.psum(down_grad.astype(jnp.bfloat16), "rep").astype(jnp.float32),
        lax.psum(gain_sums[3].astype(jnp.bfloat16), "rep").astype(jnp.float32),
    )
    return (
        hidden_out,
        hidden_grad,
        totals[0],
        totals[1],
        totals[2],
        totals[3],
        totals[4],
        totals[5],
        totals[6],
        totals[7],
        totals[8],
        totals[9],
        totals[10],
    )


LINE = 4


def shard_perm(move):
    return [(index, move(index)) for index in range(16)]


def core_swap(values):
    return lax.ppermute(values, "shard", shard_perm(lambda index: index ^ 1))


def pair_swap(values):
    return lax.ppermute(values, "shard", shard_perm(lambda index: index ^ 2))


def rep_swap(values):
    return lax.ppermute(values, "rep", [(0, 1), (1, 0)])


def line_shift(values, steps):
    return lax.ppermute(values, "shard", shard_perm(lambda index: (index + 4 * steps) % 16))


def group_sum(values):
    both = values + core_swap(values)
    return both + line_shift(both, 1) + line_shift(both, 2) + line_shift(both, 3)


def by_pair(pair, own, other):
    return jnp.where(pair == 0, own, other), jnp.where(pair == 0, other, own)


def gather_rows(weight, pair):
    return jnp.concatenate(by_pair(pair, weight, pair_swap(weight)), axis=0)


MESH_ID = pl.DeviceIdType.MESH


class Line:
    def __init__(self):
        index = lax.axis_index("shard")
        self.rep = lax.axis_index("rep")
        self.place = index // 4
        self.pair = (index // 2) % 2
        self.core = index % 2
        self.block = self.place * 2 + self.core
        self.sibling = self.at(self.place, self.pair, 1 - self.core)
        self.right = self.at(jnp.minimum(self.place + 1, LINE - 1), self.pair, self.core)
        self.left = self.at(jnp.maximum(self.place - 1, 0), self.pair, self.core)
        self.across = self.at(self.place, 1 - self.pair, self.core)
        self.partner = (1 - self.rep, index)
        self.has_right = self.place < LINE - 1
        self.has_left = self.place > 0

    def at(self, place, pair, core):
        return (self.rep, place * 4 + pair * 2 + core)

    def piece(self, p, sign):
        return (self.place + sign * (p // 2) + LINE) % LINE, (self.core + p % 2) % 2

    def meet(self, wide):
        barrier = pltpu.get_barrier_semaphore()

        def greet(device):
            pl.semaphore_signal(barrier, inc=1, device_id=device, device_id_type=MESH_ID)

        if wide:
            for p in range(1, 2 * LINE):
                place, core = self.piece(p, 1)
                greet(self.at(place, self.pair, core))
            greet(self.across)
            greet(self.partner)
            pl.semaphore_wait(barrier, 2 * LINE + 1)
            return
        greet(self.sibling)
        pl.when(self.has_right)(lambda: greet(self.right))
        pl.when(self.has_left)(lambda: greet(self.left))
        pl.semaphore_wait(
            barrier, 1 + self.has_right.astype(jnp.int32) + self.has_left.astype(jnp.int32)
        )


def remote(source, target, send_sem, recv_sem, device):
    return pltpu.make_async_remote_copy(
        src_ref=source,
        dst_ref=target,
        send_sem=send_sem,
        recv_sem=recv_sem,
        device_id=device,
        device_id_type=MESH_ID,
    )


class Spread:
    semaphores = ((2 * LINE,),) * 4 + ((2 * LINE, 2),) * 2
    slots = 6 + 2 * LINE

    def __init__(self, *weights):
        self.inputs = list(weights)
        shape = (16 * weights[0].shape[0], sum(weight.shape[1] for weight in weights) // 8)
        self.outputs = [jax.ShapeDtypeStruct(shape, jnp.bfloat16)]

    def bind(self, line, sources, targets, sems):
        self.line, self.sources, self.target = line, sources, targets[0]
        self.z_send, self.z_recv, self.y_send, self.y_recv, self.x_send, self.x_recv = sems
        self.half = sources[0].shape[0] // 2

    def slot(self, t):
        if t < 2 * LINE:
            self.start(t)
        if 3 <= t < 3 + 2 * LINE:
            self.came(t - 3)
        if 6 <= t < 6 + 2 * LINE:
            self.onward(t - 6)

    def rows(self, place, pair, core, rep):
        start = ((place * 4 + pair * 2 + core) * 2 + rep) * self.half
        return self.target.at[pl.ds(pl.multiple_of(start, self.half), self.half), :]

    def start(self, p):
        line, half = self.line, self.half
        place, core = line.piece(p, 1)
        here = self.rows(line.place, line.pair, line.core, line.rep)
        mine = pl.ds(pl.multiple_of(line.rep * half, half), half)
        at = 0
        for source in self.sources:
            n = source.shape[1] // 16
            for q in range(2):
                column = pl.multiple_of((place * 4 + q * 2 + core) * n, n)
                piece, goal = source.at[mine, pl.ds(column, n)], here.at[:, pl.ds(at, n)]
                if p == 0:
                    pltpu.make_async_copy(piece, goal, self.z_recv.at[0]).start()
                else:
                    remote(
                        piece, goal, self.z_send.at[p], self.z_recv.at[p], line.at(place, line.pair, core)
                    ).start()
                at += n

    def cross(self, p, pair):
        place, core = self.line.piece(p, -1)
        ref = self.rows(place, pair, core, self.line.rep)
        return remote(ref, ref, self.y_send.at[p], self.y_recv.at[p], self.line.across)

    def over(self, p, pair, rep, which):
        place, core = self.line.piece(p, -1)
        ref = self.rows(place, pair, core, rep)
        return remote(ref, ref, self.x_send.at[p, which], self.x_recv.at[p, which], self.line.partner)

    def came(self, p):
        line = self.line
        place, core = line.piece(p, -1)
        ref = self.rows(place, line.pair, core, line.rep)
        if p == 0:
            pltpu.make_async_copy(ref, ref, self.z_recv.at[0]).wait()
        else:
            remote(ref, ref, self.z_send.at[p], self.z_recv.at[p], line.sibling).wait_recv()
        self.cross(p, line.pair).start()
        self.over(p, line.pair, line.rep, 0).start()

    def onward(self, p):
        line = self.line
        self.cross(p, 1 - line.pair).wait_recv()
        self.over(p, 1 - line.pair, line.rep, 1).start()

    def finish(self):
        line = self.line
        for p in range(2 * LINE):
            if p > 0:
                ref = self.rows(line.place, line.pair, line.core, line.rep)
                remote(ref, ref, self.z_send.at[p], self.z_recv.at[p], line.sibling).wait_send()
            self.cross(p, line.pair).wait_send()
            for which, pair in ((0, line.pair), (1, 1 - line.pair)):
                self.over(p, pair, line.rep, which).wait_send()
                self.over(p, pair, 1 - line.rep, which).wait_recv()


class Stack:
    semaphores = ((3,),)
    slots = 3

    def __init__(self, weight):
        self.inputs = [weight]
        self.outputs = [jax.ShapeDtypeStruct((2 * weight.shape[0], weight.shape[1]), weight.dtype)]

    def bind(self, line, sources, targets, sems):
        self.line, self.sems = line, sems[0]
        self.source = sources[0]
        size = self.source.shape[0]
        self.mine = targets[0].at[pl.ds(pl.multiple_of(line.pair * size, size), size), :]

    def slot(self, t):
        if t == 2:
            self.start()

    def here(self):
        return pltpu.make_async_copy(self.source, self.mine, self.sems.at[0])

    def there(self):
        return remote(self.source, self.mine, self.sems.at[1], self.sems.at[2], self.line.across)

    def start(self):
        self.there().start()
        self.here().start()

    def finish(self):
        self.here().wait()
        self.there().wait()


class Swap:
    semaphores = ((2,),)
    slots = 1

    def __init__(self, values, shape, pick, to):
        self.inputs, self.pick, self.to = [values], pick, to
        self.outputs = [jax.ShapeDtypeStruct(shape, values.dtype)]

    def bind(self, line, sources, targets, sems):
        self.copy = remote(
            self.pick(line, sources[0]), targets[0], sems[0].at[0], sems[0].at[1], getattr(line, self.to)
        )

    def slot(self, t):
        if t == 0:
            self.copy.start()

    def finish(self):
        self.copy.wait()


class Deal:
    semaphores = ((2 * LINE,),) * 4
    slots = 3 + 2 * LINE

    def __init__(self, values, count, joint):
        rows, width = values.shape[1:]
        self.inputs, self.joint, self.count = [values], joint, count
        self.n = width // count if joint else width // (2 * count)
        shape = jax.ShapeDtypeStruct((rows, 16 * count * self.n), values.dtype)
        self.outputs = [shape] if joint else [shape, shape]

    def bind(self, line, sources, targets, sems):
        self.line, self.source, self.targets = line, sources[0], targets
        self.z_send, self.z_recv, self.x_send, self.x_recv = sems

    def columns(self, place, core, rep):
        n = self.n
        at = 0
        for index in range(self.count):
            for q in (rep,) if self.joint else (0, 1):
                yield at, pl.multiple_of((index * 16 + place * 4 + q * 2 + core) * n, n)
                at += n

    def whole(self, sem_send, sem_recv):
        ref = self.source.at[0]
        return remote(ref, ref, sem_send, sem_recv, self.line.partner)

    def start(self, p):
        line = self.line
        place, core = line.piece(p, 1)
        for at, column in self.columns(line.place, line.core, line.rep):
            piece = self.source.at[2 * place + core, :, pl.ds(at, self.n)]
            goal = self.targets[0].at[:, pl.ds(column, self.n)]
            if p == 0:
                pltpu.make_async_copy(piece, goal, self.z_recv.at[0]).start()
            else:
                remote(
                    piece, goal, self.z_send.at[p], self.z_recv.at[p], line.at(place, line.pair, core)
                ).start()

    def came(self, p):
        line = self.line
        if p == 0:
            ref = self.source.at[0]
            pltpu.make_async_copy(ref, ref, self.z_recv.at[0]).wait()
        else:
            self.whole(self.z_send.at[p], self.z_recv.at[p]).wait_recv()
        place, core = line.piece(p, -1)
        for _, column in self.columns(place, core, line.rep):
            there = pl.ds(column, self.n)
            remote(
                self.targets[0].at[:, there],
                self.targets[-1].at[:, there],
                self.x_send.at[p],
                self.x_recv.at[p],
                line.partner,
            ).start()

    def slot(self, t):
        if t < 2 * LINE:
            self.start(t)
        if 3 <= t < 3 + 2 * LINE:
            self.came(t - 3)

    def finish(self):
        for p in range(2 * LINE):
            if p > 0:
                self.whole(self.z_send.at[p], self.z_recv.at[p]).wait_send()
            self.whole(self.x_send.at[p], self.x_recv.at[p]).wait()


def line_scatter_joint(line, k, rows, parts, sib):
    return parts[2 * k + line.core, rows, :].astype(jnp.float32) + sib[k, rows, :].astype(jnp.float32)


def line_scatter_pass(line, j, step, way, parts, sib, sums, came, sib_recv, send_sem, came_sem):
    rows = pl.ds(pl.multiple_of(j * step, step), step)
    device = line.right if way == 0 else line.left
    ends = line.place == 0 if way == 0 else line.place == LINE - 1

    def copy(k):
        return remote(sums.at[k, rows], came.at[k, rows], send_sem.at[k, j], came_sem.at[k, j], device)

    for k in range(LINE - 1, 0, -1) if way == 0 else range(LINE - 1):

        @pl.when(line.place < k if way == 0 else line.place > k)
        def _():
            remote(
                parts.at[2 * k + line.core, rows], sib.at[k, rows], sib_recv.at[k, j], sib_recv.at[k, j], line.sibling
            ).wait_recv()

            @pl.when(ends)
            def _():
                sums[k, rows, :] = line_scatter_joint(line, k, rows, parts, sib).astype(jnp.bfloat16)

            @pl.when(jnp.logical_not(ends))
            def _():
                copy(k).wait_recv()
                sums[k, rows, :] = (
                    line_scatter_joint(line, k, rows, parts, sib) + came[k, rows, :].astype(jnp.float32)
                ).astype(jnp.bfloat16)

            copy(k).start()


def line_scatter_total(line, j, step, parts, sib, rights, lefts, sums, sib_recv, sends, right_recv, left_recv):
    rows = pl.ds(pl.multiple_of(j * step, step), step)
    me = line.place
    remote(
        parts.at[2 * me + line.core, rows], sib.at[me, rows], sib_recv.at[me, j], sib_recv.at[me, j], line.sibling
    ).wait_recv()

    @pl.when(line.has_left)
    def _():
        remote(sums.at[me, rows], rights.at[me, rows], sends.at[me, j], right_recv.at[me, j], line.left).wait_recv()

    @pl.when(line.has_right)
    def _():
        remote(sums.at[me, rows], lefts.at[me, rows], sends.at[me, j], left_recv.at[me, j], line.right).wait_recv()

    total = line_scatter_joint(line, me, rows, parts, sib)
    total = total + jnp.where(line.has_left, rights[me, rows, :].astype(jnp.float32), 0.0)
    return total + jnp.where(line.has_right, lefts[me, rows, :].astype(jnp.float32), 0.0)


def line_scatter_start(line, pieces, step, parts, sib, sib_send, sib_recv):
    def piece(j, carry):
        rows = pl.ds(pl.multiple_of(j * step, step), step)
        for k in range(LINE):
            remote(
                parts.at[2 * k + 1 - line.core, rows],
                sib.at[k, rows],
                sib_send.at[k, j],
                sib_recv.at[k, j],
                line.sibling,
            ).start()
        return carry

    lax.fori_loop(0, pieces, piece, 0)


def line_scatter_end(line, pieces, step, parts, sib, rights, lefts, sums, sib_send, right_send, left_send):
    def piece(j, carry):
        rows = pl.ds(pl.multiple_of(j * step, step), step)
        for k in range(LINE):
            remote(
                parts.at[2 * k + 1 - line.core, rows],
                sib.at[k, rows],
                sib_send.at[k, j],
                sib_send.at[k, j],
                line.sibling,
            ).wait_send()

            @pl.when(line.place < k)
            def _():
                remote(
                    sums.at[k, rows], rights.at[k, rows], right_send.at[k, j], right_send.at[k, j], line.right
                ).wait_send()

            @pl.when(line.place > k)
            def _():
                remote(
                    sums.at[k, rows], lefts.at[k, rows], left_send.at[k, j], left_send.at[k, j], line.left
                ).wait_send()

        return carry

    lax.fori_loop(0, pieces, piece, 0)


def gather_copy(line, k, j, step, core, gathered, way, sends, recvs):
    rows = pl.ds(pl.multiple_of(j * step, step), step)
    block = 2 * k + core
    device = (line.right, line.left, line.sibling)[way]
    ref = gathered.at[block, rows]
    return remote(ref, ref, sends.at[k, way, j], recvs.at[block, j], device)


def line_gather_own(line, j, step, gathered, sends, recvs):
    def copy(way):
        return gather_copy(line, line.place, j, step, line.core, gathered, way, sends, recvs)

    pl.when(line.has_right)(lambda: copy(0).start())
    pl.when(line.has_left)(lambda: copy(1).start())
    copy(2).start()


def line_gather_pass(line, hop, j, step, gathered, sends, recvs):
    for way in (0, 1):
        k = line.place - hop if way == 0 else line.place + hop
        there = k >= 0 if way == 0 else k < LINE
        onward = line.has_right if way == 0 else line.has_left
        k = jnp.clip(k, 0, LINE - 1)

        @pl.when(there)
        def _():
            gather_copy(line, k, j, step, line.core, gathered, way, sends, recvs).wait_recv()
            pl.when(onward)(
                lambda: gather_copy(line, k, j, step, line.core, gathered, way, sends, recvs).start()
            )
            gather_copy(line, k, j, step, line.core, gathered, 2, sends, recvs).start()


def line_gather_end(line, pieces, step, gathered, sends, recvs):
    def piece(j, carry):
        for k in range(LINE):
            gather_copy(line, k, j, step, 1 - line.core, gathered, 2, sends, recvs).wait_recv()
            gather_copy(line, k, j, step, line.core, gathered, 2, sends, recvs).wait_send()

            @pl.when((line.place >= k) & line.has_right)
            def _():
                gather_copy(line, k, j, step, line.core, gathered, 0, sends, recvs).wait_send()

            @pl.when((line.place <= k) & line.has_left)
            def _():
                gather_copy(line, k, j, step, line.core, gathered, 1, sends, recvs).wait_send()

        return carry

    lax.fori_loop(0, pieces, piece, 0)


def line_call(collective_id, pieces, middle, inputs, outputs, scatter, gather, moves=()):
    step = inputs[0].shape[-2] // pieces if inputs else 0
    low = jnp.bfloat16
    scratch = []
    if scatter:
        block = inputs[0].shape[-2:]
        scratch += [pltpu.VMEM((LINE,) + block, low) for _ in range(4)]
        scratch += [pltpu.SemaphoreType.DMA((LINE, pieces)) for _ in range(6)]
    if gather:
        scratch += [pltpu.SemaphoreType.DMA((LINE, 3, pieces)), pltpu.SemaphoreType.DMA((2 * LINE, pieces))]
    n_scratch = len(scratch)
    scratch += [pltpu.SemaphoreType.DMA(shape) for move in moves for shape in move.semaphores]
    moved = [values for move in moves for values in move.inputs]
    extras = [shape for move in moves for shape in move.outputs]

    def kernel(*refs):
        refs = list(refs)

        def take(count):
            taken = refs[:count]
            del refs[:count]
            return taken

        ins = take(len(inputs))
        given = [take(len(move.inputs)) for move in moves]
        outs = take(len(outputs))
        extra = [take(len(move.outputs)) for move in moves]
        rest = take(n_scratch)
        line = Line()
        for move, sources, targets in zip(moves, given, extra):
            move.bind(line, sources, targets, take(len(move.semaphores)))
        line.meet(bool(moves))
        if scatter:
            sib, rights, lefts, sums, sib_send, sib_recv, right_send, left_send, right_recv, left_recv = rest[:10]
            parts = ins[0]
            line_scatter_start(line, pieces, step, parts, sib, sib_send, sib_recv)
        if gather:
            sends, recvs = rest[-2:]

        def during(j, act):
            pl.when((j >= 0) & (j < pieces))(lambda: act(j))

        def finish(j):
            rows = pl.ds(pl.multiple_of(j * step, step), step)
            total = None
            if scatter:
                total = line_scatter_total(
                    line, j, step, parts, sib, rights, lefts, sums, sib_recv, right_send, right_recv, left_recv
                )
            values = middle(total, rows, j, ins, outs)
            if gather:
                outs[0][line.block, rows, :] = values.astype(low)
                line_gather_own(line, j, step, outs[0], sends, recvs)

        def slot(t, carry):
            if scatter:
                during(
                    t - line.place,
                    lambda j: line_scatter_pass(
                        line, j, step, 0, parts, sib, sums, rights, sib_recv, right_send, right_recv
                    ),
                )
                during(
                    t - (LINE - 1 - line.place),
                    lambda j: line_scatter_pass(
                        line, j, step, 1, parts, sib, sums, lefts, sib_recv, left_send, left_recv
                    ),
                )
                during(t - (LINE - 1), finish)
            if gather:
                for hop in range(1, LINE):
                    during(
                        t - hop - (LINE - 1 if scatter else 0),
                        lambda j, hop=hop: line_gather_pass(line, hop, j, step, outs[0], sends, recvs),
                    )
            return carry

        if gather and not scatter:
            lax.fori_loop(0, pieces, lambda j, carry: (finish(j), carry)[1], 0)
        slots = pieces + (LINE - 1) * (int(scatter) + int(gather)) if inputs else 0
        apart = max([move.slots for move in moves] + [0])
        if apart <= 1:
            for move in moves:
                move.slot(0)
            if inputs:
                lax.fori_loop(0, slots, slot, 0)
        else:
            for t in range(max(slots, apart)):
                for move in moves:
                    move.slot(t)
                if t < slots:
                    slot(t, 0)
        for move in moves:
            move.finish()
        if scatter:
            line_scatter_end(
                line, pieces, step, parts, sib, rights, lefts, sums, sib_send, right_send, left_send
            )
        if gather:
            line_gather_end(line, pieces, step, outs[0], sends, recvs)

    vmem = pl.BlockSpec(memory_space=pltpu.VMEM)
    whole = pl.BlockSpec(memory_space=pl.ANY)
    return pl.pallas_call(
        kernel,
        out_shape=[jax.ShapeDtypeStruct(shape, kind) for shape, kind in outputs] + extras,
        in_specs=[vmem] * len(inputs) + [whole] * len(moved),
        out_specs=[vmem] * len(outputs) + [whole] * len(extras),
        scratch_shapes=scratch,
        compiler_params=pltpu.CompilerParams(
            collective_id=collective_id, has_side_effects=True, vmem_limit_bytes=40 << 20
        ),
        cost_estimate=pl.CostEstimate(flops=10_000_000, bytes_accessed=200_000_000, transcendentals=0),
    )(*inputs, *moved)


def gather_blocks(payload, moves, collective_id):
    def middle(total, rows, j, ins, outs):
        return ins[0][rows, :]

    shape = (2 * LINE,) + payload.shape
    return line_call(collective_id, 9, middle, [payload], [(shape, jnp.bfloat16)], False, True, moves)


def attention_block(parts, hidden, gain, moves, collective_id):
    def middle(total, rows, j, ins, outs):
        outs[1][rows, :] = total
        resid = ins[1][rows, :].astype(jnp.float32) + total * rms_scale(total) * ins[2][...]
        outs[2][rows, :] = resid
        return resid

    shape = hidden.shape
    return line_call(
        collective_id, 8, middle, [parts, hidden, gain],
        [(parts.shape, jnp.bfloat16), (shape, jnp.float32), (shape, jnp.float32)], True, True, moves,
    )


def add_rows(ref, values, j):
    folded = jnp.sum(values.reshape(values.shape[0] // 8, 8, values.shape[1]), axis=0)

    @pl.when(j == 0)
    def _():
        ref[...] = folded

    @pl.when(j > 0)
    def _():
        ref[...] += folded


def ffn_block(parts, resid, cotangent, gain, collective_id):
    def middle(total, rows, j, ins, outs):
        scale = rms_scale(total)
        normed = total * scale
        grad = ins[2][rows, :].astype(jnp.float32)
        gains = ins[3][...]
        outs[1][rows, :] = (ins[1][rows, :] + normed * gains).astype(jnp.bfloat16)
        add_rows(outs[2], grad * normed, j)
        return rms_back(grad * gains, normed, scale)

    shape = resid.shape
    return line_call(
        collective_id, 8, middle, [parts, resid, cotangent, gain],
        [(parts.shape, jnp.bfloat16), (shape, jnp.bfloat16), ((8, shape[1]), jnp.float32)], True, True,
    )


def back_block(parts, cotangent, attn_out, gain, moves, collective_id):
    def middle(total, rows, j, ins, outs):
        d_resid = ins[1][rows, :].astype(jnp.float32) + total
        outs[1][rows, :] = d_resid
        attn = ins[2][rows, :]
        scale = rms_scale(attn)
        normed = attn * scale
        add_rows(outs[2], d_resid * normed, j)
        return rms_back(d_resid * ins[3][...], normed, scale)

    shape = cotangent.shape
    return line_call(
        collective_id, 8, middle, [parts, cotangent, attn_out, gain],
        [(parts.shape, jnp.bfloat16), (shape, jnp.float32), ((8, shape[1]), jnp.float32)], True, True, moves,
    )


def last_block(parts, d_resid, moves, collective_id):
    def middle(total, rows, j, ins, outs):
        outs[0][rows, :] = (ins[1][rows, :] + total).astype(jnp.bfloat16)

    return line_call(
        collective_id, 8, middle, [parts, d_resid], [(d_resid.shape, jnp.bfloat16)], True, False, moves
    )


def on_device(
    hidden_in,
    segments,
    w_query,
    w_key,
    w_value,
    w_output,
    query_gain,
    key_gain,
    attn_gain,
    w_gate,
    w_up,
    w_down,
    ffn_gain,
    out_cotangent,
):
    length, model_width = hidden_in.shape
    blocks = 2 * LINE
    heads = HEADS // blocks
    factor = HEAD_DIM ** (-0.5)
    pair = (lax.axis_index("shard") // 2) % 2
    f32 = jnp.float32

    extra = jnp.concatenate(
        [query_gain, key_gain, attn_gain, ffn_gain, segments[0].astype(jnp.bfloat16)]
    )
    extra = jnp.pad(extra[None], ((0, 15), (0, model_width - extra.shape[0])))
    payload, full_qkv, full_output = gather_blocks(
        jnp.concatenate([hidden_in, extra]), [Spread(w_query, w_key, w_value), Stack(w_output)], 0
    )
    tokens = payload[:, :length].reshape(blocks * length, model_width)
    docs = payload[:, length, 4 * length : 5 * length].astype(jnp.int32)
    gains = payload[:, length, : 4 * length].reshape(LINE, 2, 4, length)
    gains = jnp.stack(by_pair(pair, gains, pair_swap(gains)), axis=1)
    gains = jnp.moveaxis(gains, 3, 0).reshape(4, 1, model_width).astype(f32)
    gain_attn, gain_ffn = gains[2], gains[3]
    width = heads * HEAD_DIM
    head_gains = gather_rows(jnp.stack([query_gain, key_gain])[None], pair).astype(f32)
    gain_query = head_gains[:, 0].reshape(width)
    gain_key = head_gains[:, 1].reshape(width)

    earlier = jnp.sum((docs[:, None, :] < docs[:, :, None]).astype(jnp.int32), axis=2)
    positions = jnp.arange(length, dtype=jnp.int32)[None] - earlier
    half_dim = HEAD_DIM // 2
    inverse = jnp.exp(
        jnp.arange(half_dim, dtype=f32) * (-2.0 * math.log(theta_base) / HEAD_DIM)
    )
    angles = positions.astype(f32)[:, :, None] * inverse[None, None, :]
    cosines = jnp.cos(angles)[:, :, None, :]
    sines = jnp.sin(angles)[:, :, None, :]
    token_idx = jnp.arange(length)
    allowed = (docs[:, :, None] == docs[:, None, :]) & (
        token_idx[:, None] >= token_idx[None, :]
    )[None]

    def split_heads(values):
        return values.reshape(blocks, length, heads, HEAD_DIM)

    all_raw = jnp.dot(tokens, full_qkv, preferred_element_type=f32)
    query_raw, key_raw = all_raw[:, :width], all_raw[:, width : 2 * width]
    squares = group_sum(
        jnp.stack([jnp.sum(query_raw * query_raw, axis=-1), jnp.sum(key_raw * key_raw, axis=-1)])
    )
    head_scales = lax.rsqrt(squares / model_width + epsilon)
    query_unit = query_raw * head_scales[0][:, None]
    key_unit = key_raw * head_scales[1][:, None]
    query_low = rotate(split_heads(query_unit * gain_query), cosines, sines).astype(jnp.bfloat16)
    key_low = rotate(split_heads(key_unit * gain_key), cosines, sines).astype(jnp.bfloat16)
    value_low = split_heads(all_raw[:, 2 * width :].astype(jnp.bfloat16))
    scores = (
        jnp.einsum("sqhd,skhd->shqk", query_low, key_low, preferred_element_type=f32) * factor
    )
    scores = jnp.where(allowed[:, None], scores, neg_fill)
    row_peak = jnp.max(scores, axis=-1, keepdims=True)
    log_norm = row_peak + jnp.log(jnp.sum(jnp.exp(scores - row_peak), axis=-1, keepdims=True))
    attn_prob = jnp.exp(scores - log_norm)
    prob_low = attn_prob.astype(jnp.bfloat16)
    mixed_low = (
        jnp.einsum("shqk,skhd->sqhd", prob_low, value_low, preferred_element_type=f32)
        .reshape(blocks * length, width)
        .astype(jnp.bfloat16)
    )

    def to_blocks(values):
        return values.astype(jnp.bfloat16).reshape(blocks, length, model_width)

    resid_low, attn_out, resid, full_gate, full_up, full_down = attention_block(
        to_blocks(jnp.dot(mixed_low, full_output, preferred_element_type=f32)),
        hidden_in,
        gain_attn,
        [Spread(w_gate), Spread(w_up), Stack(w_down)],
        1,
    )
    resid_low = resid_low.reshape(blocks * length, model_width)

    gate_proj = jnp.dot(resid_low, full_gate, preferred_element_type=f32)
    up_proj = jnp.dot(resid_low, full_up, preferred_element_type=f32)
    gate_sig = jax.nn.sigmoid(gate_proj)
    hidden_ffn = (gate_proj * gate_sig * up_proj).astype(jnp.bfloat16)
    d_ffn_low, hidden_out, ffn_gain_term = ffn_block(
        to_blocks(jnp.dot(hidden_ffn, full_down, preferred_element_type=f32)),
        resid,
        out_cotangent,
        gain_ffn,
        2,
    )
    d_ffn_low = d_ffn_low.reshape(blocks * length, model_width)

    d_hidden_ffn = dot_back(d_ffn_low, full_down)
    d_gate_low = (d_hidden_ffn * up_proj * gate_sig * (1.0 + gate_proj * (1.0 - gate_sig))).astype(
        jnp.bfloat16
    )
    d_up_low = (d_hidden_ffn * gate_proj * gate_sig).astype(jnp.bfloat16)
    def outer(left_side, right_side):
        return lax.dot_general(
            left_side, right_side, (((0,), (0,)), ((), ())), preferred_element_type=f32
        ).astype(jnp.bfloat16)

    def joined(first, second):
        return (first.astype(f32) + second.astype(f32)).astype(jnp.bfloat16)

    ff_rows = w_down.shape[0]
    part_gate = outer(resid_low, d_gate_low)
    part_up = outer(resid_low, d_up_low)
    part_down = outer(hidden_ffn, d_ffn_low).reshape(2, ff_rows, model_width)

    def other_columns(line, ref):
        return ref.at[:, pl.ds(pl.multiple_of((1 - line.rep) * ff_rows, ff_rows), ff_rows)]

    def other_pair(line, ref):
        return ref.at[1 - line.pair]

    def other_rows(line, ref):
        return ref.at[:, 1 - line.pair]

    def same(line, ref):
        return ref

    columns = (model_width, ff_rows)
    d_attn_low, d_resid, attn_gain_term, there_gate, there_up, there_down = back_block(
        to_blocks(dot_back(d_gate_low, full_gate) + dot_back(d_up_low, full_up)),
        out_cotangent,
        attn_out,
        gain_attn,
        [
            Swap(part_gate, columns, other_columns, "partner"),
            Swap(part_up, columns, other_columns, "partner"),
            Swap(part_down, part_down.shape[1:], other_pair, "across"),
        ],
        3,
    )

    def own_columns(values):
        return lax.dynamic_slice_in_dim(values, lax.axis_index("rep") * ff_rows, ff_rows, 1)

    def own_pair(values, axis):
        return lax.dynamic_index_in_dim(values, pair, axis, keepdims=False)

    ffn_part = jnp.concatenate(
        [joined(own_columns(part_gate), there_gate), joined(own_columns(part_up), there_up)], axis=1
    ).reshape(LINE, 2, 2 * length, 2 * ff_rows)
    ffn_part = joined(own_pair(ffn_part, 1), pair_swap(own_pair(ffn_part[:, ::-1], 1)))
    down_part = joined(own_pair(part_down, 0), there_down)
    d_attn_low = d_attn_low.reshape(blocks * length, model_width)

    d_mixed_low = split_heads(dot_back(d_attn_low, full_output).astype(jnp.bfloat16))
    d_value = jnp.einsum("shqk,sqhd->skhd", prob_low, d_mixed_low, preferred_element_type=f32)
    d_prob = jnp.einsum("sqhd,skhd->shqk", d_mixed_low, value_low, preferred_element_type=f32)
    d_scores_low = (
        attn_prob * (d_prob - jnp.sum(d_prob * attn_prob, axis=-1, keepdims=True))
    ).astype(jnp.bfloat16)
    d_query_rot = (
        jnp.einsum("shqk,skhd->sqhd", d_scores_low, key_low, preferred_element_type=f32) * factor
    )
    d_key_rot = (
        jnp.einsum("shqk,sqhd->skhd", d_scores_low, query_low, preferred_element_type=f32)
        * factor
    )
    d_query_normed = rotate(d_query_rot, cosines, -sines).reshape(blocks * length, width)
    d_key_normed = rotate(d_key_rot, cosines, -sines).reshape(blocks * length, width)
    query_gain_term = jnp.sum(d_query_normed * query_unit, axis=0)
    key_gain_term = jnp.sum(d_key_normed * key_unit, axis=0)
    query_up = d_query_normed * gain_query
    key_up = d_key_normed * gain_key
    means = (
        group_sum(
            jnp.stack(
                [jnp.sum(query_up * query_unit, axis=-1), jnp.sum(key_up * key_unit, axis=-1)]
            )
        )
        / model_width
    )
    d_query_low = (head_scales[0][:, None] * (query_up - query_unit * means[0][:, None])).astype(
        jnp.bfloat16
    )
    d_key_low = (head_scales[1][:, None] * (key_up - key_unit * means[1][:, None])).astype(
        jnp.bfloat16
    )
    d_value_low = d_value.reshape(blocks * length, width).astype(jnp.bfloat16)
    d_qkv_low = jnp.concatenate([d_query_low, d_key_low, d_value_low], axis=1)
    part_qkv = outer(tokens, d_qkv_low).reshape(LINE, 2, 2 * length, 3 * width)
    part_output = outer(mixed_low, d_attn_low).reshape(2, length, model_width)
    hidden_grad, there_qkv, there_output, there_down, ffn_total = last_block(
        to_blocks(
            dot_back(d_qkv_low, full_qkv)
        ),
        d_resid,
        [
            Swap(part_qkv, (LINE, 2 * length, 3 * width), other_rows, "across"),
            Swap(part_output, (length, model_width), other_pair, "across"),
            Swap(down_part, down_part.shape, same, "partner"),
            Deal(ffn_part.reshape(blocks, length, 2 * ff_rows), 2, True),
        ],
        4,
    )
    qkv_part = joined(own_pair(part_qkv, 1), there_qkv).reshape(blocks, length, 3 * width)
    output_part = joined(own_pair(part_output, 0), there_output)
    qkv_own, qkv_there, there_output = line_call(
        5, 1, None, [], [], False, False,
        [Deal(qkv_part, 3, False), Swap(output_part, output_part.shape, same, "partner")],
    )

    def total_of(first, second):
        return first.astype(f32) + second.astype(f32)

    grad_query, grad_key, grad_value = jnp.split(total_of(qkv_own, qkv_there), 3, axis=1)
    grad_gate, grad_up = jnp.split(ffn_total.astype(f32), 2, axis=1)
    grad_output = total_of(output_part, there_output)
    grad_down = total_of(down_part, there_down)
    head_terms = jnp.stack([query_gain_term, key_gain_term]).reshape(2, 2, HEAD_DIM)
    own_term, other_term = by_pair(pair, head_terms[:, 0], head_terms[:, 1])
    head_grads = own_term + pair_swap(other_term)
    wide_grads = lax.psum_scatter(
        jnp.stack([jnp.sum(attn_gain_term, axis=0), jnp.sum(ffn_gain_term, axis=0)]),
        "shard",
        scatter_dimension=1,
        tiled=True,
    )
    gain_grads = jnp.concatenate([head_grads, wide_grads])
    gain_grads = gain_grads + rep_swap(gain_grads)
    return (
        hidden_out,
        hidden_grad,
        grad_query,
        grad_key,
        grad_value,
        grad_output,
        gain_grads[0],
        gain_grads[1],
        gain_grads[2],
        grad_gate,
        grad_up,
        grad_down,
        gain_grads[3],
    )


def solution(mesh):
    placed = (
        P(("rep", "shard"), None),
        P(("rep", "shard"), None),
        P("shard", None),
        P("shard", None),
        P("shard", None),
        P("shard", None),
        P("shard"),
        P("shard"),
        P("shard"),
        P("shard", None),
        P("shard", None),
        P("shard", None),
        P("shard"),
        P(("rep", "shard"), None),
    )
    return jax.shard_map(
        on_device if mesh.shape["shard"] == 16 else on_device_general,
        mesh=mesh,
        in_specs=placed,
        out_specs=(
            P(("rep", "shard"), None),
            P(("rep", "shard"), None),
            P("shard", None),
            P("shard", None),
            P("shard", None),
            P("shard", None),
            P("shard"),
            P("shard"),
            P("shard"),
            P("shard", None),
            P("shard", None),
            P("shard", None),
            P("shard"),
        ),
        check_vma=False,
    )
```

```python
import math

import jax
import jax.numpy as jnp
from jax import lax
from jax.experimental import pallas as pl
from jax.experimental.pallas import tpu as pltpu
from jax.sharding import PartitionSpec as P

HEADS = 16
HEAD_DIM = 128


epsilon = 1e-06
theta_base = 500000.0
neg_fill = -1e30


def rms_scale(values):
    return lax.rsqrt(jnp.mean(values * values, axis=-1, keepdims=True) + epsilon)


def rms_back(upstream, normed, row_scale):
    return row_scale * (upstream - normed * jnp.mean(upstream * normed, axis=-1, keepdims=True))


def rotate(values, cosines, sines):
    half_dim = values.shape[-1] // 2
    first_half = values[..., :half_dim]
    second = values[..., half_dim:]
    return jnp.concatenate(
        [first_half * cosines - second * sines, second * cosines + first_half * sines], axis=-1
    )


def dot_back(left_side, right_side):
    return lax.dot_general(
        left_side, right_side, (((1,), (1,)), ((), ())), preferred_element_type=jnp.float32
    )


def col_term(left_side, right_side):

    def block_term(row_start, row_count):
        return lax.dot_general(
            left_side, right_side, (((0,), (0,)), ((), ())), preferred_element_type=jnp.float32
        )

    return block_term


def on_device_general(
    hidden_in,
    segments,
    w_query,
    w_key,
    w_value,
    w_output,
    query_gain,
    key_gain,
    attn_gain,
    w_gate,
    w_up,
    w_down,
    ffn_gain,
    out_cotangent,
):
    length = hidden_in.shape[0]
    model_width = hidden_in.shape[1]
    ffn_width = w_gate.shape[1]
    factor = HEAD_DIM ** (-0.5)
    doc_row = segments[0]
    earlier = jnp.sum((doc_row[None, :] < doc_row[:, None]).astype(jnp.int32), axis=1)
    positions = jnp.arange(length, dtype=jnp.int32) - earlier
    half_dim = HEAD_DIM // 2
    inverse = jnp.exp(
        jnp.arange(half_dim, dtype=jnp.float32) * (-2.0 * math.log(theta_base) / HEAD_DIM)
    )
    angles = positions.astype(jnp.float32)[:, None] * inverse[None, :]
    cosines = jnp.cos(angles)[:, None, :]
    sines = jnp.sin(angles)[:, None, :]
    token_idx = jnp.arange(length)
    allowed = (doc_row[:, None] == doc_row[None, :]) & (token_idx[:, None] >= token_idx[None, :])

    def reduce_rows(term_fn, local_rows):
        return lax.psum_scatter(
            term_fn(jnp.int32(0), local_rows * lax.axis_size("shard")),
            "shard",
            scatter_dimension=0,
            tiled=True,
        )

    def norm_rope(raw_proj, gain_vec):
        normed = raw_proj * rms_scale(raw_proj) * gain_vec
        return rotate(normed.reshape(length, HEADS, HEAD_DIM), cosines, sines)

    def attend_scores(query_low, key_low):
        scores = (
            jnp.einsum("qhd,khd->hqk", query_low, key_low, preferred_element_type=jnp.float32)
            * factor
        )
        return jnp.where(allowed[None], scores, neg_fill)

    full_query, full_key, full_value, gain_query, gain_key = (
        lax.all_gather(w_query, "shard", axis=0, tiled=True),
        lax.all_gather(w_key, "shard", axis=0, tiled=True),
        lax.all_gather(w_value, "shard", axis=0, tiled=True),
        lax.all_gather(query_gain, "shard", axis=0, tiled=True),
        lax.all_gather(key_gain, "shard", axis=0, tiled=True),
    )
    query_raw = jnp.dot(hidden_in, full_query, preferred_element_type=jnp.float32)
    key_raw = jnp.dot(hidden_in, full_key, preferred_element_type=jnp.float32)
    query_low = norm_rope(query_raw, gain_query.astype(jnp.float32)).astype(jnp.bfloat16)
    key_low = norm_rope(key_raw, gain_key.astype(jnp.float32)).astype(jnp.bfloat16)
    value_low = (
        jnp.dot(hidden_in, full_value, preferred_element_type=jnp.float32)
        .astype(jnp.bfloat16)
        .reshape(length, HEADS, HEAD_DIM)
    )
    scores = attend_scores(query_low, key_low)
    row_peak = jnp.max(scores, axis=-1, keepdims=True)
    log_norm = row_peak + jnp.log(jnp.sum(jnp.exp(scores - row_peak), axis=-1, keepdims=True))
    attn_prob = jnp.exp(scores - log_norm)
    mixed_low = (
        jnp.einsum(
            "hqk,khd->qhd",
            attn_prob.astype(jnp.bfloat16),
            value_low,
            preferred_element_type=jnp.float32,
        )
        .reshape(length, model_width)
        .astype(jnp.bfloat16)
    )
    full_output, gain_attn = (
        lax.all_gather(w_output, "shard", axis=0, tiled=True),
        lax.all_gather(attn_gain, "shard", axis=0, tiled=True),
    )
    attn_out = jnp.dot(mixed_low, full_output, preferred_element_type=jnp.float32)
    attn_rms = rms_scale(attn_out)
    attn_normed = attn_out * attn_rms
    resid = hidden_in.astype(jnp.float32) + attn_normed * gain_attn.astype(jnp.float32)
    resid_low = resid.astype(jnp.bfloat16)
    full_gate, full_up = (
        lax.all_gather(w_gate, "shard", axis=0, tiled=True),
        lax.all_gather(w_up, "shard", axis=0, tiled=True),
    )
    gate_proj = jnp.dot(resid_low, full_gate, preferred_element_type=jnp.float32)
    up_proj = jnp.dot(resid_low, full_up, preferred_element_type=jnp.float32)
    gate_sig = jax.nn.sigmoid(gate_proj)
    hidden_ffn = (gate_proj * gate_sig * up_proj).astype(jnp.bfloat16)
    full_down, gain_ffn = (
        lax.all_gather(w_down, "shard", axis=0, tiled=True),
        lax.all_gather(ffn_gain, "shard", axis=0, tiled=True),
    )
    ffn_out = jnp.dot(hidden_ffn, full_down, preferred_element_type=jnp.float32)
    ffn_rms = rms_scale(ffn_out)
    ffn_normed = ffn_out * ffn_rms
    hidden_out = (resid + ffn_normed * gain_ffn.astype(jnp.float32)).astype(jnp.bfloat16)
    grad_out = out_cotangent.astype(jnp.float32)
    back_down, back_fgain = (
        lax.all_gather(w_down, "shard", axis=0, tiled=True),
        lax.all_gather(ffn_gain, "shard", axis=0, tiled=True),
    )
    ffn_gain_term = jnp.sum(grad_out * ffn_normed, axis=0)
    d_ffn_low = rms_back(grad_out * back_fgain.astype(jnp.float32), ffn_normed, ffn_rms).astype(
        jnp.bfloat16
    )
    down_grad = reduce_rows(col_term(hidden_ffn, d_ffn_low), w_down.shape[0])
    d_hidden_ffn = dot_back(d_ffn_low, back_down)
    d_gate_low = (d_hidden_ffn * up_proj * gate_sig * (1.0 + gate_proj * (1.0 - gate_sig))).astype(
        jnp.bfloat16
    )
    d_up_low = (d_hidden_ffn * gate_proj * gate_sig).astype(jnp.bfloat16)
    ffn_in_grad = reduce_rows(
        col_term(resid_low, jnp.concatenate([d_gate_low, d_up_low], axis=1)), w_gate.shape[0]
    )
    back_gate, back_up = (
        lax.all_gather(w_gate, "shard", axis=0, tiled=True),
        lax.all_gather(w_up, "shard", axis=0, tiled=True),
    )
    d_resid = grad_out + dot_back(d_gate_low, back_gate) + dot_back(d_up_low, back_up)
    back_output, back_again = (
        lax.all_gather(w_output, "shard", axis=0, tiled=True),
        lax.all_gather(attn_gain, "shard", axis=0, tiled=True),
    )
    attn_gain_term = jnp.sum(d_resid * attn_normed, axis=0)
    d_attn_low = rms_back(d_resid * back_again.astype(jnp.float32), attn_normed, attn_rms).astype(
        jnp.bfloat16
    )
    out_grad = reduce_rows(col_term(mixed_low, d_attn_low), w_output.shape[0])
    d_mixed_low = (
        dot_back(d_attn_low, back_output).astype(jnp.bfloat16).reshape(length, HEADS, HEAD_DIM)
    )
    scores_again = attend_scores(query_low, key_low)
    prob_again = jnp.exp(scores_again - log_norm)
    d_value = jnp.einsum(
        "hqk,qhd->khd",
        prob_again.astype(jnp.bfloat16),
        d_mixed_low,
        preferred_element_type=jnp.float32,
    )
    d_prob = jnp.einsum("qhd,khd->hqk", d_mixed_low, value_low, preferred_element_type=jnp.float32)
    d_scores_low = (
        prob_again * (d_prob - jnp.sum(d_prob * prob_again, axis=-1, keepdims=True))
    ).astype(jnp.bfloat16)
    d_query_rot = (
        jnp.einsum("hqk,khd->qhd", d_scores_low, key_low, preferred_element_type=jnp.float32)
        * factor
    )
    d_key_rot = (
        jnp.einsum("hqk,qhd->khd", d_scores_low, query_low, preferred_element_type=jnp.float32)
        * factor
    )
    back_query, back_key, back_value, back_qgain, back_kgain = (
        lax.all_gather(w_query, "shard", axis=0, tiled=True),
        lax.all_gather(w_key, "shard", axis=0, tiled=True),
        lax.all_gather(w_value, "shard", axis=0, tiled=True),
        lax.all_gather(query_gain, "shard", axis=0, tiled=True),
        lax.all_gather(key_gain, "shard", axis=0, tiled=True),
    )
    unused_query, query_pull = jax.vjp(norm_rope, query_raw, back_qgain.astype(jnp.float32))
    d_query_raw, query_gain_term = query_pull(d_query_rot)
    unused_key, key_pull = jax.vjp(norm_rope, key_raw, back_kgain.astype(jnp.float32))
    d_key_raw, key_gain_term = key_pull(d_key_rot)
    d_query_low = d_query_raw.astype(jnp.bfloat16)
    d_key_low = d_key_raw.astype(jnp.bfloat16)
    d_value_low = d_value.reshape(length, model_width).astype(jnp.bfloat16)
    qkv_grad = reduce_rows(
        col_term(hidden_in, jnp.concatenate([d_query_low, d_key_low, d_value_low], axis=1)),
        w_query.shape[0],
    )
    hidden_grad = (
        d_resid
        + dot_back(d_query_low, back_query)
        + dot_back(d_key_low, back_key)
        + dot_back(d_value_low, back_value)
    ).astype(jnp.bfloat16)
    gain_sums = (
        lax.psum_scatter(query_gain_term, "shard", scatter_dimension=0, tiled=True),
        lax.psum_scatter(key_gain_term, "shard", scatter_dimension=0, tiled=True),
        lax.psum_scatter(attn_gain_term, "shard", scatter_dimension=0, tiled=True),
        lax.psum_scatter(ffn_gain_term, "shard", scatter_dimension=0, tiled=True),
    )
    totals = (
        lax.psum(qkv_grad[:, :model_width].astype(jnp.bfloat16), "rep").astype(jnp.float32),
        lax.psum(qkv_grad[:, model_width : 2 * model_width].astype(jnp.bfloat16), "rep").astype(
            jnp.float32
        ),
        lax.psum(qkv_grad[:, 2 * model_width :].astype(jnp.bfloat16), "rep").astype(jnp.float32),
        lax.psum(out_grad.astype(jnp.bfloat16), "rep").astype(jnp.float32),
        lax.psum(gain_sums[0].astype(jnp.bfloat16), "rep").astype(jnp.float32),
        lax.psum(gain_sums[1].astype(jnp.bfloat16), "rep").astype(jnp.float32),
        lax.psum(gain_sums[2].astype(jnp.bfloat16), "rep").astype(jnp.float32),
        lax.psum(ffn_in_grad[:, :ffn_width].astype(jnp.bfloat16), "rep").astype(jnp.float32),
        lax.psum(ffn_in_grad[:, ffn_width:].astype(jnp.bfloat16), "rep").astype(jnp.float32),
        lax.psum(down_grad.astype(jnp.bfloat16), "rep").astype(jnp.float32),
        lax.psum(gain_sums[3].astype(jnp.bfloat16), "rep").astype(jnp.float32),
    )
    return (
        hidden_out,
        hidden_grad,
        totals[0],
        totals[1],
        totals[2],
        totals[3],
        totals[4],
        totals[5],
        totals[6],
        totals[7],
        totals[8],
        totals[9],
        totals[10],
    )


LINE = 4


def shard_perm(move):
    return [(index, move(index)) for index in range(16)]


def pair_swap(values):
    return lax.ppermute(values, "shard", shard_perm(lambda index: index ^ 2))


def rep_swap(values):
    return lax.ppermute(values, "rep", [(0, 1), (1, 0)])


def by_pair(pair, own, other):
    return jnp.where(pair == 0, own, other), jnp.where(pair == 0, other, own)


def gather_rows(weight, pair):
    return jnp.concatenate(by_pair(pair, weight, pair_swap(weight)), axis=0)


MESH_ID = pl.DeviceIdType.MESH


class Line:
    def __init__(self):
        index = lax.axis_index("shard")
        self.rep = lax.axis_index("rep")
        self.place = index // 4
        self.pair = (index // 2) % 2
        self.core = index % 2
        self.block = self.place * 2 + self.core
        self.sibling = self.at(self.place, self.pair, 1 - self.core)
        self.right = self.at(jnp.minimum(self.place + 1, LINE - 1), self.pair, self.core)
        self.left = self.at(jnp.maximum(self.place - 1, 0), self.pair, self.core)
        self.across = self.at(self.place, 1 - self.pair, self.core)
        self.partner = (1 - self.rep, index)
        self.has_right = self.place < LINE - 1
        self.has_left = self.place > 0

    def at(self, place, pair, core):
        return (self.rep, place * 4 + pair * 2 + core)

    def piece(self, p, sign):
        return (self.place + sign * (p // 2) + LINE) % LINE, (self.core + p % 2) % 2

    def meet(self, wide):
        barrier = pltpu.get_barrier_semaphore()

        def greet(device):
            pl.semaphore_signal(barrier, inc=1, device_id=device, device_id_type=MESH_ID)

        if wide:
            for p in range(1, 2 * LINE):
                place, core = self.piece(p, 1)
                greet(self.at(place, self.pair, core))
            greet(self.across)
            greet(self.partner)
            pl.semaphore_wait(barrier, 2 * LINE + 1)
            return
        greet(self.sibling)
        pl.when(self.has_right)(lambda: greet(self.right))
        pl.when(self.has_left)(lambda: greet(self.left))
        pl.semaphore_wait(
            barrier, 1 + self.has_right.astype(jnp.int32) + self.has_left.astype(jnp.int32)
        )


def remote(source, target, send_sem, recv_sem, device):
    return pltpu.make_async_remote_copy(
        src_ref=source,
        dst_ref=target,
        send_sem=send_sem,
        recv_sem=recv_sem,
        device_id=device,
        device_id_type=MESH_ID,
    )


class Spread:
    semaphores = ((2 * LINE,),) * 2 + ((2 * LINE, 2),) * 4
    buffers = ()
    near = True

    def __init__(self, *weights, begin=0, burst=False):
        self.inputs, self.begin, self.burst = list(weights), begin, burst
        shape = (16 * weights[0].shape[0], sum(weight.shape[1] for weight in weights) // 8)
        self.outputs = [jax.ShapeDtypeStruct(shape, jnp.bfloat16)]
        self.slots = begin + 3 + 2 * LINE

    def bind(self, line, sources, targets, sems):
        self.line, self.sources, self.target = line, sources, targets[0]
        self.z_send, self.z_recv, self.y_send, self.y_recv, self.x_send, self.x_recv = sems
        self.half = sources[0].shape[0] // 2

    def slot(self, t):
        t -= self.begin
        for p in range(2 * LINE):
            if t == (0 if self.burst else (p + 1) // 3):
                self.start(p)
        for p in range(2 * LINE):
            if t == (p + 1 if p else 0):
                self.came(p)
        for p in range(2 * LINE):
            if t == p + 3:
                self.onward(p)

    def rows(self, place, pair, core, rep):
        start = ((place * 4 + pair * 2 + core) * 2 + rep) * self.half
        return self.target.at[pl.ds(pl.multiple_of(start, self.half), self.half), :]

    def start(self, p):
        line, half = self.line, self.half
        place, core = line.piece(p, 1)
        here = self.rows(line.place, line.pair, line.core, line.rep)
        mine = pl.ds(pl.multiple_of(line.rep * half, half), half)
        at = 0
        for q in range(2):
            for source in self.sources:
                n = source.shape[1] // 16
                column = pl.multiple_of((place * 4 + q * 2 + core) * n, n)
                piece, goal = source.at[mine, pl.ds(column, n)], here.at[:, pl.ds(at, n)]
                if p == 0:
                    pltpu.make_async_copy(piece, goal, self.z_recv.at[0]).start()
                else:
                    remote(
                        piece, goal, self.z_send.at[p], self.z_recv.at[p], line.at(place, line.pair, core)
                    ).start()
                at += n

    def cross(self, p, pair, rep, which):
        place, core = self.line.piece(p, -1)
        ref = self.rows(place, pair, core, rep)
        return remote(ref, ref, self.y_send.at[p, which], self.y_recv.at[p, which], self.line.across)

    def over(self, p, pair, rep, which):
        place, core = self.line.piece(p, -1)
        ref = self.rows(place, pair, core, rep)
        return remote(ref, ref, self.x_send.at[p, which], self.x_recv.at[p, which], self.line.partner)

    def came(self, p):
        line = self.line
        place, core = line.piece(p, -1)
        ref = self.rows(place, line.pair, core, line.rep)
        if p == 0:
            pltpu.make_async_copy(ref, ref, self.z_recv.at[0]).wait()
        else:
            remote(ref, ref, self.z_send.at[p], self.z_recv.at[p], line.sibling).wait_recv()
        self.cross(p, line.pair, line.rep, 0).start()
        self.over(p, line.pair, line.rep, 0).start()

    def onward(self, p):
        line = self.line
        if p % 2:
            self.over(p, line.pair, 1 - line.rep, 0).wait_recv()
            self.cross(p, line.pair, 1 - line.rep, 1).start()
        else:
            self.cross(p, 1 - line.pair, line.rep, 0).wait_recv()
            self.over(p, 1 - line.pair, line.rep, 1).start()

    def finish(self):
        line = self.line
        pair, rep = line.pair, line.rep
        for p in range(2 * LINE):
            if p > 0:
                ref = self.rows(line.place, pair, line.core, rep)
                remote(ref, ref, self.z_send.at[p], self.z_recv.at[p], line.sibling).wait_send()
            self.cross(p, pair, rep, 0).wait_send()
            self.over(p, pair, rep, 0).wait_send()
            if p % 2:
                self.cross(p, 1 - pair, rep, 0).wait_recv()
                self.cross(p, pair, 1 - rep, 1).wait_send()
                self.cross(p, 1 - pair, 1 - rep, 1).wait_recv()
            else:
                self.over(p, pair, 1 - rep, 0).wait_recv()
                self.over(p, 1 - pair, rep, 1).wait_send()
                self.over(p, 1 - pair, 1 - rep, 1).wait_recv()


class Stack:
    buffers = ()
    near = True

    def __init__(self, weight, count):
        self.inputs, self.count = [weight], count
        self.outputs = [jax.ShapeDtypeStruct((2 * weight.shape[0], weight.shape[1]), weight.dtype)]
        self.semaphores = ((1,),) + ((count,),) * 4
        self.slots = 1 + count

    def bind(self, line, sources, targets, sems):
        self.line, self.source, self.target = line, sources[0], targets[0]
        self.local, self.y_send, self.y_recv, self.x_send, self.x_recv = sems
        self.size = self.source.shape[0]

    def here(self):
        size = self.size
        mine = self.target.at[pl.ds(pl.multiple_of(self.line.pair * size, size), size), :]
        return pltpu.make_async_copy(self.source, mine, self.local.at[0])

    def there(self, p):
        line, part = self.line, self.size // (2 * self.count)
        start = pl.multiple_of((line.rep * self.count + p) * part, part)
        goal = self.target.at[pl.ds(pl.multiple_of(line.pair * self.size + start, part), part), :]
        return remote(
            self.source.at[pl.ds(start, part), :], goal, self.y_send.at[p], self.y_recv.at[p], line.across
        )

    def onward(self, p, rep):
        line, part = self.line, self.size // (2 * self.count)
        start = (1 - line.pair) * self.size + (rep * self.count + p) * part
        ref = self.target.at[pl.ds(pl.multiple_of(start, part), part), :]
        return remote(ref, ref, self.x_send.at[p], self.x_recv.at[p], line.partner)

    def slot(self, t):
        if t == 0:
            for k in range(self.count):
                self.there(k).start()
            self.here().start()
        if 1 <= t < 1 + self.count:
            self.there(t - 1).wait_recv()
            self.onward(t - 1, self.line.rep).start()

    def finish(self):
        self.here().wait()
        for p in range(self.count):
            self.there(p).wait_send()
            self.onward(p, self.line.rep).wait_send()
            self.onward(p, 1 - self.line.rep).wait_recv()


class Swap:
    semaphores = ((2,),)
    buffers = ()
    near = True
    slots = 1

    def __init__(self, values, start, count):
        self.inputs, self.start, self.count = [values], start, count
        self.outputs = [jax.ShapeDtypeStruct((count, values.shape[1]), values.dtype)]

    def bind(self, line, sources, targets, scratch):
        sends, recvs = scratch[0].at[0], scratch[0].at[1]
        rows = sources[0].at[pl.ds(self.start, self.count), :]
        self.copy = remote(rows, targets[0], sends, recvs, line.partner)

    def slot(self, t):
        if t == 0:
            self.copy.start()

    def finish(self):
        self.copy.wait()


class Deal:
    semaphores = ((2 * LINE,),) * 4
    buffers = ()
    near = True
    slots = 3 + 2 * LINE

    def __init__(self, sources, per):
        rows, width = sources[0].shape[1:]
        self.inputs, self.per = list(sources), per
        self.n = width // per
        self.width = width * len(sources)
        self.outputs = [jax.ShapeDtypeStruct((rows, 16 * self.width), sources[0].dtype)]

    def bind(self, line, sources, targets, scratch):
        self.line, self.sources, self.target = line, sources, targets[0]
        self.z_send, self.z_recv, self.x_send, self.x_recv = scratch

    def runs(self, place, core):
        for index, source in enumerate(self.sources):
            for run in range(self.per):
                block = (index * self.per + run) * 16 + place * 4 + self.line.rep * 2 + core
                yield source, run * self.n, pl.ds(pl.multiple_of(block * self.n, self.n), self.n)

    def whole(self):
        return self.target.at[:, pl.ds(0, self.width)]

    def start(self, p):
        line = self.line
        place, core = line.piece(p, 1)
        for source, at, there in self.runs(line.place, line.core):
            piece = source.at[2 * place + core, :, pl.ds(at, self.n)]
            goal = self.target.at[:, there]
            if p == 0:
                pltpu.make_async_copy(piece, goal, self.z_recv.at[0]).start()
            else:
                remote(
                    piece, goal, self.z_send.at[p], self.z_recv.at[p], line.at(place, line.pair, core)
                ).start()

    def came(self, p):
        line, ref = self.line, self.whole()
        if p == 0:
            pltpu.make_async_copy(ref, ref, self.z_recv.at[0]).wait()
        else:
            remote(ref, ref, self.z_send.at[p], self.z_recv.at[p], line.partner).wait_recv()
        place, core = line.piece(p, -1)
        for _, _, there in self.runs(place, core):
            goal = self.target.at[:, there]
            remote(goal, goal, self.x_send.at[p], self.x_recv.at[p], line.partner).start()

    def slot(self, t):
        if t < 2 * LINE:
            self.start(t)
        if t == 0:
            self.came(0)
        if 3 <= t < 2 + 2 * LINE:
            self.came(t - 2)

    def finish(self):
        ref = self.whole()
        for p in range(2 * LINE):
            if p > 0:
                remote(ref, ref, self.z_send.at[p], self.z_recv.at[p], self.line.partner).wait_send()
            remote(ref, ref, self.x_send.at[p], self.x_recv.at[p], self.line.partner).wait()


def add_into(target, first, second):
    step = 64

    def some(index, carry):
        rows = pl.ds(pl.multiple_of(index * step, step), step)
        target[rows, :] = first[rows, :] + second[rows, :]
        return carry

    lax.fori_loop(0, target.shape[0] // step, some, 0)


class Reduce:
    near = True

    def __init__(self, values, first):
        rows, n = values.shape[0] // 8, values.shape[1] // 2
        self.inputs, self.first, self.size, self.n = [values], first, rows, n
        self.outputs = [jax.ShapeDtypeStruct((LINE, rows, n), values.dtype)]
        self.chunks = 2 * LINE if first == "partner" else LINE
        wide = n if first == "partner" else 2 * n
        self.semaphores = ((self.chunks,),) * 2 + ((LINE,),) * 2
        self.buffers = ((self.chunks, rows, wide), (LINE, rows, n), (LINE, rows, n))
        self.join_at = [3 + (5 * k) // 2 for k in range(8)] if first == "partner" else [2, 4, 6, 8]
        self.last_at = self.join_at[LINE:] if first == "partner" else [7, 8, 9, 10]
        self.slots = max(self.last_at) + 1

    def bind(self, line, sources, targets, scratch):
        self.line, self.values, self.target = line, sources[0], targets[0]
        self.send1, self.recv1, self.send2, self.recv2, self.came1, self.out2, self.came2 = scratch

    def part(self, place, pair, rep=None):
        rows = pl.ds(pl.multiple_of((place * 2 + pair) * self.size, self.size), self.size)
        if rep is None:
            return self.values.at[rows, :]
        return self.values.at[rows, pl.ds(pl.multiple_of(rep * self.n, self.n), self.n)]

    def leg1(self, k):
        line = self.line
        if self.first == "partner":
            pair = 1 - line.pair if k < LINE else line.pair
            return remote(
                self.part(k % LINE, pair, 1 - line.rep), self.came1.at[k], self.send1.at[k], self.recv1.at[k], line.partner
            )
        return remote(self.part(k, 1 - line.pair), self.came1.at[k], self.send1.at[k], self.recv1.at[k], line.across)

    def leg2(self, k):
        device = self.line.across if self.first == "partner" else self.line.partner
        return remote(self.out2.at[k], self.came2.at[k], self.send2.at[k], self.recv2.at[k], device)

    def join(self, k):
        line, n = self.line, self.n
        self.leg1(k).wait_recv()
        if self.first == "partner":
            own = self.part(k % LINE, 1 - line.pair if k < LINE else line.pair, line.rep)
            add_into(self.out2.at[k] if k < LINE else self.target.at[k - LINE], own, self.came1.at[k])
            if k < LINE:
                self.leg2(k).start()
            return
        for rep, goal in ((1 - line.rep, self.out2.at[k]), (line.rep, self.target.at[k])):
            columns = pl.ds(pl.multiple_of(rep * n, n), n)
            add_into(goal, self.part(k, line.pair, rep), self.came1.at[k, :, columns])
        self.leg2(k).start()

    def last(self, k):
        self.leg2(k).wait_recv()
        add_into(self.target.at[k], self.target.at[k], self.came2.at[k])

    def slot(self, t):
        if t == 0:
            for k in range(self.chunks):
                self.leg1(k).start()
        for k in range(self.chunks):
            if t == self.join_at[k]:
                self.join(k)
        for k in range(LINE):
            if t == self.last_at[k]:
                self.last(k)

    def finish(self):
        for k in range(self.chunks):
            self.leg1(k).wait_send()
        for k in range(LINE):
            self.leg2(k).wait_send()


class PairSum:
    near = True

    def __init__(self, values, count, at):
        self.inputs, self.count, self.at = [values], count, at
        self.outputs = [jax.ShapeDtypeStruct(values.shape[1:], values.dtype)]
        self.semaphores = ((count,),) * 2
        self.buffers = (values.shape[1:],)
        self.slots = at + 2 * count

    def bind(self, line, sources, targets, scratch):
        self.line, self.values, self.target = line, sources[0], targets[0]
        self.sends, self.recvs, self.came = scratch
        self.size = self.target.shape[0] // self.count

    def copy(self, k):
        rows = pl.ds(k * self.size, self.size)
        return remote(
            self.values.at[1 - self.line.pair, rows, :],
            self.came.at[rows, :],
            self.sends.at[k],
            self.recvs.at[k],
            self.line.across,
        )

    def slot(self, t):
        if t == 0:
            for k in range(self.count):
                self.copy(k).start()
        for k in range(self.count):
            if t == self.at + 2 * k:
                rows = pl.ds(k * self.size, self.size)
                self.copy(k).wait_recv()
                add_into(
                    self.target.at[rows, :], self.values.at[self.line.pair, rows, :], self.came.at[rows, :]
                )

    def finish(self):
        for k in range(self.count):
            self.copy(k).wait_send()


def line_scatter_joint(line, k, rows, parts, sib):
    return parts[2 * k + line.core, rows, :].astype(jnp.float32) + sib[k, rows, :].astype(jnp.float32)


def line_scatter_pass(line, j, step, way, parts, sib, sums, came, sib_recv, send_sem, came_sem):
    rows = pl.ds(pl.multiple_of(j * step, step), step)
    device = line.right if way == 0 else line.left
    ends = line.place == 0 if way == 0 else line.place == LINE - 1

    def copy(k):
        return remote(sums.at[k, rows], came.at[k, rows], send_sem.at[k, j], came_sem.at[k, j], device)

    for k in range(LINE - 1, 0, -1) if way == 0 else range(LINE - 1):

        @pl.when(line.place < k if way == 0 else line.place > k)
        def _():
            remote(
                parts.at[2 * k + line.core, rows], sib.at[k, rows], sib_recv.at[k, j], sib_recv.at[k, j], line.sibling
            ).wait_recv()

            @pl.when(ends)
            def _():
                sums[k, rows, :] = line_scatter_joint(line, k, rows, parts, sib).astype(jnp.bfloat16)

            @pl.when(jnp.logical_not(ends))
            def _():
                copy(k).wait_recv()
                sums[k, rows, :] = (
                    line_scatter_joint(line, k, rows, parts, sib) + came[k, rows, :].astype(jnp.float32)
                ).astype(jnp.bfloat16)

            copy(k).start()


def line_scatter_total(line, j, step, parts, sib, rights, lefts, sums, sib_recv, sends, right_recv, left_recv):
    rows = pl.ds(pl.multiple_of(j * step, step), step)
    me = line.place
    remote(
        parts.at[2 * me + line.core, rows], sib.at[me, rows], sib_recv.at[me, j], sib_recv.at[me, j], line.sibling
    ).wait_recv()

    @pl.when(line.has_left)
    def _():
        remote(sums.at[me, rows], rights.at[me, rows], sends.at[me, j], right_recv.at[me, j], line.left).wait_recv()

    @pl.when(line.has_right)
    def _():
        remote(sums.at[me, rows], lefts.at[me, rows], sends.at[me, j], left_recv.at[me, j], line.right).wait_recv()

    total = line_scatter_joint(line, me, rows, parts, sib)
    total = total + jnp.where(line.has_left, rights[me, rows, :].astype(jnp.float32), 0.0)
    return total + jnp.where(line.has_right, lefts[me, rows, :].astype(jnp.float32), 0.0)


def line_scatter_start(line, pieces, step, parts, sib, sib_send, sib_recv):
    def piece(j, carry):
        rows = pl.ds(pl.multiple_of(j * step, step), step)
        for k in range(LINE):
            remote(
                parts.at[2 * k + 1 - line.core, rows],
                sib.at[k, rows],
                sib_send.at[k, j],
                sib_recv.at[k, j],
                line.sibling,
            ).start()
        return carry

    lax.fori_loop(0, pieces, piece, 0)


def line_scatter_end(line, pieces, step, parts, sib, rights, lefts, sums, sib_send, right_send, left_send):
    def piece(j, carry):
        rows = pl.ds(pl.multiple_of(j * step, step), step)
        for k in range(LINE):
            remote(
                parts.at[2 * k + 1 - line.core, rows],
                sib.at[k, rows],
                sib_send.at[k, j],
                sib_send.at[k, j],
                line.sibling,
            ).wait_send()

            @pl.when(line.place < k)
            def _():
                remote(
                    sums.at[k, rows], rights.at[k, rows], right_send.at[k, j], right_send.at[k, j], line.right
                ).wait_send()

            @pl.when(line.place > k)
            def _():
                remote(
                    sums.at[k, rows], lefts.at[k, rows], left_send.at[k, j], left_send.at[k, j], line.left
                ).wait_send()

        return carry

    lax.fori_loop(0, pieces, piece, 0)


def gather_copy(line, k, j, step, core, gathered, way, sends, recvs):
    rows = pl.ds(pl.multiple_of(j * step, step), step)
    block = 2 * k + core
    device = (line.right, line.left, line.sibling)[way]
    ref = gathered.at[block, rows]
    return remote(ref, ref, sends.at[k, way, j], recvs.at[block, j], device)


def line_gather_own(line, j, step, gathered, sends, recvs):
    def copy(way):
        return gather_copy(line, line.place, j, step, line.core, gathered, way, sends, recvs)

    pl.when(line.has_right)(lambda: copy(0).start())
    pl.when(line.has_left)(lambda: copy(1).start())
    copy(2).start()


def line_gather_pass(line, hop, j, step, gathered, sends, recvs):
    for way in (0, 1):
        k = line.place - hop if way == 0 else line.place + hop
        there = k >= 0 if way == 0 else k < LINE
        onward = line.has_right if way == 0 else line.has_left
        k = jnp.clip(k, 0, LINE - 1)

        @pl.when(there)
        def _():
            gather_copy(line, k, j, step, line.core, gathered, way, sends, recvs).wait_recv()
            pl.when(onward)(
                lambda: gather_copy(line, k, j, step, line.core, gathered, way, sends, recvs).start()
            )
            gather_copy(line, k, j, step, line.core, gathered, 2, sends, recvs).start()


def line_gather_end(line, pieces, step, gathered, sends, recvs):
    def piece(j, carry):
        for k in range(LINE):
            gather_copy(line, k, j, step, 1 - line.core, gathered, 2, sends, recvs).wait_recv()
            gather_copy(line, k, j, step, line.core, gathered, 2, sends, recvs).wait_send()

            @pl.when((line.place >= k) & line.has_right)
            def _():
                gather_copy(line, k, j, step, line.core, gathered, 0, sends, recvs).wait_send()

            @pl.when((line.place <= k) & line.has_left)
            def _():
                gather_copy(line, k, j, step, line.core, gathered, 1, sends, recvs).wait_send()

        return carry

    lax.fori_loop(0, pieces, piece, 0)


def take_from(items, count):
    taken = items[:count]
    del items[:count]
    return taken


def moves_scratch(moves):
    scratch = []
    for move in moves:
        scratch += [pltpu.SemaphoreType.DMA(shape) for shape in move.semaphores]
        scratch += [pltpu.VMEM(shape, jnp.bfloat16) for shape in move.buffers]
    return scratch


def moves_specs(moves, side):
    near, far = pl.BlockSpec(memory_space=pltpu.VMEM), pl.BlockSpec(memory_space=pl.ANY)
    return [near if move.near else far for move in moves for _ in getattr(move, side)]


def line_call(collective_id, pieces, middle, inputs, outputs, scatter, gather, moves=(), limit=44):
    step = inputs[0].shape[-2] // pieces if inputs else 0
    low = jnp.bfloat16
    scratch = []
    if scatter:
        block = inputs[0].shape[-2:]
        scratch += [pltpu.VMEM((LINE,) + block, low) for _ in range(4)]
        scratch += [pltpu.SemaphoreType.DMA((LINE, pieces)) for _ in range(6)]
    if gather:
        scratch += [pltpu.SemaphoreType.DMA((LINE, 3, pieces)), pltpu.SemaphoreType.DMA((2 * LINE, pieces))]
    n_scratch = len(scratch)
    scratch += moves_scratch(moves)
    moved = [values for move in moves for values in move.inputs]
    extras = [shape for move in moves for shape in move.outputs]

    def kernel(*refs):
        refs = list(refs)

        def take(count):
            taken = refs[:count]
            del refs[:count]
            return taken

        ins = take(len(inputs))
        given = [take(len(move.inputs)) for move in moves]
        outs = take(len(outputs))
        extra = [take(len(move.outputs)) for move in moves]
        rest = take(n_scratch)
        line = Line()
        for move, sources, targets in zip(moves, given, extra):
            move.bind(line, sources, targets, take(len(move.semaphores) + len(move.buffers)))
        line.meet(bool(moves))
        if scatter:
            sib, rights, lefts, sums, sib_send, sib_recv, right_send, left_send, right_recv, left_recv = rest[:10]
            parts = ins[0]
            line_scatter_start(line, pieces, step, parts, sib, sib_send, sib_recv)
        if gather:
            sends, recvs = rest[-2:]

        def during(j, act):
            pl.when((j >= 0) & (j < pieces))(lambda: act(j))

        def finish(j):
            rows = pl.ds(pl.multiple_of(j * step, step), step)
            total = None
            if scatter:
                total = line_scatter_total(
                    line, j, step, parts, sib, rights, lefts, sums, sib_recv, right_send, right_recv, left_recv
                )
            values = middle(total, rows, j, ins, outs)
            if gather:
                outs[0][line.block, rows, :] = values.astype(low)
                line_gather_own(line, j, step, outs[0], sends, recvs)

        def slot(t, carry):
            if scatter:
                during(
                    t - line.place,
                    lambda j: line_scatter_pass(
                        line, j, step, 0, parts, sib, sums, rights, sib_recv, right_send, right_recv
                    ),
                )
                during(
                    t - (LINE - 1 - line.place),
                    lambda j: line_scatter_pass(
                        line, j, step, 1, parts, sib, sums, lefts, sib_recv, left_send, left_recv
                    ),
                )
                during(t - (LINE - 1), finish)
            if gather:
                for hop in range(1, LINE):
                    during(
                        t - hop - (LINE - 1 if scatter else 0),
                        lambda j, hop=hop: line_gather_pass(line, hop, j, step, outs[0], sends, recvs),
                    )
            return carry

        if gather and not scatter:
            lax.fori_loop(0, pieces, lambda j, carry: (finish(j), carry)[1], 0)
        slots = pieces + (LINE - 1) * (int(scatter) + int(gather)) if inputs else 0
        apart = max([move.slots for move in moves] + [0])
        if apart <= 1:
            for move in moves:
                move.slot(0)
            if inputs:
                lax.fori_loop(0, slots, slot, 0)
        else:
            for t in range(max(slots, apart)):
                for move in moves:
                    move.slot(t)
                if t < slots:
                    slot(t, 0)
        for move in moves:
            move.finish()
        if scatter:
            line_scatter_end(
                line, pieces, step, parts, sib, rights, lefts, sums, sib_send, right_send, left_send
            )
        if gather:
            line_gather_end(line, pieces, step, outs[0], sends, recvs)

    vmem = pl.BlockSpec(memory_space=pltpu.VMEM)
    return pl.pallas_call(
        kernel,
        out_shape=[jax.ShapeDtypeStruct(shape, kind) for shape, kind in outputs] + extras,
        in_specs=[vmem] * len(inputs) + moves_specs(moves, "inputs"),
        out_specs=[vmem] * len(outputs) + moves_specs(moves, "outputs"),
        scratch_shapes=scratch,
        compiler_params=pltpu.CompilerParams(
            collective_id=collective_id, has_side_effects=True, vmem_limit_bytes=limit << 20
        ),
        cost_estimate=pl.CostEstimate(flops=10_000_000, bytes_accessed=200_000_000, transcendentals=0),
    )(*inputs, *moved)


def gather_blocks(payload, moves, collective_id):
    def middle(total, rows, j, ins, outs):
        return ins[0][rows, :]

    shape = (2 * LINE,) + payload.shape
    return line_call(collective_id, 9, middle, [payload], [(shape, jnp.bfloat16)], False, True, moves)


def attention_block(parts, hidden, gain, moves, collective_id):
    def middle(total, rows, j, ins, outs):
        outs[1][rows, :] = total
        resid = ins[1][rows, :].astype(jnp.float32) + total * rms_scale(total) * ins[2][...]
        outs[2][rows, :] = resid
        return resid

    shape = hidden.shape
    return line_call(
        collective_id, 8, middle, [parts, hidden, gain],
        [(parts.shape, jnp.bfloat16), (shape, jnp.float32), (shape, jnp.float32)], True, True, moves,
    )


def add_rows(ref, values, j):
    folded = jnp.sum(values.reshape(values.shape[0] // 8, 8, values.shape[1]), axis=0)

    @pl.when(j == 0)
    def _():
        ref[...] = folded

    @pl.when(j > 0)
    def _():
        ref[...] += folded


def ffn_block(parts, resid, cotangent, gain, collective_id):
    def middle(total, rows, j, ins, outs):
        scale = rms_scale(total)
        normed = total * scale
        grad = ins[2][rows, :].astype(jnp.float32)
        gains = ins[3][...]
        outs[1][rows, :] = (ins[1][rows, :] + normed * gains).astype(jnp.bfloat16)
        add_rows(outs[2], grad * normed, j)
        return rms_back(grad * gains, normed, scale)

    shape = resid.shape
    return line_call(
        collective_id, 8, middle, [parts, resid, cotangent, gain],
        [(parts.shape, jnp.bfloat16), (shape, jnp.bfloat16), ((8, shape[1]), jnp.float32)], True, True,
    )


def back_block(parts, cotangent, attn_out, gain, moves, collective_id):
    def middle(total, rows, j, ins, outs):
        d_resid = ins[1][rows, :].astype(jnp.float32) + total
        outs[1][rows, :] = d_resid
        attn = ins[2][rows, :]
        scale = rms_scale(attn)
        normed = attn * scale
        add_rows(outs[2], d_resid * normed, j)
        return rms_back(d_resid * ins[3][...], normed, scale)

    shape = cotangent.shape
    return line_call(
        collective_id, 8, middle, [parts, cotangent, attn_out, gain],
        [(parts.shape, jnp.bfloat16), (shape, jnp.float32), ((8, shape[1]), jnp.float32)], True, True, moves, 56,
    )


def last_block(parts, d_resid, moves, collective_id):
    def middle(total, rows, j, ins, outs):
        outs[0][rows, :] = (ins[1][rows, :] + total).astype(jnp.bfloat16)

    return line_call(
        collective_id, 8, middle, [parts, d_resid], [(d_resid.shape, jnp.bfloat16)], True, False, moves
    )


def line_exchange(line, mine, came, sends, recvs):
    def copy(p):
        place, core = line.piece(p, 1)
        return remote(mine, came.at[p], sends.at[p], recvs.at[p], line.at(place, line.pair, core))

    for p in range(1, 2 * LINE):
        copy(p).start()
    total = mine[...]
    for p in range(1, 2 * LINE):
        copy(p).wait_recv()
        total = total + came[p]
    for p in range(1, 2 * LINE):
        copy(p).wait_send()
    return total


def spot(head, index):
    start = (3 * head + index) * HEAD_DIM
    return slice(start, start + HEAD_DIM)


def turn_tables(turns):
    half = turns.shape[1] // 2
    swapped = pltpu.roll(turns, half, 1)
    first = lax.broadcasted_iota(jnp.int32, turns.shape, 1) < half
    return jnp.where(first, turns, swapped), jnp.where(first, -swapped, turns)


def as_row(column):
    return jnp.broadcast_to(column, (column.shape[0], column.shape[0])).T[0:1, :]


def as_columns(row):
    return jnp.broadcast_to(row, (row.shape[1], row.shape[1])).T


def dot(left, right, left_dim, right_dim):
    return lax.dot_general(
        left, right, (((left_dim,), (right_dim,)), ((), ())), preferred_element_type=jnp.float32
    )


def heads_call(collective_id, body, inputs, outputs, scratch, rows, moves):
    blocks, length = 2 * LINE, HEAD_DIM
    scratch = [
        pltpu.VMEM((rows, length), jnp.float32),
        pltpu.VMEM((blocks, rows, length), jnp.float32),
        pltpu.SemaphoreType.DMA((blocks,)),
        pltpu.SemaphoreType.DMA((blocks,)),
    ] + scratch
    n_scratch = len(scratch)
    moved = [values for move in moves for values in move.inputs]
    extras = [shape for move in moves for shape in move.outputs]

    def kernel(*refs):
        refs = list(refs)
        ins = take_from(refs, len(inputs))
        given = [take_from(refs, len(move.inputs)) for move in moves]
        outs = take_from(refs, len(outputs))
        extra = [take_from(refs, len(move.outputs)) for move in moves]
        rest = take_from(refs, n_scratch)
        line = Line()
        for move, sources, targets in zip(moves, given, extra):
            move.bind(line, sources, targets, take_from(refs, len(move.semaphores) + len(move.buffers)))
        line.meet(True)
        passed = [0]

        def tick():
            for move in moves:
                move.slot(passed[0])
            passed[0] += 1

        body(line, ins, outs, rest, tick)
        while passed[0] < max([move.slots for move in moves] + [0]):
            tick()
        for move in moves:
            move.finish()

    vmem = pl.BlockSpec(memory_space=pltpu.VMEM)
    return pl.pallas_call(
        kernel,
        out_shape=[jax.ShapeDtypeStruct(shape, kind) for shape, kind in outputs] + extras,
        in_specs=[vmem] * len(inputs) + moves_specs(moves, "inputs"),
        out_specs=[vmem] * len(outputs) + moves_specs(moves, "outputs"),
        scratch_shapes=scratch + moves_scratch(moves),
        compiler_params=pltpu.CompilerParams(
            collective_id=collective_id, has_side_effects=True, vmem_limit_bytes=44 << 20
        ),
        cost_estimate=pl.CostEstimate(flops=10_000_000, bytes_accessed=80_000_000, transcendentals=0),
    )(*inputs, *moved)


def attend(raw, turns, bias, gains, weight, moves, collective_id):
    blocks, length = bias.shape[:2]
    width = raw.shape[2] // 3
    heads = width // HEAD_DIM
    model_width = weight.shape[1]
    low = jnp.bfloat16

    def body(line, ins, outs, scratch, tick):
        raw, turns, bias, gains, weight = ins
        parts, lows, probs, mixed, squares = outs
        mine, came, sends, recvs = scratch

        def squares_of(b, carry):
            for index in range(2):
                total = jnp.zeros((length, 1), jnp.float32)
                for h in range(heads):
                    values = raw[b, :length, spot(h, index)]
                    total = total + jnp.sum(values * values, axis=1, keepdims=True)
                mine[pl.ds(index * blocks + b, 1), :] = as_row(total)
            return carry

        tick()
        lax.fori_loop(0, blocks, squares_of, 0)
        tick()
        squares[...] = line_exchange(line, mine, came, sends, recvs)
        tick()

        def block(b, carry):
            scales = [
                lax.rsqrt(as_columns(squares[pl.ds(index * blocks + b, 1), :]) / model_width + epsilon)
                for index in range(2)
            ]
            cos, sin = turn_tables(turns[b])
            for h in range(heads):
                here = slice(h * HEAD_DIM, (h + 1) * HEAD_DIM)
                turned = []
                for index in range(2):
                    there = spot(h, index)
                    normed = raw[b, :length, there] * scales[index] * gains[index : index + 1, here]
                    turned.append((normed * cos + pltpu.roll(normed, HEAD_DIM // 2, 1) * sin).astype(low))
                    lows[b, :, there] = turned[index]
                there = spot(h, 2)
                value = raw[b, :length, there].astype(low)
                lows[b, :, there] = value
                scores = dot(turned[0], turned[1], 1, 1) * HEAD_DIM**-0.5 + bias[b]
                powers = jnp.exp(scores - jnp.max(scores, axis=1, keepdims=True))
                prob = powers / jnp.sum(powers, axis=1, keepdims=True)
                probs[b, h] = prob
                mixed[b, :, here] = dot(prob.astype(low), value, 1, 0).astype(low)
            parts[b] = dot(mixed[b], weight[...], 1, 0).astype(low)
            return carry

        for part in range(LINE):
            lax.fori_loop(2 * part, 2 * part + 2, block, 0)
            tick()

    return heads_call(
        collective_id,
        body,
        [raw, turns, bias, gains, weight],
        [
            ((blocks, length, model_width), low),
            ((blocks, length, 3 * width), low),
            ((blocks, heads, length, length), jnp.float32),
            ((blocks, length, width), low),
            ((2 * blocks, length), jnp.float32),
        ],
        [],
        2 * blocks,
        moves,
    )


def attend_back(d_attn, weight, raw, turns, gains, lows, probs, squares, wide_terms, moves, collective_id):
    blocks, rows = raw.shape[:2]
    length = lows.shape[1]
    width = raw.shape[2] // 3
    heads = width // HEAD_DIM
    model_width = weight.shape[1]
    low = jnp.bfloat16

    def body(line, ins, outs, scratch, tick):
        d_attn, weight, raw, turns, gains, lows, probs, squares = ins[:8]
        d_low, terms, wide = outs
        mine, came, sends, recvs, upstream, unit = scratch
        tick()
        terms[...] = jnp.zeros_like(terms)
        for which in range(2):
            total = jnp.sum(ins[8 + which][...], axis=0, keepdims=True)
            for index in range(model_width // length):
                row = 2 * blocks + which * (model_width // length) + index
                mine[row : row + 1, :] = total[:, index * length : (index + 1) * length]

        def block(b, carry):
            scales = [
                lax.rsqrt(as_columns(squares[pl.ds(index * blocks + b, 1), :]) / model_width + epsilon)
                for index in range(2)
            ]
            cos, sin = turn_tables(turns[b])
            d_mixed = dot(d_attn[b], weight[...], 1, 1).astype(low)
            means = [jnp.zeros((length, 1), jnp.float32)] * 2
            for h in range(heads):
                here = slice(h * HEAD_DIM, (h + 1) * HEAD_DIM)
                places = [spot(h, index) for index in range(3)]
                query, key, value = [lows[b, :, there] for there in places]
                prob = probs[b, h]
                d_out = d_mixed[:, here]
                d_low[b, :length, places[2]] = dot(prob.astype(low), d_out, 0, 0).astype(low)
                d_prob = dot(d_out, value, 1, 1)
                d_scores = (
                    prob * (d_prob - jnp.sum(d_prob * prob, axis=1, keepdims=True))
                ).astype(low)
                turned = [dot(d_scores, key, 1, 0), dot(d_scores, query, 0, 0)]
                for index in range(2):
                    d_rot = turned[index] * HEAD_DIM**-0.5
                    d_normed = d_rot * cos - pltpu.roll(d_rot, HEAD_DIM // 2, 1) * sin
                    units = raw[b, :length, places[index]] * scales[index]
                    ups = d_normed * gains[index : index + 1, here]
                    folded = (d_normed * units).reshape(length // 8, 8, HEAD_DIM)
                    side = slice((index * heads + h) * HEAD_DIM, (index * heads + h + 1) * HEAD_DIM)
                    terms[:, side] += jnp.sum(folded, axis=0)
                    upstream[b, :, side] = ups
                    unit[b, :, side] = units
                    means[index] = means[index] + jnp.sum(ups * units, axis=1, keepdims=True)
            for index in range(2):
                mine[pl.ds(index * blocks + b, 1), :] = as_row(means[index])
            return carry

        lax.fori_loop(0, blocks, block, 0)
        mine[...] = line_exchange(line, mine, came, sends, recvs)
        wide[...] = mine[2 * blocks :, :]

        def last(b, carry):
            d_low[b, length:, :] = jnp.zeros((rows - length, 3 * width), low)
            for index in range(2):
                scale = lax.rsqrt(
                    as_columns(squares[pl.ds(index * blocks + b, 1), :]) / model_width + epsilon
                )
                mean = as_columns(mine[pl.ds(index * blocks + b, 1), :]) / model_width
                for h in range(heads):
                    side = slice((index * heads + h) * HEAD_DIM, (index * heads + h + 1) * HEAD_DIM)
                    d_low[b, :length, spot(h, index)] = (
                        scale * (upstream[b, :, side] - unit[b, :, side] * mean)
                    ).astype(low)
            return carry

        lax.fori_loop(0, blocks, last, 0)

    return heads_call(
        collective_id,
        body,
        [d_attn, weight, raw, turns, gains, lows, probs, squares, *wide_terms],
        [
            (raw.shape, low),
            ((8, 2 * width), jnp.float32),
            ((2 * model_width // length, length), jnp.float32),
        ],
        [pltpu.VMEM((blocks, length, 2 * width), jnp.float32) for _ in range(2)],
        2 * blocks + 2 * model_width // length,
        moves,
    )


def on_device(
    hidden_in,
    segments,
    w_query,
    w_key,
    w_value,
    w_output,
    query_gain,
    key_gain,
    attn_gain,
    w_gate,
    w_up,
    w_down,
    ffn_gain,
    out_cotangent,
):
    length, model_width = hidden_in.shape
    blocks = 2 * LINE
    heads = HEADS // blocks
    factor = HEAD_DIM ** (-0.5)
    pair = (lax.axis_index("shard") // 2) % 2
    f32 = jnp.float32

    extra = jnp.concatenate(
        [query_gain, key_gain, attn_gain, ffn_gain, segments[0].astype(jnp.bfloat16)]
    )
    extra = jnp.pad(extra[None], ((0, 15), (0, model_width - extra.shape[0])))
    payload, full_qkv, full_output = gather_blocks(
        jnp.concatenate([hidden_in, extra]), [Spread(w_query, w_key, w_value), Stack(w_output, 2)], 0
    )
    docs = payload[:, length, 4 * length : 5 * length].astype(jnp.int32)
    gains = payload[:, length, : 4 * length].reshape(LINE, 2, 4, length)
    gains = jnp.stack(by_pair(pair, gains, pair_swap(gains)), axis=1)
    gains = jnp.moveaxis(gains, 3, 0).reshape(4, 1, model_width).astype(f32)
    gain_attn, gain_ffn = gains[2], gains[3]
    width = heads * HEAD_DIM
    head_gains = gather_rows(jnp.stack([query_gain, key_gain])[None], pair).astype(f32)
    head_gains = head_gains.transpose(1, 0, 2).reshape(2, width)

    earlier = jnp.sum((docs[:, None, :] < docs[:, :, None]).astype(jnp.int32), axis=2)
    positions = jnp.arange(length, dtype=jnp.int32)[None] - earlier
    half_dim = HEAD_DIM // 2
    inverse = jnp.exp(
        jnp.arange(half_dim, dtype=f32) * (-2.0 * math.log(theta_base) / HEAD_DIM)
    )
    angles = positions.astype(f32)[:, :, None] * inverse[None, None, :]
    turns = jnp.cos(jnp.concatenate([angles, angles - 0.5 * math.pi], axis=-1))
    token_idx = jnp.arange(length)
    allowed = (docs[:, :, None] == docs[:, None, :]) & (
        token_idx[:, None] >= token_idx[None, :]
    )[None]
    bias = jnp.where(allowed, 0.0, neg_fill)

    def to_blocks(values):
        return values.astype(jnp.bfloat16).reshape(blocks, -1, model_width)

    raw = jnp.dot(payload.reshape(-1, model_width), full_qkv, preferred_element_type=f32)
    raw = raw.reshape(blocks, -1, 3 * width)
    attn_parts, lows, probs, mixed_low, squares, full_gate = attend(
        raw, turns, bias, head_gains, full_output, [Spread(w_gate, begin=2, burst=True)], 6
    )
    mixed_low = mixed_low.reshape(blocks * length, width)
    resid_low, attn_out, resid, full_up, full_down = attention_block(
        attn_parts,
        hidden_in,
        gain_attn,
        [Spread(w_up), Stack(w_down, 8)],
        1,
    )
    resid_low = resid_low.reshape(blocks * length, model_width)

    gate_proj = jnp.dot(resid_low, full_gate, preferred_element_type=f32)
    up_proj = jnp.dot(resid_low, full_up, preferred_element_type=f32)
    gate_sig = jax.nn.sigmoid(gate_proj)
    hidden_ffn = (gate_proj * gate_sig * up_proj).astype(jnp.bfloat16)
    d_ffn_low, hidden_out, ffn_gain_term = ffn_block(
        to_blocks(jnp.dot(hidden_ffn, full_down, preferred_element_type=f32)),
        resid,
        out_cotangent,
        gain_ffn,
        2,
    )
    d_ffn_low = d_ffn_low.reshape(blocks * length, model_width)

    d_hidden_ffn = dot_back(d_ffn_low, full_down)
    d_gate_low = (d_hidden_ffn * up_proj * gate_sig * (1.0 + gate_proj * (1.0 - gate_sig))).astype(
        jnp.bfloat16
    )
    d_up_low = (d_hidden_ffn * gate_proj * gate_sig).astype(jnp.bfloat16)
    def outer(left_side, right_side):
        return lax.dot_general(
            left_side, right_side, (((0,), (0,)), ((), ())), preferred_element_type=f32
        ).astype(jnp.bfloat16)

    ff_rows = w_down.shape[0]
    part_gate = outer(resid_low, d_gate_low)
    part_up = outer(resid_low, d_up_low)
    part_down = outer(hidden_ffn, d_ffn_low).reshape(2, ff_rows, model_width)

    d_attn_low, d_resid, attn_gain_term, gate_sum, up_sum, down_part = back_block(
        to_blocks(dot_back(d_gate_low, full_gate) + dot_back(d_up_low, full_up)),
        out_cotangent,
        attn_out,
        gain_attn,
        [
            Reduce(part_gate, "partner"),
            Reduce(part_up, "partner"),
            PairSum(part_down, 4, 13),
        ],
        3,
    )

    d_qkv, head_terms, wide_terms, there_first = attend_back(
        d_attn_low, full_output, raw, turns, head_gains, lows, probs, squares,
        [attn_gain_term, ffn_gain_term], [Swap(down_part, 0, ff_rows // 2)], 7,
    )
    d_attn_low = d_attn_low.reshape(blocks * length, model_width)
    part_qkv = outer(
        payload.reshape(-1, model_width), d_qkv.reshape(-1, 3 * width)
    )
    part_output = outer(mixed_low, d_attn_low).reshape(2, length, model_width)
    hidden_grad, qkv_sum, output_part, ffn_total, there_second = last_block(
        to_blocks(
            dot_back(d_qkv[:, :length].reshape(-1, 3 * width), full_qkv)
        ),
        d_resid,
        [
            Reduce(part_qkv, "across"),
            PairSum(part_output, 1, 5),
            Deal([gate_sum.reshape(blocks, length, -1), up_sum.reshape(blocks, length, -1)], 1),
            Swap(down_part, ff_rows // 2, ff_rows // 2),
        ],
        4,
    )
    qkv_total, there_output = line_call(
        5, 1, None, [], [], False, False,
        [
            Deal([qkv_sum.reshape(blocks, length, -1)], 3),
            Swap(output_part, 0, length),
        ],
    )

    def total_of(first, second):
        return first.astype(f32) + second.astype(f32)

    grad_query, grad_key, grad_value = jnp.split(qkv_total.astype(f32), 3, axis=1)
    grad_gate, grad_up = jnp.split(ffn_total.astype(f32), 2, axis=1)
    grad_output = total_of(output_part, there_output)
    grad_down = total_of(down_part, jnp.concatenate([there_first, there_second]))
    head_terms = jnp.sum(head_terms, axis=0).reshape(2, 2, HEAD_DIM)
    own_term, other_term = by_pair(pair, head_terms[:, 0], head_terms[:, 1])
    head_grads = own_term + pair_swap(other_term)
    wide_terms = (wide_terms + pair_swap(wide_terms)).reshape(2, 16, length)
    wide_grads = lax.dynamic_index_in_dim(wide_terms, lax.axis_index("shard"), 1, keepdims=False)
    gain_grads = jnp.concatenate([head_grads, wide_grads])
    gain_grads = gain_grads + rep_swap(gain_grads)
    return (
        hidden_out,
        hidden_grad,
        grad_query,
        grad_key,
        grad_value,
        grad_output,
        gain_grads[0],
        gain_grads[1],
        gain_grads[2],
        grad_gate,
        grad_up,
        grad_down,
        gain_grads[3],
    )


def solution(mesh):
    placed = (
        P(("rep", "shard"), None),
        P(("rep", "shard"), None),
        P("shard", None),
        P("shard", None),
        P("shard", None),
        P("shard", None),
        P("shard"),
        P("shard"),
        P("shard"),
        P("shard", None),
        P("shard", None),
        P("shard", None),
        P("shard"),
        P(("rep", "shard"), None),
    )
    return jax.shard_map(
        on_device if mesh.shape["shard"] == 16 else on_device_general,
        mesh=mesh,
        in_specs=placed,
        out_specs=(
            P(("rep", "shard"), None),
            P(("rep", "shard"), None),
            P("shard", None),
            P("shard", None),
            P("shard", None),
            P("shard", None),
            P("shard"),
            P("shard"),
            P("shard"),
            P("shard", None),
            P("shard", None),
            P("shard", None),
            P("shard"),
        ),
        check_vma=False,
    )
```

```python
import math

import jax
import jax.numpy as jnp
from jax import lax
from jax.experimental import pallas as pl
from jax.experimental.pallas import tpu as pltpu
from jax.sharding import PartitionSpec as P

HEADS = 16
HEAD_DIM = 128


epsilon = 1e-06
theta_base = 500000.0
neg_fill = -1e30


def rms_scale(values):
    return lax.rsqrt(jnp.mean(values * values, axis=-1, keepdims=True) + epsilon)


def rms_back(upstream, normed, row_scale):
    return row_scale * (upstream - normed * jnp.mean(upstream * normed, axis=-1, keepdims=True))


def rotate(values, cosines, sines):
    half_dim = values.shape[-1] // 2
    first_half = values[..., :half_dim]
    second = values[..., half_dim:]
    return jnp.concatenate(
        [first_half * cosines - second * sines, second * cosines + first_half * sines], axis=-1
    )


def dot_back(left_side, right_side):
    return lax.dot_general(
        left_side, right_side, (((1,), (1,)), ((), ())), preferred_element_type=jnp.float32
    )


def col_term(left_side, right_side):

    def block_term(row_start, row_count):
        return lax.dot_general(
            left_side, right_side, (((0,), (0,)), ((), ())), preferred_element_type=jnp.float32
        )

    return block_term


def on_device_general(
    hidden_in,
    segments,
    w_query,
    w_key,
    w_value,
    w_output,
    query_gain,
    key_gain,
    attn_gain,
    w_gate,
    w_up,
    w_down,
    ffn_gain,
    out_cotangent,
):
    length = hidden_in.shape[0]
    model_width = hidden_in.shape[1]
    ffn_width = w_gate.shape[1]
    factor = HEAD_DIM ** (-0.5)
    doc_row = segments[0]
    earlier = jnp.sum((doc_row[None, :] < doc_row[:, None]).astype(jnp.int32), axis=1)
    positions = jnp.arange(length, dtype=jnp.int32) - earlier
    half_dim = HEAD_DIM // 2
    inverse = jnp.exp(
        jnp.arange(half_dim, dtype=jnp.float32) * (-2.0 * math.log(theta_base) / HEAD_DIM)
    )
    angles = positions.astype(jnp.float32)[:, None] * inverse[None, :]
    cosines = jnp.cos(angles)[:, None, :]
    sines = jnp.sin(angles)[:, None, :]
    token_idx = jnp.arange(length)
    allowed = (doc_row[:, None] == doc_row[None, :]) & (token_idx[:, None] >= token_idx[None, :])

    def reduce_rows(term_fn, local_rows):
        return lax.psum_scatter(
            term_fn(jnp.int32(0), local_rows * lax.axis_size("shard")),
            "shard",
            scatter_dimension=0,
            tiled=True,
        )

    def norm_rope(raw_proj, gain_vec):
        normed = raw_proj * rms_scale(raw_proj) * gain_vec
        return rotate(normed.reshape(length, HEADS, HEAD_DIM), cosines, sines)

    def attend_scores(query_low, key_low):
        scores = (
            jnp.einsum("qhd,khd->hqk", query_low, key_low, preferred_element_type=jnp.float32)
            * factor
        )
        return jnp.where(allowed[None], scores, neg_fill)

    full_query, full_key, full_value, gain_query, gain_key = (
        lax.all_gather(w_query, "shard", axis=0, tiled=True),
        lax.all_gather(w_key, "shard", axis=0, tiled=True),
        lax.all_gather(w_value, "shard", axis=0, tiled=True),
        lax.all_gather(query_gain, "shard", axis=0, tiled=True),
        lax.all_gather(key_gain, "shard", axis=0, tiled=True),
    )
    query_raw = jnp.dot(hidden_in, full_query, preferred_element_type=jnp.float32)
    key_raw = jnp.dot(hidden_in, full_key, preferred_element_type=jnp.float32)
    query_low = norm_rope(query_raw, gain_query.astype(jnp.float32)).astype(jnp.bfloat16)
    key_low = norm_rope(key_raw, gain_key.astype(jnp.float32)).astype(jnp.bfloat16)
    value_low = (
        jnp.dot(hidden_in, full_value, preferred_element_type=jnp.float32)
        .astype(jnp.bfloat16)
        .reshape(length, HEADS, HEAD_DIM)
    )
    scores = attend_scores(query_low, key_low)
    row_peak = jnp.max(scores, axis=-1, keepdims=True)
    log_norm = row_peak + jnp.log(jnp.sum(jnp.exp(scores - row_peak), axis=-1, keepdims=True))
    attn_prob = jnp.exp(scores - log_norm)
    mixed_low = (
        jnp.einsum(
            "hqk,khd->qhd",
            attn_prob.astype(jnp.bfloat16),
            value_low,
            preferred_element_type=jnp.float32,
        )
        .reshape(length, model_width)
        .astype(jnp.bfloat16)
    )
    full_output, gain_attn = (
        lax.all_gather(w_output, "shard", axis=0, tiled=True),
        lax.all_gather(attn_gain, "shard", axis=0, tiled=True),
    )
    attn_out = jnp.dot(mixed_low, full_output, preferred_element_type=jnp.float32)
    attn_rms = rms_scale(attn_out)
    attn_normed = attn_out * attn_rms
    resid = hidden_in.astype(jnp.float32) + attn_normed * gain_attn.astype(jnp.float32)
    resid_low = resid.astype(jnp.bfloat16)
    full_gate, full_up = (
        lax.all_gather(w_gate, "shard", axis=0, tiled=True),
        lax.all_gather(w_up, "shard", axis=0, tiled=True),
    )
    gate_proj = jnp.dot(resid_low, full_gate, preferred_element_type=jnp.float32)
    up_proj = jnp.dot(resid_low, full_up, preferred_element_type=jnp.float32)
    gate_sig = jax.nn.sigmoid(gate_proj)
    hidden_ffn = (gate_proj * gate_sig * up_proj).astype(jnp.bfloat16)
    full_down, gain_ffn = (
        lax.all_gather(w_down, "shard", axis=0, tiled=True),
        lax.all_gather(ffn_gain, "shard", axis=0, tiled=True),
    )
    ffn_out = jnp.dot(hidden_ffn, full_down, preferred_element_type=jnp.float32)
    ffn_rms = rms_scale(ffn_out)
    ffn_normed = ffn_out * ffn_rms
    hidden_out = (resid + ffn_normed * gain_ffn.astype(jnp.float32)).astype(jnp.bfloat16)
    grad_out = out_cotangent.astype(jnp.float32)
    back_down, back_fgain = (
        lax.all_gather(w_down, "shard", axis=0, tiled=True),
        lax.all_gather(ffn_gain, "shard", axis=0, tiled=True),
    )
    ffn_gain_term = jnp.sum(grad_out * ffn_normed, axis=0)
    d_ffn_low = rms_back(grad_out * back_fgain.astype(jnp.float32), ffn_normed, ffn_rms).astype(
        jnp.bfloat16
    )
    down_grad = reduce_rows(col_term(hidden_ffn, d_ffn_low), w_down.shape[0])
    d_hidden_ffn = dot_back(d_ffn_low, back_down)
    d_gate_low = (d_hidden_ffn * up_proj * gate_sig * (1.0 + gate_proj * (1.0 - gate_sig))).astype(
        jnp.bfloat16
    )
    d_up_low = (d_hidden_ffn * gate_proj * gate_sig).astype(jnp.bfloat16)
    ffn_in_grad = reduce_rows(
        col_term(resid_low, jnp.concatenate([d_gate_low, d_up_low], axis=1)), w_gate.shape[0]
    )
    back_gate, back_up = (
        lax.all_gather(w_gate, "shard", axis=0, tiled=True),
        lax.all_gather(w_up, "shard", axis=0, tiled=True),
    )
    d_resid = grad_out + dot_back(d_gate_low, back_gate) + dot_back(d_up_low, back_up)
    back_output, back_again = (
        lax.all_gather(w_output, "shard", axis=0, tiled=True),
        lax.all_gather(attn_gain, "shard", axis=0, tiled=True),
    )
    attn_gain_term = jnp.sum(d_resid * attn_normed, axis=0)
    d_attn_low = rms_back(d_resid * back_again.astype(jnp.float32), attn_normed, attn_rms).astype(
        jnp.bfloat16
    )
    out_grad = reduce_rows(col_term(mixed_low, d_attn_low), w_output.shape[0])
    d_mixed_low = (
        dot_back(d_attn_low, back_output).astype(jnp.bfloat16).reshape(length, HEADS, HEAD_DIM)
    )
    scores_again = attend_scores(query_low, key_low)
    prob_again = jnp.exp(scores_again - log_norm)
    d_value = jnp.einsum(
        "hqk,qhd->khd",
        prob_again.astype(jnp.bfloat16),
        d_mixed_low,
        preferred_element_type=jnp.float32,
    )
    d_prob = jnp.einsum("qhd,khd->hqk", d_mixed_low, value_low, preferred_element_type=jnp.float32)
    d_scores_low = (
        prob_again * (d_prob - jnp.sum(d_prob * prob_again, axis=-1, keepdims=True))
    ).astype(jnp.bfloat16)
    d_query_rot = (
        jnp.einsum("hqk,khd->qhd", d_scores_low, key_low, preferred_element_type=jnp.float32)
        * factor
    )
    d_key_rot = (
        jnp.einsum("hqk,qhd->khd", d_scores_low, query_low, preferred_element_type=jnp.float32)
        * factor
    )
    back_query, back_key, back_value, back_qgain, back_kgain = (
        lax.all_gather(w_query, "shard", axis=0, tiled=True),
        lax.all_gather(w_key, "shard", axis=0, tiled=True),
        lax.all_gather(w_value, "shard", axis=0, tiled=True),
        lax.all_gather(query_gain, "shard", axis=0, tiled=True),
        lax.all_gather(key_gain, "shard", axis=0, tiled=True),
    )
    unused_query, query_pull = jax.vjp(norm_rope, query_raw, back_qgain.astype(jnp.float32))
    d_query_raw, query_gain_term = query_pull(d_query_rot)
    unused_key, key_pull = jax.vjp(norm_rope, key_raw, back_kgain.astype(jnp.float32))
    d_key_raw, key_gain_term = key_pull(d_key_rot)
    d_query_low = d_query_raw.astype(jnp.bfloat16)
    d_key_low = d_key_raw.astype(jnp.bfloat16)
    d_value_low = d_value.reshape(length, model_width).astype(jnp.bfloat16)
    qkv_grad = reduce_rows(
        col_term(hidden_in, jnp.concatenate([d_query_low, d_key_low, d_value_low], axis=1)),
        w_query.shape[0],
    )
    hidden_grad = (
        d_resid
        + dot_back(d_query_low, back_query)
        + dot_back(d_key_low, back_key)
        + dot_back(d_value_low, back_value)
    ).astype(jnp.bfloat16)
    gain_sums = (
        lax.psum_scatter(query_gain_term, "shard", scatter_dimension=0, tiled=True),
        lax.psum_scatter(key_gain_term, "shard", scatter_dimension=0, tiled=True),
        lax.psum_scatter(attn_gain_term, "shard", scatter_dimension=0, tiled=True),
        lax.psum_scatter(ffn_gain_term, "shard", scatter_dimension=0, tiled=True),
    )
    totals = (
        lax.psum(qkv_grad[:, :model_width].astype(jnp.bfloat16), "rep").astype(jnp.float32),
        lax.psum(qkv_grad[:, model_width : 2 * model_width].astype(jnp.bfloat16), "rep").astype(
            jnp.float32
        ),
        lax.psum(qkv_grad[:, 2 * model_width :].astype(jnp.bfloat16), "rep").astype(jnp.float32),
        lax.psum(out_grad.astype(jnp.bfloat16), "rep").astype(jnp.float32),
        lax.psum(gain_sums[0].astype(jnp.bfloat16), "rep").astype(jnp.float32),
        lax.psum(gain_sums[1].astype(jnp.bfloat16), "rep").astype(jnp.float32),
        lax.psum(gain_sums[2].astype(jnp.bfloat16), "rep").astype(jnp.float32),
        lax.psum(ffn_in_grad[:, :ffn_width].astype(jnp.bfloat16), "rep").astype(jnp.float32),
        lax.psum(ffn_in_grad[:, ffn_width:].astype(jnp.bfloat16), "rep").astype(jnp.float32),
        lax.psum(down_grad.astype(jnp.bfloat16), "rep").astype(jnp.float32),
        lax.psum(gain_sums[3].astype(jnp.bfloat16), "rep").astype(jnp.float32),
    )
    return (
        hidden_out,
        hidden_grad,
        totals[0],
        totals[1],
        totals[2],
        totals[3],
        totals[4],
        totals[5],
        totals[6],
        totals[7],
        totals[8],
        totals[9],
        totals[10],
    )


LINE = 4


def shard_perm(move):
    return [(index, move(index)) for index in range(16)]


def pair_swap(values):
    return lax.ppermute(values, "shard", shard_perm(lambda index: index ^ 2))


def rep_swap(values):
    return lax.ppermute(values, "rep", [(0, 1), (1, 0)])


def by_pair(pair, own, other):
    return jnp.where(pair == 0, own, other), jnp.where(pair == 0, other, own)


def gather_rows(weight, pair):
    return jnp.concatenate(by_pair(pair, weight, pair_swap(weight)), axis=0)


MESH_ID = pl.DeviceIdType.MESH


class Line:
    def __init__(self):
        index = lax.axis_index("shard")
        self.rep = lax.axis_index("rep")
        self.place = index // 4
        self.pair = (index // 2) % 2
        self.core = index % 2
        self.block = self.place * 2 + self.core
        self.sibling = self.at(self.place, self.pair, 1 - self.core)
        self.right = self.at(jnp.minimum(self.place + 1, LINE - 1), self.pair, self.core)
        self.left = self.at(jnp.maximum(self.place - 1, 0), self.pair, self.core)
        self.across = self.at(self.place, 1 - self.pair, self.core)
        self.partner = (1 - self.rep, index)
        self.has_right = self.place < LINE - 1
        self.has_left = self.place > 0

    def at(self, place, pair, core):
        return (self.rep, place * 4 + pair * 2 + core)

    def piece(self, p, sign):
        return (self.place + sign * (p // 2) + LINE) % LINE, (self.core + p % 2) % 2

    def meet(self, wide):
        barrier = pltpu.get_barrier_semaphore()

        def greet(device):
            pl.semaphore_signal(barrier, inc=1, device_id=device, device_id_type=MESH_ID)

        if wide:
            for p in range(1, 2 * LINE):
                place, core = self.piece(p, 1)
                greet(self.at(place, self.pair, core))
            greet(self.across)
            greet(self.partner)
            pl.semaphore_wait(barrier, 2 * LINE + 1)
            return
        greet(self.sibling)
        pl.when(self.has_right)(lambda: greet(self.right))
        pl.when(self.has_left)(lambda: greet(self.left))
        pl.semaphore_wait(
            barrier, 1 + self.has_right.astype(jnp.int32) + self.has_left.astype(jnp.int32)
        )


def remote(source, target, send_sem, recv_sem, device):
    return pltpu.make_async_remote_copy(
        src_ref=source,
        dst_ref=target,
        send_sem=send_sem,
        recv_sem=recv_sem,
        device_id=device,
        device_id_type=MESH_ID,
    )


class Spread:
    semaphores = ((2 * LINE,),) * 2 + ((2 * LINE, 2),) * 4
    buffers = ()
    near = True

    def __init__(self, *weights, begin=0, burst=False):
        self.inputs, self.begin, self.burst = list(weights), begin, burst
        shape = (16 * weights[0].shape[0], sum(weight.shape[1] for weight in weights) // 8)
        self.outputs = [jax.ShapeDtypeStruct(shape, jnp.bfloat16)]
        self.slots = begin + 3 + 2 * LINE

    def bind(self, line, sources, targets, sems):
        self.line, self.sources, self.target = line, sources, targets[0]
        self.z_send, self.z_recv, self.y_send, self.y_recv, self.x_send, self.x_recv = sems
        self.half = sources[0].shape[0] // 2

    def slot(self, t):
        t -= self.begin
        for p in range(2 * LINE):
            if t == (0 if self.burst else (p + 1) // 3):
                self.start(p)
        for p in range(2 * LINE):
            if t == (p + 1 if p else 0):
                self.came(p)
        for p in range(2 * LINE):
            if t == p + 3:
                self.onward(p)

    def rows(self, place, pair, core, rep):
        start = ((place * 4 + pair * 2 + core) * 2 + rep) * self.half
        return self.target.at[pl.ds(pl.multiple_of(start, self.half), self.half), :]

    def start(self, p):
        line, half = self.line, self.half
        place, core = line.piece(p, 1)
        here = self.rows(line.place, line.pair, line.core, line.rep)
        mine = pl.ds(pl.multiple_of(line.rep * half, half), half)
        at = 0
        for q in range(2):
            for source in self.sources:
                n = source.shape[1] // 16
                column = pl.multiple_of((place * 4 + q * 2 + core) * n, n)
                piece, goal = source.at[mine, pl.ds(column, n)], here.at[:, pl.ds(at, n)]
                if p == 0:
                    pltpu.make_async_copy(piece, goal, self.z_recv.at[0]).start()
                else:
                    remote(
                        piece, goal, self.z_send.at[p], self.z_recv.at[p], line.at(place, line.pair, core)
                    ).start()
                at += n

    def cross(self, p, pair, rep, which):
        place, core = self.line.piece(p, -1)
        ref = self.rows(place, pair, core, rep)
        return remote(ref, ref, self.y_send.at[p, which], self.y_recv.at[p, which], self.line.across)

    def over(self, p, pair, rep, which):
        place, core = self.line.piece(p, -1)
        ref = self.rows(place, pair, core, rep)
        return remote(ref, ref, self.x_send.at[p, which], self.x_recv.at[p, which], self.line.partner)

    def came(self, p):
        line = self.line
        place, core = line.piece(p, -1)
        ref = self.rows(place, line.pair, core, line.rep)
        if p == 0:
            pltpu.make_async_copy(ref, ref, self.z_recv.at[0]).wait()
        else:
            remote(ref, ref, self.z_send.at[p], self.z_recv.at[p], line.sibling).wait_recv()
        self.cross(p, line.pair, line.rep, 0).start()
        self.over(p, line.pair, line.rep, 0).start()

    def onward(self, p):
        line = self.line
        if p % 2:
            self.over(p, line.pair, 1 - line.rep, 0).wait_recv()
            self.cross(p, line.pair, 1 - line.rep, 1).start()
        else:
            self.cross(p, 1 - line.pair, line.rep, 0).wait_recv()
            self.over(p, 1 - line.pair, line.rep, 1).start()

    def finish(self):
        line = self.line
        pair, rep = line.pair, line.rep
        for p in range(2 * LINE):
            if p > 0:
                ref = self.rows(line.place, pair, line.core, rep)
                remote(ref, ref, self.z_send.at[p], self.z_recv.at[p], line.sibling).wait_send()
            self.cross(p, pair, rep, 0).wait_send()
            self.over(p, pair, rep, 0).wait_send()
            if p % 2:
                self.cross(p, 1 - pair, rep, 0).wait_recv()
                self.cross(p, pair, 1 - rep, 1).wait_send()
                self.cross(p, 1 - pair, 1 - rep, 1).wait_recv()
            else:
                self.over(p, pair, 1 - rep, 0).wait_recv()
                self.over(p, 1 - pair, rep, 1).wait_send()
                self.over(p, 1 - pair, 1 - rep, 1).wait_recv()


class Stack:
    buffers = ()
    near = True

    def __init__(self, weight, count):
        self.inputs, self.count = [weight], count
        self.outputs = [jax.ShapeDtypeStruct((2 * weight.shape[0], weight.shape[1]), weight.dtype)]
        self.semaphores = ((1,),) + ((count,),) * 4
        self.slots = 1 + count

    def bind(self, line, sources, targets, sems):
        self.line, self.source, self.target = line, sources[0], targets[0]
        self.local, self.y_send, self.y_recv, self.x_send, self.x_recv = sems
        self.size = self.source.shape[0]

    def here(self):
        size = self.size
        mine = self.target.at[pl.ds(pl.multiple_of(self.line.pair * size, size), size), :]
        return pltpu.make_async_copy(self.source, mine, self.local.at[0])

    def there(self, p):
        line, part = self.line, self.size // (2 * self.count)
        start = pl.multiple_of((line.rep * self.count + p) * part, part)
        goal = self.target.at[pl.ds(pl.multiple_of(line.pair * self.size + start, part), part), :]
        return remote(
            self.source.at[pl.ds(start, part), :], goal, self.y_send.at[p], self.y_recv.at[p], line.across
        )

    def onward(self, p, rep):
        line, part = self.line, self.size // (2 * self.count)
        start = (1 - line.pair) * self.size + (rep * self.count + p) * part
        ref = self.target.at[pl.ds(pl.multiple_of(start, part), part), :]
        return remote(ref, ref, self.x_send.at[p], self.x_recv.at[p], line.partner)

    def slot(self, t):
        if t == 0:
            for k in range(self.count):
                self.there(k).start()
            self.here().start()
        if 1 <= t < 1 + self.count:
            self.there(t - 1).wait_recv()
            self.onward(t - 1, self.line.rep).start()

    def finish(self):
        self.here().wait()
        for p in range(self.count):
            self.there(p).wait_send()
            self.onward(p, self.line.rep).wait_send()
            self.onward(p, 1 - self.line.rep).wait_recv()


class Swap:
    semaphores = ((2,),)
    buffers = ()
    near = True
    slots = 1

    def __init__(self, values, start, count):
        self.inputs, self.start, self.count = [values], start, count
        self.outputs = [jax.ShapeDtypeStruct((count, values.shape[1]), values.dtype)]

    def bind(self, line, sources, targets, scratch):
        sends, recvs = scratch[0].at[0], scratch[0].at[1]
        rows = sources[0].at[pl.ds(self.start, self.count), :]
        self.copy = remote(rows, targets[0], sends, recvs, line.partner)

    def slot(self, t):
        if t == 0:
            self.copy.start()

    def finish(self):
        self.copy.wait()


class Share:
    semaphores = ((2 * LINE,),) * 2
    buffers = ()
    near = True
    slots = 1

    def __init__(self, values):
        self.inputs = [values]
        self.outputs = [jax.ShapeDtypeStruct((2 * LINE,) + values.shape, values.dtype)]

    def bind(self, line, sources, targets, scratch):
        self.line, self.source, self.target = line, sources[0], targets[0]
        self.sends, self.recvs = scratch

    def copy(self, p):
        goal = self.target.at[self.line.block]
        if p == 0:
            return pltpu.make_async_copy(self.source, goal, self.recvs.at[0])
        place, core = self.line.piece(p, 1)
        return remote(
            self.source, goal, self.sends.at[p], self.recvs.at[p], self.line.at(place, self.line.pair, core)
        )

    def slot(self, t):
        if t == 0:
            for p in range(2 * LINE):
                self.copy(p).start()

    def finish(self):
        for p in range(2 * LINE):
            self.copy(p).wait()


class Deal:
    semaphores = ((2 * LINE,),) * 4
    buffers = ()
    near = True
    slots = 3 + 2 * LINE

    def __init__(self, sources, per):
        rows, width = sources[0].shape[1:]
        self.inputs, self.per = list(sources), per
        self.n = width // per
        self.width = width * len(sources)
        self.outputs = [jax.ShapeDtypeStruct((rows, 16 * self.width), sources[0].dtype)]

    def bind(self, line, sources, targets, scratch):
        self.line, self.sources, self.target = line, sources, targets[0]
        self.z_send, self.z_recv, self.x_send, self.x_recv = scratch

    def runs(self, place, core):
        for index, source in enumerate(self.sources):
            for run in range(self.per):
                block = (index * self.per + run) * 16 + place * 4 + self.line.rep * 2 + core
                yield source, run * self.n, pl.ds(pl.multiple_of(block * self.n, self.n), self.n)

    def whole(self):
        return self.target.at[:, pl.ds(0, self.width)]

    def start(self, p):
        line = self.line
        place, core = line.piece(p, 1)
        for source, at, there in self.runs(line.place, line.core):
            piece = source.at[2 * place + core, :, pl.ds(at, self.n)]
            goal = self.target.at[:, there]
            if p == 0:
                pltpu.make_async_copy(piece, goal, self.z_recv.at[0]).start()
            else:
                remote(
                    piece, goal, self.z_send.at[p], self.z_recv.at[p], line.at(place, line.pair, core)
                ).start()

    def came(self, p):
        line, ref = self.line, self.whole()
        if p == 0:
            pltpu.make_async_copy(ref, ref, self.z_recv.at[0]).wait()
        else:
            remote(ref, ref, self.z_send.at[p], self.z_recv.at[p], line.partner).wait_recv()
        place, core = line.piece(p, -1)
        for _, _, there in self.runs(place, core):
            goal = self.target.at[:, there]
            remote(goal, goal, self.x_send.at[p], self.x_recv.at[p], line.partner).start()

    def slot(self, t):
        if t < 2 * LINE:
            self.start(t)
        if t == 0:
            self.came(0)
        if 3 <= t < 2 + 2 * LINE:
            self.came(t - 2)

    def finish(self):
        ref = self.whole()
        for p in range(2 * LINE):
            if p > 0:
                remote(ref, ref, self.z_send.at[p], self.z_recv.at[p], self.line.partner).wait_send()
            remote(ref, ref, self.x_send.at[p], self.x_recv.at[p], self.line.partner).wait()


def outer_into(target, left, row, right, column, *more):
    rows, n = target.shape
    wide = 512 if n % 512 == 0 else 384

    def some(index, carry):
        across = n // wide
        down, along = index // across, index % across
        here = pl.ds(pl.multiple_of(down * 128, 128), 128)
        there = pl.ds(pl.multiple_of(along * wide, wide), wide)
        total = lax.dot_general(
            left[:, pl.ds(pl.multiple_of(row + down * 128, 128), 128)],
            right[:, pl.ds(pl.multiple_of(column + along * wide, 128), wide)],
            (((0,), (0,)), ((), ())),
            preferred_element_type=jnp.float32,
        )
        for ref in more:
            total = total + ref[here, there].astype(jnp.float32)
        target[here, there] = total.astype(target.dtype)
        return carry

    lax.fori_loop(0, (rows // 128) * (n // wide), some, 0)


class Reduce:
    near = True

    def __init__(self, left, rights, first):
        rows, n = left.shape[1] // 8, rights[0].shape[1] // 2
        self.inputs, self.first, self.size, self.n = [left, *rights], first, rows, n
        self.outputs = [jax.ShapeDtypeStruct((LINE, rows, n), left.dtype) for _ in rights]
        self.chunks = 2 * LINE if first == "partner" else LINE
        wide = n if first == "partner" else 2 * n
        self.semaphores = ((self.chunks,),) * (2 * len(rights)) + ((LINE,),) * (2 * len(rights))
        self.buffers = ((self.chunks, rows, wide),) * (2 * len(rights))
        self.join_at = [3, 5, 8, 10] if first == "partner" else [3, 5, 7, 9]
        self.last_at = [12, 15, 16, 17] if first == "partner" else [10, 10, 10, 11]
        self.slots = max(self.last_at) + 1

    def bind(self, line, sources, targets, scratch):
        self.line, self.left, self.parts = line, sources[0], []
        count = len(targets)
        sems1, sems2, buffers = scratch[: 2 * count], scratch[2 * count : 4 * count], scratch[4 * count :]
        for index, target in enumerate(targets):
            pick = slice(2 * index, 2 * index + 2)
            self.parts.append((sources[1 + index], target, *sems1[pick], *sems2[pick], *buffers[pick]))

    def row(self, place, pair):
        return (place * 2 + pair) * self.size

    def leg1(self, part, k):
        _, _, send1, recv1, _, _, out, came = part
        device = self.line.partner if self.first == "partner" else self.line.across
        return remote(out.at[k], came.at[k], send1.at[k], recv1.at[k], device)

    def leg2(self, part, k):
        _, target, _, _, send2, recv2, out, _ = part
        device = self.line.across if self.first == "partner" else self.line.partner
        return remote(out.at[k, :, pl.ds(0, self.n)], target.at[k], send2.at[k], recv2.at[k], device)

    def produce(self, k):
        line = self.line
        for part in self.parts:
            if self.first == "partner":
                pair = 1 - line.pair if k < LINE else line.pair
                outer_into(part[6].at[k], self.left, self.row(k % LINE, pair), part[0], (1 - line.rep) * self.n)
            else:
                outer_into(part[6].at[k], self.left, self.row(k, 1 - line.pair), part[0], 0)
            self.leg1(part, k).start()

    def join(self, k):
        line, n = self.line, self.n
        for part in self.parts:
            right, _, _, _, _, _, out, came = part
            self.leg1(part, k).wait()
            goal = out.at[k, :, pl.ds(0, n)]
            if self.first == "partner":
                outer_into(goal, self.left, self.row(k, 1 - line.pair), right, line.rep * n, came.at[k])
            else:
                column = pl.multiple_of((1 - line.rep) * n, n)
                outer_into(goal, self.left, self.row(k, line.pair), right, column, came.at[k, :, pl.ds(column, n)])
            self.leg2(part, k).start()

    def last(self, k):
        line, n = self.line, self.n
        for part in self.parts:
            right, target, _, _, _, _, _, came = part
            if self.first == "partner":
                self.leg1(part, LINE + k).wait()
                mine = came.at[LINE + k]
            else:
                mine = came.at[k, :, pl.ds(pl.multiple_of(line.rep * n, n), n)]
            self.leg2(part, k).wait()
            outer_into(target.at[k], self.left, self.row(k, line.pair), right, line.rep * n, mine, target.at[k])

    def slot(self, t):
        if t < self.chunks:
            self.produce(t)
        for k in range(LINE):
            if t == self.join_at[k]:
                self.join(k)
        for k in range(LINE):
            if t == self.last_at[k]:
                self.last(k)

    def finish(self):
        pass


class PairSum:
    near = True

    def __init__(self, left, right, count, at):
        self.inputs, self.count, self.at = [left, right], count, at
        shape = (left.shape[1] // 2, right.shape[1])
        self.outputs = [jax.ShapeDtypeStruct(shape, left.dtype)]
        self.semaphores = ((count,),) * 2
        self.buffers = (shape,)
        self.slots = at + count

    def bind(self, line, sources, targets, scratch):
        self.line, self.target = line, targets[0]
        self.left, self.right = sources
        self.sends, self.recvs, self.out = scratch
        self.size = self.target.shape[0] // self.count

    def copy(self, k):
        rows = pl.ds(k * self.size, self.size)
        return remote(
            self.out.at[rows, :], self.target.at[rows, :], self.sends.at[k], self.recvs.at[k], self.line.across
        )

    def slot(self, t):
        pair, size = self.line.pair, self.size
        for k in range(self.count):
            rows = pl.ds(k * size, size)
            if t == k:
                outer_into(self.out.at[rows, :], self.left, (1 - pair) * self.count * size + k * size, self.right, 0)
                self.copy(k).start()
            if t == self.at + k:
                self.copy(k).wait()
                goal = self.target.at[rows, :]
                outer_into(goal, self.left, pair * self.count * size + k * size, self.right, 0, goal)

    def finish(self):
        pass


def line_scatter_joint(line, k, rows, parts, sib):
    return parts[2 * k + line.core, rows, :].astype(jnp.float32) + sib[k, rows, :].astype(jnp.float32)


def line_scatter_pass(line, j, step, way, parts, sib, sums, came, sib_recv, send_sem, came_sem):
    rows = pl.ds(pl.multiple_of(j * step, step), step)
    device = line.right if way == 0 else line.left
    ends = line.place == 0 if way == 0 else line.place == LINE - 1

    def copy(k):
        return remote(sums.at[k, rows], came.at[k, rows], send_sem.at[k, j], came_sem.at[k, j], device)

    for k in range(LINE - 1, 0, -1) if way == 0 else range(LINE - 1):

        @pl.when(line.place < k if way == 0 else line.place > k)
        def _():
            remote(
                parts.at[2 * k + line.core, rows], sib.at[k, rows], sib_recv.at[k, j], sib_recv.at[k, j], line.sibling
            ).wait_recv()

            @pl.when(ends)
            def _():
                sums[k, rows, :] = line_scatter_joint(line, k, rows, parts, sib).astype(jnp.bfloat16)

            @pl.when(jnp.logical_not(ends))
            def _():
                copy(k).wait_recv()
                sums[k, rows, :] = (
                    line_scatter_joint(line, k, rows, parts, sib) + came[k, rows, :].astype(jnp.float32)
                ).astype(jnp.bfloat16)

            copy(k).start()


def line_scatter_total(line, j, step, parts, sib, rights, lefts, sums, sib_recv, sends, right_recv, left_recv):
    rows = pl.ds(pl.multiple_of(j * step, step), step)
    me = line.place
    remote(
        parts.at[2 * me + line.core, rows], sib.at[me, rows], sib_recv.at[me, j], sib_recv.at[me, j], line.sibling
    ).wait_recv()

    @pl.when(line.has_left)
    def _():
        remote(sums.at[me, rows], rights.at[me, rows], sends.at[me, j], right_recv.at[me, j], line.left).wait_recv()

    @pl.when(line.has_right)
    def _():
        remote(sums.at[me, rows], lefts.at[me, rows], sends.at[me, j], left_recv.at[me, j], line.right).wait_recv()

    total = line_scatter_joint(line, me, rows, parts, sib)
    total = total + jnp.where(line.has_left, rights[me, rows, :].astype(jnp.float32), 0.0)
    return total + jnp.where(line.has_right, lefts[me, rows, :].astype(jnp.float32), 0.0)


def line_scatter_start(line, pieces, step, parts, sib, sib_send, sib_recv):
    def piece(j, carry):
        rows = pl.ds(pl.multiple_of(j * step, step), step)
        for k in range(LINE):
            remote(
                parts.at[2 * k + 1 - line.core, rows],
                sib.at[k, rows],
                sib_send.at[k, j],
                sib_recv.at[k, j],
                line.sibling,
            ).start()
        return carry

    lax.fori_loop(0, pieces, piece, 0)


def line_scatter_end(line, pieces, step, parts, sib, rights, lefts, sums, sib_send, right_send, left_send):
    def piece(j, carry):
        rows = pl.ds(pl.multiple_of(j * step, step), step)
        for k in range(LINE):
            remote(
                parts.at[2 * k + 1 - line.core, rows],
                sib.at[k, rows],
                sib_send.at[k, j],
                sib_send.at[k, j],
                line.sibling,
            ).wait_send()

            @pl.when(line.place < k)
            def _():
                remote(
                    sums.at[k, rows], rights.at[k, rows], right_send.at[k, j], right_send.at[k, j], line.right
                ).wait_send()

            @pl.when(line.place > k)
            def _():
                remote(
                    sums.at[k, rows], lefts.at[k, rows], left_send.at[k, j], left_send.at[k, j], line.left
                ).wait_send()

        return carry

    lax.fori_loop(0, pieces, piece, 0)


def gather_copy(line, k, j, step, core, gathered, way, sends, recvs):
    rows = pl.ds(pl.multiple_of(j * step, step), step)
    block = 2 * k + core
    device = (line.right, line.left, line.sibling)[way]
    ref = gathered.at[block, rows]
    return remote(ref, ref, sends.at[k, way, j], recvs.at[block, j], device)


def line_gather_own(line, j, step, gathered, sends, recvs):
    def copy(way):
        return gather_copy(line, line.place, j, step, line.core, gathered, way, sends, recvs)

    pl.when(line.has_right)(lambda: copy(0).start())
    pl.when(line.has_left)(lambda: copy(1).start())
    copy(2).start()


def line_gather_pass(line, hop, j, step, gathered, sends, recvs):
    for way in (0, 1):
        k = line.place - hop if way == 0 else line.place + hop
        there = k >= 0 if way == 0 else k < LINE
        onward = line.has_right if way == 0 else line.has_left
        k = jnp.clip(k, 0, LINE - 1)

        @pl.when(there)
        def _():
            gather_copy(line, k, j, step, line.core, gathered, way, sends, recvs).wait_recv()
            pl.when(onward)(
                lambda: gather_copy(line, k, j, step, line.core, gathered, way, sends, recvs).start()
            )
            gather_copy(line, k, j, step, line.core, gathered, 2, sends, recvs).start()


def line_gather_end(line, pieces, step, gathered, sends, recvs):
    def piece(j, carry):
        for k in range(LINE):
            gather_copy(line, k, j, step, 1 - line.core, gathered, 2, sends, recvs).wait_recv()
            gather_copy(line, k, j, step, line.core, gathered, 2, sends, recvs).wait_send()

            @pl.when((line.place >= k) & line.has_right)
            def _():
                gather_copy(line, k, j, step, line.core, gathered, 0, sends, recvs).wait_send()

            @pl.when((line.place <= k) & line.has_left)
            def _():
                gather_copy(line, k, j, step, line.core, gathered, 1, sends, recvs).wait_send()

        return carry

    lax.fori_loop(0, pieces, piece, 0)


def take_from(items, count):
    taken = items[:count]
    del items[:count]
    return taken


def moves_scratch(moves):
    scratch = []
    for move in moves:
        scratch += [pltpu.SemaphoreType.DMA(shape) for shape in move.semaphores]
        scratch += [pltpu.VMEM(shape, jnp.bfloat16) for shape in move.buffers]
    return scratch


def moves_specs(moves, side):
    near, far = pl.BlockSpec(memory_space=pltpu.VMEM), pl.BlockSpec(memory_space=pl.ANY)
    return [near if move.near else far for move in moves for _ in getattr(move, side)]


def line_call(collective_id, pieces, middle, inputs, outputs, scatter, gather, moves=(), limit=46):
    step = inputs[0].shape[-2] // pieces if inputs else 0
    low = jnp.bfloat16
    scratch = []
    if scatter:
        block = inputs[0].shape[-2:]
        scratch += [pltpu.VMEM((LINE,) + block, low) for _ in range(4)]
        scratch += [pltpu.SemaphoreType.DMA((LINE, pieces)) for _ in range(6)]
    if gather:
        scratch += [pltpu.SemaphoreType.DMA((LINE, 3, pieces)), pltpu.SemaphoreType.DMA((2 * LINE, pieces))]
    n_scratch = len(scratch)
    scratch += moves_scratch(moves)
    moved = [values for move in moves for values in move.inputs]
    extras = [shape for move in moves for shape in move.outputs]

    def kernel(*refs):
        refs = list(refs)

        def take(count):
            taken = refs[:count]
            del refs[:count]
            return taken

        ins = take(len(inputs))
        given = [take(len(move.inputs)) for move in moves]
        outs = take(len(outputs))
        extra = [take(len(move.outputs)) for move in moves]
        rest = take(n_scratch)
        line = Line()
        for move, sources, targets in zip(moves, given, extra):
            move.bind(line, sources, targets, take(len(move.semaphores) + len(move.buffers)))
        line.meet(bool(moves))
        if scatter:
            sib, rights, lefts, sums, sib_send, sib_recv, right_send, left_send, right_recv, left_recv = rest[:10]
            parts = ins[0]
            line_scatter_start(line, pieces, step, parts, sib, sib_send, sib_recv)
        if gather:
            sends, recvs = rest[-2:]

        def during(j, act):
            pl.when((j >= 0) & (j < pieces))(lambda: act(j))

        def finish(j):
            rows = pl.ds(pl.multiple_of(j * step, step), step)
            total = None
            if scatter:
                total = line_scatter_total(
                    line, j, step, parts, sib, rights, lefts, sums, sib_recv, right_send, right_recv, left_recv
                )
            values = middle(total, rows, j, ins, outs)
            if gather:
                outs[0][line.block, rows, :] = values.astype(low)
                line_gather_own(line, j, step, outs[0], sends, recvs)

        def slot(t, carry):
            if scatter:
                during(
                    t - line.place,
                    lambda j: line_scatter_pass(
                        line, j, step, 0, parts, sib, sums, rights, sib_recv, right_send, right_recv
                    ),
                )
                during(
                    t - (LINE - 1 - line.place),
                    lambda j: line_scatter_pass(
                        line, j, step, 1, parts, sib, sums, lefts, sib_recv, left_send, left_recv
                    ),
                )
                during(t - (LINE - 1), finish)
            if gather:
                for hop in range(1, LINE):
                    during(
                        t - hop - (LINE - 1 if scatter else 0),
                        lambda j, hop=hop: line_gather_pass(line, hop, j, step, outs[0], sends, recvs),
                    )
            return carry

        if gather and not scatter:
            lax.fori_loop(0, pieces, lambda j, carry: (finish(j), carry)[1], 0)
        slots = pieces + (LINE - 1) * (int(scatter) + int(gather)) if inputs else 0
        apart = max([move.slots for move in moves] + [0])
        if apart <= 1:
            for move in moves:
                move.slot(0)
            if inputs:
                lax.fori_loop(0, slots, slot, 0)
        else:
            for t in range(max(slots, apart)):
                for move in moves:
                    move.slot(t)
                if t < slots:
                    slot(t, 0)
        for move in moves:
            move.finish()
        if scatter:
            line_scatter_end(
                line, pieces, step, parts, sib, rights, lefts, sums, sib_send, right_send, left_send
            )
        if gather:
            line_gather_end(line, pieces, step, outs[0], sends, recvs)

    vmem = pl.BlockSpec(memory_space=pltpu.VMEM)
    return pl.pallas_call(
        kernel,
        out_shape=[jax.ShapeDtypeStruct(shape, kind) for shape, kind in outputs] + extras,
        in_specs=[vmem] * len(inputs) + moves_specs(moves, "inputs"),
        out_specs=[vmem] * len(outputs) + moves_specs(moves, "outputs"),
        scratch_shapes=scratch,
        compiler_params=pltpu.CompilerParams(
            collective_id=collective_id, has_side_effects=True, vmem_limit_bytes=limit << 20
        ),
        cost_estimate=pl.CostEstimate(flops=10_000_000, bytes_accessed=200_000_000, transcendentals=0),
    )(*inputs, *moved)


def gather_blocks(payload, moves, collective_id):
    def middle(total, rows, j, ins, outs):
        return ins[0][rows, :]

    shape = (2 * LINE,) + payload.shape
    return line_call(collective_id, 8, middle, [payload], [(shape, jnp.bfloat16)], False, True, moves)


def attention_block(parts, hidden, gain, moves, collective_id):
    def middle(total, rows, j, ins, outs):
        outs[1][rows, :] = total
        resid = ins[1][rows, :].astype(jnp.float32) + total * rms_scale(total) * ins[2][...]
        outs[2][rows, :] = resid
        return resid

    shape = hidden.shape
    return line_call(
        collective_id, 8, middle, [parts, hidden, gain],
        [(parts.shape, jnp.bfloat16), (shape, jnp.float32), (shape, jnp.float32)], True, True, moves,
    )


def add_rows(ref, values, j):
    folded = jnp.sum(values.reshape(values.shape[0] // 8, 8, values.shape[1]), axis=0)

    @pl.when(j == 0)
    def _():
        ref[...] = folded

    @pl.when(j > 0)
    def _():
        ref[...] += folded


def ffn_block(parts, resid, cotangent, gain, collective_id):
    def middle(total, rows, j, ins, outs):
        scale = rms_scale(total)
        normed = total * scale
        grad = ins[2][rows, :].astype(jnp.float32)
        gains = ins[3][...]
        outs[1][rows, :] = (ins[1][rows, :] + normed * gains).astype(jnp.bfloat16)
        add_rows(outs[2], grad * normed, j)
        return rms_back(grad * gains, normed, scale)

    shape = resid.shape
    return line_call(
        collective_id, 8, middle, [parts, resid, cotangent, gain],
        [(parts.shape, jnp.bfloat16), (shape, jnp.bfloat16), ((8, shape[1]), jnp.float32)], True, True,
    )


def back_block(parts, cotangent, attn_out, gain, moves, collective_id):
    def middle(total, rows, j, ins, outs):
        d_resid = ins[1][rows, :].astype(jnp.float32) + total
        outs[1][rows, :] = d_resid
        attn = ins[2][rows, :]
        scale = rms_scale(attn)
        normed = attn * scale
        add_rows(outs[2], d_resid * normed, j)
        return rms_back(d_resid * ins[3][...], normed, scale)

    shape = cotangent.shape
    return line_call(
        collective_id, 8, middle, [parts, cotangent, attn_out, gain],
        [(parts.shape, jnp.bfloat16), (shape, jnp.float32), ((8, shape[1]), jnp.float32)], True, True, moves, 56,
    )


def last_block(parts, d_resid, moves, collective_id):
    def middle(total, rows, j, ins, outs):
        outs[0][rows, :] = (ins[1][rows, :] + total).astype(jnp.bfloat16)

    return line_call(
        collective_id, 8, middle, [parts, d_resid], [(d_resid.shape, jnp.bfloat16)], True, False, moves
    )


def line_exchange(line, mine, came, sends, recvs):
    def copy(p):
        place, core = line.piece(p, 1)
        return remote(mine, came.at[p], sends.at[p], recvs.at[p], line.at(place, line.pair, core))

    for p in range(1, 2 * LINE):
        copy(p).start()
    total = mine[...]
    for p in range(1, 2 * LINE):
        copy(p).wait_recv()
        total = total + came[p]
    for p in range(1, 2 * LINE):
        copy(p).wait_send()
    return total


def spot(head, index):
    start = (3 * head + index) * HEAD_DIM
    return slice(start, start + HEAD_DIM)


def turn_tables(turns):
    half = turns.shape[1] // 2
    swapped = pltpu.roll(turns, half, 1)
    first = lax.broadcasted_iota(jnp.int32, turns.shape, 1) < half
    return jnp.where(first, turns, swapped), jnp.where(first, -swapped, turns)


def as_row(column):
    return jnp.broadcast_to(column, (column.shape[0], column.shape[0])).T[0:1, :]


def as_columns(row):
    return jnp.broadcast_to(row, (row.shape[1], row.shape[1])).T


def dot(left, right, left_dim, right_dim):
    return lax.dot_general(
        left, right, (((left_dim,), (right_dim,)), ((), ())), preferred_element_type=jnp.float32
    )


def heads_call(collective_id, body, inputs, outputs, scratch, rows, moves):
    blocks, length = 2 * LINE, HEAD_DIM
    scratch = [
        pltpu.VMEM((rows, length), jnp.float32),
        pltpu.VMEM((blocks, rows, length), jnp.float32),
        pltpu.SemaphoreType.DMA((blocks,)),
        pltpu.SemaphoreType.DMA((blocks,)),
    ] + scratch
    n_scratch = len(scratch)
    moved = [values for move in moves for values in move.inputs]
    extras = [shape for move in moves for shape in move.outputs]

    def kernel(*refs):
        refs = list(refs)
        ins = take_from(refs, len(inputs))
        given = [take_from(refs, len(move.inputs)) for move in moves]
        outs = take_from(refs, len(outputs))
        extra = [take_from(refs, len(move.outputs)) for move in moves]
        rest = take_from(refs, n_scratch)
        line = Line()
        for move, sources, targets in zip(moves, given, extra):
            move.bind(line, sources, targets, take_from(refs, len(move.semaphores) + len(move.buffers)))
        line.meet(True)
        passed = [0]

        def tick():
            for move in moves:
                move.slot(passed[0])
            passed[0] += 1

        body(line, ins, outs, rest, tick)
        while passed[0] < max([move.slots for move in moves] + [0]):
            tick()
        for move in moves:
            move.finish()

    vmem = pl.BlockSpec(memory_space=pltpu.VMEM)
    return pl.pallas_call(
        kernel,
        out_shape=[jax.ShapeDtypeStruct(shape, kind) for shape, kind in outputs] + extras,
        in_specs=[vmem] * len(inputs) + moves_specs(moves, "inputs"),
        out_specs=[vmem] * len(outputs) + moves_specs(moves, "outputs"),
        scratch_shapes=scratch + moves_scratch(moves),
        compiler_params=pltpu.CompilerParams(
            collective_id=collective_id, has_side_effects=True, vmem_limit_bytes=44 << 20
        ),
        cost_estimate=pl.CostEstimate(flops=10_000_000, bytes_accessed=80_000_000, transcendentals=0),
    )(*inputs, *moved)


def attend(tokens, full_qkv, turns, bias, gains, weight, moves, collective_id):
    blocks, length = bias.shape[:2]
    width = full_qkv.shape[1] // 3
    heads = width // HEAD_DIM
    model_width = weight.shape[1]
    low = jnp.bfloat16

    def body(line, ins, outs, scratch, tick):
        tokens, full_qkv, turns, bias, gains, weight = ins
        parts, lows, probs, mixed, squares, raw = outs
        mine, came, sends, recvs = scratch

        def squares_of(b, carry):
            raw[b] = dot(tokens[b], full_qkv[...], 1, 0)
            for index in range(2):
                total = jnp.zeros((length, 1), jnp.float32)
                for h in range(heads):
                    values = raw[b, :length, spot(h, index)]
                    total = total + jnp.sum(values * values, axis=1, keepdims=True)
                mine[pl.ds(index * blocks + b, 1), :] = as_row(total)
            return carry

        tick()
        for part in range(LINE):
            lax.fori_loop(2 * part, 2 * part + 2, squares_of, 0)
            tick()
        squares[...] = line_exchange(line, mine, came, sends, recvs)
        tick()

        def block(b, carry):
            scales = [
                lax.rsqrt(as_columns(squares[pl.ds(index * blocks + b, 1), :]) / model_width + epsilon)
                for index in range(2)
            ]
            cos, sin = turn_tables(turns[b])
            for h in range(heads):
                here = slice(h * HEAD_DIM, (h + 1) * HEAD_DIM)
                turned = []
                for index in range(2):
                    there = spot(h, index)
                    normed = raw[b, :length, there] * scales[index] * gains[index : index + 1, here]
                    turned.append((normed * cos + pltpu.roll(normed, HEAD_DIM // 2, 1) * sin).astype(low))
                    lows[b, :, there] = turned[index]
                there = spot(h, 2)
                value = raw[b, :length, there].astype(low)
                lows[b, :, there] = value
                scores = dot(turned[0], turned[1], 1, 1) * HEAD_DIM**-0.5 + bias[b]
                powers = jnp.exp(scores - jnp.max(scores, axis=1, keepdims=True))
                prob = powers / jnp.sum(powers, axis=1, keepdims=True)
                probs[b, h] = prob
                mixed[b, :, here] = dot(prob.astype(low), value, 1, 0).astype(low)
            parts[b] = dot(mixed[b], weight[...], 1, 0).astype(low)
            return carry

        for part in range(LINE):
            lax.fori_loop(2 * part, 2 * part + 2, block, 0)
            tick()

    return heads_call(
        collective_id,
        body,
        [tokens, full_qkv, turns, bias, gains, weight],
        [
            ((blocks, length, model_width), low),
            ((blocks, length, 3 * width), low),
            ((blocks, heads, length, length), jnp.float32),
            ((blocks, length, width), low),
            ((2 * blocks, length), jnp.float32),
            ((blocks, length, 3 * width), jnp.float32),
        ],
        [],
        2 * blocks,
        moves,
    )


def attend_back(d_attn, weight, raw, turns, gains, lows, probs, squares, wide_terms, full_qkv, moves, collective_id):
    blocks, length = raw.shape[:2]
    width = raw.shape[2] // 3
    heads = width // HEAD_DIM
    model_width = weight.shape[1]
    low = jnp.bfloat16

    def body(line, ins, outs, scratch, tick):
        d_attn, weight, raw, turns, gains, lows, probs, squares = ins[:8]
        d_low, terms, wide, parts = outs
        full_qkv = ins[10]
        mine, came, sends, recvs, upstream, unit = scratch
        tick()
        terms[...] = jnp.zeros_like(terms)
        for which in range(2):
            total = jnp.sum(ins[8 + which][...], axis=0, keepdims=True)
            for index in range(model_width // length):
                row = 2 * blocks + which * (model_width // length) + index
                mine[row : row + 1, :] = total[:, index * length : (index + 1) * length]

        def block(b, carry):
            scales = [
                lax.rsqrt(as_columns(squares[pl.ds(index * blocks + b, 1), :]) / model_width + epsilon)
                for index in range(2)
            ]
            cos, sin = turn_tables(turns[b])
            d_mixed = dot(d_attn[b], weight[...], 1, 1).astype(low)
            means = [jnp.zeros((length, 1), jnp.float32)] * 2
            for h in range(heads):
                here = slice(h * HEAD_DIM, (h + 1) * HEAD_DIM)
                places = [spot(h, index) for index in range(3)]
                query, key, value = [lows[b, :, there] for there in places]
                prob = probs[b, h]
                d_out = d_mixed[:, here]
                d_low[b, :length, places[2]] = dot(prob.astype(low), d_out, 0, 0).astype(low)
                d_prob = dot(d_out, value, 1, 1)
                d_scores = (
                    prob * (d_prob - jnp.sum(d_prob * prob, axis=1, keepdims=True))
                ).astype(low)
                turned = [dot(d_scores, key, 1, 0), dot(d_scores, query, 0, 0)]
                for index in range(2):
                    d_rot = turned[index] * HEAD_DIM**-0.5
                    d_normed = d_rot * cos - pltpu.roll(d_rot, HEAD_DIM // 2, 1) * sin
                    units = raw[b, :length, places[index]] * scales[index]
                    ups = d_normed * gains[index : index + 1, here]
                    folded = (d_normed * units).reshape(length // 8, 8, HEAD_DIM)
                    side = slice((index * heads + h) * HEAD_DIM, (index * heads + h + 1) * HEAD_DIM)
                    terms[:, side] += jnp.sum(folded, axis=0)
                    upstream[b, :, side] = ups
                    unit[b, :, side] = units
                    means[index] = means[index] + jnp.sum(ups * units, axis=1, keepdims=True)
            for index in range(2):
                mine[pl.ds(index * blocks + b, 1), :] = as_row(means[index])
            return carry

        lax.fori_loop(0, blocks, block, 0)
        mine[...] = line_exchange(line, mine, came, sends, recvs)
        wide[...] = mine[2 * blocks :, :]

        def last(b, carry):
            for index in range(2):
                scale = lax.rsqrt(
                    as_columns(squares[pl.ds(index * blocks + b, 1), :]) / model_width + epsilon
                )
                mean = as_columns(mine[pl.ds(index * blocks + b, 1), :]) / model_width
                for h in range(heads):
                    side = slice((index * heads + h) * HEAD_DIM, (index * heads + h + 1) * HEAD_DIM)
                    d_low[b, :length, spot(h, index)] = (
                        scale * (upstream[b, :, side] - unit[b, :, side] * mean)
                    ).astype(low)
            parts[b] = dot(d_low[b], full_qkv[...], 1, 1).astype(low)
            return carry

        lax.fori_loop(0, blocks, last, 0)

    return heads_call(
        collective_id,
        body,
        [d_attn, weight, raw, turns, gains, lows, probs, squares, *wide_terms, full_qkv],
        [
            (raw.shape, low),
            ((8, 2 * width), jnp.float32),
            ((2 * model_width // length, length), jnp.float32),
            ((blocks, length, model_width), low),
        ],
        [pltpu.VMEM((blocks, length, 2 * width), jnp.float32) for _ in range(2)],
        2 * blocks + 2 * model_width // length,
        moves,
    )


def on_device(
    hidden_in,
    segments,
    w_query,
    w_key,
    w_value,
    w_output,
    query_gain,
    key_gain,
    attn_gain,
    w_gate,
    w_up,
    w_down,
    ffn_gain,
    out_cotangent,
):
    length, model_width = hidden_in.shape
    blocks = 2 * LINE
    heads = HEADS // blocks
    factor = HEAD_DIM ** (-0.5)
    pair = (lax.axis_index("shard") // 2) % 2
    f32 = jnp.float32

    extra = jnp.concatenate(
        [query_gain, key_gain, attn_gain, ffn_gain, segments[0].astype(jnp.bfloat16)]
    )
    payload, extras, full_qkv, full_output = gather_blocks(
        hidden_in,
        [
            Share(jnp.pad(extra[None], ((0, 15), (0, 0)))),
            Spread(w_query, w_key, w_value),
            Stack(w_output, 2),
        ],
        0,
    )
    tokens = payload.reshape(-1, model_width)
    docs = extras[:, 0, 4 * length :].astype(jnp.int32)
    gains = extras[:, 0, : 4 * length].reshape(LINE, 2, 4, length)
    gains = jnp.stack(by_pair(pair, gains, pair_swap(gains)), axis=1)
    gains = jnp.moveaxis(gains, 3, 0).reshape(4, 1, model_width).astype(f32)
    gain_attn, gain_ffn = gains[2], gains[3]
    width = heads * HEAD_DIM
    head_gains = gather_rows(jnp.stack([query_gain, key_gain])[None], pair).astype(f32)
    head_gains = head_gains.transpose(1, 0, 2).reshape(2, width)

    earlier = jnp.sum((docs[:, None, :] < docs[:, :, None]).astype(jnp.int32), axis=2)
    positions = jnp.arange(length, dtype=jnp.int32)[None] - earlier
    half_dim = HEAD_DIM // 2
    inverse = jnp.exp(
        jnp.arange(half_dim, dtype=f32) * (-2.0 * math.log(theta_base) / HEAD_DIM)
    )
    angles = positions.astype(f32)[:, :, None] * inverse[None, None, :]
    turns = jnp.cos(jnp.concatenate([angles, angles - 0.5 * math.pi], axis=-1))
    token_idx = jnp.arange(length)
    allowed = (docs[:, :, None] == docs[:, None, :]) & (
        token_idx[:, None] >= token_idx[None, :]
    )[None]
    bias = jnp.where(allowed, 0.0, neg_fill)

    def to_blocks(values):
        return values.astype(jnp.bfloat16).reshape(blocks, -1, model_width)

    attn_parts, lows, probs, mixed_low, squares, raw, full_gate = attend(
        payload, full_qkv, turns, bias, head_gains, full_output, [Spread(w_gate, burst=True)], 6
    )
    mixed_low = mixed_low.reshape(blocks * length, width)
    resid_low, attn_out, resid, full_up, full_down = attention_block(
        attn_parts,
        hidden_in,
        gain_attn,
        [Spread(w_up), Stack(w_down, 8)],
        1,
    )
    resid_low = resid_low.reshape(blocks * length, model_width)

    gate_proj = jnp.dot(resid_low, full_gate, preferred_element_type=f32)
    up_proj = jnp.dot(resid_low, full_up, preferred_element_type=f32)
    gate_sig = jax.nn.sigmoid(gate_proj)
    hidden_ffn = (gate_proj * gate_sig * up_proj).astype(jnp.bfloat16)
    d_ffn_low, hidden_out, ffn_gain_term = ffn_block(
        to_blocks(jnp.dot(hidden_ffn, full_down, preferred_element_type=f32)),
        resid,
        out_cotangent,
        gain_ffn,
        2,
    )
    d_ffn_low = d_ffn_low.reshape(blocks * length, model_width)

    d_hidden_ffn = dot_back(d_ffn_low, full_down)
    d_gate_low = (d_hidden_ffn * up_proj * gate_sig * (1.0 + gate_proj * (1.0 - gate_sig))).astype(
        jnp.bfloat16
    )
    d_up_low = (d_hidden_ffn * gate_proj * gate_sig).astype(jnp.bfloat16)
    ff_rows = w_down.shape[0]
    d_attn_low, d_resid, attn_gain_term, gate_sum, up_sum, down_part = back_block(
        to_blocks(dot_back(d_gate_low, full_gate) + dot_back(d_up_low, full_up)),
        out_cotangent,
        attn_out,
        gain_attn,
        [
            Reduce(resid_low, [d_gate_low, d_up_low], "partner"),
            PairSum(hidden_ffn, d_ffn_low, 4, 13),
        ],
        3,
    )

    d_qkv, head_terms, wide_terms, back_parts, there_first = attend_back(
        d_attn_low, full_output, raw, turns, head_gains, lows, probs, squares,
        [attn_gain_term, ffn_gain_term], full_qkv, [Swap(down_part, 0, ff_rows // 2)], 7,
    )
    d_attn_low = d_attn_low.reshape(blocks * length, model_width)
    hidden_grad, qkv_sum, output_part, ffn_total, there_second = last_block(
        back_parts,
        d_resid,
        [
            Reduce(tokens, [d_qkv.reshape(-1, 3 * width)], "across"),
            PairSum(mixed_low, d_attn_low, 1, 5),
            Deal([gate_sum.reshape(blocks, length, -1), up_sum.reshape(blocks, length, -1)], 1),
            Swap(down_part, ff_rows // 2, ff_rows // 2),
        ],
        4,
    )
    qkv_total, there_output = line_call(
        5, 1, None, [], [], False, False,
        [
            Deal([qkv_sum.reshape(blocks, length, -1)], 3),
            Swap(output_part, 0, length),
        ],
    )

    def total_of(first, second):
        return first.astype(f32) + second.astype(f32)

    grad_query, grad_key, grad_value = jnp.split(qkv_total.astype(f32), 3, axis=1)
    grad_gate, grad_up = jnp.split(ffn_total.astype(f32), 2, axis=1)
    grad_output = total_of(output_part, there_output)
    grad_down = total_of(down_part, jnp.concatenate([there_first, there_second]))
    head_terms = jnp.sum(head_terms, axis=0).reshape(2, 2, HEAD_DIM)
    own_term, other_term = by_pair(pair, head_terms[:, 0], head_terms[:, 1])
    head_grads = own_term + pair_swap(other_term)
    wide_terms = (wide_terms + pair_swap(wide_terms)).reshape(2, 16, length)
    wide_grads = lax.dynamic_index_in_dim(wide_terms, lax.axis_index("shard"), 1, keepdims=False)
    gain_grads = jnp.concatenate([head_grads, wide_grads])
    gain_grads = gain_grads + rep_swap(gain_grads)
    return (
        hidden_out,
        hidden_grad,
        grad_query,
        grad_key,
        grad_value,
        grad_output,
        gain_grads[0],
        gain_grads[1],
        gain_grads[2],
        grad_gate,
        grad_up,
        grad_down,
        gain_grads[3],
    )


def solution(mesh):
    placed = (
        P(("rep", "shard"), None),
        P(("rep", "shard"), None),
        P("shard", None),
        P("shard", None),
        P("shard", None),
        P("shard", None),
        P("shard"),
        P("shard"),
        P("shard"),
        P("shard", None),
        P("shard", None),
        P("shard", None),
        P("shard"),
        P(("rep", "shard"), None),
    )
    return jax.shard_map(
        on_device if mesh.shape["shard"] == 16 else on_device_general,
        mesh=mesh,
        in_specs=placed,
        out_specs=(
            P(("rep", "shard"), None),
            P(("rep", "shard"), None),
            P("shard", None),
            P("shard", None),
            P("shard", None),
            P("shard", None),
            P("shard"),
            P("shard"),
            P("shard"),
            P("shard", None),
            P("shard", None),
            P("shard", None),
            P("shard"),
        ),
        check_vma=False,
    )
```

```python
import math

import jax
import jax.numpy as jnp
from jax import lax
from jax.experimental import pallas as pl
from jax.experimental.pallas import tpu as pltpu
from jax.sharding import PartitionSpec as P

HEADS = 16
HEAD_DIM = 128


epsilon = 1e-06
theta_base = 500000.0
neg_fill = -1e30


def rms_scale(values):
    return lax.rsqrt(jnp.mean(values * values, axis=-1, keepdims=True) + epsilon)


def rms_back(upstream, normed, row_scale):
    return row_scale * (upstream - normed * jnp.mean(upstream * normed, axis=-1, keepdims=True))


def rotate(values, cosines, sines):
    half_dim = values.shape[-1] // 2
    first_half = values[..., :half_dim]
    second = values[..., half_dim:]
    return jnp.concatenate(
        [first_half * cosines - second * sines, second * cosines + first_half * sines], axis=-1
    )


def dot_back(left_side, right_side):
    return lax.dot_general(
        left_side, right_side, (((1,), (1,)), ((), ())), preferred_element_type=jnp.float32
    )


def col_term(left_side, right_side):

    def block_term(row_start, row_count):
        return lax.dot_general(
            left_side, right_side, (((0,), (0,)), ((), ())), preferred_element_type=jnp.float32
        )

    return block_term


def on_device_general(
    hidden_in,
    segments,
    w_query,
    w_key,
    w_value,
    w_output,
    query_gain,
    key_gain,
    attn_gain,
    w_gate,
    w_up,
    w_down,
    ffn_gain,
    out_cotangent,
):
    length = hidden_in.shape[0]
    model_width = hidden_in.shape[1]
    ffn_width = w_gate.shape[1]
    factor = HEAD_DIM ** (-0.5)
    doc_row = segments[0]
    earlier = jnp.sum((doc_row[None, :] < doc_row[:, None]).astype(jnp.int32), axis=1)
    positions = jnp.arange(length, dtype=jnp.int32) - earlier
    half_dim = HEAD_DIM // 2
    inverse = jnp.exp(
        jnp.arange(half_dim, dtype=jnp.float32) * (-2.0 * math.log(theta_base) / HEAD_DIM)
    )
    angles = positions.astype(jnp.float32)[:, None] * inverse[None, :]
    cosines = jnp.cos(angles)[:, None, :]
    sines = jnp.sin(angles)[:, None, :]
    token_idx = jnp.arange(length)
    allowed = (doc_row[:, None] == doc_row[None, :]) & (token_idx[:, None] >= token_idx[None, :])

    def reduce_rows(term_fn, local_rows):
        return lax.psum_scatter(
            term_fn(jnp.int32(0), local_rows * lax.axis_size("shard")),
            "shard",
            scatter_dimension=0,
            tiled=True,
        )

    def norm_rope(raw_proj, gain_vec):
        normed = raw_proj * rms_scale(raw_proj) * gain_vec
        return rotate(normed.reshape(length, HEADS, HEAD_DIM), cosines, sines)

    def attend_scores(query_low, key_low):
        scores = (
            jnp.einsum("qhd,khd->hqk", query_low, key_low, preferred_element_type=jnp.float32)
            * factor
        )
        return jnp.where(allowed[None], scores, neg_fill)

    full_query, full_key, full_value, gain_query, gain_key = (
        lax.all_gather(w_query, "shard", axis=0, tiled=True),
        lax.all_gather(w_key, "shard", axis=0, tiled=True),
        lax.all_gather(w_value, "shard", axis=0, tiled=True),
        lax.all_gather(query_gain, "shard", axis=0, tiled=True),
        lax.all_gather(key_gain, "shard", axis=0, tiled=True),
    )
    query_raw = jnp.dot(hidden_in, full_query, preferred_element_type=jnp.float32)
    key_raw = jnp.dot(hidden_in, full_key, preferred_element_type=jnp.float32)
    query_low = norm_rope(query_raw, gain_query.astype(jnp.float32)).astype(jnp.bfloat16)
    key_low = norm_rope(key_raw, gain_key.astype(jnp.float32)).astype(jnp.bfloat16)
    value_low = (
        jnp.dot(hidden_in, full_value, preferred_element_type=jnp.float32)
        .astype(jnp.bfloat16)
        .reshape(length, HEADS, HEAD_DIM)
    )
    scores = attend_scores(query_low, key_low)
    row_peak = jnp.max(scores, axis=-1, keepdims=True)
    log_norm = row_peak + jnp.log(jnp.sum(jnp.exp(scores - row_peak), axis=-1, keepdims=True))
    attn_prob = jnp.exp(scores - log_norm)
    mixed_low = (
        jnp.einsum(
            "hqk,khd->qhd",
            attn_prob.astype(jnp.bfloat16),
            value_low,
            preferred_element_type=jnp.float32,
        )
        .reshape(length, model_width)
        .astype(jnp.bfloat16)
    )
    full_output, gain_attn = (
        lax.all_gather(w_output, "shard", axis=0, tiled=True),
        lax.all_gather(attn_gain, "shard", axis=0, tiled=True),
    )
    attn_out = jnp.dot(mixed_low, full_output, preferred_element_type=jnp.float32)
    attn_rms = rms_scale(attn_out)
    attn_normed = attn_out * attn_rms
    resid = hidden_in.astype(jnp.float32) + attn_normed * gain_attn.astype(jnp.float32)
    resid_low = resid.astype(jnp.bfloat16)
    full_gate, full_up = (
        lax.all_gather(w_gate, "shard", axis=0, tiled=True),
        lax.all_gather(w_up, "shard", axis=0, tiled=True),
    )
    gate_proj = jnp.dot(resid_low, full_gate, preferred_element_type=jnp.float32)
    up_proj = jnp.dot(resid_low, full_up, preferred_element_type=jnp.float32)
    gate_sig = jax.nn.sigmoid(gate_proj)
    hidden_ffn = (gate_proj * gate_sig * up_proj).astype(jnp.bfloat16)
    full_down, gain_ffn = (
        lax.all_gather(w_down, "shard", axis=0, tiled=True),
        lax.all_gather(ffn_gain, "shard", axis=0, tiled=True),
    )
    ffn_out = jnp.dot(hidden_ffn, full_down, preferred_element_type=jnp.float32)
    ffn_rms = rms_scale(ffn_out)
    ffn_normed = ffn_out * ffn_rms
    hidden_out = (resid + ffn_normed * gain_ffn.astype(jnp.float32)).astype(jnp.bfloat16)
    grad_out = out_cotangent.astype(jnp.float32)
    back_down, back_fgain = (
        lax.all_gather(w_down, "shard", axis=0, tiled=True),
        lax.all_gather(ffn_gain, "shard", axis=0, tiled=True),
    )
    ffn_gain_term = jnp.sum(grad_out * ffn_normed, axis=0)
    d_ffn_low = rms_back(grad_out * back_fgain.astype(jnp.float32), ffn_normed, ffn_rms).astype(
        jnp.bfloat16
    )
    down_grad = reduce_rows(col_term(hidden_ffn, d_ffn_low), w_down.shape[0])
    d_hidden_ffn = dot_back(d_ffn_low, back_down)
    d_gate_low = (d_hidden_ffn * up_proj * gate_sig * (1.0 + gate_proj * (1.0 - gate_sig))).astype(
        jnp.bfloat16
    )
    d_up_low = (d_hidden_ffn * gate_proj * gate_sig).astype(jnp.bfloat16)
    ffn_in_grad = reduce_rows(
        col_term(resid_low, jnp.concatenate([d_gate_low, d_up_low], axis=1)), w_gate.shape[0]
    )
    back_gate, back_up = (
        lax.all_gather(w_gate, "shard", axis=0, tiled=True),
        lax.all_gather(w_up, "shard", axis=0, tiled=True),
    )
    d_resid = grad_out + dot_back(d_gate_low, back_gate) + dot_back(d_up_low, back_up)
    back_output, back_again = (
        lax.all_gather(w_output, "shard", axis=0, tiled=True),
        lax.all_gather(attn_gain, "shard", axis=0, tiled=True),
    )
    attn_gain_term = jnp.sum(d_resid * attn_normed, axis=0)
    d_attn_low = rms_back(d_resid * back_again.astype(jnp.float32), attn_normed, attn_rms).astype(
        jnp.bfloat16
    )
    out_grad = reduce_rows(col_term(mixed_low, d_attn_low), w_output.shape[0])
    d_mixed_low = (
        dot_back(d_attn_low, back_output).astype(jnp.bfloat16).reshape(length, HEADS, HEAD_DIM)
    )
    scores_again = attend_scores(query_low, key_low)
    prob_again = jnp.exp(scores_again - log_norm)
    d_value = jnp.einsum(
        "hqk,qhd->khd",
        prob_again.astype(jnp.bfloat16),
        d_mixed_low,
        preferred_element_type=jnp.float32,
    )
    d_prob = jnp.einsum("qhd,khd->hqk", d_mixed_low, value_low, preferred_element_type=jnp.float32)
    d_scores_low = (
        prob_again * (d_prob - jnp.sum(d_prob * prob_again, axis=-1, keepdims=True))
    ).astype(jnp.bfloat16)
    d_query_rot = (
        jnp.einsum("hqk,khd->qhd", d_scores_low, key_low, preferred_element_type=jnp.float32)
        * factor
    )
    d_key_rot = (
        jnp.einsum("hqk,qhd->khd", d_scores_low, query_low, preferred_element_type=jnp.float32)
        * factor
    )
    back_query, back_key, back_value, back_qgain, back_kgain = (
        lax.all_gather(w_query, "shard", axis=0, tiled=True),
        lax.all_gather(w_key, "shard", axis=0, tiled=True),
        lax.all_gather(w_value, "shard", axis=0, tiled=True),
        lax.all_gather(query_gain, "shard", axis=0, tiled=True),
        lax.all_gather(key_gain, "shard", axis=0, tiled=True),
    )
    unused_query, query_pull = jax.vjp(norm_rope, query_raw, back_qgain.astype(jnp.float32))
    d_query_raw, query_gain_term = query_pull(d_query_rot)
    unused_key, key_pull = jax.vjp(norm_rope, key_raw, back_kgain.astype(jnp.float32))
    d_key_raw, key_gain_term = key_pull(d_key_rot)
    d_query_low = d_query_raw.astype(jnp.bfloat16)
    d_key_low = d_key_raw.astype(jnp.bfloat16)
    d_value_low = d_value.reshape(length, model_width).astype(jnp.bfloat16)
    qkv_grad = reduce_rows(
        col_term(hidden_in, jnp.concatenate([d_query_low, d_key_low, d_value_low], axis=1)),
        w_query.shape[0],
    )
    hidden_grad = (
        d_resid
        + dot_back(d_query_low, back_query)
        + dot_back(d_key_low, back_key)
        + dot_back(d_value_low, back_value)
    ).astype(jnp.bfloat16)
    gain_sums = (
        lax.psum_scatter(query_gain_term, "shard", scatter_dimension=0, tiled=True),
        lax.psum_scatter(key_gain_term, "shard", scatter_dimension=0, tiled=True),
        lax.psum_scatter(attn_gain_term, "shard", scatter_dimension=0, tiled=True),
        lax.psum_scatter(ffn_gain_term, "shard", scatter_dimension=0, tiled=True),
    )
    totals = (
        lax.psum(qkv_grad[:, :model_width].astype(jnp.bfloat16), "rep").astype(jnp.float32),
        lax.psum(qkv_grad[:, model_width : 2 * model_width].astype(jnp.bfloat16), "rep").astype(
            jnp.float32
        ),
        lax.psum(qkv_grad[:, 2 * model_width :].astype(jnp.bfloat16), "rep").astype(jnp.float32),
        lax.psum(out_grad.astype(jnp.bfloat16), "rep").astype(jnp.float32),
        lax.psum(gain_sums[0].astype(jnp.bfloat16), "rep").astype(jnp.float32),
        lax.psum(gain_sums[1].astype(jnp.bfloat16), "rep").astype(jnp.float32),
        lax.psum(gain_sums[2].astype(jnp.bfloat16), "rep").astype(jnp.float32),
        lax.psum(ffn_in_grad[:, :ffn_width].astype(jnp.bfloat16), "rep").astype(jnp.float32),
        lax.psum(ffn_in_grad[:, ffn_width:].astype(jnp.bfloat16), "rep").astype(jnp.float32),
        lax.psum(down_grad.astype(jnp.bfloat16), "rep").astype(jnp.float32),
        lax.psum(gain_sums[3].astype(jnp.bfloat16), "rep").astype(jnp.float32),
    )
    return (
        hidden_out,
        hidden_grad,
        totals[0],
        totals[1],
        totals[2],
        totals[3],
        totals[4],
        totals[5],
        totals[6],
        totals[7],
        totals[8],
        totals[9],
        totals[10],
    )


LINE = 4


def shard_perm(move):
    return [(index, move(index)) for index in range(16)]


def pair_swap(values):
    return lax.ppermute(values, "shard", shard_perm(lambda index: index ^ 2))


def rep_swap(values):
    return lax.ppermute(values, "rep", [(0, 1), (1, 0)])


def by_pair(pair, own, other):
    return jnp.where(pair == 0, own, other), jnp.where(pair == 0, other, own)


def gather_rows(weight, pair):
    return jnp.concatenate(by_pair(pair, weight, pair_swap(weight)), axis=0)


MESH_ID = pl.DeviceIdType.MESH


class Line:
    def __init__(self):
        index = lax.axis_index("shard")
        self.rep = lax.axis_index("rep")
        self.place = index // 4
        self.pair = (index // 2) % 2
        self.core = index % 2
        self.block = self.place * 2 + self.core
        self.sibling = self.at(self.place, self.pair, 1 - self.core)
        self.right = self.at(jnp.minimum(self.place + 1, LINE - 1), self.pair, self.core)
        self.left = self.at(jnp.maximum(self.place - 1, 0), self.pair, self.core)
        self.across = self.at(self.place, 1 - self.pair, self.core)
        self.partner = (1 - self.rep, index)
        self.has_right = self.place < LINE - 1
        self.has_left = self.place > 0

    def at(self, place, pair, core):
        return (self.rep, place * 4 + pair * 2 + core)

    def piece(self, p, sign):
        return (self.place + sign * (p // 2) + LINE) % LINE, (self.core + p % 2) % 2

    def meet(self, wide):
        barrier = pltpu.get_barrier_semaphore()

        def greet(device):
            pl.semaphore_signal(barrier, inc=1, device_id=device, device_id_type=MESH_ID)

        if wide:
            for p in range(1, 2 * LINE):
                place, core = self.piece(p, 1)
                greet(self.at(place, self.pair, core))
            greet(self.across)
            greet(self.partner)
            pl.semaphore_wait(barrier, 2 * LINE + 1)
            return
        greet(self.sibling)
        pl.when(self.has_right)(lambda: greet(self.right))
        pl.when(self.has_left)(lambda: greet(self.left))
        pl.semaphore_wait(
            barrier, 1 + self.has_right.astype(jnp.int32) + self.has_left.astype(jnp.int32)
        )


def remote(source, target, send_sem, recv_sem, device):
    return pltpu.make_async_remote_copy(
        src_ref=source,
        dst_ref=target,
        send_sem=send_sem,
        recv_sem=recv_sem,
        device_id=device,
        device_id_type=MESH_ID,
    )


class Spread:
    semaphores = ((2 * LINE,),) * 2 + ((2 * LINE, 2),) * 4
    buffers = ()
    near = False

    BESIDE_LINE = ((0, 0, 1, 1, 1, 2, 2, 2), (0, 2, 3, 4, 5, 6, 7, 8), (3, 4, 5, 6, 7, 8, 9, 10))
    BESIDE_HEADS = ((0, 0, 0, 0, 4, 4, 0, 0), (0, 1, 4, 4, 8, 8, 4, 4), (1, 2, 5, 5, 9, 9, 5, 5))

    def __init__(self, *weights, plan=BESIDE_LINE):
        self.inputs, self.plan = list(weights), plan
        shape = (16 * weights[0].shape[0], sum(weight.shape[1] for weight in weights) // 8)
        self.outputs = [jax.ShapeDtypeStruct(shape, jnp.bfloat16)]
        self.slots = max(plan[2]) + 1

    def bind(self, line, sources, targets, sems):
        self.line, self.sources, self.target = line, sources, targets[0]
        self.z_send, self.z_recv, self.y_send, self.y_recv, self.x_send, self.x_recv = sems
        self.half = sources[0].shape[0] // 2

    def slot(self, t):
        for when, act in zip(self.plan, (self.start, self.came, self.onward)):
            for p in range(2 * LINE):
                if t == when[p]:
                    act(p)

    def rows(self, place, pair, core, rep):
        start = ((place * 4 + pair * 2 + core) * 2 + rep) * self.half
        return self.target.at[pl.ds(pl.multiple_of(start, self.half), self.half), :]

    def start(self, p):
        line, half = self.line, self.half
        place, core = line.piece(p, 1)
        here = self.rows(line.place, line.pair, line.core, line.rep)
        mine = pl.ds(pl.multiple_of(line.rep * half, half), half)
        at = 0
        for q in range(2):
            for source in self.sources:
                n = source.shape[1] // 16
                column = pl.multiple_of((place * 4 + q * 2 + core) * n, n)
                piece, goal = source.at[mine, pl.ds(column, n)], here.at[:, pl.ds(at, n)]
                if p == 0:
                    pltpu.make_async_copy(piece, goal, self.z_recv.at[0]).start()
                else:
                    remote(
                        piece, goal, self.z_send.at[p], self.z_recv.at[p], line.at(place, line.pair, core)
                    ).start()
                at += n

    def cross(self, p, pair, rep, which):
        place, core = self.line.piece(p, -1)
        ref = self.rows(place, pair, core, rep)
        return remote(ref, ref, self.y_send.at[p, which], self.y_recv.at[p, which], self.line.across)

    def over(self, p, pair, rep, which):
        place, core = self.line.piece(p, -1)
        ref = self.rows(place, pair, core, rep)
        return remote(ref, ref, self.x_send.at[p, which], self.x_recv.at[p, which], self.line.partner)

    def came(self, p):
        line = self.line
        place, core = line.piece(p, -1)
        ref = self.rows(place, line.pair, core, line.rep)
        if p == 0:
            pltpu.make_async_copy(ref, ref, self.z_recv.at[0]).wait()
        else:
            remote(ref, ref, self.z_send.at[p], self.z_recv.at[p], line.sibling).wait_recv()
        self.cross(p, line.pair, line.rep, 0).start()
        self.over(p, line.pair, line.rep, 0).start()

    def onward(self, p):
        line = self.line
        if p % 2:
            self.over(p, line.pair, 1 - line.rep, 0).wait_recv()
            self.cross(p, line.pair, 1 - line.rep, 1).start()
        else:
            self.cross(p, 1 - line.pair, line.rep, 0).wait_recv()
            self.over(p, 1 - line.pair, line.rep, 1).start()

    def finish(self):
        line = self.line
        pair, rep = line.pair, line.rep
        for p in range(2 * LINE):
            if p > 0:
                ref = self.rows(line.place, pair, line.core, rep)
                remote(ref, ref, self.z_send.at[p], self.z_recv.at[p], line.sibling).wait_send()
            self.cross(p, pair, rep, 0).wait_send()
            self.over(p, pair, rep, 0).wait_send()
            if p % 2:
                self.cross(p, 1 - pair, rep, 0).wait_recv()
                self.cross(p, pair, 1 - rep, 1).wait_send()
                self.cross(p, 1 - pair, 1 - rep, 1).wait_recv()
            else:
                self.over(p, pair, 1 - rep, 0).wait_recv()
                self.over(p, 1 - pair, rep, 1).wait_send()
                self.over(p, 1 - pair, 1 - rep, 1).wait_recv()


class Stack:
    buffers = ()
    near = False

    def __init__(self, weight, count):
        self.inputs, self.count = [weight], count
        self.outputs = [jax.ShapeDtypeStruct((2 * weight.shape[0], weight.shape[1]), weight.dtype)]
        self.semaphores = ((1,),) + ((count,),) * 4
        self.slots = 1 + count

    def bind(self, line, sources, targets, sems):
        self.line, self.source, self.target = line, sources[0], targets[0]
        self.local, self.y_send, self.y_recv, self.x_send, self.x_recv = sems
        self.size = self.source.shape[0]

    def here(self):
        size = self.size
        mine = self.target.at[pl.ds(pl.multiple_of(self.line.pair * size, size), size), :]
        return pltpu.make_async_copy(self.source, mine, self.local.at[0])

    def there(self, p):
        line, part = self.line, self.size // (2 * self.count)
        start = pl.multiple_of((line.rep * self.count + p) * part, part)
        goal = self.target.at[pl.ds(pl.multiple_of(line.pair * self.size + start, part), part), :]
        return remote(
            self.source.at[pl.ds(start, part), :], goal, self.y_send.at[p], self.y_recv.at[p], line.across
        )

    def onward(self, p, rep):
        line, part = self.line, self.size // (2 * self.count)
        start = (1 - line.pair) * self.size + (rep * self.count + p) * part
        ref = self.target.at[pl.ds(pl.multiple_of(start, part), part), :]
        return remote(ref, ref, self.x_send.at[p], self.x_recv.at[p], line.partner)

    def slot(self, t):
        if t == 0:
            for k in range(self.count):
                self.there(k).start()
            self.here().start()
        if 1 <= t < 1 + self.count:
            self.there(t - 1).wait_recv()
            self.onward(t - 1, self.line.rep).start()

    def finish(self):
        self.here().wait()
        for p in range(self.count):
            self.there(p).wait_send()
            self.onward(p, self.line.rep).wait_send()
            self.onward(p, 1 - self.line.rep).wait_recv()


class Swap:
    semaphores = ((2,),)
    buffers = ()
    near = True
    slots = 1

    def __init__(self, values, start, count):
        self.inputs, self.start, self.count = [values], start, count
        self.outputs = [jax.ShapeDtypeStruct((count, values.shape[1]), values.dtype)]

    def bind(self, line, sources, targets, scratch):
        sends, recvs = scratch[0].at[0], scratch[0].at[1]
        rows = sources[0].at[pl.ds(self.start, self.count), :]
        self.copy = remote(rows, targets[0], sends, recvs, line.partner)

    def slot(self, t):
        if t == 0:
            self.copy.start()

    def finish(self):
        self.copy.wait()


class Share:
    semaphores = ((2 * LINE,),) * 2
    buffers = ()
    near = True
    slots = 1

    def __init__(self, values):
        self.inputs = [values]
        self.outputs = [jax.ShapeDtypeStruct((2 * LINE,) + values.shape, values.dtype)]

    def bind(self, line, sources, targets, scratch):
        self.line, self.source, self.target = line, sources[0], targets[0]
        self.sends, self.recvs = scratch

    def copy(self, p):
        goal = self.target.at[self.line.block]
        if p == 0:
            return pltpu.make_async_copy(self.source, goal, self.recvs.at[0])
        place, core = self.line.piece(p, 1)
        return remote(
            self.source, goal, self.sends.at[p], self.recvs.at[p], self.line.at(place, self.line.pair, core)
        )

    def slot(self, t):
        if t == 0:
            for p in range(2 * LINE):
                self.copy(p).start()

    def finish(self):
        for p in range(2 * LINE):
            self.copy(p).wait()


class Deal:
    semaphores = ((2 * LINE,),) * 4
    buffers = ()
    near = True
    slots = 3 + 2 * LINE

    def __init__(self, sources, per):
        rows, width = sources[0].shape[1:]
        self.inputs, self.per = list(sources), per
        self.n = width // per
        self.width = width * len(sources)
        self.outputs = [jax.ShapeDtypeStruct((rows, 16 * self.width), sources[0].dtype)]

    def bind(self, line, sources, targets, scratch):
        self.line, self.sources, self.target = line, sources, targets[0]
        self.z_send, self.z_recv, self.x_send, self.x_recv = scratch

    def runs(self, place, core):
        for index, source in enumerate(self.sources):
            for run in range(self.per):
                block = (index * self.per + run) * 16 + place * 4 + self.line.rep * 2 + core
                yield source, run * self.n, pl.ds(pl.multiple_of(block * self.n, self.n), self.n)

    def whole(self):
        return self.target.at[:, pl.ds(0, self.width)]

    def start(self, p):
        line = self.line
        place, core = line.piece(p, 1)
        for source, at, there in self.runs(line.place, line.core):
            piece = source.at[2 * place + core, :, pl.ds(at, self.n)]
            goal = self.target.at[:, there]
            if p == 0:
                pltpu.make_async_copy(piece, goal, self.z_recv.at[0]).start()
            else:
                remote(
                    piece, goal, self.z_send.at[p], self.z_recv.at[p], line.at(place, line.pair, core)
                ).start()

    def came(self, p):
        line, ref = self.line, self.whole()
        if p == 0:
            pltpu.make_async_copy(ref, ref, self.z_recv.at[0]).wait()
        else:
            remote(ref, ref, self.z_send.at[p], self.z_recv.at[p], line.partner).wait_recv()
        place, core = line.piece(p, -1)
        for _, _, there in self.runs(place, core):
            goal = self.target.at[:, there]
            remote(goal, goal, self.x_send.at[p], self.x_recv.at[p], line.partner).start()

    def slot(self, t):
        if t < 2 * LINE:
            self.start(t)
        if t == 0:
            self.came(0)
        if 3 <= t < 2 + 2 * LINE:
            self.came(t - 2)

    def finish(self):
        ref = self.whole()
        for p in range(2 * LINE):
            if p > 0:
                remote(ref, ref, self.z_send.at[p], self.z_recv.at[p], self.line.partner).wait_send()
            remote(ref, ref, self.x_send.at[p], self.x_recv.at[p], self.line.partner).wait()


def outer_into(target, left, row, right, column, *more):
    rows, n = target.shape
    tall = min(rows, 256)
    wide = 512 if n % 512 == 0 else 384

    def some(index, carry):
        across = n // wide
        down, along = index // across, index % across
        here = pl.ds(pl.multiple_of(down * tall, tall), tall)
        there = pl.ds(pl.multiple_of(along * wide, wide), wide)
        total = lax.dot_general(
            left[:, pl.ds(pl.multiple_of(row + down * tall, 128), tall)],
            right[:, pl.ds(pl.multiple_of(column + along * wide, 128), wide)],
            (((0,), (0,)), ((), ())),
            preferred_element_type=jnp.float32,
        )
        for ref in more:
            total = total + ref[here, there].astype(jnp.float32)
        target[here, there] = total.astype(target.dtype)
        return carry

    lax.fori_loop(0, (rows // tall) * (n // wide), some, 0)


class Reduce:
    near = True

    def __init__(self, left, rights, first):
        rows, n = left.shape[1] // 8, rights[0].shape[1] // 2
        self.inputs, self.first, self.size, self.n = [left, *rights], first, rows, n
        self.outputs = [jax.ShapeDtypeStruct((LINE, rows, n), left.dtype) for _ in rights]
        self.chunks = 2 * LINE if first == "partner" else LINE
        wide = n if first == "partner" else 2 * n
        self.semaphores = ((self.chunks,),) * (2 * len(rights)) + ((LINE,),) * (2 * len(rights))
        self.buffers = ((self.chunks, rows, wide),) * (2 * len(rights))
        self.join_at = [3, 5, 8, 10] if first == "partner" else [3, 5, 7, 9]
        self.last_at = [12, 15, 16, 17] if first == "partner" else [10, 10, 10, 11]
        self.slots = max(self.last_at) + 1

    def bind(self, line, sources, targets, scratch):
        self.line, self.left, self.parts = line, sources[0], []
        count = len(targets)
        sems1, sems2, buffers = scratch[: 2 * count], scratch[2 * count : 4 * count], scratch[4 * count :]
        for index, target in enumerate(targets):
            pick = slice(2 * index, 2 * index + 2)
            self.parts.append((sources[1 + index], target, *sems1[pick], *sems2[pick], *buffers[pick]))

    def row(self, place, pair):
        return (place * 2 + pair) * self.size

    def leg1(self, part, k):
        _, _, send1, recv1, _, _, out, came = part
        device = self.line.partner if self.first == "partner" else self.line.across
        return remote(out.at[k], came.at[k], send1.at[k], recv1.at[k], device)

    def leg2(self, part, k):
        _, target, _, _, send2, recv2, out, _ = part
        device = self.line.across if self.first == "partner" else self.line.partner
        return remote(out.at[k, :, pl.ds(0, self.n)], target.at[k], send2.at[k], recv2.at[k], device)

    def produce(self, k):
        line = self.line
        for part in self.parts:
            if self.first == "partner":
                pair = 1 - line.pair if k < LINE else line.pair
                outer_into(part[6].at[k], self.left, self.row(k % LINE, pair), part[0], (1 - line.rep) * self.n)
            else:
                outer_into(part[6].at[k], self.left, self.row(k, 1 - line.pair), part[0], 0)
            self.leg1(part, k).start()

    def join(self, k):
        line, n = self.line, self.n
        for part in self.parts:
            right, _, _, _, _, _, out, came = part
            self.leg1(part, k).wait()
            goal = out.at[k, :, pl.ds(0, n)]
            if self.first == "partner":
                outer_into(goal, self.left, self.row(k, 1 - line.pair), right, line.rep * n, came.at[k])
            else:
                column = pl.multiple_of((1 - line.rep) * n, n)
                outer_into(goal, self.left, self.row(k, line.pair), right, column, came.at[k, :, pl.ds(column, n)])
            self.leg2(part, k).start()

    def last(self, k):
        line, n = self.line, self.n
        for part in self.parts:
            right, target, _, _, _, _, _, came = part
            if self.first == "partner":
                self.leg1(part, LINE + k).wait()
                mine = came.at[LINE + k]
            else:
                mine = came.at[k, :, pl.ds(pl.multiple_of(line.rep * n, n), n)]
            self.leg2(part, k).wait()
            outer_into(target.at[k], self.left, self.row(k, line.pair), right, line.rep * n, mine, target.at[k])

    def slot(self, t):
        if t < self.chunks:
            self.produce(t)
        for k in range(LINE):
            if t == self.join_at[k]:
                self.join(k)
        for k in range(LINE):
            if t == self.last_at[k]:
                self.last(k)

    def finish(self):
        pass


class PairSum:
    near = True

    def __init__(self, left, right, count, at):
        self.inputs, self.count, self.at = [left, right], count, at
        shape = (left.shape[1] // 2, right.shape[1])
        self.outputs = [jax.ShapeDtypeStruct(shape, left.dtype)]
        self.semaphores = ((count,),) * 2
        self.buffers = (shape,)
        self.slots = at + count

    def bind(self, line, sources, targets, scratch):
        self.line, self.target = line, targets[0]
        self.left, self.right = sources
        self.sends, self.recvs, self.out = scratch
        self.size = self.target.shape[0] // self.count

    def copy(self, k):
        rows = pl.ds(k * self.size, self.size)
        return remote(
            self.out.at[rows, :], self.target.at[rows, :], self.sends.at[k], self.recvs.at[k], self.line.across
        )

    def slot(self, t):
        pair, size = self.line.pair, self.size
        for k in range(self.count):
            rows = pl.ds(k * size, size)
            if t == k:
                outer_into(self.out.at[rows, :], self.left, (1 - pair) * self.count * size + k * size, self.right, 0)
                self.copy(k).start()
            if t == self.at + k:
                self.copy(k).wait()
                goal = self.target.at[rows, :]
                outer_into(goal, self.left, pair * self.count * size + k * size, self.right, 0, goal)

    def finish(self):
        pass


def line_scatter_joint(line, k, rows, parts, sib):
    return parts[2 * k + line.core, rows, :].astype(jnp.float32) + sib[k, rows, :].astype(jnp.float32)


def line_scatter_pass(line, j, step, way, parts, sib, sums, came, sib_recv, send_sem, came_sem):
    rows = pl.ds(pl.multiple_of(j * step, step), step)
    device = line.right if way == 0 else line.left
    ends = line.place == 0 if way == 0 else line.place == LINE - 1

    def copy(k):
        return remote(sums.at[k, rows], came.at[k, rows], send_sem.at[k, j], came_sem.at[k, j], device)

    for k in range(LINE - 1, 0, -1) if way == 0 else range(LINE - 1):

        @pl.when(line.place < k if way == 0 else line.place > k)
        def _():
            remote(
                parts.at[2 * k + line.core, rows], sib.at[k, rows], sib_recv.at[k, j], sib_recv.at[k, j], line.sibling
            ).wait_recv()

            @pl.when(ends)
            def _():
                sums[k, rows, :] = line_scatter_joint(line, k, rows, parts, sib).astype(jnp.bfloat16)

            @pl.when(jnp.logical_not(ends))
            def _():
                copy(k).wait_recv()
                sums[k, rows, :] = (
                    line_scatter_joint(line, k, rows, parts, sib) + came[k, rows, :].astype(jnp.float32)
                ).astype(jnp.bfloat16)

            copy(k).start()


def line_scatter_total(line, j, step, parts, sib, rights, lefts, sums, sib_recv, sends, right_recv, left_recv):
    rows = pl.ds(pl.multiple_of(j * step, step), step)
    me = line.place
    remote(
        parts.at[2 * me + line.core, rows], sib.at[me, rows], sib_recv.at[me, j], sib_recv.at[me, j], line.sibling
    ).wait_recv()

    @pl.when(line.has_left)
    def _():
        remote(sums.at[me, rows], rights.at[me, rows], sends.at[me, j], right_recv.at[me, j], line.left).wait_recv()

    @pl.when(line.has_right)
    def _():
        remote(sums.at[me, rows], lefts.at[me, rows], sends.at[me, j], left_recv.at[me, j], line.right).wait_recv()

    total = line_scatter_joint(line, me, rows, parts, sib)
    total = total + jnp.where(line.has_left, rights[me, rows, :].astype(jnp.float32), 0.0)
    return total + jnp.where(line.has_right, lefts[me, rows, :].astype(jnp.float32), 0.0)


def line_scatter_start(line, j, step, parts, sib, sib_send, sib_recv):
    rows = pl.ds(pl.multiple_of(j * step, step), step)
    for k in range(LINE):
        remote(
            parts.at[2 * k + 1 - line.core, rows], sib.at[k, rows], sib_send.at[k, j], sib_recv.at[k, j], line.sibling
        ).start()


def line_scatter_end(line, j, step, parts, sib, rights, lefts, sums, sib_send, right_send, left_send):
    rows = pl.ds(pl.multiple_of(j * step, step), step)
    for k in range(LINE):
        remote(
            parts.at[2 * k + 1 - line.core, rows], sib.at[k, rows], sib_send.at[k, j], sib_send.at[k, j], line.sibling
        ).wait_send()

        @pl.when(line.place < k)
        def _():
            remote(
                sums.at[k, rows], rights.at[k, rows], right_send.at[k, j], right_send.at[k, j], line.right
            ).wait_send()

        @pl.when(line.place > k)
        def _():
            remote(
                sums.at[k, rows], lefts.at[k, rows], left_send.at[k, j], left_send.at[k, j], line.left
            ).wait_send()


def gather_copy(line, k, j, step, core, gathered, way, sends, recvs):
    rows = pl.ds(pl.multiple_of(j * step, step), step)
    block = 2 * k + core
    device = (line.right, line.left, line.sibling)[way]
    ref = gathered.at[block, rows]
    return remote(ref, ref, sends.at[k, way, j], recvs.at[block, j], device)


def line_gather_own(line, j, step, gathered, sends, recvs):
    def copy(way):
        return gather_copy(line, line.place, j, step, line.core, gathered, way, sends, recvs)

    pl.when(line.has_right)(lambda: copy(0).start())
    pl.when(line.has_left)(lambda: copy(1).start())
    copy(2).start()


def line_gather_pass(line, hop, j, step, gathered, sends, recvs):
    for way in (0, 1):
        k = line.place - hop if way == 0 else line.place + hop
        there = k >= 0 if way == 0 else k < LINE
        onward = line.has_right if way == 0 else line.has_left
        k = jnp.clip(k, 0, LINE - 1)

        @pl.when(there)
        def _():
            gather_copy(line, k, j, step, line.core, gathered, way, sends, recvs).wait_recv()
            pl.when(onward)(
                lambda: gather_copy(line, k, j, step, line.core, gathered, way, sends, recvs).start()
            )
            gather_copy(line, k, j, step, line.core, gathered, 2, sends, recvs).start()


def line_gather_end(line, j, step, gathered, sends, recvs):
    for k in range(LINE):
        gather_copy(line, k, j, step, 1 - line.core, gathered, 2, sends, recvs).wait_recv()
        gather_copy(line, k, j, step, line.core, gathered, 2, sends, recvs).wait_send()

        @pl.when((line.place >= k) & line.has_right)
        def _():
            gather_copy(line, k, j, step, line.core, gathered, 0, sends, recvs).wait_send()

        @pl.when((line.place <= k) & line.has_left)
        def _():
            gather_copy(line, k, j, step, line.core, gathered, 1, sends, recvs).wait_send()


def take_from(items, count):
    taken = items[:count]
    del items[:count]
    return taken


def moves_scratch(moves):
    scratch = []
    for move in moves:
        scratch += [pltpu.SemaphoreType.DMA(shape) for shape in move.semaphores]
        scratch += [pltpu.VMEM(shape, jnp.bfloat16) for shape in move.buffers]
    return scratch


def moves_specs(moves, side):
    near, far = pl.BlockSpec(memory_space=pltpu.VMEM), pl.BlockSpec(memory_space=pl.ANY)
    return [
        near if move.near or side == "outputs" else far for move in moves for _ in getattr(move, side)
    ]


def line_call(collective_id, pieces, middle, inputs, outputs, scatter, gather, moves=(), limit=46):
    step = inputs[0].shape[-2] // pieces if inputs else 0
    low = jnp.bfloat16
    scratch = []
    if scatter:
        block = inputs[0].shape[-2:]
        scratch += [pltpu.VMEM((LINE,) + block, low) for _ in range(4)]
        scratch += [pltpu.SemaphoreType.DMA((LINE, pieces)) for _ in range(6)]
    if gather:
        scratch += [pltpu.SemaphoreType.DMA((LINE, 3, pieces)), pltpu.SemaphoreType.DMA((2 * LINE, pieces))]
    n_scratch = len(scratch)
    scratch += moves_scratch(moves)
    moved = [values for move in moves for values in move.inputs]
    extras = [shape for move in moves for shape in move.outputs]

    def kernel(*refs):
        refs = list(refs)

        def take(count):
            taken = refs[:count]
            del refs[:count]
            return taken

        ins = take(len(inputs))
        given = [take(len(move.inputs)) for move in moves]
        outs = take(len(outputs))
        extra = [take(len(move.outputs)) for move in moves]
        rest = take(n_scratch)
        line = Line()
        for move, sources, targets in zip(moves, given, extra):
            move.bind(line, sources, targets, take(len(move.semaphores) + len(move.buffers)))
        line.meet(bool(moves))
        if scatter:
            sib, rights, lefts, sums, sib_send, sib_recv, right_send, left_send, right_recv, left_recv = rest[:10]
            parts = ins[0]
            for j in range(2):
                line_scatter_start(line, j, step, parts, sib, sib_send, sib_recv)
        if gather:
            sends, recvs = rest[-2:]

        hops = (LINE - 1) * (int(scatter) + int(gather))

        def during(j, act):
            pl.when((j >= 0) & (j < pieces))(lambda: act(j))

        def finish(j):
            rows = pl.ds(pl.multiple_of(j * step, step), step)
            total = None
            if scatter:
                total = line_scatter_total(
                    line, j, step, parts, sib, rights, lefts, sums, sib_recv, right_send, right_recv, left_recv
                )
            values = middle(total, rows, j, ins, outs)
            if gather:
                outs[0][line.block, rows, :] = values.astype(low)
                line_gather_own(line, j, step, outs[0], sends, recvs)

        def slot(t, carry):
            if scatter:
                during(t + 2, lambda j: line_scatter_start(line, j, step, parts, sib, sib_send, sib_recv))
                during(
                    t - line.place,
                    lambda j: line_scatter_pass(
                        line, j, step, 0, parts, sib, sums, rights, sib_recv, right_send, right_recv
                    ),
                )
                during(
                    t - (LINE - 1 - line.place),
                    lambda j: line_scatter_pass(
                        line, j, step, 1, parts, sib, sums, lefts, sib_recv, left_send, left_recv
                    ),
                )
                during(t - (LINE - 1), finish)
            if gather:
                for hop in range(1, LINE):
                    during(
                        t - hop - (LINE - 1 if scatter else 0),
                        lambda j, hop=hop: line_gather_pass(line, hop, j, step, outs[0], sends, recvs),
                    )
                during(t - hops - 1, lambda j: line_gather_end(line, j, step, outs[0], sends, recvs))
            if scatter:
                during(
                    t - LINE,
                    lambda j: line_scatter_end(
                        line, j, step, parts, sib, rights, lefts, sums, sib_send, right_send, left_send
                    ),
                )
            return carry

        if gather and not scatter:
            lax.fori_loop(0, pieces, lambda j, carry: (finish(j), carry)[1], 0)
        slots = pieces + hops + 1 if inputs else 0
        apart = max([move.slots for move in moves] + [0])
        if apart <= 1:
            for move in moves:
                move.slot(0)
            if inputs:
                lax.fori_loop(0, slots, slot, 0)
        else:
            for t in range(max(slots, apart)):
                for move in moves:
                    move.slot(t)
                if t < slots:
                    slot(t, 0)
        for move in moves:
            move.finish()

    vmem = pl.BlockSpec(memory_space=pltpu.VMEM)
    return pl.pallas_call(
        kernel,
        out_shape=[jax.ShapeDtypeStruct(shape, kind) for shape, kind in outputs] + extras,
        in_specs=[vmem] * len(inputs) + moves_specs(moves, "inputs"),
        out_specs=[vmem] * len(outputs) + moves_specs(moves, "outputs"),
        scratch_shapes=scratch,
        compiler_params=pltpu.CompilerParams(
            collective_id=collective_id, has_side_effects=True, vmem_limit_bytes=limit << 20
        ),
        cost_estimate=pl.CostEstimate(flops=10_000_000, bytes_accessed=200_000_000, transcendentals=0),
    )(*inputs, *moved)


def gather_blocks(payload, moves, collective_id):
    def middle(total, rows, j, ins, outs):
        return ins[0][rows, :]

    shape = (2 * LINE,) + payload.shape
    return line_call(collective_id, 8, middle, [payload], [(shape, jnp.bfloat16)], False, True, moves, 58)


def attention_block(parts, hidden, gain, moves, collective_id):
    def middle(total, rows, j, ins, outs):
        outs[1][rows, :] = total
        resid = ins[1][rows, :].astype(jnp.float32) + total * rms_scale(total) * ins[2][...]
        outs[2][rows, :] = resid
        return resid

    shape = hidden.shape
    return line_call(
        collective_id, 8, middle, [parts, hidden, gain],
        [(parts.shape, jnp.bfloat16), (shape, jnp.float32), (shape, jnp.float32)], True, True, moves,
    )


def add_rows(ref, values, j):
    folded = jnp.sum(values.reshape(values.shape[0] // 8, 8, values.shape[1]), axis=0)

    @pl.when(j == 0)
    def _():
        ref[...] = folded

    @pl.when(j > 0)
    def _():
        ref[...] += folded


def ffn_block(parts, resid, cotangent, gain, collective_id):
    def middle(total, rows, j, ins, outs):
        scale = rms_scale(total)
        normed = total * scale
        grad = ins[2][rows, :].astype(jnp.float32)
        gains = ins[3][...]
        outs[1][rows, :] = (ins[1][rows, :] + normed * gains).astype(jnp.bfloat16)
        add_rows(outs[2], grad * normed, j)
        return rms_back(grad * gains, normed, scale)

    shape = resid.shape
    return line_call(
        collective_id, 8, middle, [parts, resid, cotangent, gain],
        [(parts.shape, jnp.bfloat16), (shape, jnp.bfloat16), ((8, shape[1]), jnp.float32)], True, True,
    )


def back_block(parts, cotangent, attn_out, gain, moves, collective_id):
    def middle(total, rows, j, ins, outs):
        d_resid = ins[1][rows, :].astype(jnp.float32) + total
        outs[1][rows, :] = d_resid
        attn = ins[2][rows, :]
        scale = rms_scale(attn)
        normed = attn * scale
        add_rows(outs[2], d_resid * normed, j)
        return rms_back(d_resid * ins[3][...], normed, scale)

    shape = cotangent.shape
    return line_call(
        collective_id, 8, middle, [parts, cotangent, attn_out, gain],
        [(parts.shape, jnp.bfloat16), (shape, jnp.float32), ((8, shape[1]), jnp.float32)], True, True, moves, 56,
    )


def last_block(parts, d_resid, moves, collective_id):
    def middle(total, rows, j, ins, outs):
        outs[0][rows, :] = (ins[1][rows, :] + total).astype(jnp.bfloat16)

    return line_call(
        collective_id, 8, middle, [parts, d_resid], [(d_resid.shape, jnp.bfloat16)], True, False, moves
    )


def line_exchange(line, mine, came, sends, recvs):
    def copy(p):
        place, core = line.piece(p, 1)
        return remote(mine, came.at[p], sends.at[p], recvs.at[p], line.at(place, line.pair, core))

    for p in range(1, 2 * LINE):
        copy(p).start()
    total = mine[...]
    for p in range(1, 2 * LINE):
        copy(p).wait_recv()
        total = total + came[p]
    for p in range(1, 2 * LINE):
        copy(p).wait_send()
    return total


def spot(head, index):
    start = (3 * head + index) * HEAD_DIM
    return slice(start, start + HEAD_DIM)


def turn_tables(turns):
    half = turns.shape[1] // 2
    swapped = pltpu.roll(turns, half, 1)
    first = lax.broadcasted_iota(jnp.int32, turns.shape, 1) < half
    return jnp.where(first, turns, swapped), jnp.where(first, -swapped, turns)


def as_row(column):
    return jnp.broadcast_to(column, (column.shape[0], column.shape[0])).T[0:1, :]


def as_columns(row):
    return jnp.broadcast_to(row, (row.shape[1], row.shape[1])).T


def dot(left, right, left_dim, right_dim):
    return lax.dot_general(
        left, right, (((left_dim,), (right_dim,)), ((), ())), preferred_element_type=jnp.float32
    )


def heads_call(collective_id, body, inputs, outputs, scratch, rows, moves):
    blocks, length = 2 * LINE, HEAD_DIM
    scratch = [
        pltpu.VMEM((rows, length), jnp.float32),
        pltpu.VMEM((blocks, rows, length), jnp.float32),
        pltpu.SemaphoreType.DMA((blocks,)),
        pltpu.SemaphoreType.DMA((blocks,)),
    ] + scratch
    n_scratch = len(scratch)
    moved = [values for move in moves for values in move.inputs]
    extras = [shape for move in moves for shape in move.outputs]

    def kernel(*refs):
        refs = list(refs)
        ins = take_from(refs, len(inputs))
        given = [take_from(refs, len(move.inputs)) for move in moves]
        outs = take_from(refs, len(outputs))
        extra = [take_from(refs, len(move.outputs)) for move in moves]
        rest = take_from(refs, n_scratch)
        line = Line()
        for move, sources, targets in zip(moves, given, extra):
            move.bind(line, sources, targets, take_from(refs, len(move.semaphores) + len(move.buffers)))
        line.meet(True)
        passed = [0]

        def tick():
            for move in moves:
                move.slot(passed[0])
            passed[0] += 1

        body(line, ins, outs, rest, tick)
        while passed[0] < max([move.slots for move in moves] + [0]):
            tick()
        for move in moves:
            move.finish()

    vmem = pl.BlockSpec(memory_space=pltpu.VMEM)
    return pl.pallas_call(
        kernel,
        out_shape=[jax.ShapeDtypeStruct(shape, kind) for shape, kind in outputs] + extras,
        in_specs=[vmem] * len(inputs) + moves_specs(moves, "inputs"),
        out_specs=[vmem] * len(outputs) + moves_specs(moves, "outputs"),
        scratch_shapes=scratch + moves_scratch(moves),
        compiler_params=pltpu.CompilerParams(
            collective_id=collective_id, has_side_effects=True, vmem_limit_bytes=44 << 20
        ),
        cost_estimate=pl.CostEstimate(flops=10_000_000, bytes_accessed=80_000_000, transcendentals=0),
    )(*inputs, *moved)


def attend(tokens, full_qkv, turns, bias, gains, weight, moves, collective_id):
    blocks, length = bias.shape[:2]
    width = full_qkv.shape[1] // 3
    heads = width // HEAD_DIM
    model_width = weight.shape[1]
    low = jnp.bfloat16

    def body(line, ins, outs, scratch, tick):
        tokens, full_qkv, turns, bias, gains, weight = ins
        parts, lows, probs, mixed, squares, raw = outs
        mine, came, sends, recvs = scratch

        def squares_of(two, carry):
            both = pl.ds(2 * two, 2)
            product = dot(tokens[both].reshape(2 * length, model_width), full_qkv[...], 1, 0)
            raw[both] = product.reshape(2, length, 3 * width)
            for b, index in ((2 * two, 0), (2 * two, 1), (2 * two + 1, 0), (2 * two + 1, 1)):
                total = jnp.zeros((length, 1), jnp.float32)
                for h in range(heads):
                    values = raw[b, :length, spot(h, index)]
                    total = total + jnp.sum(values * values, axis=1, keepdims=True)
                mine[pl.ds(index * blocks + b, 1), :] = as_row(total)
            return carry

        tick()
        for part in range(LINE):
            squares_of(part, 0)
            tick()
        squares[...] = line_exchange(line, mine, came, sends, recvs)
        tick()

        def block(b, carry):
            scales = [
                lax.rsqrt(as_columns(squares[pl.ds(index * blocks + b, 1), :]) / model_width + epsilon)
                for index in range(2)
            ]
            cos, sin = turn_tables(turns[b])
            for h in range(heads):
                here = slice(h * HEAD_DIM, (h + 1) * HEAD_DIM)
                turned = []
                for index in range(2):
                    there = spot(h, index)
                    normed = raw[b, :length, there] * scales[index] * gains[index : index + 1, here]
                    turned.append((normed * cos + pltpu.roll(normed, HEAD_DIM // 2, 1) * sin).astype(low))
                    lows[b, :, there] = turned[index]
                there = spot(h, 2)
                value = raw[b, :length, there].astype(low)
                lows[b, :, there] = value
                scores = dot(turned[0], turned[1], 1, 1) * HEAD_DIM**-0.5 + bias[b]
                powers = jnp.exp(scores - jnp.max(scores, axis=1, keepdims=True))
                prob = powers / jnp.sum(powers, axis=1, keepdims=True)
                probs[b, h] = prob
                mixed[b, :, here] = dot(prob.astype(low), value, 1, 0).astype(low)
            return carry

        for part in range(LINE):
            lax.fori_loop(2 * part, 2 * part + 2, block, 0)
            both = pl.ds(2 * part, 2)
            product = dot(mixed[both].reshape(2 * length, width), weight[...], 1, 0)
            parts[both] = product.astype(low).reshape(2, length, model_width)
            tick()

    return heads_call(
        collective_id,
        body,
        [tokens, full_qkv, turns, bias, gains, weight],
        [
            ((blocks, length, model_width), low),
            ((blocks, length, 3 * width), low),
            ((blocks, heads, length, length), jnp.float32),
            ((blocks, length, width), low),
            ((2 * blocks, length), jnp.float32),
            ((blocks, length, 3 * width), jnp.float32),
        ],
        [],
        2 * blocks,
        moves,
    )


def attend_back(d_attn, weight, raw, turns, gains, lows, probs, squares, wide_terms, full_qkv, moves, collective_id):
    blocks, length = raw.shape[:2]
    width = raw.shape[2] // 3
    heads = width // HEAD_DIM
    model_width = weight.shape[1]
    low = jnp.bfloat16

    def body(line, ins, outs, scratch, tick):
        d_attn, weight, raw, turns, gains, lows, probs, squares = ins[:8]
        d_low, terms, wide, parts = outs
        full_qkv = ins[10]
        mine, came, sends, recvs, upstream, unit, d_mixed = scratch
        tick()
        terms[...] = jnp.zeros_like(terms)
        for which in range(2):
            total = jnp.sum(ins[8 + which][...], axis=0, keepdims=True)
            for index in range(model_width // length):
                row = 2 * blocks + which * (model_width // length) + index
                mine[row : row + 1, :] = total[:, index * length : (index + 1) * length]

        def block(b, carry):
            scales = [
                lax.rsqrt(as_columns(squares[pl.ds(index * blocks + b, 1), :]) / model_width + epsilon)
                for index in range(2)
            ]
            cos, sin = turn_tables(turns[b])
            means = [jnp.zeros((length, 1), jnp.float32)] * 2
            for h in range(heads):
                here = slice(h * HEAD_DIM, (h + 1) * HEAD_DIM)
                places = [spot(h, index) for index in range(3)]
                query, key, value = [lows[b, :, there] for there in places]
                prob = probs[b, h]
                d_out = d_mixed[b, :, here]
                d_low[b, :length, places[2]] = dot(prob.astype(low), d_out, 0, 0).astype(low)
                d_prob = dot(d_out, value, 1, 1)
                d_scores = (
                    prob * (d_prob - jnp.sum(d_prob * prob, axis=1, keepdims=True))
                ).astype(low)
                turned = [dot(d_scores, key, 1, 0), dot(d_scores, query, 0, 0)]
                for index in range(2):
                    d_rot = turned[index] * HEAD_DIM**-0.5
                    d_normed = d_rot * cos - pltpu.roll(d_rot, HEAD_DIM // 2, 1) * sin
                    units = raw[b, :length, places[index]] * scales[index]
                    ups = d_normed * gains[index : index + 1, here]
                    folded = (d_normed * units).reshape(length // 8, 8, HEAD_DIM)
                    side = slice((index * heads + h) * HEAD_DIM, (index * heads + h + 1) * HEAD_DIM)
                    terms[:, side] += jnp.sum(folded, axis=0)
                    upstream[b, :, side] = ups
                    unit[b, :, side] = units
                    means[index] = means[index] + jnp.sum(ups * units, axis=1, keepdims=True)
            for index in range(2):
                mine[pl.ds(index * blocks + b, 1), :] = as_row(means[index])
            return carry

        def mix(two, carry):
            both = pl.ds(2 * two, 2)
            product = dot(d_attn[both].reshape(2 * length, model_width), weight[...], 1, 1)
            d_mixed[both] = product.astype(low).reshape(2, length, width)
            return carry

        lax.fori_loop(0, LINE, mix, 0)
        lax.fori_loop(0, blocks, block, 0)
        mine[...] = line_exchange(line, mine, came, sends, recvs)
        wide[...] = mine[2 * blocks :, :]

        def last(b, carry):
            for index in range(2):
                scale = lax.rsqrt(
                    as_columns(squares[pl.ds(index * blocks + b, 1), :]) / model_width + epsilon
                )
                mean = as_columns(mine[pl.ds(index * blocks + b, 1), :]) / model_width
                for h in range(heads):
                    side = slice((index * heads + h) * HEAD_DIM, (index * heads + h + 1) * HEAD_DIM)
                    d_low[b, :length, spot(h, index)] = (
                        scale * (upstream[b, :, side] - unit[b, :, side] * mean)
                    ).astype(low)
            return carry

        def lasts(two, carry):
            lax.fori_loop(2 * two, 2 * two + 2, last, 0)
            both = pl.ds(2 * two, 2)
            product = dot(d_low[both].reshape(2 * length, 3 * width), full_qkv[...], 1, 1)
            parts[both] = product.astype(low).reshape(2, length, model_width)
            return carry

        lax.fori_loop(0, LINE, lasts, 0)

    return heads_call(
        collective_id,
        body,
        [d_attn, weight, raw, turns, gains, lows, probs, squares, *wide_terms, full_qkv],
        [
            (raw.shape, low),
            ((8, 2 * width), jnp.float32),
            ((2 * model_width // length, length), jnp.float32),
            ((blocks, length, model_width), low),
        ],
        [pltpu.VMEM((blocks, length, 2 * width), jnp.float32) for _ in range(2)]
        + [pltpu.VMEM((blocks, length, width), low)],
        2 * blocks + 2 * model_width // length,
        moves,
    )


def on_device(
    hidden_in,
    segments,
    w_query,
    w_key,
    w_value,
    w_output,
    query_gain,
    key_gain,
    attn_gain,
    w_gate,
    w_up,
    w_down,
    ffn_gain,
    out_cotangent,
):
    length, model_width = hidden_in.shape
    blocks = 2 * LINE
    heads = HEADS // blocks
    factor = HEAD_DIM ** (-0.5)
    pair = (lax.axis_index("shard") // 2) % 2
    f32 = jnp.float32

    extra = jnp.stack([query_gain, key_gain, attn_gain, ffn_gain, segments[0].astype(jnp.bfloat16)])
    payload, extras, full_qkv, full_output = gather_blocks(
        hidden_in,
        [
            Share(jnp.pad(extra, ((0, 11), (0, 0)))),
            Spread(w_query, w_key, w_value),
            Stack(w_output, 2),
        ],
        0,
    )
    tokens = payload.reshape(-1, model_width)
    docs = extras[:, 4].astype(jnp.int32)
    gains = extras[:, :4].reshape(LINE, 2, 4, length)
    gains = jnp.stack(by_pair(pair, gains, pair_swap(gains)), axis=1)
    gains = jnp.moveaxis(gains, 3, 0).reshape(4, 1, model_width).astype(f32)
    gain_attn, gain_ffn = gains[2], gains[3]
    width = heads * HEAD_DIM
    head_gains = gather_rows(jnp.stack([query_gain, key_gain])[None], pair).astype(f32)
    head_gains = head_gains.transpose(1, 0, 2).reshape(2, width)

    earlier = jnp.sum((docs[:, None, :] < docs[:, :, None]).astype(jnp.int32), axis=2)
    positions = jnp.arange(length, dtype=jnp.int32)[None] - earlier
    half_dim = HEAD_DIM // 2
    inverse = jnp.exp(
        jnp.arange(half_dim, dtype=f32) * (-2.0 * math.log(theta_base) / HEAD_DIM)
    )
    angles = positions.astype(f32)[:, :, None] * inverse[None, None, :]
    turns = jnp.cos(jnp.concatenate([angles, angles - 0.5 * math.pi], axis=-1))
    token_idx = jnp.arange(length)
    allowed = (docs[:, :, None] == docs[:, None, :]) & (
        token_idx[:, None] >= token_idx[None, :]
    )[None]
    bias = jnp.where(allowed, 0.0, neg_fill)

    def to_blocks(values):
        return values.astype(jnp.bfloat16).reshape(blocks, -1, model_width)

    attn_parts, lows, probs, mixed_low, squares, raw, full_gate = attend(
        payload, full_qkv, turns, bias, head_gains, full_output, [Spread(w_gate, plan=Spread.BESIDE_HEADS)], 6
    )
    mixed_low = mixed_low.reshape(blocks * length, width)
    resid_low, attn_out, resid, full_up, full_down = attention_block(
        attn_parts,
        hidden_in,
        gain_attn,
        [Spread(w_up), Stack(w_down, 8)],
        1,
    )
    resid_low = resid_low.reshape(blocks * length, model_width)

    gate_proj = jnp.dot(resid_low, full_gate, preferred_element_type=f32)
    up_proj = jnp.dot(resid_low, full_up, preferred_element_type=f32)
    gate_sig = jax.nn.sigmoid(gate_proj)
    hidden_ffn = (gate_proj * gate_sig * up_proj).astype(jnp.bfloat16)
    d_ffn_low, hidden_out, ffn_gain_term = ffn_block(
        to_blocks(jnp.dot(hidden_ffn, full_down, preferred_element_type=f32)),
        resid,
        out_cotangent,
        gain_ffn,
        2,
    )
    d_ffn_low = d_ffn_low.reshape(blocks * length, model_width)

    d_hidden_ffn = dot_back(d_ffn_low, full_down)
    d_gate_low = (d_hidden_ffn * up_proj * gate_sig * (1.0 + gate_proj * (1.0 - gate_sig))).astype(
        jnp.bfloat16
    )
    d_up_low = (d_hidden_ffn * gate_proj * gate_sig).astype(jnp.bfloat16)
    ff_rows = w_down.shape[0]
    d_attn_low, d_resid, attn_gain_term, gate_sum, up_sum, down_part = back_block(
        to_blocks(dot_back(d_gate_low, full_gate) + dot_back(d_up_low, full_up)),
        out_cotangent,
        attn_out,
        gain_attn,
        [
            Reduce(resid_low, [d_gate_low, d_up_low], "partner"),
            PairSum(hidden_ffn, d_ffn_low, 4, 13),
        ],
        3,
    )

    d_qkv, head_terms, wide_terms, back_parts, there_first = attend_back(
        d_attn_low, full_output, raw, turns, head_gains, lows, probs, squares,
        [attn_gain_term, ffn_gain_term], full_qkv, [Swap(down_part, 0, ff_rows // 2)], 7,
    )
    d_attn_low = d_attn_low.reshape(blocks * length, model_width)
    hidden_grad, qkv_sum, output_part, ffn_total, there_second = last_block(
        back_parts,
        d_resid,
        [
            Reduce(tokens, [d_qkv.reshape(-1, 3 * width)], "across"),
            PairSum(mixed_low, d_attn_low, 1, 5),
            Deal([gate_sum.reshape(blocks, length, -1), up_sum.reshape(blocks, length, -1)], 1),
            Swap(down_part, ff_rows // 2, ff_rows // 2),
        ],
        4,
    )
    qkv_total, there_output = line_call(
        5, 1, None, [], [], False, False,
        [
            Deal([qkv_sum.reshape(blocks, length, -1)], 3),
            Swap(output_part, 0, length),
        ],
    )

    def total_of(first, second):
        return first.astype(f32) + second.astype(f32)

    grad_query, grad_key, grad_value = jnp.split(qkv_total.astype(f32), 3, axis=1)
    grad_gate, grad_up = jnp.split(ffn_total.astype(f32), 2, axis=1)
    grad_output = total_of(output_part, there_output)
    grad_down = total_of(down_part, jnp.concatenate([there_first, there_second]))
    head_terms = jnp.sum(head_terms, axis=0).reshape(2, 2, HEAD_DIM)
    own_term, other_term = by_pair(pair, head_terms[:, 0], head_terms[:, 1])
    head_grads = own_term + pair_swap(other_term)
    wide_terms = (wide_terms + pair_swap(wide_terms)).reshape(2, 16, length)
    wide_grads = lax.dynamic_index_in_dim(wide_terms, lax.axis_index("shard"), 1, keepdims=False)
    gain_grads = jnp.concatenate([head_grads, wide_grads])
    gain_grads = gain_grads + rep_swap(gain_grads)
    return (
        hidden_out,
        hidden_grad,
        grad_query,
        grad_key,
        grad_value,
        grad_output,
        gain_grads[0],
        gain_grads[1],
        gain_grads[2],
        grad_gate,
        grad_up,
        grad_down,
        gain_grads[3],
    )


def solution(mesh):
    placed = (
        P(("rep", "shard"), None),
        P(("rep", "shard"), None),
        P("shard", None),
        P("shard", None),
        P("shard", None),
        P("shard", None),
        P("shard"),
        P("shard"),
        P("shard"),
        P("shard", None),
        P("shard", None),
        P("shard", None),
        P("shard"),
        P(("rep", "shard"), None),
    )
    return jax.shard_map(
        on_device if mesh.shape["shard"] == 16 else on_device_general,
        mesh=mesh,
        in_specs=placed,
        out_specs=(
            P(("rep", "shard"), None),
            P(("rep", "shard"), None),
            P("shard", None),
            P("shard", None),
            P("shard", None),
            P("shard", None),
            P("shard"),
            P("shard"),
            P("shard"),
            P("shard", None),
            P("shard", None),
            P("shard", None),
            P("shard"),
        ),
        check_vma=False,
    )
```

```python
import math

import jax
import jax.numpy as jnp
from jax import lax
from jax.experimental import pallas as pl
from jax.experimental.pallas import tpu as pltpu
from jax.sharding import PartitionSpec as P

HEADS = 16
HEAD_DIM = 128


epsilon = 1e-06
theta_base = 500000.0
neg_fill = -1e30


def rms_scale(values):
    return lax.rsqrt(jnp.mean(values * values, axis=-1, keepdims=True) + epsilon)


def rms_back(upstream, normed, row_scale):
    return row_scale * (upstream - normed * jnp.mean(upstream * normed, axis=-1, keepdims=True))


def rotate(values, cosines, sines):
    half_dim = values.shape[-1] // 2
    first_half = values[..., :half_dim]
    second = values[..., half_dim:]
    return jnp.concatenate(
        [first_half * cosines - second * sines, second * cosines + first_half * sines], axis=-1
    )


def dot_back(left_side, right_side):
    return lax.dot_general(
        left_side, right_side, (((1,), (1,)), ((), ())), preferred_element_type=jnp.float32
    )


def col_term(left_side, right_side):

    def block_term(row_start, row_count):
        return lax.dot_general(
            left_side, right_side, (((0,), (0,)), ((), ())), preferred_element_type=jnp.float32
        )

    return block_term


def on_device_general(
    hidden_in,
    segments,
    w_query,
    w_key,
    w_value,
    w_output,
    query_gain,
    key_gain,
    attn_gain,
    w_gate,
    w_up,
    w_down,
    ffn_gain,
    out_cotangent,
):
    length = hidden_in.shape[0]
    model_width = hidden_in.shape[1]
    ffn_width = w_gate.shape[1]
    factor = HEAD_DIM ** (-0.5)
    doc_row = segments[0]
    earlier = jnp.sum((doc_row[None, :] < doc_row[:, None]).astype(jnp.int32), axis=1)
    positions = jnp.arange(length, dtype=jnp.int32) - earlier
    half_dim = HEAD_DIM // 2
    inverse = jnp.exp(
        jnp.arange(half_dim, dtype=jnp.float32) * (-2.0 * math.log(theta_base) / HEAD_DIM)
    )
    angles = positions.astype(jnp.float32)[:, None] * inverse[None, :]
    cosines = jnp.cos(angles)[:, None, :]
    sines = jnp.sin(angles)[:, None, :]
    token_idx = jnp.arange(length)
    allowed = (doc_row[:, None] == doc_row[None, :]) & (token_idx[:, None] >= token_idx[None, :])

    def reduce_rows(term_fn, local_rows):
        return lax.psum_scatter(
            term_fn(jnp.int32(0), local_rows * lax.axis_size("shard")),
            "shard",
            scatter_dimension=0,
            tiled=True,
        )

    def norm_rope(raw_proj, gain_vec):
        normed = raw_proj * rms_scale(raw_proj) * gain_vec
        return rotate(normed.reshape(length, HEADS, HEAD_DIM), cosines, sines)

    def attend_scores(query_low, key_low):
        scores = (
            jnp.einsum("qhd,khd->hqk", query_low, key_low, preferred_element_type=jnp.float32)
            * factor
        )
        return jnp.where(allowed[None], scores, neg_fill)

    full_query, full_key, full_value, gain_query, gain_key = (
        lax.all_gather(w_query, "shard", axis=0, tiled=True),
        lax.all_gather(w_key, "shard", axis=0, tiled=True),
        lax.all_gather(w_value, "shard", axis=0, tiled=True),
        lax.all_gather(query_gain, "shard", axis=0, tiled=True),
        lax.all_gather(key_gain, "shard", axis=0, tiled=True),
    )
    query_raw = jnp.dot(hidden_in, full_query, preferred_element_type=jnp.float32)
    key_raw = jnp.dot(hidden_in, full_key, preferred_element_type=jnp.float32)
    query_low = norm_rope(query_raw, gain_query.astype(jnp.float32)).astype(jnp.bfloat16)
    key_low = norm_rope(key_raw, gain_key.astype(jnp.float32)).astype(jnp.bfloat16)
    value_low = (
        jnp.dot(hidden_in, full_value, preferred_element_type=jnp.float32)
        .astype(jnp.bfloat16)
        .reshape(length, HEADS, HEAD_DIM)
    )
    scores = attend_scores(query_low, key_low)
    row_peak = jnp.max(scores, axis=-1, keepdims=True)
    log_norm = row_peak + jnp.log(jnp.sum(jnp.exp(scores - row_peak), axis=-1, keepdims=True))
    attn_prob = jnp.exp(scores - log_norm)
    mixed_low = (
        jnp.einsum(
            "hqk,khd->qhd",
            attn_prob.astype(jnp.bfloat16),
            value_low,
            preferred_element_type=jnp.float32,
        )
        .reshape(length, model_width)
        .astype(jnp.bfloat16)
    )
    full_output, gain_attn = (
        lax.all_gather(w_output, "shard", axis=0, tiled=True),
        lax.all_gather(attn_gain, "shard", axis=0, tiled=True),
    )
    attn_out = jnp.dot(mixed_low, full_output, preferred_element_type=jnp.float32)
    attn_rms = rms_scale(attn_out)
    attn_normed = attn_out * attn_rms
    resid = hidden_in.astype(jnp.float32) + attn_normed * gain_attn.astype(jnp.float32)
    resid_low = resid.astype(jnp.bfloat16)
    full_gate, full_up = (
        lax.all_gather(w_gate, "shard", axis=0, tiled=True),
        lax.all_gather(w_up, "shard", axis=0, tiled=True),
    )
    gate_proj = jnp.dot(resid_low, full_gate, preferred_element_type=jnp.float32)
    up_proj = jnp.dot(resid_low, full_up, preferred_element_type=jnp.float32)
    gate_sig = jax.nn.sigmoid(gate_proj)
    hidden_ffn = (gate_proj * gate_sig * up_proj).astype(jnp.bfloat16)
    full_down, gain_ffn = (
        lax.all_gather(w_down, "shard", axis=0, tiled=True),
        lax.all_gather(ffn_gain, "shard", axis=0, tiled=True),
    )
    ffn_out = jnp.dot(hidden_ffn, full_down, preferred_element_type=jnp.float32)
    ffn_rms = rms_scale(ffn_out)
    ffn_normed = ffn_out * ffn_rms
    hidden_out = (resid + ffn_normed * gain_ffn.astype(jnp.float32)).astype(jnp.bfloat16)
    grad_out = out_cotangent.astype(jnp.float32)
    back_down, back_fgain = (
        lax.all_gather(w_down, "shard", axis=0, tiled=True),
        lax.all_gather(ffn_gain, "shard", axis=0, tiled=True),
    )
    ffn_gain_term = jnp.sum(grad_out * ffn_normed, axis=0)
    d_ffn_low = rms_back(grad_out * back_fgain.astype(jnp.float32), ffn_normed, ffn_rms).astype(
        jnp.bfloat16
    )
    down_grad = reduce_rows(col_term(hidden_ffn, d_ffn_low), w_down.shape[0])
    d_hidden_ffn = dot_back(d_ffn_low, back_down)
    d_gate_low = (d_hidden_ffn * up_proj * gate_sig * (1.0 + gate_proj * (1.0 - gate_sig))).astype(
        jnp.bfloat16
    )
    d_up_low = (d_hidden_ffn * gate_proj * gate_sig).astype(jnp.bfloat16)
    ffn_in_grad = reduce_rows(
        col_term(resid_low, jnp.concatenate([d_gate_low, d_up_low], axis=1)), w_gate.shape[0]
    )
    back_gate, back_up = (
        lax.all_gather(w_gate, "shard", axis=0, tiled=True),
        lax.all_gather(w_up, "shard", axis=0, tiled=True),
    )
    d_resid = grad_out + dot_back(d_gate_low, back_gate) + dot_back(d_up_low, back_up)
    back_output, back_again = (
        lax.all_gather(w_output, "shard", axis=0, tiled=True),
        lax.all_gather(attn_gain, "shard", axis=0, tiled=True),
    )
    attn_gain_term = jnp.sum(d_resid * attn_normed, axis=0)
    d_attn_low = rms_back(d_resid * back_again.astype(jnp.float32), attn_normed, attn_rms).astype(
        jnp.bfloat16
    )
    out_grad = reduce_rows(col_term(mixed_low, d_attn_low), w_output.shape[0])
    d_mixed_low = (
        dot_back(d_attn_low, back_output).astype(jnp.bfloat16).reshape(length, HEADS, HEAD_DIM)
    )
    scores_again = attend_scores(query_low, key_low)
    prob_again = jnp.exp(scores_again - log_norm)
    d_value = jnp.einsum(
        "hqk,qhd->khd",
        prob_again.astype(jnp.bfloat16),
        d_mixed_low,
        preferred_element_type=jnp.float32,
    )
    d_prob = jnp.einsum("qhd,khd->hqk", d_mixed_low, value_low, preferred_element_type=jnp.float32)
    d_scores_low = (
        prob_again * (d_prob - jnp.sum(d_prob * prob_again, axis=-1, keepdims=True))
    ).astype(jnp.bfloat16)
    d_query_rot = (
        jnp.einsum("hqk,khd->qhd", d_scores_low, key_low, preferred_element_type=jnp.float32)
        * factor
    )
    d_key_rot = (
        jnp.einsum("hqk,qhd->khd", d_scores_low, query_low, preferred_element_type=jnp.float32)
        * factor
    )
    back_query, back_key, back_value, back_qgain, back_kgain = (
        lax.all_gather(w_query, "shard", axis=0, tiled=True),
        lax.all_gather(w_key, "shard", axis=0, tiled=True),
        lax.all_gather(w_value, "shard", axis=0, tiled=True),
        lax.all_gather(query_gain, "shard", axis=0, tiled=True),
        lax.all_gather(key_gain, "shard", axis=0, tiled=True),
    )
    unused_query, query_pull = jax.vjp(norm_rope, query_raw, back_qgain.astype(jnp.float32))
    d_query_raw, query_gain_term = query_pull(d_query_rot)
    unused_key, key_pull = jax.vjp(norm_rope, key_raw, back_kgain.astype(jnp.float32))
    d_key_raw, key_gain_term = key_pull(d_key_rot)
    d_query_low = d_query_raw.astype(jnp.bfloat16)
    d_key_low = d_key_raw.astype(jnp.bfloat16)
    d_value_low = d_value.reshape(length, model_width).astype(jnp.bfloat16)
    qkv_grad = reduce_rows(
        col_term(hidden_in, jnp.concatenate([d_query_low, d_key_low, d_value_low], axis=1)),
        w_query.shape[0],
    )
    hidden_grad = (
        d_resid
        + dot_back(d_query_low, back_query)
        + dot_back(d_key_low, back_key)
        + dot_back(d_value_low, back_value)
    ).astype(jnp.bfloat16)
    gain_sums = (
        lax.psum_scatter(query_gain_term, "shard", scatter_dimension=0, tiled=True),
        lax.psum_scatter(key_gain_term, "shard", scatter_dimension=0, tiled=True),
        lax.psum_scatter(attn_gain_term, "shard", scatter_dimension=0, tiled=True),
        lax.psum_scatter(ffn_gain_term, "shard", scatter_dimension=0, tiled=True),
    )
    totals = (
        lax.psum(qkv_grad[:, :model_width].astype(jnp.bfloat16), "rep").astype(jnp.float32),
        lax.psum(qkv_grad[:, model_width : 2 * model_width].astype(jnp.bfloat16), "rep").astype(
            jnp.float32
        ),
        lax.psum(qkv_grad[:, 2 * model_width :].astype(jnp.bfloat16), "rep").astype(jnp.float32),
        lax.psum(out_grad.astype(jnp.bfloat16), "rep").astype(jnp.float32),
        lax.psum(gain_sums[0].astype(jnp.bfloat16), "rep").astype(jnp.float32),
        lax.psum(gain_sums[1].astype(jnp.bfloat16), "rep").astype(jnp.float32),
        lax.psum(gain_sums[2].astype(jnp.bfloat16), "rep").astype(jnp.float32),
        lax.psum(ffn_in_grad[:, :ffn_width].astype(jnp.bfloat16), "rep").astype(jnp.float32),
        lax.psum(ffn_in_grad[:, ffn_width:].astype(jnp.bfloat16), "rep").astype(jnp.float32),
        lax.psum(down_grad.astype(jnp.bfloat16), "rep").astype(jnp.float32),
        lax.psum(gain_sums[3].astype(jnp.bfloat16), "rep").astype(jnp.float32),
    )
    return (
        hidden_out,
        hidden_grad,
        totals[0],
        totals[1],
        totals[2],
        totals[3],
        totals[4],
        totals[5],
        totals[6],
        totals[7],
        totals[8],
        totals[9],
        totals[10],
    )


LINE = 4


def shard_perm(move):
    return [(index, move(index)) for index in range(16)]


def pair_swap(values):
    return lax.ppermute(values, "shard", shard_perm(lambda index: index ^ 2))


def by_pair(pair, own, other):
    return jnp.where(pair == 0, own, other), jnp.where(pair == 0, other, own)


def gather_rows(weight, pair):
    return jnp.concatenate(by_pair(pair, weight, pair_swap(weight)), axis=0)


MESH_ID = pl.DeviceIdType.MESH


class Line:
    def __init__(self):
        index = lax.axis_index("shard")
        self.rep = lax.axis_index("rep")
        self.place = index // 4
        self.pair = (index // 2) % 2
        self.core = index % 2
        self.block = self.place * 2 + self.core
        self.sibling = self.at(self.place, self.pair, 1 - self.core)
        self.right = self.at(jnp.minimum(self.place + 1, LINE - 1), self.pair, self.core)
        self.left = self.at(jnp.maximum(self.place - 1, 0), self.pair, self.core)
        self.across = self.at(self.place, 1 - self.pair, self.core)
        self.partner = (1 - self.rep, index)
        self.diagonal = (1 - self.rep, self.across[1])
        self.has_right = self.place < LINE - 1
        self.has_left = self.place > 0

    def at(self, place, pair, core):
        return (self.rep, place * 4 + pair * 2 + core)

    def piece(self, p, sign):
        return (self.place + sign * (p // 2) + LINE) % LINE, (self.core + p % 2) % 2

    def meet(self, wide):
        barrier = pltpu.get_barrier_semaphore()

        def greet(device):
            pl.semaphore_signal(barrier, inc=1, device_id=device, device_id_type=MESH_ID)

        if wide:
            for p in range(1, 2 * LINE):
                place, core = self.piece(p, 1)
                greet(self.at(place, self.pair, core))
            greet(self.across)
            greet(self.partner)
            greet(self.diagonal)
            pl.semaphore_wait(barrier, 2 * LINE + 2)
            return
        greet(self.sibling)
        pl.when(self.has_right)(lambda: greet(self.right))
        pl.when(self.has_left)(lambda: greet(self.left))
        pl.semaphore_wait(
            barrier, 1 + self.has_right.astype(jnp.int32) + self.has_left.astype(jnp.int32)
        )


def remote(source, target, send_sem, recv_sem, device):
    return pltpu.make_async_remote_copy(
        src_ref=source,
        dst_ref=target,
        send_sem=send_sem,
        recv_sem=recv_sem,
        device_id=device,
        device_id_type=MESH_ID,
    )


class Spread:
    semaphores = ((2 * LINE,),) * 2 + ((2 * LINE, 2),) * 4
    buffers = ()
    near = False

    BESIDE_LINE = ((0, 0, 1, 1, 1, 2, 2, 2), (0, 2, 3, 4, 5, 6, 7, 8), (3, 4, 5, 6, 7, 8, 9, 10))
    BESIDE_HEADS = ((0, 0, 0, 0, 4, 4, 0, 0), (0, 1, 4, 4, 8, 8, 4, 4), (1, 2, 5, 5, 9, 9, 5, 5))

    def __init__(self, *weights, plan=BESIDE_LINE):
        self.inputs, self.plan = list(weights), plan
        shape = (16 * weights[0].shape[0], sum(weight.shape[1] for weight in weights) // 8)
        self.outputs = [jax.ShapeDtypeStruct(shape, jnp.bfloat16)]
        self.slots = max(plan[2]) + 1

    def bind(self, line, sources, targets, sems):
        self.line, self.sources, self.target = line, sources, targets[0]
        self.z_send, self.z_recv, self.y_send, self.y_recv, self.x_send, self.x_recv = sems
        self.half = sources[0].shape[0] // 2

    def slot(self, t):
        for when, act in zip(self.plan, (self.start, self.came, self.onward)):
            for p in range(2 * LINE):
                if t == when[p]:
                    act(p)

    def rows(self, place, pair, core, rep):
        start = ((place * 4 + pair * 2 + core) * 2 + rep) * self.half
        return self.target.at[pl.ds(pl.multiple_of(start, self.half), self.half), :]

    def start(self, p):
        line, half = self.line, self.half
        place, core = line.piece(p, 1)
        here = self.rows(line.place, line.pair, line.core, line.rep)
        mine = pl.ds(pl.multiple_of(line.rep * half, half), half)
        at = 0
        for q in range(2):
            for source in self.sources:
                n = source.shape[1] // 16
                column = pl.multiple_of((place * 4 + q * 2 + core) * n, n)
                piece, goal = source.at[mine, pl.ds(column, n)], here.at[:, pl.ds(at, n)]
                if p == 0:
                    pltpu.make_async_copy(piece, goal, self.z_recv.at[0]).start()
                else:
                    remote(
                        piece, goal, self.z_send.at[p], self.z_recv.at[p], line.at(place, line.pair, core)
                    ).start()
                at += n

    def cross(self, p, pair, rep, which):
        place, core = self.line.piece(p, -1)
        ref = self.rows(place, pair, core, rep)
        return remote(ref, ref, self.y_send.at[p, which], self.y_recv.at[p, which], self.line.across)

    def over(self, p, pair, rep, which):
        place, core = self.line.piece(p, -1)
        ref = self.rows(place, pair, core, rep)
        return remote(ref, ref, self.x_send.at[p, which], self.x_recv.at[p, which], self.line.partner)

    def came(self, p):
        line = self.line
        place, core = line.piece(p, -1)
        ref = self.rows(place, line.pair, core, line.rep)
        if p == 0:
            pltpu.make_async_copy(ref, ref, self.z_recv.at[0]).wait()
        else:
            remote(ref, ref, self.z_send.at[p], self.z_recv.at[p], line.sibling).wait_recv()
        self.cross(p, line.pair, line.rep, 0).start()
        self.over(p, line.pair, line.rep, 0).start()

    def onward(self, p):
        line = self.line
        if p % 2:
            self.over(p, line.pair, 1 - line.rep, 0).wait_recv()
            self.cross(p, line.pair, 1 - line.rep, 1).start()
        else:
            self.cross(p, 1 - line.pair, line.rep, 0).wait_recv()
            self.over(p, 1 - line.pair, line.rep, 1).start()

    def finish(self):
        line = self.line
        pair, rep = line.pair, line.rep
        for p in range(2 * LINE):
            if p > 0:
                ref = self.rows(line.place, pair, line.core, rep)
                remote(ref, ref, self.z_send.at[p], self.z_recv.at[p], line.sibling).wait_send()
            self.cross(p, pair, rep, 0).wait_send()
            self.over(p, pair, rep, 0).wait_send()
            if p % 2:
                self.cross(p, 1 - pair, rep, 0).wait_recv()
                self.cross(p, pair, 1 - rep, 1).wait_send()
                self.cross(p, 1 - pair, 1 - rep, 1).wait_recv()
            else:
                self.over(p, pair, 1 - rep, 0).wait_recv()
                self.over(p, 1 - pair, rep, 1).wait_send()
                self.over(p, 1 - pair, 1 - rep, 1).wait_recv()


class Stack:
    buffers = ()
    near = False

    def __init__(self, weight, count):
        self.inputs, self.count = [weight], count
        self.outputs = [jax.ShapeDtypeStruct((2 * weight.shape[0], weight.shape[1]), weight.dtype)]
        self.semaphores = ((1,),) + ((count,),) * 4
        self.slots = 1 + count

    def bind(self, line, sources, targets, sems):
        self.line, self.source, self.target = line, sources[0], targets[0]
        self.local, self.y_send, self.y_recv, self.x_send, self.x_recv = sems
        self.size = self.source.shape[0]

    def here(self):
        size = self.size
        mine = self.target.at[pl.ds(pl.multiple_of(self.line.pair * size, size), size), :]
        return pltpu.make_async_copy(self.source, mine, self.local.at[0])

    def there(self, p):
        line, part = self.line, self.size // (2 * self.count)
        start = pl.multiple_of((line.rep * self.count + p) * part, part)
        goal = self.target.at[pl.ds(pl.multiple_of(line.pair * self.size + start, part), part), :]
        return remote(
            self.source.at[pl.ds(start, part), :], goal, self.y_send.at[p], self.y_recv.at[p], line.across
        )

    def onward(self, p, rep):
        line, part = self.line, self.size // (2 * self.count)
        start = (1 - line.pair) * self.size + (rep * self.count + p) * part
        ref = self.target.at[pl.ds(pl.multiple_of(start, part), part), :]
        return remote(ref, ref, self.x_send.at[p], self.x_recv.at[p], line.partner)

    def slot(self, t):
        if t == 0:
            for k in range(self.count):
                self.there(k).start()
            self.here().start()
        if 1 <= t < 1 + self.count:
            self.there(t - 1).wait_recv()
            self.onward(t - 1, self.line.rep).start()

    def finish(self):
        self.here().wait()
        for p in range(self.count):
            self.there(p).wait_send()
            self.onward(p, self.line.rep).wait_send()
            self.onward(p, 1 - self.line.rep).wait_recv()


class Swap:
    semaphores = ((2,),)
    buffers = ()
    near = True

    def __init__(self, values, start, count, at=0):
        self.made = values if isinstance(values, PairSum) else None
        shape = values.outputs[0] if self.made else values
        self.inputs = [] if self.made else [values]
        self.start, self.count, self.at, self.slots = start, count, at, at + 1
        self.outputs = [jax.ShapeDtypeStruct((count, shape.shape[1]), shape.dtype)]

    def bind(self, line, sources, targets, scratch):
        source = self.made.target if self.made else sources[0]
        sends, recvs = scratch[0].at[0], scratch[0].at[1]
        rows = source.at[pl.ds(self.start, self.count), :]
        self.copy = remote(rows, targets[0], sends, recvs, line.partner)

    def slot(self, t):
        if t == self.at:
            self.copy.start()

    def finish(self):
        self.copy.wait()


class Four:
    semaphores = ((3,),) * 2
    buffers = ()
    near = True
    slots = 1

    def __init__(self, values):
        self.inputs = [values]
        self.outputs = [jax.ShapeDtypeStruct(values.shape, values.dtype)] * 3

    def bind(self, line, sources, targets, scratch):
        devices = (line.across, line.partner, line.diagonal)
        self.copies = [
            remote(sources[0], target, scratch[0].at[index], scratch[1].at[index], device)
            for index, (target, device) in enumerate(zip(targets, devices))
        ]

    def slot(self, t):
        if t == 0:
            for copy in self.copies:
                copy.start()

    def finish(self):
        for copy in self.copies:
            copy.wait()


class Share:
    semaphores = ((2 * LINE,),) * 2
    buffers = ()
    near = True
    slots = 1

    def __init__(self, values):
        self.inputs = [values]
        self.outputs = [jax.ShapeDtypeStruct((2 * LINE,) + values.shape, values.dtype)]

    def bind(self, line, sources, targets, scratch):
        self.line, self.source, self.target = line, sources[0], targets[0]
        self.sends, self.recvs = scratch

    def copy(self, p):
        goal = self.target.at[self.line.block]
        if p == 0:
            return pltpu.make_async_copy(self.source, goal, self.recvs.at[0])
        place, core = self.line.piece(p, 1)
        return remote(
            self.source, goal, self.sends.at[p], self.recvs.at[p], self.line.at(place, self.line.pair, core)
        )

    def slot(self, t):
        if t == 0:
            for p in range(2 * LINE):
                self.copy(p).start()

    def finish(self):
        for p in range(2 * LINE):
            self.copy(p).wait()


class Deal:
    semaphores = ((2 * LINE,),) * 4
    buffers = ()
    near = True

    def __init__(self, sources, per, at=0):
        self.made = sources if isinstance(sources, Reduce) else None
        shapes = sources.outputs if self.made else sources
        self.inputs = [] if self.made else list(sources)
        self.rows, width = shapes[0].shape[1] // 2, shapes[0].shape[2]
        self.per, self.at, self.n = per, at, width // per
        self.width = width * len(shapes)
        self.slots = at + 2 + 2 * LINE
        self.outputs = [jax.ShapeDtypeStruct((self.rows, 16 * self.width), shapes[0].dtype)]

    def bind(self, line, sources, targets, scratch):
        self.line, self.target = line, targets[0]
        self.sources = [part[1] for part in self.made.parts] if self.made else sources
        self.z_send, self.z_recv, self.x_send, self.x_recv = scratch

    def runs(self, place, core):
        for index, source in enumerate(self.sources):
            for run in range(self.per):
                block = (index * self.per + run) * 16 + place * 4 + self.line.rep * 2 + core
                yield source, run * self.n, pl.ds(pl.multiple_of(block * self.n, self.n), self.n)

    def whole(self):
        return self.target.at[:, pl.ds(0, self.width)]

    def start(self, p):
        line = self.line
        place, core = line.piece(p, 1)
        for source, at, there in self.runs(line.place, line.core):
            rows = pl.ds(pl.multiple_of(core * self.rows, self.rows), self.rows)
            piece = source.at[place, rows, pl.ds(at, self.n)]
            goal = self.target.at[:, there]
            if p == 0:
                pltpu.make_async_copy(piece, goal, self.z_recv.at[0]).start()
            else:
                remote(
                    piece, goal, self.z_send.at[p], self.z_recv.at[p], line.at(place, line.pair, core)
                ).start()

    def came(self, p):
        line, ref = self.line, self.whole()
        if p == 0:
            pltpu.make_async_copy(ref, ref, self.z_recv.at[0]).wait()
        else:
            remote(ref, ref, self.z_send.at[p], self.z_recv.at[p], line.partner).wait_recv()
        place, core = line.piece(p, -1)
        for _, _, there in self.runs(place, core):
            goal = self.target.at[:, there]
            remote(goal, goal, self.x_send.at[p], self.x_recv.at[p], line.partner).start()

    def slot(self, t):
        t -= self.at
        for p in range(2 * LINE):
            if t == (0 if self.made else p):
                self.start(p)
        for p in range(2 * LINE):
            if t == (p if self.made or p == 0 else p + 2):
                self.came(p)

    def finish(self):
        ref = self.whole()
        for p in range(2 * LINE):
            if p > 0:
                remote(ref, ref, self.z_send.at[p], self.z_recv.at[p], self.line.partner).wait_send()
            remote(ref, ref, self.x_send.at[p], self.x_recv.at[p], self.line.partner).wait()


def outer_into(target, left, row, right, column, *more):
    rows, n = target.shape
    tall = min(rows, 256)
    wide = 512 if n % 512 == 0 else 384

    def some(index, carry):
        across = n // wide
        down, along = index // across, index % across
        here = pl.ds(pl.multiple_of(down * tall, tall), tall)
        there = pl.ds(pl.multiple_of(along * wide, wide), wide)
        total = lax.dot_general(
            left[:, pl.ds(pl.multiple_of(row + down * tall, 128), tall)],
            right[:, pl.ds(pl.multiple_of(column + along * wide, 128), wide)],
            (((0,), (0,)), ((), ())),
            preferred_element_type=jnp.float32,
        )
        for ref in more:
            total = total + ref[here, there].astype(jnp.float32)
        target[here, there] = total.astype(target.dtype)
        return carry

    lax.fori_loop(0, (rows // tall) * (n // wide), some, 0)


class Reduce:
    near = True

    def __init__(self, left, rights, first):
        rows, n = left.shape[1] // 8, rights[0].shape[1] // 2
        self.inputs, self.first, self.size, self.n = [left, *rights], first, rows, n
        self.outputs = [jax.ShapeDtypeStruct((LINE, rows, n), left.dtype) for _ in rights]
        self.chunks = 2 * LINE if first == "partner" else LINE
        wide = n if first == "partner" else 2 * n
        self.semaphores = ((self.chunks,),) * (2 * len(rights)) + ((LINE,),) * (2 * len(rights))
        self.buffers = ((self.chunks, rows, wide),) * (2 * len(rights))
        self.join_at = [3, 5, 8, 10] if first == "partner" else [3, 4, 5, 7]
        self.last_at = [12, 15, 16, 17] if first == "partner" else [6, 7, 8, 9]
        self.slots = max(self.last_at) + 1

    def bind(self, line, sources, targets, scratch):
        self.line, self.left, self.parts = line, sources[0], []
        count = len(targets)
        sems1, sems2, buffers = scratch[: 2 * count], scratch[2 * count : 4 * count], scratch[4 * count :]
        for index, target in enumerate(targets):
            pick = slice(2 * index, 2 * index + 2)
            self.parts.append((sources[1 + index], target, *sems1[pick], *sems2[pick], *buffers[pick]))

    def row(self, place, pair):
        return (place * 2 + pair) * self.size

    def leg1(self, part, k):
        _, _, send1, recv1, _, _, out, came = part
        device = self.line.partner if self.first == "partner" else self.line.across
        return remote(out.at[k], came.at[k], send1.at[k], recv1.at[k], device)

    def leg2(self, part, k):
        _, target, _, _, send2, recv2, out, _ = part
        device = self.line.across if self.first == "partner" else self.line.partner
        return remote(out.at[k, :, pl.ds(0, self.n)], target.at[k], send2.at[k], recv2.at[k], device)

    def produce(self, k):
        line = self.line
        for part in self.parts:
            if self.first == "partner":
                pair = 1 - line.pair if k < LINE else line.pair
                outer_into(part[6].at[k], self.left, self.row(k % LINE, pair), part[0], (1 - line.rep) * self.n)
            else:
                outer_into(part[6].at[k], self.left, self.row(k, 1 - line.pair), part[0], 0)
            self.leg1(part, k).start()

    def join(self, k):
        line, n = self.line, self.n
        for part in self.parts:
            right, _, _, _, _, _, out, came = part
            self.leg1(part, k).wait()
            goal = out.at[k, :, pl.ds(0, n)]
            if self.first == "partner":
                outer_into(goal, self.left, self.row(k, 1 - line.pair), right, line.rep * n, came.at[k])
            else:
                column = pl.multiple_of((1 - line.rep) * n, n)
                outer_into(goal, self.left, self.row(k, line.pair), right, column, came.at[k, :, pl.ds(column, n)])
            self.leg2(part, k).start()

    def last(self, k):
        line, n = self.line, self.n
        for part in self.parts:
            right, target, _, _, _, _, _, came = part
            if self.first == "partner":
                self.leg1(part, LINE + k).wait()
                mine = came.at[LINE + k]
            else:
                mine = came.at[k, :, pl.ds(pl.multiple_of(line.rep * n, n), n)]
            self.leg2(part, k).wait()
            outer_into(target.at[k], self.left, self.row(k, line.pair), right, line.rep * n, mine, target.at[k])

    def slot(self, t):
        if t < self.chunks:
            self.produce(t)
        for k in range(LINE):
            if t == self.join_at[k]:
                self.join(k)
        for k in range(LINE):
            if t == self.last_at[k]:
                self.last(k)

    def finish(self):
        pass


class PairSum:
    near = True

    def __init__(self, left, right, count, at):
        self.inputs, self.count, self.at = [left, right], count, at
        shape = (left.shape[1] // 2, right.shape[1])
        self.outputs = [jax.ShapeDtypeStruct(shape, left.dtype)]
        self.semaphores = ((count,),) * 2
        self.buffers = (shape,)
        self.slots = at + count

    def bind(self, line, sources, targets, scratch):
        self.line, self.target = line, targets[0]
        self.left, self.right = sources
        self.sends, self.recvs, self.out = scratch
        self.size = self.target.shape[0] // self.count

    def copy(self, k):
        rows = pl.ds(k * self.size, self.size)
        return remote(
            self.out.at[rows, :], self.target.at[rows, :], self.sends.at[k], self.recvs.at[k], self.line.across
        )

    def slot(self, t):
        pair, size = self.line.pair, self.size
        for k in range(self.count):
            rows = pl.ds(k * size, size)
            if t == k:
                outer_into(self.out.at[rows, :], self.left, (1 - pair) * self.count * size + k * size, self.right, 0)
                self.copy(k).start()
            if t == self.at + k:
                self.copy(k).wait()
                goal = self.target.at[rows, :]
                outer_into(goal, self.left, pair * self.count * size + k * size, self.right, 0, goal)

    def finish(self):
        pass


def line_scatter_joint(line, k, rows, parts, sib):
    return parts[2 * k + line.core, rows, :].astype(jnp.float32) + sib[k, rows, :].astype(jnp.float32)


def line_scatter_pass(line, j, step, way, parts, sib, sums, came, sib_recv, send_sem, came_sem):
    rows = pl.ds(pl.multiple_of(j * step, step), step)
    device = line.right if way == 0 else line.left
    ends = line.place == 0 if way == 0 else line.place == LINE - 1

    def copy(k):
        return remote(sums.at[k, rows], came.at[k, rows], send_sem.at[k, j], came_sem.at[k, j], device)

    for k in range(LINE - 1, 0, -1) if way == 0 else range(LINE - 1):

        @pl.when(line.place < k if way == 0 else line.place > k)
        def _():
            remote(
                parts.at[2 * k + line.core, rows], sib.at[k, rows], sib_recv.at[k, j], sib_recv.at[k, j], line.sibling
            ).wait_recv()

            @pl.when(ends)
            def _():
                sums[k, rows, :] = line_scatter_joint(line, k, rows, parts, sib).astype(jnp.bfloat16)

            @pl.when(jnp.logical_not(ends))
            def _():
                copy(k).wait_recv()
                sums[k, rows, :] = (
                    line_scatter_joint(line, k, rows, parts, sib) + came[k, rows, :].astype(jnp.float32)
                ).astype(jnp.bfloat16)

            copy(k).start()


def line_scatter_total(line, j, step, parts, sib, rights, lefts, sums, sib_recv, sends, right_recv, left_recv):
    rows = pl.ds(pl.multiple_of(j * step, step), step)
    me = line.place
    remote(
        parts.at[2 * me + line.core, rows], sib.at[me, rows], sib_recv.at[me, j], sib_recv.at[me, j], line.sibling
    ).wait_recv()

    @pl.when(line.has_left)
    def _():
        remote(sums.at[me, rows], rights.at[me, rows], sends.at[me, j], right_recv.at[me, j], line.left).wait_recv()

    @pl.when(line.has_right)
    def _():
        remote(sums.at[me, rows], lefts.at[me, rows], sends.at[me, j], left_recv.at[me, j], line.right).wait_recv()

    total = line_scatter_joint(line, me, rows, parts, sib)
    total = total + jnp.where(line.has_left, rights[me, rows, :].astype(jnp.float32), 0.0)
    return total + jnp.where(line.has_right, lefts[me, rows, :].astype(jnp.float32), 0.0)


def line_scatter_start(line, j, step, parts, sib, sib_send, sib_recv):
    rows = pl.ds(pl.multiple_of(j * step, step), step)
    for k in range(LINE):
        remote(
            parts.at[2 * k + 1 - line.core, rows], sib.at[k, rows], sib_send.at[k, j], sib_recv.at[k, j], line.sibling
        ).start()


def line_scatter_end(line, j, step, parts, sib, rights, lefts, sums, sib_send, right_send, left_send):
    rows = pl.ds(pl.multiple_of(j * step, step), step)
    for k in range(LINE):
        remote(
            parts.at[2 * k + 1 - line.core, rows], sib.at[k, rows], sib_send.at[k, j], sib_send.at[k, j], line.sibling
        ).wait_send()

        @pl.when(line.place < k)
        def _():
            remote(
                sums.at[k, rows], rights.at[k, rows], right_send.at[k, j], right_send.at[k, j], line.right
            ).wait_send()

        @pl.when(line.place > k)
        def _():
            remote(
                sums.at[k, rows], lefts.at[k, rows], left_send.at[k, j], left_send.at[k, j], line.left
            ).wait_send()


def gather_copy(line, k, j, step, core, gathered, way, sends, recvs):
    rows = pl.ds(pl.multiple_of(j * step, step), step)
    block = 2 * k + core
    device = (line.right, line.left, line.sibling)[way]
    ref = gathered.at[block, rows]
    return remote(ref, ref, sends.at[k, way, j], recvs.at[block, j], device)


def line_gather_own(line, j, step, gathered, sends, recvs):
    def copy(way):
        return gather_copy(line, line.place, j, step, line.core, gathered, way, sends, recvs)

    pl.when(line.has_right)(lambda: copy(0).start())
    pl.when(line.has_left)(lambda: copy(1).start())
    copy(2).start()


def line_gather_pass(line, hop, j, step, gathered, sends, recvs):
    for way in (0, 1):
        k = line.place - hop if way == 0 else line.place + hop
        there = k >= 0 if way == 0 else k < LINE
        onward = line.has_right if way == 0 else line.has_left
        k = jnp.clip(k, 0, LINE - 1)

        @pl.when(there)
        def _():
            gather_copy(line, k, j, step, line.core, gathered, way, sends, recvs).wait_recv()
            pl.when(onward)(
                lambda: gather_copy(line, k, j, step, line.core, gathered, way, sends, recvs).start()
            )
            gather_copy(line, k, j, step, line.core, gathered, 2, sends, recvs).start()


def line_gather_end(line, j, step, gathered, sends, recvs):
    for k in range(LINE):
        gather_copy(line, k, j, step, 1 - line.core, gathered, 2, sends, recvs).wait_recv()
        gather_copy(line, k, j, step, line.core, gathered, 2, sends, recvs).wait_send()

        @pl.when((line.place >= k) & line.has_right)
        def _():
            gather_copy(line, k, j, step, line.core, gathered, 0, sends, recvs).wait_send()

        @pl.when((line.place <= k) & line.has_left)
        def _():
            gather_copy(line, k, j, step, line.core, gathered, 1, sends, recvs).wait_send()


def take_from(items, count):
    taken = items[:count]
    del items[:count]
    return taken


def moves_scratch(moves):
    scratch = []
    for move in moves:
        scratch += [pltpu.SemaphoreType.DMA(shape) for shape in move.semaphores]
        scratch += [pltpu.VMEM(shape, jnp.bfloat16) for shape in move.buffers]
    return scratch


def moves_specs(moves, side):
    near, far = pl.BlockSpec(memory_space=pltpu.VMEM), pl.BlockSpec(memory_space=pl.ANY)
    return [
        near if move.near or side == "outputs" else far for move in moves for _ in getattr(move, side)
    ]


def line_call(collective_id, pieces, middle, inputs, outputs, scatter, gather, moves=(), limit=46):
    step = inputs[0].shape[-2] // pieces if inputs else 0
    low = jnp.bfloat16
    scratch = []
    if scatter:
        block = inputs[0].shape[-2:]
        scratch += [pltpu.VMEM((LINE,) + block, low) for _ in range(4)]
        scratch += [pltpu.SemaphoreType.DMA((LINE, pieces)) for _ in range(6)]
    if gather:
        scratch += [pltpu.SemaphoreType.DMA((LINE, 3, pieces)), pltpu.SemaphoreType.DMA((2 * LINE, pieces))]
    n_scratch = len(scratch)
    scratch += moves_scratch(moves)
    moved = [values for move in moves for values in move.inputs]
    extras = [shape for move in moves for shape in move.outputs]

    def kernel(*refs):
        refs = list(refs)

        def take(count):
            taken = refs[:count]
            del refs[:count]
            return taken

        ins = take(len(inputs))
        given = [take(len(move.inputs)) for move in moves]
        outs = take(len(outputs))
        extra = [take(len(move.outputs)) for move in moves]
        rest = take(n_scratch)
        line = Line()
        for move, sources, targets in zip(moves, given, extra):
            move.bind(line, sources, targets, take(len(move.semaphores) + len(move.buffers)))
        line.meet(bool(moves))
        if scatter:
            sib, rights, lefts, sums, sib_send, sib_recv, right_send, left_send, right_recv, left_recv = rest[:10]
            parts = ins[0]
            for j in range(2):
                line_scatter_start(line, j, step, parts, sib, sib_send, sib_recv)
        if gather:
            sends, recvs = rest[-2:]

        hops = (LINE - 1) * (int(scatter) + int(gather))

        def during(j, act):
            pl.when((j >= 0) & (j < pieces))(lambda: act(j))

        def finish(j):
            rows = pl.ds(pl.multiple_of(j * step, step), step)
            total = None
            if scatter:
                total = line_scatter_total(
                    line, j, step, parts, sib, rights, lefts, sums, sib_recv, right_send, right_recv, left_recv
                )
            values = middle(total, rows, j, ins, outs)
            if gather:
                outs[0][line.block, rows, :] = values.astype(low)
                line_gather_own(line, j, step, outs[0], sends, recvs)

        def slot(t, carry):
            if scatter:
                during(t + 2, lambda j: line_scatter_start(line, j, step, parts, sib, sib_send, sib_recv))
                during(
                    t - line.place,
                    lambda j: line_scatter_pass(
                        line, j, step, 0, parts, sib, sums, rights, sib_recv, right_send, right_recv
                    ),
                )
                during(
                    t - (LINE - 1 - line.place),
                    lambda j: line_scatter_pass(
                        line, j, step, 1, parts, sib, sums, lefts, sib_recv, left_send, left_recv
                    ),
                )
                during(t - (LINE - 1), finish)
            if gather:
                for hop in range(1, LINE):
                    during(
                        t - hop - (LINE - 1 if scatter else 0),
                        lambda j, hop=hop: line_gather_pass(line, hop, j, step, outs[0], sends, recvs),
                    )
                during(t - hops - 1, lambda j: line_gather_end(line, j, step, outs[0], sends, recvs))
            if scatter:
                during(
                    t - LINE,
                    lambda j: line_scatter_end(
                        line, j, step, parts, sib, rights, lefts, sums, sib_send, right_send, left_send
                    ),
                )
            return carry

        if gather and not scatter:
            lax.fori_loop(0, pieces, lambda j, carry: (finish(j), carry)[1], 0)
        slots = pieces + hops + 1 if inputs else 0
        apart = max([move.slots for move in moves] + [0])
        if apart <= 1:
            for move in moves:
                move.slot(0)
            if inputs:
                lax.fori_loop(0, slots, slot, 0)
        else:
            for t in range(max(slots, apart)):
                for move in moves:
                    move.slot(t)
                if t < slots:
                    slot(t, 0)
        for move in moves:
            move.finish()

    vmem = pl.BlockSpec(memory_space=pltpu.VMEM)
    return pl.pallas_call(
        kernel,
        out_shape=[jax.ShapeDtypeStruct(shape, kind) for shape, kind in outputs] + extras,
        in_specs=[vmem] * len(inputs) + moves_specs(moves, "inputs"),
        out_specs=[vmem] * len(outputs) + moves_specs(moves, "outputs"),
        scratch_shapes=scratch,
        compiler_params=pltpu.CompilerParams(
            collective_id=collective_id, has_side_effects=True, vmem_limit_bytes=limit << 20
        ),
        cost_estimate=pl.CostEstimate(flops=10_000_000, bytes_accessed=200_000_000, transcendentals=0),
    )(*inputs, *moved)


def gather_blocks(payload, moves, collective_id):
    def middle(total, rows, j, ins, outs):
        return ins[0][rows, :]

    shape = (2 * LINE,) + payload.shape
    return line_call(collective_id, 8, middle, [payload], [(shape, jnp.bfloat16)], False, True, moves, 58)


def attention_block(parts, hidden, gain, moves, collective_id):
    def middle(total, rows, j, ins, outs):
        outs[1][rows, :] = total
        resid = ins[1][rows, :].astype(jnp.float32) + total * rms_scale(total) * ins[2][...]
        outs[2][rows, :] = resid
        return resid

    shape = hidden.shape
    return line_call(
        collective_id, 8, middle, [parts, hidden, gain],
        [(parts.shape, jnp.bfloat16), (shape, jnp.float32), (shape, jnp.float32)], True, True, moves,
    )


def add_rows(ref, values, j):
    folded = jnp.sum(values.reshape(values.shape[0] // 8, 8, values.shape[1]), axis=0)

    @pl.when(j == 0)
    def _():
        ref[...] = folded

    @pl.when(j > 0)
    def _():
        ref[...] += folded


def ffn_block(parts, resid, cotangent, gain, collective_id):
    def middle(total, rows, j, ins, outs):
        scale = rms_scale(total)
        normed = total * scale
        grad = ins[2][rows, :].astype(jnp.float32)
        gains = ins[3][...]
        outs[1][rows, :] = (ins[1][rows, :] + normed * gains).astype(jnp.bfloat16)
        add_rows(outs[2], grad * normed, j)
        return rms_back(grad * gains, normed, scale)

    shape = resid.shape
    return line_call(
        collective_id, 8, middle, [parts, resid, cotangent, gain],
        [(parts.shape, jnp.bfloat16), (shape, jnp.bfloat16), ((8, shape[1]), jnp.float32)], True, True,
    )


def back_block(parts, cotangent, attn_out, gain, moves, collective_id):
    def middle(total, rows, j, ins, outs):
        d_resid = ins[1][rows, :].astype(jnp.float32) + total
        outs[1][rows, :] = d_resid
        attn = ins[2][rows, :]
        scale = rms_scale(attn)
        normed = attn * scale
        add_rows(outs[2], d_resid * normed, j)
        return rms_back(d_resid * ins[3][...], normed, scale)

    shape = cotangent.shape
    return line_call(
        collective_id, 8, middle, [parts, cotangent, attn_out, gain],
        [(parts.shape, jnp.bfloat16), (shape, jnp.float32), ((8, shape[1]), jnp.float32)], True, True, moves, 56,
    )


def last_block(parts, d_resid, moves, collective_id):
    def middle(total, rows, j, ins, outs):
        outs[0][rows, :] = (ins[1][rows, :] + total).astype(jnp.bfloat16)

    return line_call(
        collective_id, 8, middle, [parts, d_resid], [(d_resid.shape, jnp.bfloat16)], True, False, moves, 48
    )


def line_exchange(line, mine, came, sends, recvs):
    def copy(p):
        place, core = line.piece(p, 1)
        return remote(mine, came.at[p], sends.at[p], recvs.at[p], line.at(place, line.pair, core))

    for p in range(1, 2 * LINE):
        copy(p).start()
    total = mine[...]
    for p in range(1, 2 * LINE):
        copy(p).wait_recv()
        total = total + came[p]
    for p in range(1, 2 * LINE):
        copy(p).wait_send()
    return total


def spot(head, index):
    start = (3 * head + index) * HEAD_DIM
    return slice(start, start + HEAD_DIM)


def turn_tables(turns):
    half = turns.shape[1] // 2
    swapped = pltpu.roll(turns, half, 1)
    first = lax.broadcasted_iota(jnp.int32, turns.shape, 1) < half
    return jnp.where(first, turns, swapped), jnp.where(first, -swapped, turns)


def as_row(column):
    return jnp.broadcast_to(column, (column.shape[0], column.shape[0])).T[0:1, :]


def as_columns(row):
    return jnp.broadcast_to(row, (row.shape[1], row.shape[1])).T


def dot(left, right, left_dim, right_dim):
    return lax.dot_general(
        left, right, (((left_dim,), (right_dim,)), ((), ())), preferred_element_type=jnp.float32
    )


def heads_call(collective_id, body, inputs, outputs, scratch, rows, moves):
    blocks, length = 2 * LINE, HEAD_DIM
    scratch = [
        pltpu.VMEM((rows, length), jnp.float32),
        pltpu.VMEM((blocks, rows, length), jnp.float32),
        pltpu.SemaphoreType.DMA((blocks,)),
        pltpu.SemaphoreType.DMA((blocks,)),
    ] + scratch
    n_scratch = len(scratch)
    moved = [values for move in moves for values in move.inputs]
    extras = [shape for move in moves for shape in move.outputs]

    def kernel(*refs):
        refs = list(refs)
        ins = take_from(refs, len(inputs))
        given = [take_from(refs, len(move.inputs)) for move in moves]
        outs = take_from(refs, len(outputs))
        extra = [take_from(refs, len(move.outputs)) for move in moves]
        rest = take_from(refs, n_scratch)
        line = Line()
        for move, sources, targets in zip(moves, given, extra):
            move.bind(line, sources, targets, take_from(refs, len(move.semaphores) + len(move.buffers)))
        line.meet(True)
        passed = [0]

        def tick():
            for move in moves:
                move.slot(passed[0])
            passed[0] += 1

        body(line, ins, outs, rest, tick)
        while passed[0] < max([move.slots for move in moves] + [0]):
            tick()
        for move in moves:
            move.finish()

    vmem = pl.BlockSpec(memory_space=pltpu.VMEM)
    return pl.pallas_call(
        kernel,
        out_shape=[jax.ShapeDtypeStruct(shape, kind) for shape, kind in outputs] + extras,
        in_specs=[vmem] * len(inputs) + moves_specs(moves, "inputs"),
        out_specs=[vmem] * len(outputs) + moves_specs(moves, "outputs"),
        scratch_shapes=scratch + moves_scratch(moves),
        compiler_params=pltpu.CompilerParams(
            collective_id=collective_id, has_side_effects=True, vmem_limit_bytes=44 << 20
        ),
        cost_estimate=pl.CostEstimate(flops=10_000_000, bytes_accessed=80_000_000, transcendentals=0),
    )(*inputs, *moved)


def attend(tokens, full_qkv, turns, bias, gains, weight, moves, collective_id):
    blocks, length = bias.shape[:2]
    width = full_qkv.shape[1] // 3
    heads = width // HEAD_DIM
    model_width = weight.shape[1]
    low = jnp.bfloat16

    def body(line, ins, outs, scratch, tick):
        tokens, full_qkv, turns, bias, gains, weight = ins
        parts, lows, probs, mixed, squares, raw = outs
        mine, came, sends, recvs = scratch

        def squares_of(two, carry):
            both = pl.ds(2 * two, 2)
            product = dot(tokens[both].reshape(2 * length, model_width), full_qkv[...], 1, 0)
            raw[both] = product.reshape(2, length, 3 * width)
            for b, index in ((2 * two, 0), (2 * two, 1), (2 * two + 1, 0), (2 * two + 1, 1)):
                total = jnp.zeros((length, 1), jnp.float32)
                for h in range(heads):
                    values = raw[b, :length, spot(h, index)]
                    total = total + jnp.sum(values * values, axis=1, keepdims=True)
                mine[pl.ds(index * blocks + b, 1), :] = as_row(total)
            return carry

        tick()
        for part in range(LINE):
            squares_of(part, 0)
            tick()
        squares[...] = line_exchange(line, mine, came, sends, recvs)
        tick()

        def block(b, carry):
            scales = [
                lax.rsqrt(as_columns(squares[pl.ds(index * blocks + b, 1), :]) / model_width + epsilon)
                for index in range(2)
            ]
            cos, sin = turn_tables(turns[b])
            for h in range(heads):
                here = slice(h * HEAD_DIM, (h + 1) * HEAD_DIM)
                turned = []
                for index in range(2):
                    there = spot(h, index)
                    normed = raw[b, :length, there] * scales[index] * gains[index : index + 1, here]
                    turned.append((normed * cos + pltpu.roll(normed, HEAD_DIM // 2, 1) * sin).astype(low))
                    lows[b, :, there] = turned[index]
                there = spot(h, 2)
                value = raw[b, :length, there].astype(low)
                lows[b, :, there] = value
                scores = dot(turned[0], turned[1], 1, 1) * HEAD_DIM**-0.5 + bias[b]
                powers = jnp.exp(scores - jnp.max(scores, axis=1, keepdims=True))
                prob = powers / jnp.sum(powers, axis=1, keepdims=True)
                probs[b, h] = prob
                mixed[b, :, here] = dot(prob.astype(low), value, 1, 0).astype(low)
            return carry

        for part in range(LINE):
            lax.fori_loop(2 * part, 2 * part + 2, block, 0)
            both = pl.ds(2 * part, 2)
            product = dot(mixed[both].reshape(2 * length, width), weight[...], 1, 0)
            parts[both] = product.astype(low).reshape(2, length, model_width)
            tick()

    return heads_call(
        collective_id,
        body,
        [tokens, full_qkv, turns, bias, gains, weight],
        [
            ((blocks, length, model_width), low),
            ((blocks, length, 3 * width), low),
            ((blocks, heads, length, length), jnp.float32),
            ((blocks, length, width), low),
            ((2 * blocks, length), jnp.float32),
            ((blocks, length, 3 * width), jnp.float32),
        ],
        [],
        2 * blocks,
        moves,
    )


def attend_back(d_attn, weight, raw, turns, gains, lows, probs, squares, wide_terms, full_qkv, moves, collective_id):
    blocks, length = raw.shape[:2]
    width = raw.shape[2] // 3
    heads = width // HEAD_DIM
    model_width = weight.shape[1]
    low = jnp.bfloat16

    def body(line, ins, outs, scratch, tick):
        d_attn, weight, raw, turns, gains, lows, probs, squares = ins[:8]
        d_low, wide, parts = outs
        full_qkv = ins[10]
        mine, came, sends, recvs, upstream, unit, d_mixed, terms = scratch
        tick()
        terms[...] = jnp.zeros_like(terms)
        for which in range(2):
            total = jnp.sum(ins[8 + which][...], axis=0, keepdims=True)
            for index in range(model_width // length):
                row = 2 * blocks + which * (model_width // length) + index
                mine[row : row + 1, :] = total[:, index * length : (index + 1) * length]

        def block(b, carry):
            scales = [
                lax.rsqrt(as_columns(squares[pl.ds(index * blocks + b, 1), :]) / model_width + epsilon)
                for index in range(2)
            ]
            cos, sin = turn_tables(turns[b])
            means = [jnp.zeros((length, 1), jnp.float32)] * 2
            for h in range(heads):
                here = slice(h * HEAD_DIM, (h + 1) * HEAD_DIM)
                places = [spot(h, index) for index in range(3)]
                query, key, value = [lows[b, :, there] for there in places]
                prob = probs[b, h]
                d_out = d_mixed[b, :, here]
                d_low[b, :length, places[2]] = dot(prob.astype(low), d_out, 0, 0).astype(low)
                d_prob = dot(d_out, value, 1, 1)
                d_scores = (
                    prob * (d_prob - jnp.sum(d_prob * prob, axis=1, keepdims=True))
                ).astype(low)
                turned = [dot(d_scores, key, 1, 0), dot(d_scores, query, 0, 0)]
                for index in range(2):
                    d_rot = turned[index] * HEAD_DIM**-0.5
                    d_normed = d_rot * cos - pltpu.roll(d_rot, HEAD_DIM // 2, 1) * sin
                    units = raw[b, :length, places[index]] * scales[index]
                    ups = d_normed * gains[index : index + 1, here]
                    folded = (d_normed * units).reshape(length // 8, 8, HEAD_DIM)
                    side = slice((index * heads + h) * HEAD_DIM, (index * heads + h + 1) * HEAD_DIM)
                    terms[:, side] += jnp.sum(folded, axis=0)
                    upstream[b, :, side] = ups
                    unit[b, :, side] = units
                    means[index] = means[index] + jnp.sum(ups * units, axis=1, keepdims=True)
            for index in range(2):
                mine[pl.ds(index * blocks + b, 1), :] = as_row(means[index])
            return carry

        def mix(two, carry):
            both = pl.ds(2 * two, 2)
            product = dot(d_attn[both].reshape(2 * length, model_width), weight[...], 1, 1)
            d_mixed[both] = product.astype(low).reshape(2, length, width)
            return carry

        lax.fori_loop(0, LINE, mix, 0)
        lax.fori_loop(0, blocks, block, 0)
        mine[...] = line_exchange(line, mine, came, sends, recvs)
        count = 2 * model_width // length
        wide[:count, :] = mine[2 * blocks :, :]
        wide[count:, :] = jnp.zeros((8, length), jnp.float32)
        for index in range(2 * heads):
            sums = jnp.sum(terms[:, index * length : (index + 1) * length], axis=0, keepdims=True)
            wide[count + index : count + index + 1, :] = sums

        def last(b, carry):
            for index in range(2):
                scale = lax.rsqrt(
                    as_columns(squares[pl.ds(index * blocks + b, 1), :]) / model_width + epsilon
                )
                mean = as_columns(mine[pl.ds(index * blocks + b, 1), :]) / model_width
                for h in range(heads):
                    side = slice((index * heads + h) * HEAD_DIM, (index * heads + h + 1) * HEAD_DIM)
                    d_low[b, :length, spot(h, index)] = (
                        scale * (upstream[b, :, side] - unit[b, :, side] * mean)
                    ).astype(low)
            return carry

        def lasts(two, carry):
            lax.fori_loop(2 * two, 2 * two + 2, last, 0)
            both = pl.ds(2 * two, 2)
            product = dot(d_low[both].reshape(2 * length, 3 * width), full_qkv[...], 1, 1)
            parts[both] = product.astype(low).reshape(2, length, model_width)
            return carry

        lax.fori_loop(0, LINE, lasts, 0)

    return heads_call(
        collective_id,
        body,
        [d_attn, weight, raw, turns, gains, lows, probs, squares, *wide_terms, full_qkv],
        [
            (raw.shape, low),
            ((2 * model_width // length + 8, length), jnp.float32),
            ((blocks, length, model_width), low),
        ],
        [pltpu.VMEM((blocks, length, 2 * width), jnp.float32) for _ in range(2)]
        + [pltpu.VMEM((blocks, length, width), low), pltpu.VMEM((8, 2 * width), jnp.float32)],
        2 * blocks + 2 * model_width // length,
        moves,
    )


def on_device(
    hidden_in,
    segments,
    w_query,
    w_key,
    w_value,
    w_output,
    query_gain,
    key_gain,
    attn_gain,
    w_gate,
    w_up,
    w_down,
    ffn_gain,
    out_cotangent,
):
    length, model_width = hidden_in.shape
    blocks = 2 * LINE
    heads = HEADS // blocks
    factor = HEAD_DIM ** (-0.5)
    pair = (lax.axis_index("shard") // 2) % 2
    f32 = jnp.float32

    extra = jnp.stack([query_gain, key_gain, attn_gain, ffn_gain, segments[0].astype(jnp.bfloat16)])
    payload, extras, full_qkv, full_output = gather_blocks(
        hidden_in,
        [
            Share(jnp.pad(extra, ((0, 11), (0, 0)))),
            Spread(w_query, w_key, w_value),
            Stack(w_output, 2),
        ],
        0,
    )
    tokens = payload.reshape(-1, model_width)
    docs = extras[:, 4].astype(jnp.int32)
    gains = extras[:, :4].reshape(LINE, 2, 4, length)
    gains = jnp.stack(by_pair(pair, gains, pair_swap(gains)), axis=1)
    gains = jnp.moveaxis(gains, 3, 0).reshape(4, 1, model_width).astype(f32)
    gain_attn, gain_ffn = gains[2], gains[3]
    width = heads * HEAD_DIM
    head_gains = gather_rows(jnp.stack([query_gain, key_gain])[None], pair).astype(f32)
    head_gains = head_gains.transpose(1, 0, 2).reshape(2, width)

    earlier = jnp.sum((docs[:, None, :] < docs[:, :, None]).astype(jnp.int32), axis=2)
    positions = jnp.arange(length, dtype=jnp.int32)[None] - earlier
    half_dim = HEAD_DIM // 2
    inverse = jnp.exp(
        jnp.arange(half_dim, dtype=f32) * (-2.0 * math.log(theta_base) / HEAD_DIM)
    )
    angles = positions.astype(f32)[:, :, None] * inverse[None, None, :]
    turns = jnp.cos(jnp.concatenate([angles, angles - 0.5 * math.pi], axis=-1))
    token_idx = jnp.arange(length)
    allowed = (docs[:, :, None] == docs[:, None, :]) & (
        token_idx[:, None] >= token_idx[None, :]
    )[None]
    bias = jnp.where(allowed, 0.0, neg_fill)

    def to_blocks(values):
        return values.astype(jnp.bfloat16).reshape(blocks, -1, model_width)

    attn_parts, lows, probs, mixed_low, squares, raw, full_gate = attend(
        payload, full_qkv, turns, bias, head_gains, full_output, [Spread(w_gate, plan=Spread.BESIDE_HEADS)], 6
    )
    mixed_low = mixed_low.reshape(blocks * length, width)
    resid_low, attn_out, resid, full_up, full_down = attention_block(
        attn_parts,
        hidden_in,
        gain_attn,
        [Spread(w_up), Stack(w_down, 8)],
        1,
    )
    resid_low = resid_low.reshape(blocks * length, model_width)

    gate_proj = jnp.dot(resid_low, full_gate, preferred_element_type=f32)
    up_proj = jnp.dot(resid_low, full_up, preferred_element_type=f32)
    gate_sig = jax.nn.sigmoid(gate_proj)
    hidden_ffn = (gate_proj * gate_sig * up_proj).astype(jnp.bfloat16)
    d_ffn_low, hidden_out, ffn_gain_term = ffn_block(
        to_blocks(jnp.dot(hidden_ffn, full_down, preferred_element_type=f32)),
        resid,
        out_cotangent,
        gain_ffn,
        2,
    )
    d_ffn_low = d_ffn_low.reshape(blocks * length, model_width)

    d_hidden_ffn = dot_back(d_ffn_low, full_down)
    d_gate_low = (d_hidden_ffn * up_proj * gate_sig * (1.0 + gate_proj * (1.0 - gate_sig))).astype(
        jnp.bfloat16
    )
    d_up_low = (d_hidden_ffn * gate_proj * gate_sig).astype(jnp.bfloat16)
    ff_rows = w_down.shape[0]
    d_attn_low, d_resid, attn_gain_term, gate_sum, up_sum, down_part = back_block(
        to_blocks(dot_back(d_gate_low, full_gate) + dot_back(d_up_low, full_up)),
        out_cotangent,
        attn_out,
        gain_attn,
        [
            Reduce(resid_low, [d_gate_low, d_up_low], "partner"),
            PairSum(hidden_ffn, d_ffn_low, 4, 13),
        ],
        3,
    )

    d_qkv, gain_sums, back_parts, there_first = attend_back(
        d_attn_low, full_output, raw, turns, head_gains, lows, probs, squares,
        [attn_gain_term, ffn_gain_term], full_qkv, [Swap(down_part, 0, ff_rows // 2)], 7,
    )
    d_attn_low = d_attn_low.reshape(blocks * length, model_width)
    qkv_sum = Reduce(tokens, [d_qkv.reshape(-1, 3 * width)], "across")
    output_sum = PairSum(mixed_low, d_attn_low, 1, 5)
    hidden_grad, _, output_part, ffn_total, there_second, qkv_total, there_output, *there_gains = last_block(
        back_parts,
        d_resid,
        [
            qkv_sum,
            output_sum,
            Deal([gate_sum, up_sum], 1),
            Swap(down_part, ff_rows // 2, ff_rows // 2, 2),
            Deal(qkv_sum, 3, 9),
            Swap(output_sum, 0, length, 8),
            Four(gain_sums),
        ],
        4,
    )

    def total_of(first, second):
        return first.astype(f32) + second.astype(f32)

    grad_query, grad_key, grad_value = jnp.split(qkv_total.astype(f32), 3, axis=1)
    grad_gate, grad_up = jnp.split(ffn_total.astype(f32), 2, axis=1)
    grad_output = total_of(output_part, there_output)
    grad_down = total_of(down_part, jnp.concatenate([there_first, there_second]))
    gain_sums = (gain_sums + there_gains[0]) + (there_gains[1] + there_gains[2])
    wide_grads = lax.dynamic_index_in_dim(
        gain_sums[:32].reshape(2, 16, length), lax.axis_index("shard"), 1, keepdims=False
    )
    head_grads = lax.dynamic_index_in_dim(gain_sums[32:36].reshape(2, 2, length), pair, 1, keepdims=False)
    gain_grads = jnp.concatenate([head_grads, wide_grads])
    return (
        hidden_out,
        hidden_grad,
        grad_query,
        grad_key,
        grad_value,
        grad_output,
        gain_grads[0],
        gain_grads[1],
        gain_grads[2],
        grad_gate,
        grad_up,
        grad_down,
        gain_grads[3],
    )


def solution(mesh):
    placed = (
        P(("rep", "shard"), None),
        P(("rep", "shard"), None),
        P("shard", None),
        P("shard", None),
        P("shard", None),
        P("shard", None),
        P("shard"),
        P("shard"),
        P("shard"),
        P("shard", None),
        P("shard", None),
        P("shard", None),
        P("shard"),
        P(("rep", "shard"), None),
    )
    return jax.shard_map(
        on_device if mesh.shape["shard"] == 16 else on_device_general,
        mesh=mesh,
        in_specs=placed,
        out_specs=(
            P(("rep", "shard"), None),
            P(("rep", "shard"), None),
            P("shard", None),
            P("shard", None),
            P("shard", None),
            P("shard", None),
            P("shard"),
            P("shard"),
            P("shard"),
            P("shard", None),
            P("shard", None),
            P("shard", None),
            P("shard"),
        ),
        check_vma=False,
    )
```

```python
import math

import jax
import jax.numpy as jnp
from jax import lax
from jax.experimental import pallas as pl
from jax.experimental.pallas import tpu as pltpu
from jax.sharding import PartitionSpec as P

HEADS = 16
HEAD_DIM = 128


epsilon = 1e-06
theta_base = 500000.0
neg_fill = -1e30


def rms_scale(values):
    return lax.rsqrt(jnp.mean(values * values, axis=-1, keepdims=True) + epsilon)


def rms_back(upstream, normed, row_scale):
    return row_scale * (upstream - normed * jnp.mean(upstream * normed, axis=-1, keepdims=True))


def rotate(values, cosines, sines):
    half_dim = values.shape[-1] // 2
    first_half = values[..., :half_dim]
    second = values[..., half_dim:]
    return jnp.concatenate(
        [first_half * cosines - second * sines, second * cosines + first_half * sines], axis=-1
    )


def dot_back(left_side, right_side):
    return lax.dot_general(
        left_side, right_side, (((1,), (1,)), ((), ())), preferred_element_type=jnp.float32
    )


def col_term(left_side, right_side):

    def block_term(row_start, row_count):
        return lax.dot_general(
            left_side, right_side, (((0,), (0,)), ((), ())), preferred_element_type=jnp.float32
        )

    return block_term


def on_device_general(
    hidden_in,
    segments,
    w_query,
    w_key,
    w_value,
    w_output,
    query_gain,
    key_gain,
    attn_gain,
    w_gate,
    w_up,
    w_down,
    ffn_gain,
    out_cotangent,
):
    length = hidden_in.shape[0]
    model_width = hidden_in.shape[1]
    ffn_width = w_gate.shape[1]
    factor = HEAD_DIM ** (-0.5)
    doc_row = segments[0]
    earlier = jnp.sum((doc_row[None, :] < doc_row[:, None]).astype(jnp.int32), axis=1)
    positions = jnp.arange(length, dtype=jnp.int32) - earlier
    half_dim = HEAD_DIM // 2
    inverse = jnp.exp(
        jnp.arange(half_dim, dtype=jnp.float32) * (-2.0 * math.log(theta_base) / HEAD_DIM)
    )
    angles = positions.astype(jnp.float32)[:, None] * inverse[None, :]
    cosines = jnp.cos(angles)[:, None, :]
    sines = jnp.sin(angles)[:, None, :]
    token_idx = jnp.arange(length)
    allowed = (doc_row[:, None] == doc_row[None, :]) & (token_idx[:, None] >= token_idx[None, :])

    def reduce_rows(term_fn, local_rows):
        return lax.psum_scatter(
            term_fn(jnp.int32(0), local_rows * lax.axis_size("shard")),
            "shard",
            scatter_dimension=0,
            tiled=True,
        )

    def norm_rope(raw_proj, gain_vec):
        normed = raw_proj * rms_scale(raw_proj) * gain_vec
        return rotate(normed.reshape(length, HEADS, HEAD_DIM), cosines, sines)

    def attend_scores(query_low, key_low):
        scores = (
            jnp.einsum("qhd,khd->hqk", query_low, key_low, preferred_element_type=jnp.float32)
            * factor
        )
        return jnp.where(allowed[None], scores, neg_fill)

    full_query, full_key, full_value, gain_query, gain_key = (
        lax.all_gather(w_query, "shard", axis=0, tiled=True),
        lax.all_gather(w_key, "shard", axis=0, tiled=True),
        lax.all_gather(w_value, "shard", axis=0, tiled=True),
        lax.all_gather(query_gain, "shard", axis=0, tiled=True),
        lax.all_gather(key_gain, "shard", axis=0, tiled=True),
    )
    query_raw = jnp.dot(hidden_in, full_query, preferred_element_type=jnp.float32)
    key_raw = jnp.dot(hidden_in, full_key, preferred_element_type=jnp.float32)
    query_low = norm_rope(query_raw, gain_query.astype(jnp.float32)).astype(jnp.bfloat16)
    key_low = norm_rope(key_raw, gain_key.astype(jnp.float32)).astype(jnp.bfloat16)
    value_low = (
        jnp.dot(hidden_in, full_value, preferred_element_type=jnp.float32)
        .astype(jnp.bfloat16)
        .reshape(length, HEADS, HEAD_DIM)
    )
    scores = attend_scores(query_low, key_low)
    row_peak = jnp.max(scores, axis=-1, keepdims=True)
    log_norm = row_peak + jnp.log(jnp.sum(jnp.exp(scores - row_peak), axis=-1, keepdims=True))
    attn_prob = jnp.exp(scores - log_norm)
    mixed_low = (
        jnp.einsum(
            "hqk,khd->qhd",
            attn_prob.astype(jnp.bfloat16),
            value_low,
            preferred_element_type=jnp.float32,
        )
        .reshape(length, model_width)
        .astype(jnp.bfloat16)
    )
    full_output, gain_attn = (
        lax.all_gather(w_output, "shard", axis=0, tiled=True),
        lax.all_gather(attn_gain, "shard", axis=0, tiled=True),
    )
    attn_out = jnp.dot(mixed_low, full_output, preferred_element_type=jnp.float32)
    attn_rms = rms_scale(attn_out)
    attn_normed = attn_out * attn_rms
    resid = hidden_in.astype(jnp.float32) + attn_normed * gain_attn.astype(jnp.float32)
    resid_low = resid.astype(jnp.bfloat16)
    full_gate, full_up = (
        lax.all_gather(w_gate, "shard", axis=0, tiled=True),
        lax.all_gather(w_up, "shard", axis=0, tiled=True),
    )
    gate_proj = jnp.dot(resid_low, full_gate, preferred_element_type=jnp.float32)
    up_proj = jnp.dot(resid_low, full_up, preferred_element_type=jnp.float32)
    gate_sig = jax.nn.sigmoid(gate_proj)
    hidden_ffn = (gate_proj * gate_sig * up_proj).astype(jnp.bfloat16)
    full_down, gain_ffn = (
        lax.all_gather(w_down, "shard", axis=0, tiled=True),
        lax.all_gather(ffn_gain, "shard", axis=0, tiled=True),
    )
    ffn_out = jnp.dot(hidden_ffn, full_down, preferred_element_type=jnp.float32)
    ffn_rms = rms_scale(ffn_out)
    ffn_normed = ffn_out * ffn_rms
    hidden_out = (resid + ffn_normed * gain_ffn.astype(jnp.float32)).astype(jnp.bfloat16)
    grad_out = out_cotangent.astype(jnp.float32)
    back_down, back_fgain = (
        lax.all_gather(w_down, "shard", axis=0, tiled=True),
        lax.all_gather(ffn_gain, "shard", axis=0, tiled=True),
    )
    ffn_gain_term = jnp.sum(grad_out * ffn_normed, axis=0)
    d_ffn_low = rms_back(grad_out * back_fgain.astype(jnp.float32), ffn_normed, ffn_rms).astype(
        jnp.bfloat16
    )
    down_grad = reduce_rows(col_term(hidden_ffn, d_ffn_low), w_down.shape[0])
    d_hidden_ffn = dot_back(d_ffn_low, back_down)
    d_gate_low = (d_hidden_ffn * up_proj * gate_sig * (1.0 + gate_proj * (1.0 - gate_sig))).astype(
        jnp.bfloat16
    )
    d_up_low = (d_hidden_ffn * gate_proj * gate_sig).astype(jnp.bfloat16)
    ffn_in_grad = reduce_rows(
        col_term(resid_low, jnp.concatenate([d_gate_low, d_up_low], axis=1)), w_gate.shape[0]
    )
    back_gate, back_up = (
        lax.all_gather(w_gate, "shard", axis=0, tiled=True),
        lax.all_gather(w_up, "shard", axis=0, tiled=True),
    )
    d_resid = grad_out + dot_back(d_gate_low, back_gate) + dot_back(d_up_low, back_up)
    back_output, back_again = (
        lax.all_gather(w_output, "shard", axis=0, tiled=True),
        lax.all_gather(attn_gain, "shard", axis=0, tiled=True),
    )
    attn_gain_term = jnp.sum(d_resid * attn_normed, axis=0)
    d_attn_low = rms_back(d_resid * back_again.astype(jnp.float32), attn_normed, attn_rms).astype(
        jnp.bfloat16
    )
    out_grad = reduce_rows(col_term(mixed_low, d_attn_low), w_output.shape[0])
    d_mixed_low = (
        dot_back(d_attn_low, back_output).astype(jnp.bfloat16).reshape(length, HEADS, HEAD_DIM)
    )
    scores_again = attend_scores(query_low, key_low)
    prob_again = jnp.exp(scores_again - log_norm)
    d_value = jnp.einsum(
        "hqk,qhd->khd",
        prob_again.astype(jnp.bfloat16),
        d_mixed_low,
        preferred_element_type=jnp.float32,
    )
    d_prob = jnp.einsum("qhd,khd->hqk", d_mixed_low, value_low, preferred_element_type=jnp.float32)
    d_scores_low = (
        prob_again * (d_prob - jnp.sum(d_prob * prob_again, axis=-1, keepdims=True))
    ).astype(jnp.bfloat16)
    d_query_rot = (
        jnp.einsum("hqk,khd->qhd", d_scores_low, key_low, preferred_element_type=jnp.float32)
        * factor
    )
    d_key_rot = (
        jnp.einsum("hqk,qhd->khd", d_scores_low, query_low, preferred_element_type=jnp.float32)
        * factor
    )
    back_query, back_key, back_value, back_qgain, back_kgain = (
        lax.all_gather(w_query, "shard", axis=0, tiled=True),
        lax.all_gather(w_key, "shard", axis=0, tiled=True),
        lax.all_gather(w_value, "shard", axis=0, tiled=True),
        lax.all_gather(query_gain, "shard", axis=0, tiled=True),
        lax.all_gather(key_gain, "shard", axis=0, tiled=True),
    )
    unused_query, query_pull = jax.vjp(norm_rope, query_raw, back_qgain.astype(jnp.float32))
    d_query_raw, query_gain_term = query_pull(d_query_rot)
    unused_key, key_pull = jax.vjp(norm_rope, key_raw, back_kgain.astype(jnp.float32))
    d_key_raw, key_gain_term = key_pull(d_key_rot)
    d_query_low = d_query_raw.astype(jnp.bfloat16)
    d_key_low = d_key_raw.astype(jnp.bfloat16)
    d_value_low = d_value.reshape(length, model_width).astype(jnp.bfloat16)
    qkv_grad = reduce_rows(
        col_term(hidden_in, jnp.concatenate([d_query_low, d_key_low, d_value_low], axis=1)),
        w_query.shape[0],
    )
    hidden_grad = (
        d_resid
        + dot_back(d_query_low, back_query)
        + dot_back(d_key_low, back_key)
        + dot_back(d_value_low, back_value)
    ).astype(jnp.bfloat16)
    gain_sums = (
        lax.psum_scatter(query_gain_term, "shard", scatter_dimension=0, tiled=True),
        lax.psum_scatter(key_gain_term, "shard", scatter_dimension=0, tiled=True),
        lax.psum_scatter(attn_gain_term, "shard", scatter_dimension=0, tiled=True),
        lax.psum_scatter(ffn_gain_term, "shard", scatter_dimension=0, tiled=True),
    )
    totals = (
        lax.psum(qkv_grad[:, :model_width].astype(jnp.bfloat16), "rep").astype(jnp.float32),
        lax.psum(qkv_grad[:, model_width : 2 * model_width].astype(jnp.bfloat16), "rep").astype(
            jnp.float32
        ),
        lax.psum(qkv_grad[:, 2 * model_width :].astype(jnp.bfloat16), "rep").astype(jnp.float32),
        lax.psum(out_grad.astype(jnp.bfloat16), "rep").astype(jnp.float32),
        lax.psum(gain_sums[0].astype(jnp.bfloat16), "rep").astype(jnp.float32),
        lax.psum(gain_sums[1].astype(jnp.bfloat16), "rep").astype(jnp.float32),
        lax.psum(gain_sums[2].astype(jnp.bfloat16), "rep").astype(jnp.float32),
        lax.psum(ffn_in_grad[:, :ffn_width].astype(jnp.bfloat16), "rep").astype(jnp.float32),
        lax.psum(ffn_in_grad[:, ffn_width:].astype(jnp.bfloat16), "rep").astype(jnp.float32),
        lax.psum(down_grad.astype(jnp.bfloat16), "rep").astype(jnp.float32),
        lax.psum(gain_sums[3].astype(jnp.bfloat16), "rep").astype(jnp.float32),
    )
    return (
        hidden_out,
        hidden_grad,
        totals[0],
        totals[1],
        totals[2],
        totals[3],
        totals[4],
        totals[5],
        totals[6],
        totals[7],
        totals[8],
        totals[9],
        totals[10],
    )


LINE = 4


def shard_perm(move):
    return [(index, move(index)) for index in range(16)]


def pair_swap(values):
    return lax.ppermute(values, "shard", shard_perm(lambda index: index ^ 2))


def by_pair(pair, own, other):
    return jnp.where(pair == 0, own, other), jnp.where(pair == 0, other, own)


def gather_rows(weight, pair):
    return jnp.concatenate(by_pair(pair, weight, pair_swap(weight)), axis=0)


MESH_ID = pl.DeviceIdType.MESH


class Line:
    def __init__(self):
        index = lax.axis_index("shard")
        self.rep = lax.axis_index("rep")
        self.place = index // 4
        self.pair = (index // 2) % 2
        self.core = index % 2
        self.block = self.place * 2 + self.core
        self.sibling = self.at(self.place, self.pair, 1 - self.core)
        self.right = self.at(jnp.minimum(self.place + 1, LINE - 1), self.pair, self.core)
        self.left = self.at(jnp.maximum(self.place - 1, 0), self.pair, self.core)
        self.across = self.at(self.place, 1 - self.pair, self.core)
        self.partner = (1 - self.rep, index)
        self.diagonal = (1 - self.rep, self.across[1])
        self.has_right = self.place < LINE - 1
        self.has_left = self.place > 0

    def at(self, place, pair, core):
        return (self.rep, place * 4 + pair * 2 + core)

    def piece(self, p, sign):
        return (self.place + sign * (p // 2) + LINE) % LINE, (self.core + p % 2) % 2

    def meet(self, wide):
        barrier = pltpu.get_barrier_semaphore()

        def greet(device):
            pl.semaphore_signal(barrier, inc=1, device_id=device, device_id_type=MESH_ID)

        if wide:
            for p in range(1, 2 * LINE):
                place, core = self.piece(p, 1)
                greet(self.at(place, self.pair, core))
            greet(self.across)
            greet(self.partner)
            greet(self.diagonal)
            pl.semaphore_wait(barrier, 2 * LINE + 2)
            return
        greet(self.sibling)
        pl.when(self.has_right)(lambda: greet(self.right))
        pl.when(self.has_left)(lambda: greet(self.left))
        pl.semaphore_wait(
            barrier, 1 + self.has_right.astype(jnp.int32) + self.has_left.astype(jnp.int32)
        )


def remote(source, target, send_sem, recv_sem, device):
    return pltpu.make_async_remote_copy(
        src_ref=source,
        dst_ref=target,
        send_sem=send_sem,
        recv_sem=recv_sem,
        device_id=device,
        device_id_type=MESH_ID,
    )


class Spread:
    semaphores = ((2 * LINE,),) * 2 + ((2 * LINE, 2),) * 4
    buffers = ()
    near = False

    BESIDE_LINE = ((0, 0, 1, 1, 1, 2, 2, 2), (0, 2, 3, 4, 5, 6, 7, 8), (3, 4, 5, 6, 7, 8, 9, 10))
    BESIDE_HEADS = ((0, 0, 0, 0, 4, 4, 0, 0), (0, 1, 4, 4, 8, 8, 4, 4), (1, 2, 5, 5, 9, 9, 5, 5))

    def __init__(self, *weights, plan=BESIDE_LINE):
        self.inputs, self.plan = list(weights), plan
        shape = (16 * weights[0].shape[0], sum(weight.shape[1] for weight in weights) // 8)
        self.outputs = [jax.ShapeDtypeStruct(shape, jnp.bfloat16)]
        self.slots = max(plan[2]) + 1

    def bind(self, line, sources, targets, sems):
        self.line, self.sources, self.target = line, sources, targets[0]
        self.z_send, self.z_recv, self.y_send, self.y_recv, self.x_send, self.x_recv = sems
        self.half = sources[0].shape[0] // 2

    def slot(self, t):
        for when, act in zip(self.plan, (self.start, self.came, self.onward)):
            for p in range(2 * LINE):
                if t == when[p]:
                    act(p)

    def rows(self, place, pair, core, rep):
        start = ((place * 4 + pair * 2 + core) * 2 + rep) * self.half
        return self.target.at[pl.ds(pl.multiple_of(start, self.half), self.half), :]

    def start(self, p):
        line, half = self.line, self.half
        place, core = line.piece(p, 1)
        here = self.rows(line.place, line.pair, line.core, line.rep)
        mine = pl.ds(pl.multiple_of(line.rep * half, half), half)
        at = 0
        for q in range(2):
            for source in self.sources:
                n = source.shape[1] // 16
                column = pl.multiple_of((place * 4 + q * 2 + core) * n, n)
                piece, goal = source.at[mine, pl.ds(column, n)], here.at[:, pl.ds(at, n)]
                if p == 0:
                    pltpu.make_async_copy(piece, goal, self.z_recv.at[0]).start()
                else:
                    remote(
                        piece, goal, self.z_send.at[p], self.z_recv.at[p], line.at(place, line.pair, core)
                    ).start()
                at += n

    def cross(self, p, pair, rep, which):
        place, core = self.line.piece(p, -1)
        ref = self.rows(place, pair, core, rep)
        return remote(ref, ref, self.y_send.at[p, which], self.y_recv.at[p, which], self.line.across)

    def over(self, p, pair, rep, which):
        place, core = self.line.piece(p, -1)
        ref = self.rows(place, pair, core, rep)
        return remote(ref, ref, self.x_send.at[p, which], self.x_recv.at[p, which], self.line.partner)

    def came(self, p):
        line = self.line
        place, core = line.piece(p, -1)
        ref = self.rows(place, line.pair, core, line.rep)
        if p == 0:
            pltpu.make_async_copy(ref, ref, self.z_recv.at[0]).wait()
        else:
            remote(ref, ref, self.z_send.at[p], self.z_recv.at[p], line.sibling).wait_recv()
        self.cross(p, line.pair, line.rep, 0).start()
        self.over(p, line.pair, line.rep, 0).start()

    def onward(self, p):
        line = self.line
        if p % 2:
            self.over(p, line.pair, 1 - line.rep, 0).wait_recv()
            self.cross(p, line.pair, 1 - line.rep, 1).start()
        else:
            self.cross(p, 1 - line.pair, line.rep, 0).wait_recv()
            self.over(p, 1 - line.pair, line.rep, 1).start()

    def finish(self):
        line = self.line
        for p in range(1, 2 * LINE):
            ref = self.rows(line.place, line.pair, line.core, line.rep)
            remote(ref, ref, self.z_send.at[p], self.z_recv.at[p], line.sibling).wait_send()
        self.finish_over()

    def finish_over(self):
        line = self.line
        pair, rep = line.pair, line.rep
        for p in range(2 * LINE):
            self.cross(p, pair, rep, 0).wait_send()
            self.over(p, pair, rep, 0).wait_send()
            if p % 2:
                self.cross(p, 1 - pair, rep, 0).wait_recv()
                self.cross(p, pair, 1 - rep, 1).wait_send()
                self.cross(p, 1 - pair, 1 - rep, 1).wait_recv()
            else:
                self.over(p, pair, 1 - rep, 0).wait_recv()
                self.over(p, 1 - pair, rep, 1).wait_send()
                self.over(p, 1 - pair, 1 - rep, 1).wait_recv()


class SpreadLine:
    semaphores = ((2 * LINE,),) * 2
    buffers = ()
    near = False

    def __init__(self, weight, at):
        self.inputs, self.at, self.slots = [weight], at, at + 1
        shape = (2 * LINE, weight.shape[0] // 2, weight.shape[1] // 8)
        self.outputs = [jax.ShapeDtypeStruct(shape, weight.dtype)]

    def bind(self, line, sources, targets, scratch):
        self.line, self.source, self.target = line, sources[0], targets[0]
        self.sends, self.recvs = scratch

    def slot(self, t):
        if t != self.at:
            return
        line, half, n = self.line, self.target.shape[1], self.target.shape[2] // 2
        mine = pl.ds(pl.multiple_of(line.rep * half, half), half)
        for p in range(2 * LINE):
            place, core = line.piece(p, 1)
            for q in range(2):
                column = pl.multiple_of((place * 4 + q * 2 + core) * n, n)
                piece, goal = self.source.at[mine, pl.ds(column, n)], self.target.at[p, :, pl.ds(q * n, n)]
                if p == 0:
                    pltpu.make_async_copy(piece, goal, self.recvs.at[0]).start()
                else:
                    device = line.at(place, line.pair, core)
                    remote(piece, goal, self.sends.at[p], self.recvs.at[p], device).start()

    def finish(self):
        for p in range(2 * LINE):
            ref = self.target.at[p]
            if p == 0:
                pltpu.make_async_copy(ref, ref, self.recvs.at[0]).wait()
            else:
                remote(ref, ref, self.sends.at[p], self.recvs.at[p], self.line.sibling).wait()


class SpreadOver(Spread):
    semaphores = ((2 * LINE,),) + ((2 * LINE, 2),) * 4

    def __init__(self, pieces):
        self.inputs, self.half = [pieces], pieces.shape[1]
        shape = (2 * pieces.shape[0] * 2 * pieces.shape[1], pieces.shape[2])
        self.outputs = [jax.ShapeDtypeStruct(shape, pieces.dtype)]
        self.slots = 7 + LINE

    def bind(self, line, sources, targets, scratch):
        self.line, self.pieces, self.target = line, sources[0], targets[0]
        self.local, self.y_send, self.y_recv, self.x_send, self.x_recv = scratch

    def here(self, p):
        place, core = self.line.piece(p, -1)
        goal = self.rows(place, self.line.pair, core, self.line.rep)
        return pltpu.make_async_copy(self.pieces.at[p], goal, self.local.at[p])

    def cross(self, p, pair, rep, which):
        place, core = self.line.piece(p, -1)
        ref = self.rows(place, pair, core, rep)
        source = ref if which else self.pieces.at[p]
        return remote(source, ref, self.y_send.at[p, which], self.y_recv.at[p, which], self.line.across)

    def over(self, p, pair, rep, which):
        place, core = self.line.piece(p, -1)
        ref = self.rows(place, pair, core, rep)
        source = ref if which else self.pieces.at[p]
        return remote(source, ref, self.x_send.at[p, which], self.x_recv.at[p, which], self.line.partner)

    def slot(self, t):
        line = self.line
        for p in range(2 * LINE):
            if t == p // 2:
                self.cross(p, line.pair, line.rep, 0).start()
                self.over(p, line.pair, line.rep, 0).start()
                self.here(p).start()
            if t == 7 + p // 2:
                self.onward(p)

    def finish(self):
        for p in range(2 * LINE):
            self.here(p).wait()
        self.finish_over()


class Stack:
    buffers = ()
    near = False

    def __init__(self, weight, count, lag):
        self.inputs, self.count, self.lag = [weight], count, lag
        self.outputs = [jax.ShapeDtypeStruct((2 * weight.shape[0], weight.shape[1]), weight.dtype)]
        self.semaphores = ((1,),) + ((count,),) * 4
        self.slots = lag + count

    def bind(self, line, sources, targets, sems):
        self.line, self.source, self.target = line, sources[0], targets[0]
        self.local, self.y_send, self.y_recv, self.x_send, self.x_recv = sems
        self.size = self.source.shape[0]

    def here(self):
        size = self.size
        mine = self.target.at[pl.ds(pl.multiple_of(self.line.pair * size, size), size), :]
        return pltpu.make_async_copy(self.source, mine, self.local.at[0])

    def there(self, p):
        line, part = self.line, self.size // (2 * self.count)
        start = pl.multiple_of((line.rep * self.count + p) * part, part)
        goal = self.target.at[pl.ds(pl.multiple_of(line.pair * self.size + start, part), part), :]
        return remote(
            self.source.at[pl.ds(start, part), :], goal, self.y_send.at[p], self.y_recv.at[p], line.across
        )

    def onward(self, p, rep):
        line, part = self.line, self.size // (2 * self.count)
        start = (1 - line.pair) * self.size + (rep * self.count + p) * part
        ref = self.target.at[pl.ds(pl.multiple_of(start, part), part), :]
        return remote(ref, ref, self.x_send.at[p], self.x_recv.at[p], line.partner)

    def slot(self, t):
        if t == 0:
            for k in range(self.count):
                self.there(k).start()
            self.here().start()
        if self.lag <= t < self.lag + self.count:
            self.there(t - self.lag).wait_recv()
            self.onward(t - self.lag, self.line.rep).start()

    def finish(self):
        self.here().wait()
        for p in range(self.count):
            self.there(p).wait_send()
            self.onward(p, self.line.rep).wait_send()
            self.onward(p, 1 - self.line.rep).wait_recv()


class Swap:
    semaphores = ((2,),)
    buffers = ()
    near = True

    def __init__(self, values, start, count, at=0):
        self.made = values if isinstance(values, PairSum) else None
        shape = values.outputs[0] if self.made else values
        self.inputs = [] if self.made else [values]
        self.start, self.count, self.at, self.slots = start, count, at, at + 1
        self.outputs = [jax.ShapeDtypeStruct((count, shape.shape[1]), shape.dtype)]

    def bind(self, line, sources, targets, scratch):
        source = self.made.target if self.made else sources[0]
        sends, recvs = scratch[0].at[0], scratch[0].at[1]
        rows = source.at[pl.ds(self.start, self.count), :]
        self.copy = remote(rows, targets[0], sends, recvs, line.partner)

    def slot(self, t):
        if t == self.at:
            self.copy.start()

    def finish(self):
        self.copy.wait()


class Four:
    semaphores = ((3,),) * 2
    buffers = ()
    near = True
    slots = 1

    def __init__(self, values):
        self.inputs = [values]
        self.outputs = [jax.ShapeDtypeStruct(values.shape, values.dtype)] * 3

    def bind(self, line, sources, targets, scratch):
        devices = (line.across, line.partner, line.diagonal)
        self.copies = [
            remote(sources[0], target, scratch[0].at[index], scratch[1].at[index], device)
            for index, (target, device) in enumerate(zip(targets, devices))
        ]

    def slot(self, t):
        if t == 0:
            for copy in self.copies:
                copy.start()

    def finish(self):
        for copy in self.copies:
            copy.wait()


class Share:
    semaphores = ((2 * LINE,),) * 2
    buffers = ()
    near = True
    slots = 1

    def __init__(self, values):
        self.inputs = [values]
        self.outputs = [jax.ShapeDtypeStruct((2 * LINE,) + values.shape, values.dtype)]

    def bind(self, line, sources, targets, scratch):
        self.line, self.source, self.target = line, sources[0], targets[0]
        self.sends, self.recvs = scratch

    def copy(self, p):
        goal = self.target.at[self.line.block]
        if p == 0:
            return pltpu.make_async_copy(self.source, goal, self.recvs.at[0])
        place, core = self.line.piece(p, 1)
        return remote(
            self.source, goal, self.sends.at[p], self.recvs.at[p], self.line.at(place, self.line.pair, core)
        )

    def slot(self, t):
        if t == 0:
            for p in range(2 * LINE):
                self.copy(p).start()

    def finish(self):
        for p in range(2 * LINE):
            self.copy(p).wait()


class Deal:
    semaphores = ((2 * LINE,),) * 4
    buffers = ()
    near = True

    def __init__(self, sources, per, at=0):
        self.made = sources if isinstance(sources, Reduce) else None
        shapes = sources.outputs if self.made else sources
        self.inputs = [] if self.made else list(sources)
        self.rows, width = shapes[0].shape[1] // 2, shapes[0].shape[2]
        self.per, self.at, self.n = per, at, width // per
        self.width = width * len(shapes)
        self.slots = at + 2 + 2 * LINE
        self.outputs = [jax.ShapeDtypeStruct((self.rows, 16 * self.width), shapes[0].dtype)]

    def bind(self, line, sources, targets, scratch):
        self.line, self.target = line, targets[0]
        self.sources = [part[1] for part in self.made.parts] if self.made else sources
        self.z_send, self.z_recv, self.x_send, self.x_recv = scratch

    def runs(self, place, core):
        for index, source in enumerate(self.sources):
            for run in range(self.per):
                block = (index * self.per + run) * 16 + place * 4 + self.line.rep * 2 + core
                yield source, run * self.n, pl.ds(pl.multiple_of(block * self.n, self.n), self.n)

    def whole(self):
        return self.target.at[:, pl.ds(0, self.width)]

    def start(self, p):
        line = self.line
        place, core = line.piece(p, 1)
        for source, at, there in self.runs(line.place, line.core):
            rows = pl.ds(pl.multiple_of(core * self.rows, self.rows), self.rows)
            piece = source.at[place, rows, pl.ds(at, self.n)]
            goal = self.target.at[:, there]
            if p == 0:
                pltpu.make_async_copy(piece, goal, self.z_recv.at[0]).start()
            else:
                remote(
                    piece, goal, self.z_send.at[p], self.z_recv.at[p], line.at(place, line.pair, core)
                ).start()

    def came(self, p):
        line, ref = self.line, self.whole()
        if p == 0:
            pltpu.make_async_copy(ref, ref, self.z_recv.at[0]).wait()
        else:
            remote(ref, ref, self.z_send.at[p], self.z_recv.at[p], line.partner).wait_recv()
        place, core = line.piece(p, -1)
        for _, _, there in self.runs(place, core):
            goal = self.target.at[:, there]
            remote(goal, goal, self.x_send.at[p], self.x_recv.at[p], line.partner).start()

    def slot(self, t):
        t -= self.at
        for p in range(2 * LINE):
            if t == (0 if self.made else p):
                self.start(p)
        for p in range(2 * LINE):
            if t == (p if self.made or p == 0 else p + 2):
                self.came(p)

    def finish(self):
        ref = self.whole()
        for p in range(2 * LINE):
            if p > 0:
                remote(ref, ref, self.z_send.at[p], self.z_recv.at[p], self.line.partner).wait_send()
            remote(ref, ref, self.x_send.at[p], self.x_recv.at[p], self.line.partner).wait()


def outer_into(target, left, row, right, column, *more):
    rows, n = target.shape
    tall = min(rows, 256)
    wide = 512 if n % 512 == 0 else 384

    def some(index, carry):
        across = n // wide
        down, along = index // across, index % across
        here = pl.ds(pl.multiple_of(down * tall, tall), tall)
        there = pl.ds(pl.multiple_of(along * wide, wide), wide)
        total = lax.dot_general(
            left[:, pl.ds(pl.multiple_of(row + down * tall, 128), tall)],
            right[:, pl.ds(pl.multiple_of(column + along * wide, 128), wide)],
            (((0,), (0,)), ((), ())),
            preferred_element_type=jnp.float32,
        )
        for ref in more:
            total = total + ref[here, there].astype(jnp.float32)
        target[here, there] = total.astype(target.dtype)
        return carry

    lax.fori_loop(0, (rows // tall) * (n // wide), some, 0)


class Reduce:
    near = True

    def __init__(self, left, rights, first):
        rows, n = left.shape[1] // 8, rights[0].shape[1] // 2
        self.inputs, self.first, self.size, self.n = [left, *rights], first, rows, n
        self.outputs = [jax.ShapeDtypeStruct((LINE, rows, n), left.dtype) for _ in rights]
        self.chunks = 2 * LINE if first == "partner" else LINE
        wide = n if first == "partner" else 2 * n
        self.semaphores = ((self.chunks,),) * (2 * len(rights)) + ((LINE,),) * (2 * len(rights))
        self.buffers = ((self.chunks, rows, wide),) * (2 * len(rights))
        self.join_at = [3, 5, 8, 10] if first == "partner" else [3, 4, 5, 7]
        self.last_at = [12, 15, 16, 17] if first == "partner" else [6, 7, 8, 9]
        self.slots = max(self.last_at) + 1

    def bind(self, line, sources, targets, scratch):
        self.line, self.left, self.parts = line, sources[0], []
        count = len(targets)
        sems1, sems2, buffers = scratch[: 2 * count], scratch[2 * count : 4 * count], scratch[4 * count :]
        for index, target in enumerate(targets):
            pick = slice(2 * index, 2 * index + 2)
            self.parts.append((sources[1 + index], target, *sems1[pick], *sems2[pick], *buffers[pick]))

    def row(self, place, pair):
        return (place * 2 + pair) * self.size

    def leg1(self, part, k):
        _, _, send1, recv1, _, _, out, came = part
        device = self.line.partner if self.first == "partner" else self.line.across
        return remote(out.at[k], came.at[k], send1.at[k], recv1.at[k], device)

    def leg2(self, part, k):
        _, target, _, _, send2, recv2, out, _ = part
        device = self.line.across if self.first == "partner" else self.line.partner
        return remote(out.at[k, :, pl.ds(0, self.n)], target.at[k], send2.at[k], recv2.at[k], device)

    def produce(self, k):
        line = self.line
        for part in self.parts:
            if self.first == "partner":
                pair = 1 - line.pair if k < LINE else line.pair
                outer_into(part[6].at[k], self.left, self.row(k % LINE, pair), part[0], (1 - line.rep) * self.n)
            else:
                outer_into(part[6].at[k], self.left, self.row(k, 1 - line.pair), part[0], 0)
            self.leg1(part, k).start()

    def join(self, k):
        line, n = self.line, self.n
        for part in self.parts:
            right, _, _, _, _, _, out, came = part
            self.leg1(part, k).wait()
            goal = out.at[k, :, pl.ds(0, n)]
            if self.first == "partner":
                outer_into(goal, self.left, self.row(k, 1 - line.pair), right, line.rep * n, came.at[k])
            else:
                column = pl.multiple_of((1 - line.rep) * n, n)
                outer_into(goal, self.left, self.row(k, line.pair), right, column, came.at[k, :, pl.ds(column, n)])
            self.leg2(part, k).start()

    def last(self, k):
        line, n = self.line, self.n
        for part in self.parts:
            right, target, _, _, _, _, _, came = part
            if self.first == "partner":
                self.leg1(part, LINE + k).wait()
                mine = came.at[LINE + k]
            else:
                mine = came.at[k, :, pl.ds(pl.multiple_of(line.rep * n, n), n)]
            self.leg2(part, k).wait()
            outer_into(target.at[k], self.left, self.row(k, line.pair), right, line.rep * n, mine, target.at[k])

    def slot(self, t):
        if t < self.chunks:
            self.produce(t)
        for k in range(LINE):
            if t == self.join_at[k]:
                self.join(k)
        for k in range(LINE):
            if t == self.last_at[k]:
                self.last(k)

    def finish(self):
        pass


class PairSum:
    near = True

    def __init__(self, left, right, count, at):
        self.inputs, self.count, self.at = [left, right], count, at
        shape = (left.shape[1] // 2, right.shape[1])
        self.outputs = [jax.ShapeDtypeStruct(shape, left.dtype)]
        self.semaphores = ((count,),) * 2
        self.buffers = (shape,)
        self.slots = at + count

    def bind(self, line, sources, targets, scratch):
        self.line, self.target = line, targets[0]
        self.left, self.right = sources
        self.sends, self.recvs, self.out = scratch
        self.size = self.target.shape[0] // self.count

    def copy(self, k):
        rows = pl.ds(k * self.size, self.size)
        return remote(
            self.out.at[rows, :], self.target.at[rows, :], self.sends.at[k], self.recvs.at[k], self.line.across
        )

    def slot(self, t):
        pair, size = self.line.pair, self.size
        for k in range(self.count):
            rows = pl.ds(k * size, size)
            if t == k:
                outer_into(self.out.at[rows, :], self.left, (1 - pair) * self.count * size + k * size, self.right, 0)
                self.copy(k).start()
            if t == self.at + k:
                self.copy(k).wait()
                goal = self.target.at[rows, :]
                outer_into(goal, self.left, pair * self.count * size + k * size, self.right, 0, goal)

    def finish(self):
        pass


def line_scatter_joint(line, k, rows, parts, sib):
    return parts[2 * k + line.core, rows, :].astype(jnp.float32) + sib[k, rows, :].astype(jnp.float32)


def line_scatter_pass(line, j, step, way, parts, sib, sums, came, sib_recv, send_sem, came_sem):
    rows = pl.ds(pl.multiple_of(j * step, step), step)
    device = line.right if way == 0 else line.left
    ends = line.place == 0 if way == 0 else line.place == LINE - 1

    def copy(k):
        return remote(sums.at[k, rows], came.at[k, rows], send_sem.at[k, j], came_sem.at[k, j], device)

    for k in range(LINE - 1, 0, -1) if way == 0 else range(LINE - 1):

        @pl.when(line.place < k if way == 0 else line.place > k)
        def _():
            remote(
                parts.at[2 * k + line.core, rows], sib.at[k, rows], sib_recv.at[k, j], sib_recv.at[k, j], line.sibling
            ).wait_recv()

            @pl.when(ends)
            def _():
                sums[k, rows, :] = line_scatter_joint(line, k, rows, parts, sib).astype(jnp.bfloat16)

            @pl.when(jnp.logical_not(ends))
            def _():
                copy(k).wait_recv()
                sums[k, rows, :] = (
                    line_scatter_joint(line, k, rows, parts, sib) + came[k, rows, :].astype(jnp.float32)
                ).astype(jnp.bfloat16)

            copy(k).start()


def line_scatter_total(line, j, step, parts, sib, rights, lefts, sums, sib_recv, sends, right_recv, left_recv):
    rows = pl.ds(pl.multiple_of(j * step, step), step)
    me = line.place
    remote(
        parts.at[2 * me + line.core, rows], sib.at[me, rows], sib_recv.at[me, j], sib_recv.at[me, j], line.sibling
    ).wait_recv()

    @pl.when(line.has_left)
    def _():
        remote(sums.at[me, rows], rights.at[me, rows], sends.at[me, j], right_recv.at[me, j], line.left).wait_recv()

    @pl.when(line.has_right)
    def _():
        remote(sums.at[me, rows], lefts.at[me, rows], sends.at[me, j], left_recv.at[me, j], line.right).wait_recv()

    total = line_scatter_joint(line, me, rows, parts, sib)
    total = total + jnp.where(line.has_left, rights[me, rows, :].astype(jnp.float32), 0.0)
    return total + jnp.where(line.has_right, lefts[me, rows, :].astype(jnp.float32), 0.0)


def line_scatter_start(line, j, step, parts, sib, sib_send, sib_recv):
    rows = pl.ds(pl.multiple_of(j * step, step), step)
    for k in range(LINE):
        remote(
            parts.at[2 * k + 1 - line.core, rows], sib.at[k, rows], sib_send.at[k, j], sib_recv.at[k, j], line.sibling
        ).start()


def line_scatter_end(line, j, step, parts, sib, rights, lefts, sums, sib_send, right_send, left_send):
    rows = pl.ds(pl.multiple_of(j * step, step), step)
    for k in range(LINE):
        remote(
            parts.at[2 * k + 1 - line.core, rows], sib.at[k, rows], sib_send.at[k, j], sib_send.at[k, j], line.sibling
        ).wait_send()

        @pl.when(line.place < k)
        def _():
            remote(
                sums.at[k, rows], rights.at[k, rows], right_send.at[k, j], right_send.at[k, j], line.right
            ).wait_send()

        @pl.when(line.place > k)
        def _():
            remote(
                sums.at[k, rows], lefts.at[k, rows], left_send.at[k, j], left_send.at[k, j], line.left
            ).wait_send()


def gather_copy(line, k, j, step, core, gathered, way, sends, recvs):
    rows = pl.ds(pl.multiple_of(j * step, step), step)
    block = 2 * k + core
    device = (line.right, line.left, line.sibling)[way]
    ref = gathered.at[block, rows]
    return remote(ref, ref, sends.at[k, way, j], recvs.at[block, j], device)


def line_gather_own(line, j, step, gathered, sends, recvs):
    def copy(way):
        return gather_copy(line, line.place, j, step, line.core, gathered, way, sends, recvs)

    pl.when(line.has_right)(lambda: copy(0).start())
    pl.when(line.has_left)(lambda: copy(1).start())
    copy(2).start()


def line_gather_pass(line, hop, j, step, gathered, sends, recvs):
    for way in (0, 1):
        k = line.place - hop if way == 0 else line.place + hop
        there = k >= 0 if way == 0 else k < LINE
        onward = line.has_right if way == 0 else line.has_left
        k = jnp.clip(k, 0, LINE - 1)

        @pl.when(there)
        def _():
            gather_copy(line, k, j, step, line.core, gathered, way, sends, recvs).wait_recv()
            pl.when(onward)(
                lambda: gather_copy(line, k, j, step, line.core, gathered, way, sends, recvs).start()
            )
            gather_copy(line, k, j, step, line.core, gathered, 2, sends, recvs).start()


def line_gather_end(line, j, step, gathered, sends, recvs):
    for k in range(LINE):
        gather_copy(line, k, j, step, 1 - line.core, gathered, 2, sends, recvs).wait_recv()
        gather_copy(line, k, j, step, line.core, gathered, 2, sends, recvs).wait_send()

        @pl.when((line.place >= k) & line.has_right)
        def _():
            gather_copy(line, k, j, step, line.core, gathered, 0, sends, recvs).wait_send()

        @pl.when((line.place <= k) & line.has_left)
        def _():
            gather_copy(line, k, j, step, line.core, gathered, 1, sends, recvs).wait_send()


def take_from(items, count):
    taken = items[:count]
    del items[:count]
    return taken


def moves_scratch(moves):
    scratch = []
    for move in moves:
        scratch += [pltpu.SemaphoreType.DMA(shape) for shape in move.semaphores]
        scratch += [pltpu.VMEM(shape, jnp.bfloat16) for shape in move.buffers]
    return scratch


def moves_specs(moves, side):
    near, far = pl.BlockSpec(memory_space=pltpu.VMEM), pl.BlockSpec(memory_space=pl.ANY)
    return [
        near if move.near or side == "outputs" else far for move in moves for _ in getattr(move, side)
    ]


def line_call(collective_id, pieces, middle, inputs, outputs, scatter, gather, moves=(), limit=46):
    step = inputs[0].shape[-2] // pieces if inputs else 0
    low = jnp.bfloat16
    scratch = []
    if scatter:
        block = inputs[0].shape[-2:]
        scratch += [pltpu.VMEM((LINE,) + block, low) for _ in range(4)]
        scratch += [pltpu.SemaphoreType.DMA((LINE, pieces)) for _ in range(6)]
    if gather:
        scratch += [pltpu.SemaphoreType.DMA((LINE, 3, pieces)), pltpu.SemaphoreType.DMA((2 * LINE, pieces))]
    n_scratch = len(scratch)
    scratch += moves_scratch(moves)
    moved = [values for move in moves for values in move.inputs]
    extras = [shape for move in moves for shape in move.outputs]

    def kernel(*refs):
        refs = list(refs)

        def take(count):
            taken = refs[:count]
            del refs[:count]
            return taken

        ins = take(len(inputs))
        given = [take(len(move.inputs)) for move in moves]
        outs = take(len(outputs))
        extra = [take(len(move.outputs)) for move in moves]
        rest = take(n_scratch)
        line = Line()
        for move, sources, targets in zip(moves, given, extra):
            move.bind(line, sources, targets, take(len(move.semaphores) + len(move.buffers)))
        line.meet(bool(moves))
        if scatter:
            sib, rights, lefts, sums, sib_send, sib_recv, right_send, left_send, right_recv, left_recv = rest[:10]
            parts = ins[0]
            for j in range(2):
                line_scatter_start(line, j, step, parts, sib, sib_send, sib_recv)
        if gather:
            sends, recvs = rest[-2:]

        hops = (LINE - 1) * (int(scatter) + int(gather))

        def during(j, act):
            pl.when((j >= 0) & (j < pieces))(lambda: act(j))

        def finish(j):
            rows = pl.ds(pl.multiple_of(j * step, step), step)
            total = None
            if scatter:
                total = line_scatter_total(
                    line, j, step, parts, sib, rights, lefts, sums, sib_recv, right_send, right_recv, left_recv
                )
            values = middle(total, rows, j, ins, outs)
            if gather:
                outs[0][line.block, rows, :] = values.astype(low)
                line_gather_own(line, j, step, outs[0], sends, recvs)

        def slot(t, carry):
            if scatter:
                during(t + 2, lambda j: line_scatter_start(line, j, step, parts, sib, sib_send, sib_recv))
                during(
                    t - line.place,
                    lambda j: line_scatter_pass(
                        line, j, step, 0, parts, sib, sums, rights, sib_recv, right_send, right_recv
                    ),
                )
                during(
                    t - (LINE - 1 - line.place),
                    lambda j: line_scatter_pass(
                        line, j, step, 1, parts, sib, sums, lefts, sib_recv, left_send, left_recv
                    ),
                )
                during(t - (LINE - 1), finish)
            if gather:
                for hop in range(1, LINE):
                    during(
                        t - hop - (LINE - 1 if scatter else 0),
                        lambda j, hop=hop: line_gather_pass(line, hop, j, step, outs[0], sends, recvs),
                    )
                during(t - hops - 1, lambda j: line_gather_end(line, j, step, outs[0], sends, recvs))
            if scatter:
                during(
                    t - LINE,
                    lambda j: line_scatter_end(
                        line, j, step, parts, sib, rights, lefts, sums, sib_send, right_send, left_send
                    ),
                )
            return carry

        if gather and not scatter:
            lax.fori_loop(0, pieces, lambda j, carry: (finish(j), carry)[1], 0)
        slots = pieces + hops + 1 if inputs else 0
        apart = max([move.slots for move in moves] + [0])
        if apart <= 1:
            for move in moves:
                move.slot(0)
            if inputs:
                lax.fori_loop(0, slots, slot, 0)
        else:
            for t in range(max(slots, apart)):
                for move in moves:
                    move.slot(t)
                if t < slots:
                    slot(t, 0)
        for move in moves:
            move.finish()

    vmem = pl.BlockSpec(memory_space=pltpu.VMEM)
    return pl.pallas_call(
        kernel,
        out_shape=[jax.ShapeDtypeStruct(shape, kind) for shape, kind in outputs] + extras,
        in_specs=[vmem] * len(inputs) + moves_specs(moves, "inputs"),
        out_specs=[vmem] * len(outputs) + moves_specs(moves, "outputs"),
        scratch_shapes=scratch,
        compiler_params=pltpu.CompilerParams(
            collective_id=collective_id, has_side_effects=True, vmem_limit_bytes=limit << 20
        ),
        cost_estimate=pl.CostEstimate(flops=10_000_000, bytes_accessed=200_000_000, transcendentals=0),
    )(*inputs, *moved)


def gather_blocks(payload, moves, collective_id):
    def middle(total, rows, j, ins, outs):
        return ins[0][rows, :]

    shape = (2 * LINE,) + payload.shape
    return line_call(collective_id, 8, middle, [payload], [(shape, jnp.bfloat16)], False, True, moves, 58)


def attention_block(parts, hidden, gain, moves, collective_id):
    def middle(total, rows, j, ins, outs):
        outs[1][rows, :] = total
        resid = ins[1][rows, :].astype(jnp.float32) + total * rms_scale(total) * ins[2][...]
        outs[2][rows, :] = resid
        return resid

    shape = hidden.shape
    return line_call(
        collective_id, 8, middle, [parts, hidden, gain],
        [(parts.shape, jnp.bfloat16), (shape, jnp.float32), (shape, jnp.float32)], True, True, moves,
    )


def add_rows(ref, values, j):
    folded = jnp.sum(values.reshape(values.shape[0] // 8, 8, values.shape[1]), axis=0)

    @pl.when(j == 0)
    def _():
        ref[...] = folded

    @pl.when(j > 0)
    def _():
        ref[...] += folded


def ffn_block(parts, resid, cotangent, gain, collective_id):
    def middle(total, rows, j, ins, outs):
        scale = rms_scale(total)
        normed = total * scale
        grad = ins[2][rows, :].astype(jnp.float32)
        gains = ins[3][...]
        outs[1][rows, :] = (ins[1][rows, :] + normed * gains).astype(jnp.bfloat16)
        add_rows(outs[2], grad * normed, j)
        return rms_back(grad * gains, normed, scale)

    shape = resid.shape
    return line_call(
        collective_id, 8, middle, [parts, resid, cotangent, gain],
        [(parts.shape, jnp.bfloat16), (shape, jnp.bfloat16), ((8, shape[1]), jnp.float32)], True, True,
    )


def back_block(parts, cotangent, attn_out, gain, moves, collective_id):
    def middle(total, rows, j, ins, outs):
        d_resid = ins[1][rows, :].astype(jnp.float32) + total
        outs[1][rows, :] = d_resid
        attn = ins[2][rows, :]
        scale = rms_scale(attn)
        normed = attn * scale
        add_rows(outs[2], d_resid * normed, j)
        return rms_back(d_resid * ins[3][...], normed, scale)

    shape = cotangent.shape
    return line_call(
        collective_id, 8, middle, [parts, cotangent, attn_out, gain],
        [(parts.shape, jnp.bfloat16), (shape, jnp.float32), ((8, shape[1]), jnp.float32)], True, True, moves, 56,
    )


def last_block(parts, d_resid, moves, collective_id):
    def middle(total, rows, j, ins, outs):
        outs[0][rows, :] = (ins[1][rows, :] + total).astype(jnp.bfloat16)

    return line_call(
        collective_id, 8, middle, [parts, d_resid], [(d_resid.shape, jnp.bfloat16)], True, False, moves, 48
    )


def line_exchange(line, mine, came, sends, recvs):
    def copy(p):
        place, core = line.piece(p, 1)
        return remote(mine, came.at[p], sends.at[p], recvs.at[p], line.at(place, line.pair, core))

    for p in range(1, 2 * LINE):
        copy(p).start()
    total = mine[...]
    for p in range(1, 2 * LINE):
        copy(p).wait_recv()
        total = total + came[p]
    for p in range(1, 2 * LINE):
        copy(p).wait_send()
    return total


def spot(head, index):
    start = (3 * head + index) * HEAD_DIM
    return slice(start, start + HEAD_DIM)


def turn_tables(turns):
    half = turns.shape[1] // 2
    swapped = pltpu.roll(turns, half, 1)
    first = lax.broadcasted_iota(jnp.int32, turns.shape, 1) < half
    return jnp.where(first, turns, swapped), jnp.where(first, -swapped, turns)


def as_row(column):
    return jnp.broadcast_to(column, (column.shape[0], column.shape[0])).T[0:1, :]


def as_columns(row):
    return jnp.broadcast_to(row, (row.shape[1], row.shape[1])).T


def dot(left, right, left_dim, right_dim):
    return lax.dot_general(
        left, right, (((left_dim,), (right_dim,)), ((), ())), preferred_element_type=jnp.float32
    )


def heads_call(collective_id, body, inputs, outputs, scratch, rows, moves):
    blocks, length = 2 * LINE, HEAD_DIM
    scratch = [
        pltpu.VMEM((rows, length), jnp.float32),
        pltpu.VMEM((blocks, rows, length), jnp.float32),
        pltpu.SemaphoreType.DMA((blocks,)),
        pltpu.SemaphoreType.DMA((blocks,)),
    ] + scratch
    n_scratch = len(scratch)
    moved = [values for move in moves for values in move.inputs]
    extras = [shape for move in moves for shape in move.outputs]

    def kernel(*refs):
        refs = list(refs)
        ins = take_from(refs, len(inputs))
        given = [take_from(refs, len(move.inputs)) for move in moves]
        outs = take_from(refs, len(outputs))
        extra = [take_from(refs, len(move.outputs)) for move in moves]
        rest = take_from(refs, n_scratch)
        line = Line()
        for move, sources, targets in zip(moves, given, extra):
            move.bind(line, sources, targets, take_from(refs, len(move.semaphores) + len(move.buffers)))
        line.meet(True)
        passed = [0]

        def tick():
            for move in moves:
                move.slot(passed[0])
            passed[0] += 1

        body(line, ins, outs, rest, tick)
        while passed[0] < max([move.slots for move in moves] + [0]):
            tick()
        for move in moves:
            move.finish()

    vmem = pl.BlockSpec(memory_space=pltpu.VMEM)
    return pl.pallas_call(
        kernel,
        out_shape=[jax.ShapeDtypeStruct(shape, kind) for shape, kind in outputs] + extras,
        in_specs=[vmem] * len(inputs) + moves_specs(moves, "inputs"),
        out_specs=[vmem] * len(outputs) + moves_specs(moves, "outputs"),
        scratch_shapes=scratch + moves_scratch(moves),
        compiler_params=pltpu.CompilerParams(
            collective_id=collective_id, has_side_effects=True, vmem_limit_bytes=44 << 20
        ),
        cost_estimate=pl.CostEstimate(flops=10_000_000, bytes_accessed=80_000_000, transcendentals=0),
    )(*inputs, *moved)


def attend(tokens, full_qkv, turns, bias, gains, weight, moves, collective_id):
    blocks, length = bias.shape[:2]
    width = full_qkv.shape[1] // 3
    heads = width // HEAD_DIM
    model_width = weight.shape[1]
    low = jnp.bfloat16

    def body(line, ins, outs, scratch, tick):
        tokens, full_qkv, turns, bias, gains, weight = ins
        parts, lows, probs, mixed, squares, raw = outs
        mine, came, sends, recvs = scratch

        def squares_of(two, carry):
            both = pl.ds(2 * two, 2)
            product = dot(tokens[both].reshape(2 * length, model_width), full_qkv[...], 1, 0)
            raw[both] = product.reshape(2, length, 3 * width)
            for b, index in ((2 * two, 0), (2 * two, 1), (2 * two + 1, 0), (2 * two + 1, 1)):
                total = jnp.zeros((length, 1), jnp.float32)
                for h in range(heads):
                    values = raw[b, :length, spot(h, index)]
                    total = total + jnp.sum(values * values, axis=1, keepdims=True)
                mine[pl.ds(index * blocks + b, 1), :] = as_row(total)
            return carry

        tick()
        for part in range(LINE):
            squares_of(part, 0)
            tick()
        squares[...] = line_exchange(line, mine, came, sends, recvs)
        tick()

        def block(b, carry):
            scales = [
                lax.rsqrt(as_columns(squares[pl.ds(index * blocks + b, 1), :]) / model_width + epsilon)
                for index in range(2)
            ]
            cos, sin = turn_tables(turns[b])
            for h in range(heads):
                here = slice(h * HEAD_DIM, (h + 1) * HEAD_DIM)
                turned = []
                for index in range(2):
                    there = spot(h, index)
                    normed = raw[b, :length, there] * scales[index] * gains[index : index + 1, here]
                    turned.append((normed * cos + pltpu.roll(normed, HEAD_DIM // 2, 1) * sin).astype(low))
                    lows[b, :, there] = turned[index]
                there = spot(h, 2)
                value = raw[b, :length, there].astype(low)
                lows[b, :, there] = value
                scores = dot(turned[0], turned[1], 1, 1) * HEAD_DIM**-0.5 + bias[b]
                powers = jnp.exp(scores - jnp.max(scores, axis=1, keepdims=True))
                prob = powers / jnp.sum(powers, axis=1, keepdims=True)
                probs[b, h] = prob
                mixed[b, :, here] = dot(prob.astype(low), value, 1, 0).astype(low)
            return carry

        for part in range(LINE):
            lax.fori_loop(2 * part, 2 * part + 2, block, 0)
            both = pl.ds(2 * part, 2)
            product = dot(mixed[both].reshape(2 * length, width), weight[...], 1, 0)
            parts[both] = product.astype(low).reshape(2, length, model_width)
            tick()

    return heads_call(
        collective_id,
        body,
        [tokens, full_qkv, turns, bias, gains, weight],
        [
            ((blocks, length, model_width), low),
            ((blocks, length, 3 * width), low),
            ((blocks, heads, length, length), jnp.float32),
            ((blocks, length, width), low),
            ((2 * blocks, length), jnp.float32),
            ((blocks, length, 3 * width), jnp.float32),
        ],
        [],
        2 * blocks,
        moves,
    )


def attend_back(d_attn, weight, raw, turns, gains, lows, probs, squares, wide_terms, full_qkv, moves, collective_id):
    blocks, length = raw.shape[:2]
    width = raw.shape[2] // 3
    heads = width // HEAD_DIM
    model_width = weight.shape[1]
    low = jnp.bfloat16

    def body(line, ins, outs, scratch, tick):
        d_attn, weight, raw, turns, gains, lows, probs, squares = ins[:8]
        d_low, wide, parts = outs
        full_qkv = ins[10]
        mine, came, sends, recvs, upstream, unit, d_mixed, terms = scratch
        tick()
        terms[...] = jnp.zeros_like(terms)
        for which in range(2):
            total = jnp.sum(ins[8 + which][...], axis=0, keepdims=True)
            for index in range(model_width // length):
                row = 2 * blocks + which * (model_width // length) + index
                mine[row : row + 1, :] = total[:, index * length : (index + 1) * length]

        def block(b, carry):
            scales = [
                lax.rsqrt(as_columns(squares[pl.ds(index * blocks + b, 1), :]) / model_width + epsilon)
                for index in range(2)
            ]
            cos, sin = turn_tables(turns[b])
            means = [jnp.zeros((length, 1), jnp.float32)] * 2
            for h in range(heads):
                here = slice(h * HEAD_DIM, (h + 1) * HEAD_DIM)
                places = [spot(h, index) for index in range(3)]
                query, key, value = [lows[b, :, there] for there in places]
                prob = probs[b, h]
                d_out = d_mixed[b, :, here]
                d_low[b, :length, places[2]] = dot(prob.astype(low), d_out, 0, 0).astype(low)
                d_prob = dot(d_out, value, 1, 1)
                d_scores = (
                    prob * (d_prob - jnp.sum(d_prob * prob, axis=1, keepdims=True))
                ).astype(low)
                turned = [dot(d_scores, key, 1, 0), dot(d_scores, query, 0, 0)]
                for index in range(2):
                    d_rot = turned[index] * HEAD_DIM**-0.5
                    d_normed = d_rot * cos - pltpu.roll(d_rot, HEAD_DIM // 2, 1) * sin
                    units = raw[b, :length, places[index]] * scales[index]
                    ups = d_normed * gains[index : index + 1, here]
                    folded = (d_normed * units).reshape(length // 8, 8, HEAD_DIM)
                    side = slice((index * heads + h) * HEAD_DIM, (index * heads + h + 1) * HEAD_DIM)
                    terms[:, side] += jnp.sum(folded, axis=0)
                    upstream[b, :, side] = ups
                    unit[b, :, side] = units
                    means[index] = means[index] + jnp.sum(ups * units, axis=1, keepdims=True)
            for index in range(2):
                mine[pl.ds(index * blocks + b, 1), :] = as_row(means[index])
            return carry

        def mix(two, carry):
            both = pl.ds(2 * two, 2)
            product = dot(d_attn[both].reshape(2 * length, model_width), weight[...], 1, 1)
            d_mixed[both] = product.astype(low).reshape(2, length, width)
            return carry

        lax.fori_loop(0, LINE, mix, 0)
        lax.fori_loop(0, blocks, block, 0)
        mine[...] = line_exchange(line, mine, came, sends, recvs)
        count = 2 * model_width // length
        wide[:count, :] = mine[2 * blocks :, :]
        wide[count:, :] = jnp.zeros((8, length), jnp.float32)
        for index in range(2 * heads):
            sums = jnp.sum(terms[:, index * length : (index + 1) * length], axis=0, keepdims=True)
            wide[count + index : count + index + 1, :] = sums

        def last(b, carry):
            for index in range(2):
                scale = lax.rsqrt(
                    as_columns(squares[pl.ds(index * blocks + b, 1), :]) / model_width + epsilon
                )
                mean = as_columns(mine[pl.ds(index * blocks + b, 1), :]) / model_width
                for h in range(heads):
                    side = slice((index * heads + h) * HEAD_DIM, (index * heads + h + 1) * HEAD_DIM)
                    d_low[b, :length, spot(h, index)] = (
                        scale * (upstream[b, :, side] - unit[b, :, side] * mean)
                    ).astype(low)
            return carry

        def lasts(two, carry):
            lax.fori_loop(2 * two, 2 * two + 2, last, 0)
            both = pl.ds(2 * two, 2)
            product = dot(d_low[both].reshape(2 * length, 3 * width), full_qkv[...], 1, 1)
            parts[both] = product.astype(low).reshape(2, length, model_width)
            return carry

        lax.fori_loop(0, LINE, lasts, 0)

    return heads_call(
        collective_id,
        body,
        [d_attn, weight, raw, turns, gains, lows, probs, squares, *wide_terms, full_qkv],
        [
            (raw.shape, low),
            ((2 * model_width // length + 8, length), jnp.float32),
            ((blocks, length, model_width), low),
        ],
        [pltpu.VMEM((blocks, length, 2 * width), jnp.float32) for _ in range(2)]
        + [pltpu.VMEM((blocks, length, width), low), pltpu.VMEM((8, 2 * width), jnp.float32)],
        2 * blocks + 2 * model_width // length,
        moves,
    )


def on_device(
    hidden_in,
    segments,
    w_query,
    w_key,
    w_value,
    w_output,
    query_gain,
    key_gain,
    attn_gain,
    w_gate,
    w_up,
    w_down,
    ffn_gain,
    out_cotangent,
):
    length, model_width = hidden_in.shape
    blocks = 2 * LINE
    heads = HEADS // blocks
    factor = HEAD_DIM ** (-0.5)
    pair = (lax.axis_index("shard") // 2) % 2
    f32 = jnp.float32

    extra = jnp.stack([query_gain, key_gain, attn_gain, ffn_gain, segments[0].astype(jnp.bfloat16)])
    payload, extras, full_qkv, full_output = gather_blocks(
        hidden_in,
        [
            Share(jnp.pad(extra, ((0, 11), (0, 0)))),
            Spread(w_query, w_key, w_value),
            Stack(w_output, 2, 1),
        ],
        0,
    )
    tokens = payload.reshape(-1, model_width)
    docs = extras[:, 4].astype(jnp.int32)
    gains = extras[:, :4].reshape(LINE, 2, 4, length)
    gains = jnp.stack(by_pair(pair, gains, pair_swap(gains)), axis=1)
    gains = jnp.moveaxis(gains, 3, 0).reshape(4, 1, model_width).astype(f32)
    gain_attn, gain_ffn = gains[2], gains[3]
    width = heads * HEAD_DIM
    head_gains = gather_rows(jnp.stack([query_gain, key_gain])[None], pair).astype(f32)
    head_gains = head_gains.transpose(1, 0, 2).reshape(2, width)

    earlier = jnp.sum((docs[:, None, :] < docs[:, :, None]).astype(jnp.int32), axis=2)
    positions = jnp.arange(length, dtype=jnp.int32)[None] - earlier
    half_dim = HEAD_DIM // 2
    inverse = jnp.exp(
        jnp.arange(half_dim, dtype=f32) * (-2.0 * math.log(theta_base) / HEAD_DIM)
    )
    angles = positions.astype(f32)[:, :, None] * inverse[None, None, :]
    turns = jnp.cos(jnp.concatenate([angles, angles - 0.5 * math.pi], axis=-1))
    token_idx = jnp.arange(length)
    allowed = (docs[:, :, None] == docs[:, None, :]) & (
        token_idx[:, None] >= token_idx[None, :]
    )[None]
    bias = jnp.where(allowed, 0.0, neg_fill)

    def to_blocks(values):
        return values.astype(jnp.bfloat16).reshape(blocks, -1, model_width)

    attn_parts, lows, probs, mixed_low, squares, raw, full_gate, up_pieces = attend(
        payload, full_qkv, turns, bias, head_gains, full_output, [Spread(w_gate, plan=Spread.BESIDE_HEADS), SpreadLine(w_up, 5)], 6
    )
    mixed_low = mixed_low.reshape(blocks * length, width)
    resid_low, attn_out, resid, full_up, full_down = attention_block(
        attn_parts,
        hidden_in,
        gain_attn,
        [SpreadOver(up_pieces), Stack(w_down, 8, 3)],
        1,
    )
    resid_low = resid_low.reshape(blocks * length, model_width)

    gate_proj = jnp.dot(resid_low, full_gate, preferred_element_type=f32)
    up_proj = jnp.dot(resid_low, full_up, preferred_element_type=f32)
    gate_sig = jax.nn.sigmoid(gate_proj)
    hidden_ffn = (gate_proj * gate_sig * up_proj).astype(jnp.bfloat16)
    d_ffn_low, hidden_out, ffn_gain_term = ffn_block(
        to_blocks(jnp.dot(hidden_ffn, full_down, preferred_element_type=f32)),
        resid,
        out_cotangent,
        gain_ffn,
        2,
    )
    d_ffn_low = d_ffn_low.reshape(blocks * length, model_width)

    d_hidden_ffn = dot_back(d_ffn_low, full_down)
    d_gate_low = (d_hidden_ffn * up_proj * gate_sig * (1.0 + gate_proj * (1.0 - gate_sig))).astype(
        jnp.bfloat16
    )
    d_up_low = (d_hidden_ffn * gate_proj * gate_sig).astype(jnp.bfloat16)
    ff_rows = w_down.shape[0]
    d_attn_low, d_resid, attn_gain_term, gate_sum, up_sum, down_part = back_block(
        to_blocks(dot_back(d_gate_low, full_gate) + dot_back(d_up_low, full_up)),
        out_cotangent,
        attn_out,
        gain_attn,
        [
            Reduce(resid_low, [d_gate_low, d_up_low], "partner"),
            PairSum(hidden_ffn, d_ffn_low, 4, 13),
        ],
        3,
    )

    d_qkv, gain_sums, back_parts, there_first = attend_back(
        d_attn_low, full_output, raw, turns, head_gains, lows, probs, squares,
        [attn_gain_term, ffn_gain_term], full_qkv, [Swap(down_part, 0, ff_rows // 2)], 7,
    )
    d_attn_low = d_attn_low.reshape(blocks * length, model_width)
    qkv_sum = Reduce(tokens, [d_qkv.reshape(-1, 3 * width)], "across")
    output_sum = PairSum(mixed_low, d_attn_low, 1, 5)
    hidden_grad, _, output_part, ffn_total, there_second, qkv_total, there_output, *there_gains = last_block(
        back_parts,
        d_resid,
        [
            qkv_sum,
            output_sum,
            Deal([gate_sum, up_sum], 1),
            Swap(down_part, ff_rows // 2, ff_rows // 2, 2),
            Deal(qkv_sum, 3, 9),
            Swap(output_sum, 0, length, 8),
            Four(gain_sums),
        ],
        4,
    )

    def total_of(first, second):
        return first.astype(f32) + second.astype(f32)

    grad_query, grad_key, grad_value = jnp.split(qkv_total.astype(f32), 3, axis=1)
    grad_gate, grad_up = jnp.split(ffn_total.astype(f32), 2, axis=1)
    grad_output = total_of(output_part, there_output)
    grad_down = total_of(down_part, jnp.concatenate([there_first, there_second]))
    gain_sums = (gain_sums + there_gains[0]) + (there_gains[1] + there_gains[2])
    wide_grads = lax.dynamic_index_in_dim(
        gain_sums[:32].reshape(2, 16, length), lax.axis_index("shard"), 1, keepdims=False
    )
    head_grads = lax.dynamic_index_in_dim(gain_sums[32:36].reshape(2, 2, length), pair, 1, keepdims=False)
    gain_grads = jnp.concatenate([head_grads, wide_grads])
    return (
        hidden_out,
        hidden_grad,
        grad_query,
        grad_key,
        grad_value,
        grad_output,
        gain_grads[0],
        gain_grads[1],
        gain_grads[2],
        grad_gate,
        grad_up,
        grad_down,
        gain_grads[3],
    )


def solution(mesh):
    placed = (
        P(("rep", "shard"), None),
        P(("rep", "shard"), None),
        P("shard", None),
        P("shard", None),
        P("shard", None),
        P("shard", None),
        P("shard"),
        P("shard"),
        P("shard"),
        P("shard", None),
        P("shard", None),
        P("shard", None),
        P("shard"),
        P(("rep", "shard"), None),
    )
    return jax.shard_map(
        on_device if mesh.shape["shard"] == 16 else on_device_general,
        mesh=mesh,
        in_specs=placed,
        out_specs=(
            P(("rep", "shard"), None),
            P(("rep", "shard"), None),
            P("shard", None),
            P("shard", None),
            P("shard", None),
            P("shard", None),
            P("shard"),
            P("shard"),
            P("shard"),
            P("shard", None),
            P("shard", None),
            P("shard", None),
            P("shard"),
        ),
        check_vma=False,
    )
```

```python
import math

import jax
import jax.numpy as jnp
from jax import lax
from jax.experimental import pallas as pl
from jax.experimental.pallas import tpu as pltpu
from jax.sharding import PartitionSpec as P

HEADS = 16
HEAD_DIM = 128


epsilon = 1e-06
theta_base = 500000.0
neg_fill = -1e30


def rms_scale(values):
    return lax.rsqrt(jnp.mean(values * values, axis=-1, keepdims=True) + epsilon)


def rms_back(upstream, normed, row_scale):
    return row_scale * (upstream - normed * jnp.mean(upstream * normed, axis=-1, keepdims=True))


def rotate(values, cosines, sines):
    half_dim = values.shape[-1] // 2
    first_half = values[..., :half_dim]
    second = values[..., half_dim:]
    return jnp.concatenate(
        [first_half * cosines - second * sines, second * cosines + first_half * sines], axis=-1
    )


def dot_back(left_side, right_side):
    return lax.dot_general(
        left_side, right_side, (((1,), (1,)), ((), ())), preferred_element_type=jnp.float32
    )


def col_term(left_side, right_side):

    def block_term(row_start, row_count):
        return lax.dot_general(
            left_side, right_side, (((0,), (0,)), ((), ())), preferred_element_type=jnp.float32
        )

    return block_term


def on_device_general(
    hidden_in,
    segments,
    w_query,
    w_key,
    w_value,
    w_output,
    query_gain,
    key_gain,
    attn_gain,
    w_gate,
    w_up,
    w_down,
    ffn_gain,
    out_cotangent,
):
    length = hidden_in.shape[0]
    model_width = hidden_in.shape[1]
    ffn_width = w_gate.shape[1]
    factor = HEAD_DIM ** (-0.5)
    doc_row = segments[0]
    earlier = jnp.sum((doc_row[None, :] < doc_row[:, None]).astype(jnp.int32), axis=1)
    positions = jnp.arange(length, dtype=jnp.int32) - earlier
    half_dim = HEAD_DIM // 2
    inverse = jnp.exp(
        jnp.arange(half_dim, dtype=jnp.float32) * (-2.0 * math.log(theta_base) / HEAD_DIM)
    )
    angles = positions.astype(jnp.float32)[:, None] * inverse[None, :]
    cosines = jnp.cos(angles)[:, None, :]
    sines = jnp.sin(angles)[:, None, :]
    token_idx = jnp.arange(length)
    allowed = (doc_row[:, None] == doc_row[None, :]) & (token_idx[:, None] >= token_idx[None, :])

    def reduce_rows(term_fn, local_rows):
        return lax.psum_scatter(
            term_fn(jnp.int32(0), local_rows * lax.axis_size("shard")),
            "shard",
            scatter_dimension=0,
            tiled=True,
        )

    def norm_rope(raw_proj, gain_vec):
        normed = raw_proj * rms_scale(raw_proj) * gain_vec
        return rotate(normed.reshape(length, HEADS, HEAD_DIM), cosines, sines)

    def attend_scores(query_low, key_low):
        scores = (
            jnp.einsum("qhd,khd->hqk", query_low, key_low, preferred_element_type=jnp.float32)
            * factor
        )
        return jnp.where(allowed[None], scores, neg_fill)

    full_query, full_key, full_value, gain_query, gain_key = (
        lax.all_gather(w_query, "shard", axis=0, tiled=True),
        lax.all_gather(w_key, "shard", axis=0, tiled=True),
        lax.all_gather(w_value, "shard", axis=0, tiled=True),
        lax.all_gather(query_gain, "shard", axis=0, tiled=True),
        lax.all_gather(key_gain, "shard", axis=0, tiled=True),
    )
    query_raw = jnp.dot(hidden_in, full_query, preferred_element_type=jnp.float32)
    key_raw = jnp.dot(hidden_in, full_key, preferred_element_type=jnp.float32)
    query_low = norm_rope(query_raw, gain_query.astype(jnp.float32)).astype(jnp.bfloat16)
    key_low = norm_rope(key_raw, gain_key.astype(jnp.float32)).astype(jnp.bfloat16)
    value_low = (
        jnp.dot(hidden_in, full_value, preferred_element_type=jnp.float32)
        .astype(jnp.bfloat16)
        .reshape(length, HEADS, HEAD_DIM)
    )
    scores = attend_scores(query_low, key_low)
    row_peak = jnp.max(scores, axis=-1, keepdims=True)
    log_norm = row_peak + jnp.log(jnp.sum(jnp.exp(scores - row_peak), axis=-1, keepdims=True))
    attn_prob = jnp.exp(scores - log_norm)
    mixed_low = (
        jnp.einsum(
            "hqk,khd->qhd",
            attn_prob.astype(jnp.bfloat16),
            value_low,
            preferred_element_type=jnp.float32,
        )
        .reshape(length, model_width)
        .astype(jnp.bfloat16)
    )
    full_output, gain_attn = (
        lax.all_gather(w_output, "shard", axis=0, tiled=True),
        lax.all_gather(attn_gain, "shard", axis=0, tiled=True),
    )
    attn_out = jnp.dot(mixed_low, full_output, preferred_element_type=jnp.float32)
    attn_rms = rms_scale(attn_out)
    attn_normed = attn_out * attn_rms
    resid = hidden_in.astype(jnp.float32) + attn_normed * gain_attn.astype(jnp.float32)
    resid_low = resid.astype(jnp.bfloat16)
    full_gate, full_up = (
        lax.all_gather(w_gate, "shard", axis=0, tiled=True),
        lax.all_gather(w_up, "shard", axis=0, tiled=True),
    )
    gate_proj = jnp.dot(resid_low, full_gate, preferred_element_type=jnp.float32)
    up_proj = jnp.dot(resid_low, full_up, preferred_element_type=jnp.float32)
    gate_sig = jax.nn.sigmoid(gate_proj)
    hidden_ffn = (gate_proj * gate_sig * up_proj).astype(jnp.bfloat16)
    full_down, gain_ffn = (
        lax.all_gather(w_down, "shard", axis=0, tiled=True),
        lax.all_gather(ffn_gain, "shard", axis=0, tiled=True),
    )
    ffn_out = jnp.dot(hidden_ffn, full_down, preferred_element_type=jnp.float32)
    ffn_rms = rms_scale(ffn_out)
    ffn_normed = ffn_out * ffn_rms
    hidden_out = (resid + ffn_normed * gain_ffn.astype(jnp.float32)).astype(jnp.bfloat16)
    grad_out = out_cotangent.astype(jnp.float32)
    back_down, back_fgain = (
        lax.all_gather(w_down, "shard", axis=0, tiled=True),
        lax.all_gather(ffn_gain, "shard", axis=0, tiled=True),
    )
    ffn_gain_term = jnp.sum(grad_out * ffn_normed, axis=0)
    d_ffn_low = rms_back(grad_out * back_fgain.astype(jnp.float32), ffn_normed, ffn_rms).astype(
        jnp.bfloat16
    )
    down_grad = reduce_rows(col_term(hidden_ffn, d_ffn_low), w_down.shape[0])
    d_hidden_ffn = dot_back(d_ffn_low, back_down)
    d_gate_low = (d_hidden_ffn * up_proj * gate_sig * (1.0 + gate_proj * (1.0 - gate_sig))).astype(
        jnp.bfloat16
    )
    d_up_low = (d_hidden_ffn * gate_proj * gate_sig).astype(jnp.bfloat16)
    ffn_in_grad = reduce_rows(
        col_term(resid_low, jnp.concatenate([d_gate_low, d_up_low], axis=1)), w_gate.shape[0]
    )
    back_gate, back_up = (
        lax.all_gather(w_gate, "shard", axis=0, tiled=True),
        lax.all_gather(w_up, "shard", axis=0, tiled=True),
    )
    d_resid = grad_out + dot_back(d_gate_low, back_gate) + dot_back(d_up_low, back_up)
    back_output, back_again = (
        lax.all_gather(w_output, "shard", axis=0, tiled=True),
        lax.all_gather(attn_gain, "shard", axis=0, tiled=True),
    )
    attn_gain_term = jnp.sum(d_resid * attn_normed, axis=0)
    d_attn_low = rms_back(d_resid * back_again.astype(jnp.float32), attn_normed, attn_rms).astype(
        jnp.bfloat16
    )
    out_grad = reduce_rows(col_term(mixed_low, d_attn_low), w_output.shape[0])
    d_mixed_low = (
        dot_back(d_attn_low, back_output).astype(jnp.bfloat16).reshape(length, HEADS, HEAD_DIM)
    )
    scores_again = attend_scores(query_low, key_low)
    prob_again = jnp.exp(scores_again - log_norm)
    d_value = jnp.einsum(
        "hqk,qhd->khd",
        prob_again.astype(jnp.bfloat16),
        d_mixed_low,
        preferred_element_type=jnp.float32,
    )
    d_prob = jnp.einsum("qhd,khd->hqk", d_mixed_low, value_low, preferred_element_type=jnp.float32)
    d_scores_low = (
        prob_again * (d_prob - jnp.sum(d_prob * prob_again, axis=-1, keepdims=True))
    ).astype(jnp.bfloat16)
    d_query_rot = (
        jnp.einsum("hqk,khd->qhd", d_scores_low, key_low, preferred_element_type=jnp.float32)
        * factor
    )
    d_key_rot = (
        jnp.einsum("hqk,qhd->khd", d_scores_low, query_low, preferred_element_type=jnp.float32)
        * factor
    )
    back_query, back_key, back_value, back_qgain, back_kgain = (
        lax.all_gather(w_query, "shard", axis=0, tiled=True),
        lax.all_gather(w_key, "shard", axis=0, tiled=True),
        lax.all_gather(w_value, "shard", axis=0, tiled=True),
        lax.all_gather(query_gain, "shard", axis=0, tiled=True),
        lax.all_gather(key_gain, "shard", axis=0, tiled=True),
    )
    unused_query, query_pull = jax.vjp(norm_rope, query_raw, back_qgain.astype(jnp.float32))
    d_query_raw, query_gain_term = query_pull(d_query_rot)
    unused_key, key_pull = jax.vjp(norm_rope, key_raw, back_kgain.astype(jnp.float32))
    d_key_raw, key_gain_term = key_pull(d_key_rot)
    d_query_low = d_query_raw.astype(jnp.bfloat16)
    d_key_low = d_key_raw.astype(jnp.bfloat16)
    d_value_low = d_value.reshape(length, model_width).astype(jnp.bfloat16)
    qkv_grad = reduce_rows(
        col_term(hidden_in, jnp.concatenate([d_query_low, d_key_low, d_value_low], axis=1)),
        w_query.shape[0],
    )
    hidden_grad = (
        d_resid
        + dot_back(d_query_low, back_query)
        + dot_back(d_key_low, back_key)
        + dot_back(d_value_low, back_value)
    ).astype(jnp.bfloat16)
    gain_sums = (
        lax.psum_scatter(query_gain_term, "shard", scatter_dimension=0, tiled=True),
        lax.psum_scatter(key_gain_term, "shard", scatter_dimension=0, tiled=True),
        lax.psum_scatter(attn_gain_term, "shard", scatter_dimension=0, tiled=True),
        lax.psum_scatter(ffn_gain_term, "shard", scatter_dimension=0, tiled=True),
    )
    totals = (
        lax.psum(qkv_grad[:, :model_width].astype(jnp.bfloat16), "rep").astype(jnp.float32),
        lax.psum(qkv_grad[:, model_width : 2 * model_width].astype(jnp.bfloat16), "rep").astype(
            jnp.float32
        ),
        lax.psum(qkv_grad[:, 2 * model_width :].astype(jnp.bfloat16), "rep").astype(jnp.float32),
        lax.psum(out_grad.astype(jnp.bfloat16), "rep").astype(jnp.float32),
        lax.psum(gain_sums[0].astype(jnp.bfloat16), "rep").astype(jnp.float32),
        lax.psum(gain_sums[1].astype(jnp.bfloat16), "rep").astype(jnp.float32),
        lax.psum(gain_sums[2].astype(jnp.bfloat16), "rep").astype(jnp.float32),
        lax.psum(ffn_in_grad[:, :ffn_width].astype(jnp.bfloat16), "rep").astype(jnp.float32),
        lax.psum(ffn_in_grad[:, ffn_width:].astype(jnp.bfloat16), "rep").astype(jnp.float32),
        lax.psum(down_grad.astype(jnp.bfloat16), "rep").astype(jnp.float32),
        lax.psum(gain_sums[3].astype(jnp.bfloat16), "rep").astype(jnp.float32),
    )
    return (
        hidden_out,
        hidden_grad,
        totals[0],
        totals[1],
        totals[2],
        totals[3],
        totals[4],
        totals[5],
        totals[6],
        totals[7],
        totals[8],
        totals[9],
        totals[10],
    )


LINE = 4


def shard_perm(move):
    return [(index, move(index)) for index in range(16)]


def pair_swap(values):
    return lax.ppermute(values, "shard", shard_perm(lambda index: index ^ 2))


def by_pair(pair, own, other):
    return jnp.where(pair == 0, own, other), jnp.where(pair == 0, other, own)


def gather_rows(weight, pair):
    return jnp.concatenate(by_pair(pair, weight, pair_swap(weight)), axis=0)


MESH_ID = pl.DeviceIdType.MESH


class Line:
    def __init__(self):
        index = lax.axis_index("shard")
        self.rep = lax.axis_index("rep")
        self.place = index // 4
        self.pair = (index // 2) % 2
        self.core = index % 2
        self.block = self.place * 2 + self.core
        self.sibling = self.at(self.place, self.pair, 1 - self.core)
        self.right = self.at(jnp.minimum(self.place + 1, LINE - 1), self.pair, self.core)
        self.left = self.at(jnp.maximum(self.place - 1, 0), self.pair, self.core)
        self.across = self.at(self.place, 1 - self.pair, self.core)
        self.partner = (1 - self.rep, index)
        self.diagonal = (1 - self.rep, self.across[1])
        self.has_right = self.place < LINE - 1
        self.has_left = self.place > 0

    def at(self, place, pair, core):
        return (self.rep, place * 4 + pair * 2 + core)

    def piece(self, p, sign):
        return (self.place + sign * (p // 2) + LINE) % LINE, (self.core + p % 2) % 2

    def meet(self, wide):
        barrier = pltpu.get_barrier_semaphore()

        def greet(device):
            pl.semaphore_signal(barrier, inc=1, device_id=device, device_id_type=MESH_ID)

        if wide:
            for p in range(1, 2 * LINE):
                place, core = self.piece(p, 1)
                greet(self.at(place, self.pair, core))
            greet(self.across)
            greet(self.partner)
            greet(self.diagonal)
            pl.semaphore_wait(barrier, 2 * LINE + 2)
            return
        greet(self.sibling)
        pl.when(self.has_right)(lambda: greet(self.right))
        pl.when(self.has_left)(lambda: greet(self.left))
        pl.semaphore_wait(
            barrier, 1 + self.has_right.astype(jnp.int32) + self.has_left.astype(jnp.int32)
        )


def remote(source, target, send_sem, recv_sem, device):
    return pltpu.make_async_remote_copy(
        src_ref=source,
        dst_ref=target,
        send_sem=send_sem,
        recv_sem=recv_sem,
        device_id=device,
        device_id_type=MESH_ID,
    )


class Spread:
    semaphores = ((2 * LINE,),) * 2 + ((2 * LINE, 2),) * 4
    buffers = ()
    near = False

    BESIDE_LINE = ((0, 0, 1, 1, 1, 2, 2, 2), (0, 2, 3, 4, 5, 6, 7, 8), (3, 4, 5, 6, 7, 8, 9, 10))
    BESIDE_HEADS = ((0, 0, 0, 0, 4, 4, 0, 0), (0, 1, 4, 4, 8, 8, 4, 4), (1, 2, 5, 5, 9, 9, 5, 5))

    def __init__(self, *weights, plan=BESIDE_LINE):
        self.inputs, self.plan = list(weights), plan
        shape = (16 * weights[0].shape[0], sum(weight.shape[1] for weight in weights) // 8)
        self.outputs = [jax.ShapeDtypeStruct(shape, jnp.bfloat16)]
        self.slots = max(plan[2]) + 1

    def bind(self, line, sources, targets, sems):
        self.line, self.sources, self.target = line, sources, targets[0]
        self.z_send, self.z_recv, self.y_send, self.y_recv, self.x_send, self.x_recv = sems
        self.half = sources[0].shape[0] // 2

    def slot(self, t):
        for when, act in zip(self.plan, (self.start, self.came, self.onward)):
            for p in range(2 * LINE):
                if t == when[p]:
                    act(p)

    def rows(self, place, pair, core, rep):
        start = ((place * 4 + pair * 2 + core) * 2 + rep) * self.half
        return self.target.at[pl.ds(pl.multiple_of(start, self.half), self.half), :]

    def start(self, p):
        line, half = self.line, self.half
        place, core = line.piece(p, 1)
        here = self.rows(line.place, line.pair, line.core, line.rep)
        mine = pl.ds(pl.multiple_of(line.rep * half, half), half)
        at = 0
        for q in range(2):
            for source in self.sources:
                n = source.shape[1] // 16
                column = pl.multiple_of((place * 4 + q * 2 + core) * n, n)
                piece, goal = source.at[mine, pl.ds(column, n)], here.at[:, pl.ds(at, n)]
                if p == 0:
                    pltpu.make_async_copy(piece, goal, self.z_recv.at[0]).start()
                else:
                    remote(
                        piece, goal, self.z_send.at[p], self.z_recv.at[p], line.at(place, line.pair, core)
                    ).start()
                at += n

    def cross(self, p, pair, rep, which):
        place, core = self.line.piece(p, -1)
        ref = self.rows(place, pair, core, rep)
        return remote(ref, ref, self.y_send.at[p, which], self.y_recv.at[p, which], self.line.across)

    def over(self, p, pair, rep, which):
        place, core = self.line.piece(p, -1)
        ref = self.rows(place, pair, core, rep)
        return remote(ref, ref, self.x_send.at[p, which], self.x_recv.at[p, which], self.line.partner)

    def came(self, p):
        line = self.line
        place, core = line.piece(p, -1)
        ref = self.rows(place, line.pair, core, line.rep)
        if p == 0:
            pltpu.make_async_copy(ref, ref, self.z_recv.at[0]).wait()
        else:
            remote(ref, ref, self.z_send.at[p], self.z_recv.at[p], line.sibling).wait_recv()
        self.cross(p, line.pair, line.rep, 0).start()
        self.over(p, line.pair, line.rep, 0).start()

    def onward(self, p):
        line = self.line
        if p % 2:
            self.over(p, line.pair, 1 - line.rep, 0).wait_recv()
            self.cross(p, line.pair, 1 - line.rep, 1).start()
        else:
            self.cross(p, 1 - line.pair, line.rep, 0).wait_recv()
            self.over(p, 1 - line.pair, line.rep, 1).start()

    def finish(self):
        line = self.line
        for p in range(1, 2 * LINE):
            ref = self.rows(line.place, line.pair, line.core, line.rep)
            remote(ref, ref, self.z_send.at[p], self.z_recv.at[p], line.sibling).wait_send()
        self.finish_over()

    def finish_over(self):
        line = self.line
        pair, rep = line.pair, line.rep
        for p in range(2 * LINE):
            self.cross(p, pair, rep, 0).wait_send()
            self.over(p, pair, rep, 0).wait_send()
            if p % 2:
                self.cross(p, 1 - pair, rep, 0).wait_recv()
                self.cross(p, pair, 1 - rep, 1).wait_send()
                self.cross(p, 1 - pair, 1 - rep, 1).wait_recv()
            else:
                self.over(p, pair, 1 - rep, 0).wait_recv()
                self.over(p, 1 - pair, rep, 1).wait_send()
                self.over(p, 1 - pair, 1 - rep, 1).wait_recv()


class SpreadLine:
    semaphores = ((2 * LINE,),) * 2
    buffers = ()
    near = False

    def __init__(self, weight, at):
        self.inputs, self.at, self.slots = [weight], at, at + 1
        shape = (2 * LINE, weight.shape[0] // 2, weight.shape[1] // 8)
        self.outputs = [jax.ShapeDtypeStruct(shape, weight.dtype)]

    def bind(self, line, sources, targets, scratch):
        self.line, self.source, self.target = line, sources[0], targets[0]
        self.sends, self.recvs = scratch

    def slot(self, t):
        if t != self.at:
            return
        line, half, n = self.line, self.target.shape[1], self.target.shape[2] // 2
        mine = pl.ds(pl.multiple_of(line.rep * half, half), half)
        for p in range(2 * LINE):
            place, core = line.piece(p, 1)
            for q in range(2):
                column = pl.multiple_of((place * 4 + q * 2 + core) * n, n)
                piece, goal = self.source.at[mine, pl.ds(column, n)], self.target.at[p, :, pl.ds(q * n, n)]
                if p == 0:
                    pltpu.make_async_copy(piece, goal, self.recvs.at[0]).start()
                else:
                    device = line.at(place, line.pair, core)
                    remote(piece, goal, self.sends.at[p], self.recvs.at[p], device).start()

    def finish(self):
        for p in range(2 * LINE):
            ref = self.target.at[p]
            if p == 0:
                pltpu.make_async_copy(ref, ref, self.recvs.at[0]).wait()
            else:
                remote(ref, ref, self.sends.at[p], self.recvs.at[p], self.line.sibling).wait()


class SpreadOver(Spread):
    semaphores = ((2 * LINE,),) + ((2 * LINE, 2),) * 4

    def __init__(self, pieces):
        self.inputs, self.half = [pieces], pieces.shape[1]
        shape = (2 * pieces.shape[0] * 2 * pieces.shape[1], pieces.shape[2])
        self.outputs = [jax.ShapeDtypeStruct(shape, pieces.dtype)]
        self.slots = 7 + LINE

    def bind(self, line, sources, targets, scratch):
        self.line, self.pieces, self.target = line, sources[0], targets[0]
        self.local, self.y_send, self.y_recv, self.x_send, self.x_recv = scratch

    def here(self, p):
        place, core = self.line.piece(p, -1)
        goal = self.rows(place, self.line.pair, core, self.line.rep)
        return pltpu.make_async_copy(self.pieces.at[p], goal, self.local.at[p])

    def cross(self, p, pair, rep, which):
        place, core = self.line.piece(p, -1)
        ref = self.rows(place, pair, core, rep)
        source = ref if which else self.pieces.at[p]
        return remote(source, ref, self.y_send.at[p, which], self.y_recv.at[p, which], self.line.across)

    def over(self, p, pair, rep, which):
        place, core = self.line.piece(p, -1)
        ref = self.rows(place, pair, core, rep)
        source = ref if which else self.pieces.at[p]
        return remote(source, ref, self.x_send.at[p, which], self.x_recv.at[p, which], self.line.partner)

    def slot(self, t):
        line = self.line
        for p in range(2 * LINE):
            if t == p // 2:
                self.cross(p, line.pair, line.rep, 0).start()
                self.over(p, line.pair, line.rep, 0).start()
                self.here(p).start()
            if t == 7 + p // 2:
                self.onward(p)

    def finish(self):
        for p in range(2 * LINE):
            self.here(p).wait()
        self.finish_over()


class Stack:
    buffers = ()
    near = False

    def __init__(self, weight, count, lag):
        self.inputs, self.count, self.lag = [weight], count, lag
        self.outputs = [jax.ShapeDtypeStruct((2 * weight.shape[0], weight.shape[1]), weight.dtype)]
        self.semaphores = ((1,),) + ((count,),) * 4
        self.slots = lag + count

    def bind(self, line, sources, targets, sems):
        self.line, self.source, self.target = line, sources[0], targets[0]
        self.local, self.y_send, self.y_recv, self.x_send, self.x_recv = sems
        self.size = self.source.shape[0]

    def here(self):
        size = self.size
        mine = self.target.at[pl.ds(pl.multiple_of(self.line.pair * size, size), size), :]
        return pltpu.make_async_copy(self.source, mine, self.local.at[0])

    def there(self, p):
        line, part = self.line, self.size // (2 * self.count)
        start = pl.multiple_of((line.rep * self.count + p) * part, part)
        goal = self.target.at[pl.ds(pl.multiple_of(line.pair * self.size + start, part), part), :]
        return remote(
            self.source.at[pl.ds(start, part), :], goal, self.y_send.at[p], self.y_recv.at[p], line.across
        )

    def onward(self, p, rep):
        line, part = self.line, self.size // (2 * self.count)
        start = (1 - line.pair) * self.size + (rep * self.count + p) * part
        ref = self.target.at[pl.ds(pl.multiple_of(start, part), part), :]
        return remote(ref, ref, self.x_send.at[p], self.x_recv.at[p], line.partner)

    def slot(self, t):
        if t == 0:
            for k in range(self.count):
                self.there(k).start()
            self.here().start()
        if self.lag <= t < self.lag + self.count:
            self.there(t - self.lag).wait_recv()
            self.onward(t - self.lag, self.line.rep).start()

    def finish(self):
        self.here().wait()
        for p in range(self.count):
            self.there(p).wait_send()
            self.onward(p, self.line.rep).wait_send()
            self.onward(p, 1 - self.line.rep).wait_recv()


class Swap:
    semaphores = ((2,),)
    buffers = ()
    near = True

    def __init__(self, values, start, count, at=0):
        self.made = values if isinstance(values, PairSum) else None
        shape = values.outputs[0] if self.made else values
        self.inputs = [] if self.made else [values]
        self.start, self.count, self.at, self.slots = start, count, at, at + 1
        self.outputs = [jax.ShapeDtypeStruct((count, shape.shape[1]), shape.dtype)]

    def bind(self, line, sources, targets, scratch):
        source = self.made.target if self.made else sources[0]
        sends, recvs = scratch[0].at[0], scratch[0].at[1]
        rows = source.at[pl.ds(self.start, self.count), :]
        self.copy = remote(rows, targets[0], sends, recvs, line.partner)

    def slot(self, t):
        if t == self.at:
            self.copy.start()

    def finish(self):
        self.copy.wait()


class Four:
    semaphores = ((3,),) * 2
    buffers = ()
    near = True
    slots = 1

    def __init__(self, values):
        self.inputs = [values]
        self.outputs = [jax.ShapeDtypeStruct(values.shape, values.dtype)] * 3

    def bind(self, line, sources, targets, scratch):
        devices = (line.across, line.partner, line.diagonal)
        self.copies = [
            remote(sources[0], target, scratch[0].at[index], scratch[1].at[index], device)
            for index, (target, device) in enumerate(zip(targets, devices))
        ]

    def slot(self, t):
        if t == 0:
            for copy in self.copies:
                copy.start()

    def finish(self):
        for copy in self.copies:
            copy.wait()


class Share:
    semaphores = ((2 * LINE,),) * 2
    buffers = ()
    near = True
    slots = 1

    def __init__(self, values):
        self.inputs = [values]
        self.outputs = [jax.ShapeDtypeStruct((2 * LINE,) + values.shape, values.dtype)]

    def bind(self, line, sources, targets, scratch):
        self.line, self.source, self.target = line, sources[0], targets[0]
        self.sends, self.recvs = scratch

    def copy(self, p):
        goal = self.target.at[self.line.block]
        if p == 0:
            return pltpu.make_async_copy(self.source, goal, self.recvs.at[0])
        place, core = self.line.piece(p, 1)
        return remote(
            self.source, goal, self.sends.at[p], self.recvs.at[p], self.line.at(place, self.line.pair, core)
        )

    def slot(self, t):
        if t == 0:
            for p in range(2 * LINE):
                self.copy(p).start()

    def finish(self):
        for p in range(2 * LINE):
            self.copy(p).wait()


class Deal:
    semaphores = ((2 * LINE,),) * 4
    buffers = ()
    near = True

    def __init__(self, sources, per, at=0):
        self.made = sources if isinstance(sources, Reduce) else None
        shapes = sources.outputs if self.made else sources
        self.inputs = [] if self.made else list(sources)
        self.rows, width = shapes[0].shape[1] // 2, shapes[0].shape[2]
        self.per, self.at, self.n = per, at, width // per
        self.width = width * len(shapes)
        self.slots = at + 2 + 2 * LINE
        self.outputs = [jax.ShapeDtypeStruct((self.rows, 16 * self.width), shapes[0].dtype)]

    def bind(self, line, sources, targets, scratch):
        self.line, self.target = line, targets[0]
        self.sources = [part[1] for part in self.made.parts] if self.made else sources
        self.z_send, self.z_recv, self.x_send, self.x_recv = scratch

    def runs(self, place, core):
        for index, source in enumerate(self.sources):
            for run in range(self.per):
                block = (index * self.per + run) * 16 + place * 4 + self.line.rep * 2 + core
                yield source, run * self.n, pl.ds(pl.multiple_of(block * self.n, self.n), self.n)

    def whole(self):
        return self.target.at[:, pl.ds(0, self.width)]

    def start(self, p):
        line = self.line
        place, core = line.piece(p, 1)
        for source, at, there in self.runs(line.place, line.core):
            rows = pl.ds(pl.multiple_of(core * self.rows, self.rows), self.rows)
            piece = source.at[place, rows, pl.ds(at, self.n)]
            goal = self.target.at[:, there]
            if p == 0:
                pltpu.make_async_copy(piece, goal, self.z_recv.at[0]).start()
            else:
                remote(
                    piece, goal, self.z_send.at[p], self.z_recv.at[p], line.at(place, line.pair, core)
                ).start()

    def came(self, p):
        line, ref = self.line, self.whole()
        if p == 0:
            pltpu.make_async_copy(ref, ref, self.z_recv.at[0]).wait()
        else:
            remote(ref, ref, self.z_send.at[p], self.z_recv.at[p], line.partner).wait_recv()
        place, core = line.piece(p, -1)
        for _, _, there in self.runs(place, core):
            goal = self.target.at[:, there]
            remote(goal, goal, self.x_send.at[p], self.x_recv.at[p], line.partner).start()

    def slot(self, t):
        t -= self.at
        for p in range(2 * LINE):
            if t == (0 if self.made else p):
                self.start(p)
        for p in range(2 * LINE):
            if t == (p if self.made or p == 0 else p + 2):
                self.came(p)

    def finish(self):
        ref = self.whole()
        for p in range(2 * LINE):
            if p > 0:
                remote(ref, ref, self.z_send.at[p], self.z_recv.at[p], self.line.partner).wait_send()
            remote(ref, ref, self.x_send.at[p], self.x_recv.at[p], self.line.partner).wait()


def outer_into(target, left, row, right, column, *more):
    rows, n = target.shape
    tall = min(rows, 256)
    wide = 512 if n % 512 == 0 else 384

    def some(index, carry):
        across = n // wide
        down, along = index // across, index % across
        here = pl.ds(pl.multiple_of(down * tall, tall), tall)
        there = pl.ds(pl.multiple_of(along * wide, wide), wide)
        total = lax.dot_general(
            left[:, pl.ds(pl.multiple_of(row + down * tall, 128), tall)],
            right[:, pl.ds(pl.multiple_of(column + along * wide, 128), wide)],
            (((0,), (0,)), ((), ())),
            preferred_element_type=jnp.float32,
        )
        for ref in more:
            total = total + ref[here, there].astype(jnp.float32)
        target[here, there] = total.astype(target.dtype)
        return carry

    lax.fori_loop(0, (rows // tall) * (n // wide), some, 0)


class Reduce:
    near = True

    def __init__(self, left, rights, first):
        rows, n = left.shape[1] // 8, rights[0].shape[1] // 2
        self.inputs, self.first, self.size, self.n = [left, *rights], first, rows, n
        self.outputs = [jax.ShapeDtypeStruct((LINE, rows, n), left.dtype) for _ in rights]
        self.chunks = 2 * LINE if first == "partner" else LINE
        wide = n if first == "partner" else 2 * n
        self.semaphores = ((self.chunks,),) * (2 * len(rights)) + ((LINE,),) * (2 * len(rights))
        self.buffers = ((self.chunks, rows, wide),) * (2 * len(rights))
        self.join_at = [3, 5, 8, 10] if first == "partner" else [3, 4, 5, 7]
        self.last_at = [12, 15, 16, 17] if first == "partner" else [6, 7, 8, 9]
        self.slots = max(self.last_at) + 1

    def bind(self, line, sources, targets, scratch):
        self.line, self.left, self.parts = line, sources[0], []
        count = len(targets)
        sems1, sems2, buffers = scratch[: 2 * count], scratch[2 * count : 4 * count], scratch[4 * count :]
        for index, target in enumerate(targets):
            pick = slice(2 * index, 2 * index + 2)
            self.parts.append((sources[1 + index], target, *sems1[pick], *sems2[pick], *buffers[pick]))

    def row(self, place, pair):
        return (place * 2 + pair) * self.size

    def leg1(self, part, k):
        _, _, send1, recv1, _, _, out, came = part
        device = self.line.partner if self.first == "partner" else self.line.across
        return remote(out.at[k], came.at[k], send1.at[k], recv1.at[k], device)

    def leg2(self, part, k):
        _, target, _, _, send2, recv2, out, _ = part
        device = self.line.across if self.first == "partner" else self.line.partner
        return remote(out.at[k, :, pl.ds(0, self.n)], target.at[k], send2.at[k], recv2.at[k], device)

    def produce(self, k):
        line = self.line
        for part in self.parts:
            if self.first == "partner":
                pair = 1 - line.pair if k < LINE else line.pair
                outer_into(part[6].at[k], self.left, self.row(k % LINE, pair), part[0], (1 - line.rep) * self.n)
            else:
                outer_into(part[6].at[k], self.left, self.row(k, 1 - line.pair), part[0], 0)
            self.leg1(part, k).start()

    def join(self, k):
        line, n = self.line, self.n
        for part in self.parts:
            right, _, _, _, _, _, out, came = part
            self.leg1(part, k).wait()
            goal = out.at[k, :, pl.ds(0, n)]
            if self.first == "partner":
                outer_into(goal, self.left, self.row(k, 1 - line.pair), right, line.rep * n, came.at[k])
            else:
                column = pl.multiple_of((1 - line.rep) * n, n)
                outer_into(goal, self.left, self.row(k, line.pair), right, column, came.at[k, :, pl.ds(column, n)])
            self.leg2(part, k).start()

    def last(self, k):
        line, n = self.line, self.n
        for part in self.parts:
            right, target, _, _, _, _, _, came = part
            if self.first == "partner":
                self.leg1(part, LINE + k).wait()
                mine = came.at[LINE + k]
            else:
                mine = came.at[k, :, pl.ds(pl.multiple_of(line.rep * n, n), n)]
            self.leg2(part, k).wait()
            outer_into(target.at[k], self.left, self.row(k, line.pair), right, line.rep * n, mine, target.at[k])

    def slot(self, t):
        if t < self.chunks:
            self.produce(t)
        for k in range(LINE):
            if t == self.join_at[k]:
                self.join(k)
        for k in range(LINE):
            if t == self.last_at[k]:
                self.last(k)

    def finish(self):
        pass


class PairSum:
    near = True

    def __init__(self, left, right, count, at):
        self.inputs, self.count, self.at = [left, right], count, at
        shape = (left.shape[1] // 2, right.shape[1])
        self.outputs = [jax.ShapeDtypeStruct(shape, left.dtype)]
        self.semaphores = ((count,),) * 2
        self.buffers = (shape,)
        self.slots = at + count

    def bind(self, line, sources, targets, scratch):
        self.line, self.target = line, targets[0]
        self.left, self.right = sources
        self.sends, self.recvs, self.out = scratch
        self.size = self.target.shape[0] // self.count

    def copy(self, k):
        rows = pl.ds(k * self.size, self.size)
        return remote(
            self.out.at[rows, :], self.target.at[rows, :], self.sends.at[k], self.recvs.at[k], self.line.across
        )

    def slot(self, t):
        pair, size = self.line.pair, self.size
        for k in range(self.count):
            rows = pl.ds(k * size, size)
            if t == k:
                outer_into(self.out.at[rows, :], self.left, (1 - pair) * self.count * size + k * size, self.right, 0)
                self.copy(k).start()
            if t == self.at + k:
                self.copy(k).wait()
                goal = self.target.at[rows, :]
                outer_into(goal, self.left, pair * self.count * size + k * size, self.right, 0, goal)

    def finish(self):
        pass


def line_scatter_joint(line, k, rows, parts, sib):
    return parts[2 * k + line.core, rows, :].astype(jnp.float32) + sib[k, rows, :].astype(jnp.float32)


def line_scatter_pass(line, j, step, way, parts, sib, sums, came, sib_recv, send_sem, came_sem):
    rows = pl.ds(pl.multiple_of(j * step, step), step)
    device = line.right if way == 0 else line.left
    ends = line.place == 0 if way == 0 else line.place == LINE - 1

    def copy(k):
        return remote(sums.at[k, rows], came.at[k, rows], send_sem.at[k, j], came_sem.at[k, j], device)

    for k in range(LINE - 1, 0, -1) if way == 0 else range(LINE - 1):

        @pl.when(line.place < k if way == 0 else line.place > k)
        def _():
            remote(
                parts.at[2 * k + line.core, rows], sib.at[k, rows], sib_recv.at[k, j], sib_recv.at[k, j], line.sibling
            ).wait_recv()

            @pl.when(ends)
            def _():
                sums[k, rows, :] = line_scatter_joint(line, k, rows, parts, sib).astype(jnp.bfloat16)

            @pl.when(jnp.logical_not(ends))
            def _():
                copy(k).wait_recv()
                sums[k, rows, :] = (
                    line_scatter_joint(line, k, rows, parts, sib) + came[k, rows, :].astype(jnp.float32)
                ).astype(jnp.bfloat16)

            copy(k).start()


def line_scatter_total(line, j, step, parts, sib, rights, lefts, sums, sib_recv, sends, right_recv, left_recv):
    rows = pl.ds(pl.multiple_of(j * step, step), step)
    me = line.place
    remote(
        parts.at[2 * me + line.core, rows], sib.at[me, rows], sib_recv.at[me, j], sib_recv.at[me, j], line.sibling
    ).wait_recv()

    @pl.when(line.has_left)
    def _():
        remote(sums.at[me, rows], rights.at[me, rows], sends.at[me, j], right_recv.at[me, j], line.left).wait_recv()

    @pl.when(line.has_right)
    def _():
        remote(sums.at[me, rows], lefts.at[me, rows], sends.at[me, j], left_recv.at[me, j], line.right).wait_recv()

    total = line_scatter_joint(line, me, rows, parts, sib)
    total = total + jnp.where(line.has_left, rights[me, rows, :].astype(jnp.float32), 0.0)
    return total + jnp.where(line.has_right, lefts[me, rows, :].astype(jnp.float32), 0.0)


def line_scatter_start(line, j, step, parts, sib, sib_send, sib_recv):
    rows = pl.ds(pl.multiple_of(j * step, step), step)
    for k in range(LINE):
        remote(
            parts.at[2 * k + 1 - line.core, rows], sib.at[k, rows], sib_send.at[k, j], sib_recv.at[k, j], line.sibling
        ).start()


def line_scatter_end(line, j, step, parts, sib, rights, lefts, sums, sib_send, right_send, left_send):
    rows = pl.ds(pl.multiple_of(j * step, step), step)
    for k in range(LINE):
        remote(
            parts.at[2 * k + 1 - line.core, rows], sib.at[k, rows], sib_send.at[k, j], sib_send.at[k, j], line.sibling
        ).wait_send()

        @pl.when(line.place < k)
        def _():
            remote(
                sums.at[k, rows], rights.at[k, rows], right_send.at[k, j], right_send.at[k, j], line.right
            ).wait_send()

        @pl.when(line.place > k)
        def _():
            remote(
                sums.at[k, rows], lefts.at[k, rows], left_send.at[k, j], left_send.at[k, j], line.left
            ).wait_send()


def gather_copy(line, k, j, step, core, gathered, way, sends, recvs):
    rows = pl.ds(pl.multiple_of(j * step, step), step)
    block = 2 * k + core
    device = (line.right, line.left, line.sibling)[way]
    ref = gathered.at[block, rows]
    return remote(ref, ref, sends.at[k, way, j], recvs.at[block, j], device)


def line_gather_own(line, j, step, gathered, sends, recvs):
    def copy(way):
        return gather_copy(line, line.place, j, step, line.core, gathered, way, sends, recvs)

    pl.when(line.has_right)(lambda: copy(0).start())
    pl.when(line.has_left)(lambda: copy(1).start())
    copy(2).start()


def line_gather_pass(line, hop, j, step, gathered, sends, recvs):
    for way in (0, 1):
        k = line.place - hop if way == 0 else line.place + hop
        there = k >= 0 if way == 0 else k < LINE
        onward = line.has_right if way == 0 else line.has_left
        k = jnp.clip(k, 0, LINE - 1)

        @pl.when(there)
        def _():
            gather_copy(line, k, j, step, line.core, gathered, way, sends, recvs).wait_recv()
            pl.when(onward)(
                lambda: gather_copy(line, k, j, step, line.core, gathered, way, sends, recvs).start()
            )
            gather_copy(line, k, j, step, line.core, gathered, 2, sends, recvs).start()


def line_gather_end(line, j, step, gathered, sends, recvs):
    for k in range(LINE):
        gather_copy(line, k, j, step, 1 - line.core, gathered, 2, sends, recvs).wait_recv()
        gather_copy(line, k, j, step, line.core, gathered, 2, sends, recvs).wait_send()

        @pl.when((line.place >= k) & line.has_right)
        def _():
            gather_copy(line, k, j, step, line.core, gathered, 0, sends, recvs).wait_send()

        @pl.when((line.place <= k) & line.has_left)
        def _():
            gather_copy(line, k, j, step, line.core, gathered, 1, sends, recvs).wait_send()


def take_from(items, count):
    taken = items[:count]
    del items[:count]
    return taken


def moves_scratch(moves):
    scratch = []
    for move in moves:
        scratch += [pltpu.SemaphoreType.DMA(shape) for shape in move.semaphores]
        scratch += [pltpu.VMEM(shape, jnp.bfloat16) for shape in move.buffers]
    return scratch


def moves_specs(moves, side):
    near, far = pl.BlockSpec(memory_space=pltpu.VMEM), pl.BlockSpec(memory_space=pl.ANY)
    return [
        near if move.near or side == "outputs" else far for move in moves for _ in getattr(move, side)
    ]


def line_call(collective_id, pieces, middle, inputs, outputs, scatter, gather, moves=(), limit=46):
    step = inputs[0].shape[-2] // pieces if inputs else 0
    low = jnp.bfloat16
    scratch = []
    if scatter:
        block = inputs[0].shape[-2:]
        scratch += [pltpu.VMEM((LINE,) + block, low) for _ in range(4)]
        scratch += [pltpu.SemaphoreType.DMA((LINE, pieces)) for _ in range(6)]
    if gather:
        scratch += [pltpu.SemaphoreType.DMA((LINE, 3, pieces)), pltpu.SemaphoreType.DMA((2 * LINE, pieces))]
    n_scratch = len(scratch)
    scratch += moves_scratch(moves)
    moved = [values for move in moves for values in move.inputs]
    extras = [shape for move in moves for shape in move.outputs]

    def kernel(*refs):
        refs = list(refs)

        def take(count):
            taken = refs[:count]
            del refs[:count]
            return taken

        ins = take(len(inputs))
        given = [take(len(move.inputs)) for move in moves]
        outs = take(len(outputs))
        extra = [take(len(move.outputs)) for move in moves]
        rest = take(n_scratch)
        line = Line()
        for move, sources, targets in zip(moves, given, extra):
            move.bind(line, sources, targets, take(len(move.semaphores) + len(move.buffers)))
        line.meet(bool(moves))
        if scatter:
            sib, rights, lefts, sums, sib_send, sib_recv, right_send, left_send, right_recv, left_recv = rest[:10]
            parts = ins[0]
            for j in range(2):
                line_scatter_start(line, j, step, parts, sib, sib_send, sib_recv)
        if gather:
            sends, recvs = rest[-2:]

        hops = (LINE - 1) * (int(scatter) + int(gather))

        def during(j, act):
            pl.when((j >= 0) & (j < pieces))(lambda: act(j))

        def finish(j):
            rows = pl.ds(pl.multiple_of(j * step, step), step)
            total = None
            if scatter:
                total = line_scatter_total(
                    line, j, step, parts, sib, rights, lefts, sums, sib_recv, right_send, right_recv, left_recv
                )
            values = middle(total, rows, j, ins, outs)
            if gather:
                outs[0][line.block, rows, :] = values.astype(low)
                line_gather_own(line, j, step, outs[0], sends, recvs)

        def slot(t, carry):
            if scatter:
                during(t + 2, lambda j: line_scatter_start(line, j, step, parts, sib, sib_send, sib_recv))
                during(
                    t - line.place,
                    lambda j: line_scatter_pass(
                        line, j, step, 0, parts, sib, sums, rights, sib_recv, right_send, right_recv
                    ),
                )
                during(
                    t - (LINE - 1 - line.place),
                    lambda j: line_scatter_pass(
                        line, j, step, 1, parts, sib, sums, lefts, sib_recv, left_send, left_recv
                    ),
                )
                during(t - (LINE - 1), finish)
            if gather:
                for hop in range(1, LINE):
                    during(
                        t - hop - (LINE - 1 if scatter else 0),
                        lambda j, hop=hop: line_gather_pass(line, hop, j, step, outs[0], sends, recvs),
                    )
                during(t - hops - 1, lambda j: line_gather_end(line, j, step, outs[0], sends, recvs))
            if scatter:
                during(
                    t - LINE,
                    lambda j: line_scatter_end(
                        line, j, step, parts, sib, rights, lefts, sums, sib_send, right_send, left_send
                    ),
                )
            return carry

        if gather and not scatter:
            lax.fori_loop(0, pieces, lambda j, carry: (finish(j), carry)[1], 0)
        slots = pieces + hops + 1 if inputs else 0
        apart = max([move.slots for move in moves] + [0])
        if apart <= 1:
            for move in moves:
                move.slot(0)
            if inputs:
                lax.fori_loop(0, slots, slot, 0)
        else:
            for t in range(max(slots, apart)):
                for move in moves:
                    move.slot(t)
                if t < slots:
                    slot(t, 0)
        for move in moves:
            move.finish()

    vmem = pl.BlockSpec(memory_space=pltpu.VMEM)
    return pl.pallas_call(
        kernel,
        out_shape=[jax.ShapeDtypeStruct(shape, kind) for shape, kind in outputs] + extras,
        in_specs=[vmem] * len(inputs) + moves_specs(moves, "inputs"),
        out_specs=[vmem] * len(outputs) + moves_specs(moves, "outputs"),
        scratch_shapes=scratch,
        compiler_params=pltpu.CompilerParams(
            collective_id=collective_id, has_side_effects=True, vmem_limit_bytes=limit << 20
        ),
        cost_estimate=pl.CostEstimate(flops=10_000_000, bytes_accessed=200_000_000, transcendentals=0),
    )(*inputs, *moved)


def gather_blocks(payload, moves, collective_id):
    def middle(total, rows, j, ins, outs):
        return ins[0][rows, :]

    shape = (2 * LINE,) + payload.shape
    return line_call(collective_id, 8, middle, [payload], [(shape, jnp.bfloat16)], False, True, moves, 58)


def attention_block(parts, hidden, gain, moves, collective_id):
    def middle(total, rows, j, ins, outs):
        outs[1][rows, :] = total
        resid = ins[1][rows, :].astype(jnp.float32) + total * rms_scale(total) * ins[2][...]
        outs[2][rows, :] = resid
        return resid

    shape = hidden.shape
    return line_call(
        collective_id, 8, middle, [parts, hidden, gain],
        [(parts.shape, jnp.bfloat16), (shape, jnp.float32), (shape, jnp.float32)], True, True, moves,
    )


def add_rows(ref, values, j):
    folded = jnp.sum(values.reshape(values.shape[0] // 8, 8, values.shape[1]), axis=0)

    @pl.when(j == 0)
    def _():
        ref[...] = folded

    @pl.when(j > 0)
    def _():
        ref[...] += folded


def ffn_block(parts, resid, cotangent, gain, collective_id):
    def middle(total, rows, j, ins, outs):
        scale = rms_scale(total)
        normed = total * scale
        grad = ins[2][rows, :].astype(jnp.float32)
        gains = ins[3][...]
        outs[1][rows, :] = (ins[1][rows, :] + normed * gains).astype(jnp.bfloat16)
        add_rows(outs[2], grad * normed, j)
        return rms_back(grad * gains, normed, scale)

    shape = resid.shape
    return line_call(
        collective_id, 8, middle, [parts, resid, cotangent, gain],
        [(parts.shape, jnp.bfloat16), (shape, jnp.bfloat16), ((8, shape[1]), jnp.float32)], True, True,
    )


def back_block(parts, cotangent, attn_out, gain, moves, collective_id):
    def middle(total, rows, j, ins, outs):
        d_resid = ins[1][rows, :].astype(jnp.float32) + total
        outs[1][rows, :] = d_resid
        attn = ins[2][rows, :]
        scale = rms_scale(attn)
        normed = attn * scale
        add_rows(outs[2], d_resid * normed, j)
        return rms_back(d_resid * ins[3][...], normed, scale)

    shape = cotangent.shape
    return line_call(
        collective_id, 8, middle, [parts, cotangent, attn_out, gain],
        [(parts.shape, jnp.bfloat16), (shape, jnp.float32), ((8, shape[1]), jnp.float32)], True, True, moves, 56,
    )


def last_block(parts, d_resid, moves, collective_id):
    def middle(total, rows, j, ins, outs):
        outs[0][rows, :] = (ins[1][rows, :] + total).astype(jnp.bfloat16)

    return line_call(
        collective_id, 8, middle, [parts, d_resid], [(d_resid.shape, jnp.bfloat16)], True, False, moves, 48
    )


def line_exchange(line, mine, came, sends, recvs):
    def copy(p):
        place, core = line.piece(p, 1)
        return remote(mine, came.at[p], sends.at[p], recvs.at[p], line.at(place, line.pair, core))

    for p in range(1, 2 * LINE):
        copy(p).start()
    total = mine[...]
    for p in range(1, 2 * LINE):
        copy(p).wait_recv()
        total = total + came[p]
    for p in range(1, 2 * LINE):
        copy(p).wait_send()
    return total


def spot(head, index):
    start = (3 * head + index) * HEAD_DIM
    return slice(start, start + HEAD_DIM)


def turn_tables(turns):
    half = turns.shape[1] // 2
    swapped = pltpu.roll(turns, half, 1)
    first = lax.broadcasted_iota(jnp.int32, turns.shape, 1) < half
    return jnp.where(first, turns, swapped), jnp.where(first, -swapped, turns)


def as_row(column):
    return jnp.broadcast_to(column, (column.shape[0], column.shape[0])).T[0:1, :]


def as_columns(row):
    return jnp.broadcast_to(row, (row.shape[1], row.shape[1])).T


def dot(left, right, left_dim, right_dim):
    return lax.dot_general(
        left, right, (((left_dim,), (right_dim,)), ((), ())), preferred_element_type=jnp.float32
    )


def heads_call(collective_id, body, inputs, outputs, scratch, rows, moves):
    blocks, length = 2 * LINE, HEAD_DIM
    scratch = [
        pltpu.VMEM((rows, length), jnp.float32),
        pltpu.VMEM((blocks, rows, length), jnp.float32),
        pltpu.SemaphoreType.DMA((blocks,)),
        pltpu.SemaphoreType.DMA((blocks,)),
    ] + scratch
    n_scratch = len(scratch)
    moved = [values for move in moves for values in move.inputs]
    extras = [shape for move in moves for shape in move.outputs]

    def kernel(*refs):
        refs = list(refs)
        ins = take_from(refs, len(inputs))
        given = [take_from(refs, len(move.inputs)) for move in moves]
        outs = take_from(refs, len(outputs))
        extra = [take_from(refs, len(move.outputs)) for move in moves]
        rest = take_from(refs, n_scratch)
        line = Line()
        for move, sources, targets in zip(moves, given, extra):
            move.bind(line, sources, targets, take_from(refs, len(move.semaphores) + len(move.buffers)))
        line.meet(True)
        passed = [0]

        def tick():
            for move in moves:
                move.slot(passed[0])
            passed[0] += 1

        body(line, ins, outs, rest, tick)
        while passed[0] < max([move.slots for move in moves] + [0]):
            tick()
        for move in moves:
            move.finish()

    vmem = pl.BlockSpec(memory_space=pltpu.VMEM)
    return pl.pallas_call(
        kernel,
        out_shape=[jax.ShapeDtypeStruct(shape, kind) for shape, kind in outputs] + extras,
        in_specs=[vmem] * len(inputs) + moves_specs(moves, "inputs"),
        out_specs=[vmem] * len(outputs) + moves_specs(moves, "outputs"),
        scratch_shapes=scratch + moves_scratch(moves),
        compiler_params=pltpu.CompilerParams(
            collective_id=collective_id, has_side_effects=True, vmem_limit_bytes=44 << 20
        ),
        cost_estimate=pl.CostEstimate(flops=10_000_000, bytes_accessed=80_000_000, transcendentals=0),
    )(*inputs, *moved)


def attend(tokens, full_qkv, turns, bias, gains, weight, moves, collective_id):
    blocks, length = bias.shape[:2]
    width = full_qkv.shape[1] // 3
    heads = width // HEAD_DIM
    model_width = weight.shape[1]
    low = jnp.bfloat16

    def body(line, ins, outs, scratch, tick):
        tokens, full_qkv, turns, bias, gains, weight = ins
        parts, lows, probs, mixed, squares, raw = outs
        mine, came, sends, recvs = scratch

        def squares_of(two, carry):
            both = pl.ds(2 * two, 2)
            product = dot(tokens[both].reshape(2 * length, model_width), full_qkv[...], 1, 0)
            raw[both] = product.reshape(2, length, 3 * width)
            for b, index in ((2 * two, 0), (2 * two, 1), (2 * two + 1, 0), (2 * two + 1, 1)):
                total = jnp.zeros((length, 1), jnp.float32)
                for h in range(heads):
                    values = raw[b, :length, spot(h, index)]
                    total = total + jnp.sum(values * values, axis=1, keepdims=True)
                mine[pl.ds(index * blocks + b, 1), :] = as_row(total)
            return carry

        tick()
        for part in range(LINE):
            squares_of(part, 0)
            tick()
        squares[...] = line_exchange(line, mine, came, sends, recvs)
        tick()

        def block(b, carry):
            scales = [
                lax.rsqrt(as_columns(squares[pl.ds(index * blocks + b, 1), :]) / model_width + epsilon)
                for index in range(2)
            ]
            cos, sin = turn_tables(turns[b])
            for h in range(heads):
                here = slice(h * HEAD_DIM, (h + 1) * HEAD_DIM)
                turned = []
                for index in range(2):
                    there = spot(h, index)
                    normed = raw[b, :length, there] * scales[index] * gains[index : index + 1, here]
                    turned.append((normed * cos + pltpu.roll(normed, HEAD_DIM // 2, 1) * sin).astype(low))
                    lows[b, :, there] = turned[index]
                there = spot(h, 2)
                value = raw[b, :length, there].astype(low)
                lows[b, :, there] = value
                scores = dot(turned[0], turned[1], 1, 1) * HEAD_DIM**-0.5 + bias[b]
                powers = jnp.exp(scores - jnp.max(scores, axis=1, keepdims=True))
                prob = powers / jnp.sum(powers, axis=1, keepdims=True)
                probs[b, h] = prob
                mixed[b, :, here] = dot(prob.astype(low), value, 1, 0).astype(low)
            return carry

        for part in range(LINE):
            lax.fori_loop(2 * part, 2 * part + 2, block, 0)
            both = pl.ds(2 * part, 2)
            product = dot(mixed[both].reshape(2 * length, width), weight[...], 1, 0)
            parts[both] = product.astype(low).reshape(2, length, model_width)
            tick()

    return heads_call(
        collective_id,
        body,
        [tokens, full_qkv, turns, bias, gains, weight],
        [
            ((blocks, length, model_width), low),
            ((blocks, length, 3 * width), low),
            ((blocks, heads, length, length), jnp.float32),
            ((blocks, length, width), low),
            ((2 * blocks, length), jnp.float32),
            ((blocks, length, 3 * width), jnp.float32),
        ],
        [],
        2 * blocks,
        moves,
    )


def attend_back(d_attn, weight, raw, turns, gains, lows, probs, squares, wide_terms, full_qkv, moves, collective_id):
    blocks, length = raw.shape[:2]
    width = raw.shape[2] // 3
    heads = width // HEAD_DIM
    model_width = weight.shape[1]
    low = jnp.bfloat16

    def body(line, ins, outs, scratch, tick):
        d_attn, weight, raw, turns, gains, lows, probs, squares = ins[:8]
        d_low, wide, parts = outs
        full_qkv = ins[10]
        mine, came, sends, recvs, upstream, unit, d_mixed, terms = scratch
        tick()
        terms[...] = jnp.zeros_like(terms)
        for which in range(2):
            total = jnp.sum(ins[8 + which][...], axis=0, keepdims=True)
            for index in range(model_width // length):
                row = 2 * blocks + which * (model_width // length) + index
                mine[row : row + 1, :] = total[:, index * length : (index + 1) * length]

        def block(b, carry):
            scales = [
                lax.rsqrt(as_columns(squares[pl.ds(index * blocks + b, 1), :]) / model_width + epsilon)
                for index in range(2)
            ]
            cos, sin = turn_tables(turns[b])
            means = [jnp.zeros((length, 1), jnp.float32)] * 2
            for h in range(heads):
                here = slice(h * HEAD_DIM, (h + 1) * HEAD_DIM)
                places = [spot(h, index) for index in range(3)]
                query, key, value = [lows[b, :, there] for there in places]
                prob = probs[b, h]
                d_out = d_mixed[b, :, here]
                d_low[b, :length, places[2]] = dot(prob.astype(low), d_out, 0, 0).astype(low)
                d_prob = dot(d_out, value, 1, 1)
                d_scores = (
                    prob * (d_prob - jnp.sum(d_prob * prob, axis=1, keepdims=True))
                ).astype(low)
                turned = [dot(d_scores, key, 1, 0), dot(d_scores, query, 0, 0)]
                for index in range(2):
                    d_rot = turned[index] * HEAD_DIM**-0.5
                    d_normed = d_rot * cos - pltpu.roll(d_rot, HEAD_DIM // 2, 1) * sin
                    units = raw[b, :length, places[index]] * scales[index]
                    ups = d_normed * gains[index : index + 1, here]
                    folded = (d_normed * units).reshape(length // 8, 8, HEAD_DIM)
                    side = slice((index * heads + h) * HEAD_DIM, (index * heads + h + 1) * HEAD_DIM)
                    terms[:, side] += jnp.sum(folded, axis=0)
                    upstream[b, :, side] = ups
                    unit[b, :, side] = units
                    means[index] = means[index] + jnp.sum(ups * units, axis=1, keepdims=True)
            for index in range(2):
                mine[pl.ds(index * blocks + b, 1), :] = as_row(means[index])
            return carry

        def mix(two, carry):
            both = pl.ds(2 * two, 2)
            product = dot(d_attn[both].reshape(2 * length, model_width), weight[...], 1, 1)
            d_mixed[both] = product.astype(low).reshape(2, length, width)
            return carry

        lax.fori_loop(0, LINE, mix, 0)
        lax.fori_loop(0, blocks, block, 0)
        mine[...] = line_exchange(line, mine, came, sends, recvs)
        count = 2 * model_width // length
        wide[:count, :] = mine[2 * blocks :, :]
        wide[count:, :] = jnp.zeros((8, length), jnp.float32)
        for index in range(2 * heads):
            sums = jnp.sum(terms[:, index * length : (index + 1) * length], axis=0, keepdims=True)
            wide[count + index : count + index + 1, :] = sums

        def last(b, carry):
            for index in range(2):
                scale = lax.rsqrt(
                    as_columns(squares[pl.ds(index * blocks + b, 1), :]) / model_width + epsilon
                )
                mean = as_columns(mine[pl.ds(index * blocks + b, 1), :]) / model_width
                for h in range(heads):
                    side = slice((index * heads + h) * HEAD_DIM, (index * heads + h + 1) * HEAD_DIM)
                    d_low[b, :length, spot(h, index)] = (
                        scale * (upstream[b, :, side] - unit[b, :, side] * mean)
                    ).astype(low)
            return carry

        def lasts(two, carry):
            lax.fori_loop(2 * two, 2 * two + 2, last, 0)
            both = pl.ds(2 * two, 2)
            product = dot(d_low[both].reshape(2 * length, 3 * width), full_qkv[...], 1, 1)
            parts[both] = product.astype(low).reshape(2, length, model_width)
            return carry

        lax.fori_loop(0, LINE, lasts, 0)

    return heads_call(
        collective_id,
        body,
        [d_attn, weight, raw, turns, gains, lows, probs, squares, *wide_terms, full_qkv],
        [
            (raw.shape, low),
            ((2 * model_width // length + 8, length), jnp.float32),
            ((blocks, length, model_width), low),
        ],
        [pltpu.VMEM((blocks, length, 2 * width), jnp.float32) for _ in range(2)]
        + [pltpu.VMEM((blocks, length, width), low), pltpu.VMEM((8, 2 * width), jnp.float32)],
        2 * blocks + 2 * model_width // length,
        moves,
    )


def on_device(
    hidden_in,
    segments,
    w_query,
    w_key,
    w_value,
    w_output,
    query_gain,
    key_gain,
    attn_gain,
    w_gate,
    w_up,
    w_down,
    ffn_gain,
    out_cotangent,
):
    length, model_width = hidden_in.shape
    blocks = 2 * LINE
    heads = HEADS // blocks
    factor = HEAD_DIM ** (-0.5)
    pair = (lax.axis_index("shard") // 2) % 2
    f32 = jnp.float32

    extra = jnp.stack([query_gain, key_gain, attn_gain, ffn_gain, segments[0].astype(jnp.bfloat16)])
    payload, extras, full_qkv, full_output = gather_blocks(
        hidden_in,
        [
            Share(jnp.pad(extra, ((0, 11), (0, 0)))),
            Spread(w_query, w_key, w_value),
            Stack(w_output, 2, 1),
        ],
        0,
    )
    tokens = payload.reshape(-1, model_width)
    docs = extras[:, 4].astype(jnp.int32)
    gains = extras[:, :4].reshape(LINE, 2, 4, length)
    gains = jnp.stack(by_pair(pair, gains, pair_swap(gains)), axis=1)
    gains = jnp.moveaxis(gains, 3, 0).reshape(4, 1, model_width).astype(f32)
    gain_attn, gain_ffn = gains[2], gains[3]
    width = heads * HEAD_DIM
    head_gains = gather_rows(jnp.stack([query_gain, key_gain])[None], pair).astype(f32)
    head_gains = head_gains.transpose(1, 0, 2).reshape(2, width)

    earlier = jnp.sum((docs[:, None, :] < docs[:, :, None]).astype(jnp.int32), axis=2)
    positions = jnp.arange(length, dtype=jnp.int32)[None] - earlier
    half_dim = HEAD_DIM // 2
    inverse = jnp.exp(
        jnp.arange(half_dim, dtype=f32) * (-2.0 * math.log(theta_base) / HEAD_DIM)
    )
    angles = positions.astype(f32)[:, :, None] * inverse[None, None, :]
    turns = jnp.cos(jnp.concatenate([angles, angles - 0.5 * math.pi], axis=-1))
    token_idx = jnp.arange(length)
    allowed = (docs[:, :, None] == docs[:, None, :]) & (
        token_idx[:, None] >= token_idx[None, :]
    )[None]
    bias = jnp.where(allowed, 0.0, neg_fill)

    def to_blocks(values):
        return values.astype(jnp.bfloat16).reshape(blocks, -1, model_width)

    attn_parts, lows, probs, mixed_low, squares, raw, full_gate, up_pieces = attend(
        payload, full_qkv, turns, bias, head_gains, full_output, [Spread(w_gate, plan=Spread.BESIDE_HEADS), SpreadLine(w_up, 5)], 6
    )
    mixed_low = mixed_low.reshape(blocks * length, width)
    resid_low, attn_out, resid, full_up, full_down = attention_block(
        attn_parts,
        hidden_in,
        gain_attn,
        [SpreadOver(up_pieces), Stack(w_down, 8, 3)],
        1,
    )
    resid_low = resid_low.reshape(blocks * length, model_width)

    gate_proj = jnp.dot(resid_low, full_gate, preferred_element_type=f32)
    up_proj = jnp.dot(resid_low, full_up, preferred_element_type=f32)
    gate_sig = jax.nn.sigmoid(gate_proj)
    hidden_ffn = (gate_proj * gate_sig * up_proj).astype(jnp.bfloat16)
    d_ffn_low, hidden_out, ffn_gain_term = ffn_block(
        to_blocks(jnp.dot(hidden_ffn, full_down, preferred_element_type=f32)),
        resid,
        out_cotangent,
        gain_ffn,
        2,
    )
    d_ffn_low = d_ffn_low.reshape(blocks * length, model_width)

    d_hidden_ffn = dot_back(d_ffn_low, full_down)
    d_gate_low = (d_hidden_ffn * up_proj * gate_sig * (1.0 + gate_proj * (1.0 - gate_sig))).astype(
        jnp.bfloat16
    )
    d_up_low = (d_hidden_ffn * gate_proj * gate_sig).astype(jnp.bfloat16)
    ff_rows = w_down.shape[0]
    d_attn_low, d_resid, attn_gain_term, gate_sum, up_sum, down_part = back_block(
        to_blocks(dot_back(d_gate_low, full_gate) + dot_back(d_up_low, full_up)),
        out_cotangent,
        attn_out,
        gain_attn,
        [
            Reduce(resid_low, [d_gate_low, d_up_low], "partner"),
            PairSum(hidden_ffn, d_ffn_low, 4, 13),
        ],
        3,
    )

    d_qkv, gain_sums, back_parts, there_first = attend_back(
        d_attn_low, full_output, raw, turns, head_gains, lows, probs, squares,
        [attn_gain_term, ffn_gain_term], full_qkv, [Swap(down_part, 0, ff_rows // 4)], 7,
    )
    d_attn_low = d_attn_low.reshape(blocks * length, model_width)
    qkv_sum = Reduce(tokens, [d_qkv.reshape(-1, 3 * width)], "across")
    output_sum = PairSum(mixed_low, d_attn_low, 1, 5)
    hidden_grad, _, output_part, ffn_total, there_second, qkv_total, there_output, *there_gains = last_block(
        back_parts,
        d_resid,
        [
            qkv_sum,
            output_sum,
            Deal([gate_sum, up_sum], 1),
            Swap(down_part, ff_rows // 4, 3 * ff_rows // 4, 2),
            Deal(qkv_sum, 3, 9),
            Swap(output_sum, 0, length, 8),
            Four(gain_sums),
        ],
        4,
    )

    def total_of(first, second):
        return first.astype(f32) + second.astype(f32)

    grad_query, grad_key, grad_value = jnp.split(qkv_total.astype(f32), 3, axis=1)
    grad_gate, grad_up = jnp.split(ffn_total.astype(f32), 2, axis=1)
    grad_output = total_of(output_part, there_output)
    grad_down = total_of(down_part, jnp.concatenate([there_first, there_second]))
    gain_sums = (gain_sums + there_gains[0]) + (there_gains[1] + there_gains[2])
    wide_grads = lax.dynamic_index_in_dim(
        gain_sums[:32].reshape(2, 16, length), lax.axis_index("shard"), 1, keepdims=False
    )
    head_grads = lax.dynamic_index_in_dim(gain_sums[32:36].reshape(2, 2, length), pair, 1, keepdims=False)
    gain_grads = jnp.concatenate([head_grads, wide_grads])
    return (
        hidden_out,
        hidden_grad,
        grad_query,
        grad_key,
        grad_value,
        grad_output,
        gain_grads[0],
        gain_grads[1],
        gain_grads[2],
        grad_gate,
        grad_up,
        grad_down,
        gain_grads[3],
    )


def solution(mesh):
    placed = (
        P(("rep", "shard"), None),
        P(("rep", "shard"), None),
        P("shard", None),
        P("shard", None),
        P("shard", None),
        P("shard", None),
        P("shard"),
        P("shard"),
        P("shard"),
        P("shard", None),
        P("shard", None),
        P("shard", None),
        P("shard"),
        P(("rep", "shard"), None),
    )
    return jax.shard_map(
        on_device if mesh.shape["shard"] == 16 else on_device_general,
        mesh=mesh,
        in_specs=placed,
        out_specs=(
            P(("rep", "shard"), None),
            P(("rep", "shard"), None),
            P("shard", None),
            P("shard", None),
            P("shard", None),
            P("shard", None),
            P("shard"),
            P("shard"),
            P("shard"),
            P("shard", None),
            P("shard", None),
            P("shard", None),
            P("shard"),
        ),
        check_vma=False,
    )
```
